32 devices in a mesh: fsdp: 4 (over y, core), ctx: 4 (over z), tp: 2 (over x).
Axes of the slice: x: 2, y: 2, z: 4, core: 2. Of those that a mesh axis runs over, the one named last changes fastest.
Arguments:
- hidden_in: bfloat16 [2, 4, 1024, 2048], P(None, 'fsdp', ('ctx', 'tp')), may hold values from -6 to 6
- cotangent: bfloat16 [2, 4, 1024, 2048], P(None, 'fsdp', ('ctx', 'tp')), may hold values from -6 to 6
- block_ids: int32 [2, 4, 1024], P(None, 'fsdp'), may hold values from 0 to 7, never falling along the last dimension, each value on 1 to 256 neighbouring positions
- positions: int32 [2, 4, 1024], P(None, 'fsdp', 'ctx'), may hold values from 0 to 5115, as said below
- attn_gain: bfloat16 [2048], P(('fsdp', 'ctx')), may hold values from 0.5 to 1.5
- wqkv: bfloat16 [2048, 4096], P(('fsdp', 'ctx'), 'tp'), may hold values from -0.125 to 0.125
- wo: bfloat16 [2048, 2048], P('tp', ('fsdp', 'ctx')), may hold values from -0.75 to 0.75
- ffn_gain: bfloat16 [2048], P(('fsdp', 'ctx')), may hold values from 0.5 to 1.5
- w_gate: bfloat16 [2048, 8192], P(('fsdp', 'ctx'), 'tp'), may hold values from -0.125 to 0.125
- w_up: bfloat16 [2048, 8192], P(('fsdp', 'ctx'), 'tp'), may hold values from -0.125 to 0.125
- w_down: bfloat16 [8192, 2048], P('tp', ('fsdp', 'ctx')), may hold values from -0.09375 to 0.09375
Outputs:
- hidden_out: bfloat16 [2, 4, 1024, 2048], P(None, 'fsdp', ('ctx', 'tp'))
- grad_in: bfloat16 [2, 4, 1024, 2048], P(None, 'fsdp', ('ctx', 'tp'))
- grad_attn_gain: float32 [2048], P(('fsdp', 'ctx'))
- grad_wqkv: float32 [2048, 4096], P(('fsdp', 'ctx'), 'tp')
- grad_wo: float32 [2048, 2048], P('tp', ('fsdp', 'ctx'))
- grad_ffn_gain: float32 [2048], P(('fsdp', 'ctx'))
- grad_gate: float32 [2048, 8192], P(('fsdp', 'ctx'), 'tp')
- grad_up: float32 [2048, 8192], P(('fsdp', 'ctx'), 'tp')
- grad_down: float32 [8192, 2048], P('tp', ('fsdp', 'ctx'))
The draws below stay inside these ranges and needn't reach their ends.
Inputs may be any that keep to these rules, and one draw needn't show every extreme that they name: `block_ids`: within each sequence block ids never fall and each block holds 1 to 256 tokens. Within each sequence positions rise from token to token by a step of 1 to 4; a sequence starts at a position from 0 to 1023.
All inputs are finite; a program needn't handle non-finite values.
Results may differ from the reference program's by a relative error of at most 0.02.
Values may be sent and summed in bfloat16 or wider, within the bound.
A program may use at most 192 MiB of HBM per device.

```python
import math
import jax
import jax.numpy as jnp
import numpy as np
from jax import lax

D = 2048
HEADS = 16
KV_HEADS = 8
HEAD_DIM = 128
FF = 8192
BLOCK = 256
MICRO = 2
SEQS = 4
LENGTH = 1024


def draw_positions(key, part):
    key = jax.random.fold_in(key, 7)
    key_first, key_second, key_third, key_fourth = jax.random.split(key, 4)
    seq_total = MICRO * SEQS
    starts = jax.random.randint(key_first, (seq_total,), 1, LENGTH - 1)
    low_slot = jax.random.randint(key_second, (), 0, seq_total)
    high_slot = (low_slot + 1 + jax.random.randint(key_third, (), 0, seq_total - 1)) % seq_total
    slots = jnp.arange(seq_total, dtype=jnp.int32)
    starts = jnp.where(slots == low_slot, 0, jnp.where(slots == high_slot, LENGTH - 1, starts))
    strides = jax.random.randint(key_fourth, (seq_total, LENGTH - 1), 1, 5)
    strides = jnp.where((slots == high_slot)[:, None], 4, strides)
    offsets = jnp.concatenate([jnp.zeros((seq_total, 1), jnp.int32), jnp.cumsum(strides, axis=1).astype(jnp.int32)], axis=1)
    return (starts[:, None] + offsets).reshape(MICRO, SEQS, LENGTH).astype(jnp.int32)


def spiked(values, rng, source, target, blocks, factor):
    owner, partner = [(jnp.arange(values.shape[axis_at]) // (values.shape[axis_at] // blocks)).reshape([-1 if axis == axis_at else 1 for axis in range(values.ndim)]) for axis_at in (source, target)]
    chosen = jax.random.permutation(rng, blocks)[partner]
    strong = (owner == chosen) | (owner == (partner + blocks // 2) % blocks)
    return jnp.where(strong, factor * values, values)


def level_of(key, dims, shards, smallest, top_value):
    factor_of = 1.0
    for axis_at, shards_of in shards:
        draws = jax.random.uniform(jax.random.fold_in(jax.random.fold_in(key, 6), axis_at), (shards_of,), jnp.float32, smallest / len(shards), top_value / len(shards))
        factor_of = factor_of * jnp.repeat(jnp.exp(draws), dims[axis_at] // shards_of).reshape((-1,) + (1,) * (len(dims) - 1 - axis_at))
    return factor_of


def length_profile(count, total, bound, slope):
    loads = [(1 << 20) // math.isqrt(rank ** slope) + 1 for rank in range(2, count + 1)]
    surplus, given = total - bound - (count - 1), [1] * (count - 1)
    while surplus > 0:
        movable = [i for i in range(count - 1) if given[i] < bound]
        whole, left = sum([loads[i] for i in movable]), surplus
        for i in movable:
            addition = min(bound - given[i], max(1, left * loads[i] // whole), surplus)
            given[i] = given[i] + addition
            surplus = surplus - addition
    return np.array([bound] + given)


def uneven(own_key, amount, total, bound, lean):
    if amount == 2:
        one = jax.random.randint(own_key, (), max(1, total - bound), min(bound, total - 1) + 1)
        return jnp.stack([one, total - one])
    lengths = jnp.asarray(length_profile(amount, total, bound, lean), jnp.int32)
    couples = (amount - 1) // 2
    source_of, sink = lengths[1:1 + 2 * couples:2], lengths[2:2 + 2 * couples:2]
    margin = jnp.minimum(source_of - 1, bound - sink)
    passed = jax.random.randint(jax.random.fold_in(own_key, 1), (couples,), 0, 1 << 20) % (margin + 1)
    lengths = lengths.at[1:1 + 2 * couples:2].set(source_of - passed).at[2:2 + 2 * couples:2].set(sink + passed)
    return lengths[jax.random.permutation(jax.random.fold_in(own_key, 2), amount)]


def scatter_about(stream_key, dims, spread, bound, pieces=(), held_as=jnp.bfloat16):
    entries = jax.random.normal(stream_key, dims, jnp.float32) * spread
    if len(pieces) > 0:
        entries = level_of(stream_key, dims, pieces, -0.22, 0.18) * entries
    return jnp.clip(entries, min=-bound, max=bound).astype(held_as)


def heavy_noise(stream_key, extent, scale, bound, pieces, heavy, kind=jnp.bfloat16):
    drawn = scale * jax.random.normal(stream_key, extent, jnp.float32)
    if pieces:
        drawn = drawn * level_of(stream_key, extent, pieces, -0.22, 0.18)
    return jnp.clip(spiked(drawn, jax.random.fold_in(stream_key, 3), *heavy), -bound, bound).astype(kind)


def setup_inputs(seed: int = 0) -> dict:
    streams_of = jax.random.split(jax.random.key(seed), 12)
    hidden_in = scatter_about(streams_of[0], (MICRO, SEQS, LENGTH, D), 1.0, 6.0, ((1, 4), (2, 8)))
    cotangent = heavy_noise(streams_of[1], (MICRO, SEQS, LENGTH, D), 1.0, 6.0, ((1, 4), (2, 8)), (1, 3, 4, 2.0))
    block_ids = jax.vmap(lambda own: jnp.searchsorted(jnp.cumsum(uneven(own, 2 * LENGTH // BLOCK, LENGTH, BLOCK, 0)), jnp.arange(LENGTH), side="right"))(jax.random.split(streams_of[2], MICRO * SEQS)).reshape((MICRO, SEQS, LENGTH)).astype(jnp.int32)
    positions = draw_positions(jax.random.fold_in(streams_of[11], 71), 0)
    attn_gain = jnp.clip(1.0 + 0.1 * jax.random.normal(streams_of[4], (D,), jnp.float32), 0.5, 1.5).astype(jnp.bfloat16)
    wqkv = scatter_about(streams_of[5], (D, (HEADS + 2 * KV_HEADS) * HEAD_DIM), D ** -0.5, 0.125, ((0, 16), (1, 2)))
    wo = scatter_about(streams_of[6], (HEADS * HEAD_DIM, D), (HEADS * HEAD_DIM // 32) ** -0.5, 0.75, ((0, 2), (1, 16)))
    ffn_gain = jnp.clip(1.0 + 0.1 * jax.random.normal(streams_of[7], (D,), jnp.float32), 0.5, 1.5).astype(jnp.bfloat16)
    w_gate = scatter_about(streams_of[8], (D, FF), D ** -0.5, 0.125, ((0, 16), (1, 2)))
    w_up = scatter_about(streams_of[9], (D, FF), D ** -0.5, 0.125, ((0, 16), (1, 2)))
    w_down = scatter_about(streams_of[10], (FF, D), (FF // 2) ** -0.5, 0.09375, ((0, 2), (1, 16)))
    return dict(hidden_in=hidden_in, cotangent=cotangent, block_ids=block_ids, positions=positions, attn_gain=attn_gain, wqkv=wqkv, wo=wo, ffn_gain=ffn_gain, w_gate=w_gate, w_up=w_up, w_down=w_down)


EPS = 1e-05
THETA = 1000000.0
MASKED = -1e+30
HIGH_ACCURACY = lax.Precision.HIGHEST

@jax.custom_vjp
def low(v):
    return lax.optimization_barrier(v.astype(jnp.bfloat16)).astype(jnp.float32)

@jax.custom_vjp
def low_back(v):
    return v

def low_keep(v):
    return (low(v), None)

def low_pass(kept, grad):
    return (grad,)

def back_keep(v):
    return (v, None)

def back_low(kept, grad):
    return (low(grad),)
low.defvjp(low_keep, low_pass)
low_back.defvjp(back_keep, back_low)

def rope_tables(position_ids):
    half_dim = HEAD_DIM // 2
    inverse = THETA ** (-(jnp.arange(half_dim, dtype=jnp.float32) * 2.0 / HEAD_DIM))
    angles = position_ids.astype(jnp.float32)[..., None] * inverse
    angles = jnp.concatenate([angles, angles], axis=-1)
    return (jnp.cos(angles), jnp.sin(angles))

def turned(values):
    half_dim = values.shape[-1] // 2
    return jnp.concatenate([-values[..., half_dim:], values[..., :half_dim]], axis=-1)

def product(left, right):
    return jnp.dot(left, right, precision=HIGH_ACCURACY)

def block_layer(stream, attn_gain, wqkv, wo, ffn_gain, w_gate, w_up, w_down, seq_ids, cos_table, sin_table):
    length = stream.shape[0]
    group_size = HEADS // KV_HEADS
    factor_one = lax.rsqrt(lax.optimization_barrier(jnp.mean(stream * stream, axis=-1, keepdims=True)) + EPS)
    attention_input = low(stream * factor_one * attn_gain)
    projection_output = low_back(product(attention_input, wqkv)).reshape(length, KV_HEADS, group_size + 2, HEAD_DIM)
    cos_heads = cos_table[:, None, None]
    sin_heads = sin_table[:, None, None]
    cos_keys = cos_table[:, None]
    sin_keys = sin_table[:, None]
    query_part = projection_output[:, :, :group_size]
    key_part = projection_output[:, :, group_size]
    query_rows_local = low(query_part * cos_heads + turned(query_part) * sin_heads)
    key_matrix_rows = low(key_part * cos_keys + turned(key_part) * sin_keys)
    value_matrix_rows = low(projection_output[:, :, group_size + 1])
    unnormalized_scores = low_back(jnp.einsum('bjxo,ajo->jxba', query_rows_local, key_matrix_rows, precision=HIGH_ACCURACY))
    allowed = seq_ids[None, :] <= seq_ids[:, None]
    scores = jnp.where(allowed, unnormalized_scores * HEAD_DIM ** (-0.5), MASKED)
    attention_probability = low(jax.nn.softmax(scores, axis=-1))
    combined_head_output = jnp.einsum('rpab,brw->arpw', attention_probability, value_matrix_rows, precision=HIGH_ACCURACY)
    combined_head_output = low(low_back(combined_head_output.reshape(length, HEADS * HEAD_DIM)))
    stream_mid = stream + low_back(product(combined_head_output, wo))
    factor_two = lax.rsqrt(lax.optimization_barrier(jnp.mean(stream_mid * stream_mid, axis=-1, keepdims=True)) + EPS)
    feedforward_input = low(stream_mid * factor_two * ffn_gain)
    gate_preactivation = low_back(product(feedforward_input, w_gate))
    up_preactivation = low_back(product(feedforward_input, w_up))
    hidden_activation = low(jax.nn.silu(gate_preactivation) * up_preactivation)
    return stream_mid + low_back(product(hidden_activation, w_down))

def reference(hidden_in, cotangent, block_ids, positions, attn_gain, wqkv, wo, ffn_gain, w_gate, w_up, w_down):
    weight_list = tuple((member.astype(jnp.float32) for member in (attn_gain, wqkv, wo, ffn_gain, w_gate, w_up, w_down)))
    seq_total = MICRO * SEQS
    streams = hidden_in.reshape(seq_total, LENGTH, D)
    out_grads = cotangent.reshape(seq_total, LENGTH, D)
    seq_ids = block_ids.reshape(seq_total, LENGTH)
    position_ids = positions.reshape(seq_total, LENGTH)

    def one_sequence(totals, member):
        stream, grad_out, ids_row, pos_row = member
        cos_table, sin_table = rope_tables(pos_row)

        def forward(stream_in, *params):
            return block_layer(stream_in, *params, ids_row, cos_table, sin_table)
        result, pullback = jax.vjp(forward, stream.astype(jnp.float32), *weight_list)
        gradients = pullback(grad_out.astype(jnp.float32))
        totals = tuple((total + grad for total, grad in zip(totals, gradients[1:])))
        return (totals, (result.astype(jnp.bfloat16), gradients[0].astype(jnp.bfloat16)))
    initial = tuple((jnp.zeros(member.shape, jnp.float32) for member in weight_list))
    totals, (out_rows, grad_rows) = lax.scan(one_sequence, initial, (streams, out_grads, seq_ids, position_ids))
    out_shape = (MICRO, SEQS, LENGTH, D)
    return (out_rows.reshape(out_shape), grad_rows.reshape(out_shape), totals[0], totals[1], totals[2], totals[3], totals[4], totals[5], totals[6])
```

```python
import functools

import jax
import jax.numpy as jnp
from jax import lax
from jax.sharding import PartitionSpec as P
from jax.experimental import pallas as pl
from jax.experimental.pallas import tpu as pltpu

HEADS = 16
KV_HEADS = 8
HEAD_DIM = 128


EPS = 1e-05
THETA = 1000000.0
MASKED = -1e30


def rope_tables(position_ids):
    half_dim = HEAD_DIM // 2
    inverse = THETA ** (-(jnp.arange(half_dim, dtype=jnp.float32) * 2.0 / HEAD_DIM))
    angles = position_ids.astype(jnp.float32)[..., None] * inverse
    angles = jnp.concatenate([angles, angles], axis=-1)
    return (jnp.cos(angles), jnp.sin(angles))


def turned(values):
    half_dim = values.shape[-1] // 2
    return jnp.concatenate([-values[..., half_dim:], values[..., :half_dim]], axis=-1)


def turned_back(values):
    half_dim = values.shape[-1] // 2
    return jnp.concatenate([values[..., half_dim:], -values[..., :half_dim]], axis=-1)


def norm_rows(stream, gain_row):
    factor = lax.rsqrt(jnp.mean(stream * stream, axis=-1, keepdims=True) + EPS)
    normed = stream * factor
    return (normed, factor, (normed * gain_row).astype(jnp.bfloat16))


def groups_of(fsdp, inner):
    near = [[high * inner + low for low in range(inner)] for high in range(fsdp // inner)]
    far = [[high * inner + low for high in range(fsdp // inner)] for low in range(inner)]
    return near, far


def general_body(
    hidden_in, cotangent, block_ids, positions, attn_gain, wqkv, wo, ffn_gain, w_gate, w_up, w_down
):
    fsdp, ctx, tp = lax.axis_size("fsdp"), lax.axis_size("ctx"), lax.axis_size("tp")
    inner = KV_HEADS // tp
    outer = fsdp // inner
    near, far = groups_of(fsdp, inner)
    micro, _, rows, width = hidden_in.shape
    score_scale = HEAD_DIM ** (-0.5)
    f_at, c_at = lax.axis_index("fsdp"), lax.axis_index("ctx")
    swap = [
        ((high * inner + low) * ctx + c, (high * inner + c) * ctx + low)
        for high in range(outer)
        for low in range(inner)
        for c in range(ctx)
    ]

    def rehome(array):
        return lax.ppermute(array, ("fsdp", "ctx"), swap)

    def trade(pieces):
        return lax.all_to_all(pieces, "fsdp", 0, 0, axis_index_groups=near)

    def spread(block):
        both = lax.all_gather(block, "tp")
        return lax.all_gather(both, "fsdp", axis_index_groups=near)

    def fold(parts):
        half = lax.psum_scatter(
            parts.astype(jnp.bfloat16), "fsdp", scatter_dimension=0, axis_index_groups=near
        )
        return lax.psum_scatter(half, "tp", scatter_dimension=0).astype(jnp.float32)

    def gather_levels(pieces):
        up = lax.all_gather(pieces, "ctx")
        if outer == 1:
            return up[None]
        return lax.all_gather(up, "fsdp", axis_index_groups=far)

    def scatter_levels(pieces):
        if outer == 1:
            pieces = pieces[0]
        else:
            pieces = lax.psum_scatter(pieces, "fsdp", scatter_dimension=0, axis_index_groups=far)
        return lax.psum_scatter(pieces, "ctx", scatter_dimension=0)

    def fetch_columns(shard):
        block, cols = shard.shape
        pieces = trade(shard.reshape(block, inner, cols // inner).transpose(1, 0, 2))
        whole = gather_levels(pieces).transpose(0, 2, 1, 3, 4)
        return whole.reshape(-1, cols // inner)

    def fetch_rows(shard):
        length, block = shard.shape
        pieces = trade(shard.reshape(inner, length // inner, block))
        whole = gather_levels(pieces).transpose(3, 0, 2, 1, 4)
        return whole.reshape(length // inner, -1)

    def return_columns(grad):
        total, cols = grad.shape
        grad = grad.astype(jnp.bfloat16).reshape(outer, inner, ctx, -1, cols)
        mine = trade(scatter_levels(grad.transpose(0, 2, 1, 3, 4)))
        return mine.transpose(1, 0, 2).reshape(mine.shape[1], -1).astype(jnp.float32)

    def return_rows(grad):
        length, total = grad.shape
        grad = grad.astype(jnp.bfloat16).reshape(length, outer, inner, ctx, -1)
        mine = trade(scatter_levels(grad.transpose(1, 3, 2, 0, 4)))
        return mine.reshape(inner * length, -1).astype(jnp.float32)

    def dot(left, right, dims):
        return lax.dot_general(left, right, (dims, ((), ())), preferred_element_type=jnp.float32)

    gains = lax.all_gather(jnp.stack([attn_gain, ffn_gain]), ("fsdp", "ctx"))
    gain_attn = gains[:, 0].reshape(-1).astype(jnp.float32)
    gain_ffn = gains[:, 1].reshape(-1).astype(jnp.float32)
    span = positions.shape[2]
    ids_here = lax.dynamic_slice_in_dim(block_ids[:, 0], c_at * span, span, 1)
    marks = lax.all_gather(jnp.stack([positions[:, 0], ids_here]), ("fsdp", "ctx"))
    my_seq = f_at // inner * inner + c_at
    marks = lax.dynamic_slice_in_dim(marks, my_seq * ctx, ctx, 0)
    marks = marks.transpose(1, 2, 0, 3).reshape(2, micro, ctx * span)
    pos, ids = marks[0], marks[1]

    weight_qkv = fetch_columns(wqkv)
    weight_out = fetch_rows(wo)
    weight_gate = fetch_columns(w_gate)
    weight_up = fetch_columns(w_up)
    weight_down = fetch_rows(w_down)

    stream = rehome(hidden_in).reshape(micro * rows, width).astype(jnp.float32)
    grad_out_low = rehome(cotangent).reshape(micro * rows, width)
    grad_out = grad_out_low.astype(jnp.float32)

    def to_heads(flat):
        split = flat.reshape(inner * tp, micro, rows, -1, HEAD_DIM).transpose(1, 0, 2, 3, 4)
        return split.reshape(micro, inner * tp * rows, -1, HEAD_DIM)

    def from_heads(heads):
        split = heads.reshape(micro, inner * tp, rows, -1).transpose(1, 0, 2, 3)
        return split.reshape(inner * tp * micro * rows, -1)

    normed_one, factor_one, attn_rows = norm_rows(stream, gain_attn)
    attn_in = spread(attn_rows).reshape(-1, width)
    projected = to_heads(dot(attn_in, weight_qkv, ((1,), (0,))))
    group = HEADS // KV_HEADS
    cos_table, sin_table = rope_tables(pos)
    cos_heads, sin_heads = cos_table[:, :, None], sin_table[:, :, None]
    turning = projected[:, :, : group + 1]
    turning = (turning * cos_heads + turned(turning) * sin_heads).astype(jnp.bfloat16)
    queries, keys = turning[:, :, :group], turning[:, :, group]
    values = projected[:, :, group + 1].astype(jnp.bfloat16)
    allowed = (ids[:, None, :] <= ids[:, :, None])[:, None]
    raw = jnp.einsum("blge,bme->bglm", queries, keys, preferred_element_type=jnp.float32)
    scores = jnp.where(allowed, raw * score_scale, MASKED)
    row_max = jnp.max(scores, axis=-1, keepdims=True)
    exponent = jnp.exp(scores - row_max)
    prob = exponent / jnp.sum(exponent, axis=-1, keepdims=True)
    prob_low = prob.astype(jnp.bfloat16)
    mixed = jnp.einsum("bglm,bme->blge", prob_low, values, preferred_element_type=jnp.float32)
    mixed = from_heads(mixed.astype(jnp.bfloat16))
    out_part = dot(mixed, weight_out, ((1,), (0,)))
    stream_mid = stream + fold(out_part.reshape(inner, tp, -1, width))
    normed_two, factor_two, ffn_rows = norm_rows(stream_mid, gain_ffn)
    ffn_in = spread(ffn_rows).reshape(-1, width)
    dy = spread(grad_out_low).reshape(-1, width)

    gate_pre = dot(ffn_in, weight_gate, ((1,), (0,)))
    up_pre = dot(ffn_in, weight_up, ((1,), (0,)))
    gate_sig = jax.nn.sigmoid(gate_pre)
    gate_act = gate_pre * gate_sig
    hidden = (gate_act * up_pre).astype(jnp.bfloat16)
    grad_hidden = dot(dy, weight_down, ((1,), (1,)))
    grad_gate_pre = (
        grad_hidden * up_pre * gate_sig * (1.0 + gate_pre * (1.0 - gate_sig))
    ).astype(jnp.bfloat16)
    grad_up_pre = (grad_hidden * gate_act).astype(jnp.bfloat16)
    grad_ffn_part = dot(grad_gate_pre, weight_gate, ((1,), (1,))) + dot(
        grad_up_pre, weight_up, ((1,), (1,))
    )
    grad_ffn_in = fold(grad_ffn_part.reshape(inner, tp, -1, width))
    down_part = dot(hidden, weight_down, ((1,), (0,)))
    stream_out = stream_mid + fold(down_part.reshape(inner, tp, -1, width))
    grad_down = return_rows(dot(hidden, dy, ((0,), (0,))))
    grad_gate = return_columns(dot(ffn_in, grad_gate_pre, ((0,), (0,))))
    grad_up = return_columns(dot(ffn_in, grad_up_pre, ((0,), (0,))))

    def back_rows(grad, normed, factor, gain_row):
        grad_normed = grad * gain_row
        inner_mean = jnp.mean(grad_normed * normed, axis=-1, keepdims=True)
        return factor * (grad_normed - normed * inner_mean), jnp.sum(grad * normed, axis=0)

    mid_norm, gain_ffn_part = back_rows(grad_ffn_in, normed_two, factor_two, gain_ffn)
    grad_mid = grad_out + mid_norm
    grad_mid_low = spread(grad_mid.astype(jnp.bfloat16)).reshape(-1, width)
    grad_mixed = to_heads(dot(grad_mid_low, weight_out, ((1,), (1,))).astype(jnp.bfloat16))
    grad_wo = return_rows(dot(mixed, grad_mid_low, ((0,), (0,))))
    grad_prob = jnp.einsum("blge,bme->bglm", grad_mixed, values, preferred_element_type=jnp.float32)
    inner_prob = jnp.sum(grad_prob * prob, axis=-1, keepdims=True)
    grad_scores = (score_scale * prob * (grad_prob - inner_prob)).astype(jnp.bfloat16)
    grad_queries = jnp.einsum(
        "bglm,bme->blge", grad_scores, keys, preferred_element_type=jnp.float32
    )
    grad_keys = jnp.einsum(
        "bglm,blge->bme", grad_scores, queries, preferred_element_type=jnp.float32
    )
    grad_values = jnp.einsum(
        "bglm,blge->bme", prob_low, grad_mixed, preferred_element_type=jnp.float32
    )
    grad_turning = jnp.concatenate([grad_queries, grad_keys[:, :, None]], axis=2)
    grad_turning = grad_turning * cos_heads + turned_back(grad_turning * sin_heads)
    grad_projected = jnp.concatenate([grad_turning, grad_values[:, :, None]], axis=2)
    grad_projected = from_heads(grad_projected.astype(jnp.bfloat16))
    grad_attn_in = fold(
        dot(grad_projected, weight_qkv, ((1,), (1,))).reshape(inner, tp, -1, width)
    )
    grad_wqkv = return_columns(dot(attn_in, grad_projected, ((0,), (0,))))
    in_norm, gain_attn_part = back_rows(grad_attn_in, normed_one, factor_one, gain_attn)
    grad_in = (grad_mid + in_norm).astype(jnp.bfloat16)

    gain_parts = jnp.stack([gain_attn_part, gain_ffn_part], axis=1).reshape(fsdp * ctx, -1, 2)
    gain_sums = lax.psum_scatter(gain_parts, ("fsdp", "ctx"), scatter_dimension=0)
    gain_sums = lax.psum(gain_sums, "tp")

    def home(array):
        return rehome(array.reshape(micro, 1, rows, width))

    return (
        home(stream_out.astype(jnp.bfloat16)),
        home(grad_in),
        gain_sums[:, 0],
        grad_wqkv,
        grad_wo,
        gain_sums[:, 1],
        grad_gate,
        grad_up,
        grad_down,
    )


MESH = pl.DeviceIdType.MESH
ROWS = 128
LANES = 128
NARROW = jnp.bfloat16
WIDE = jnp.float32
HALF = HEAD_DIM // 2
SCALE = HEAD_DIM ** (-0.5)
ANYWHERE = pl.BlockSpec(memory_space=pl.ANY)


class Place:
    def __init__(self):
        f, c, t = lax.axis_index("fsdp"), lax.axis_index("ctx"), lax.axis_index("tp")
        self.f, self.c, self.t = f, c, t
        fs, fy = f + 1 - 2 * (f % 2), (f + 2) % 4
        fd = (fs + 2) % 4
        self.fs, self.fy, self.fd = fs, fy, fd
        self.c1, self.c2 = c + 1 - 2 * (c % 2), (c + 2) % 4
        self.c3 = (self.c1 + 2) % 4
        self.side, self.core, self.row = (f, c, 1 - t), (fs, c, t), (fy, c, t)
        self.cross = (fd, c, t)
        self.z1, self.z2 = (f, self.c1, t), (f, self.c2, t)
        self.swap = (c, f, t)
        self.b, self.b_side = f * 2 + t, f * 2 + 1 - t
        self.b_row, self.b_far = fy * 2 + t, fy * 2 + 1 - t
        self.b_core, self.b_core_side = fs * 2 + t, fs * 2 + 1 - t
        self.b_core_row, self.b_core_far = fd * 2 + t, fd * 2 + 1 - t


class Sent:
    def __init__(self, copy, landing):
        self.copy, self.landing = copy, landing

    def arrive(self):
        self.landing.wait_recv()

    def leave(self):
        self.copy.wait_send()


class Post:
    def __init__(self, send_sems, recv_sems, local_sems):
        self.sems = send_sems, recv_sems
        self.local_sems = local_sems
        self.n, self.n_local = 0, 0
        self.out, self.kept = [], []

    def make(self, source, target, device, lands):
        sems = dict(
            send_sem=self.sems[0].at[self.n],
            recv_sem=self.sems[1].at[self.n],
            device_id=device,
            device_id_type=MESH,
        )
        self.n += 1
        copy = pltpu.make_async_remote_copy(src_ref=source, dst_ref=target, **sems)
        landing = pltpu.make_async_remote_copy(src_ref=lands, dst_ref=lands, **sems)
        return Sent(copy, landing)

    def send(self, source, target, device, lands):
        sent = self.make(source, target, device, lands)
        sent.copy.start()
        self.out.append(sent)
        return sent

    def keep(self, source, target):
        copy = pltpu.make_async_copy(source, target, self.local_sems.at[self.n_local])
        self.n_local += 1
        copy.start()
        self.kept.append(copy)
        return copy

    def close(self):
        for sent in self.out:
            sent.leave()
        for copy in self.kept:
            copy.wait()
        self.out, self.kept = [], []


def meet(devices):
    bar = pltpu.get_barrier_semaphore()
    for device in devices:
        pl.semaphore_signal(bar, inc=1, device_id=device, device_id_type=MESH)
    pl.semaphore_wait(bar, len(devices))


class Spread:
    def __init__(self, post, at, out):
        self.post, self.at, self.out = post, at, out
        self.sent = {}

    def slot(self, block, half):
        return self.out.at[block, pl.ds(half * ROWS, ROWS)]

    def own(self, half, source):
        at, mine = self.at, self.slot(self.at.b, half)
        self.sent["side", half] = self.post.send(source, mine, at.side, self.slot(at.b_side, half))
        self.sent["row", half] = self.post.send(source, mine, at.row, self.slot(at.b_row, half))
        self.sent["core", half] = self.post.send(source, mine, at.core, self.slot(at.b_core, half))
        self.post.keep(source, mine)

    def pass_on(self, name, half, block, lands):
        here = self.slot(block, half)
        self.sent[name, half] = self.post.send(
            here, here, self.at.core, self.slot(lands, half)
        )

    def relay(self, half):
        at = self.at
        first = ("side", "row") if half == 0 else ("row", "side")
        for name in first:
            self.sent[name, half].arrive()
            block = at.b_side if name == "side" else at.b_row
            here = self.slot(block, half)
            if half == 0 and name == "side":
                self.sent["far", 0] = self.post.send(here, here, at.row, self.slot(at.b_far, 0))
            if half == 1 and name == "row":
                self.sent["far", 1] = self.post.send(here, here, at.side, self.slot(at.b_far, 1))
            lands = at.b_core_side if name == "side" else at.b_core_row
            self.pass_on("core_" + name, half, block, lands)

    def corner(self):
        for half in range(2):
            self.sent["far", half].arrive()
            self.pass_on("core_far", half, self.at.b_far, self.at.b_core_far)

    def finish(self):
        for name in ("core", "core_side", "core_row", "core_far"):
            for half in range(2):
                self.sent[name, half].arrive()


SPREAD_COPIES, SPREAD_KEPT = 14, 2


class Fold:
    copies = 10

    def __init__(self, post, at, part, scratch):
        self.post, self.at, self.part = post, at, part
        self.got, self.give, self.far, self.side, self.row, self.gx, self.gy, self.held = scratch

    @staticmethod
    def scratch(width):
        return [
            pltpu.VMEM((4, 2 * ROWS, width), NARROW),
            pltpu.VMEM((4, 2 * ROWS, width), NARROW),
            pltpu.VMEM((2, ROWS, width), NARROW),
            pltpu.VMEM((2, ROWS, width), NARROW),
            pltpu.VMEM((2, ROWS, width), NARROW),
            pltpu.VMEM((3, ROWS, width), NARROW),
            pltpu.VMEM((3, ROWS, width), NARROW),
            pltpu.VMEM((4, ROWS, width), WIDE),
        ]

    def to_core(self, slot, block):
        self.give[slot] = self.part(block).astype(NARROW)
        return self.post.send(self.give.at[slot], self.got.at[slot], self.at.core, self.got.at[slot])

    def first(self):
        at, post = self.at, self.post
        sent = self.to_core(3, at.b_core_far)
        value = self.part(at.b_far)
        sent.arrive()
        value = (value + self.got[3].astype(WIDE)).astype(NARROW)
        self.far[0] = value[:ROWS]
        self.far[1] = value[ROWS:]
        self.far_x = post.send(self.far.at[0], self.gx.at[0], at.side, self.gx.at[0])
        self.far_y = post.send(self.far.at[1], self.gy.at[0], at.row, self.gy.at[0])
        sent = self.to_core(1, at.b_core_side)
        value = self.part(at.b_side)
        sent.arrive()
        value = value + self.got[1].astype(WIDE)
        self.side[0] = value[:ROWS].astype(NARROW)
        self.held[2] = value[ROWS:]
        self.side_x = post.send(self.side.at[0], self.gx.at[1], at.side, self.gx.at[1])
        sent = self.to_core(2, at.b_core_row)
        value = self.part(at.b_row)
        sent.arrive()
        value = value + self.got[2].astype(WIDE)
        self.row[1] = value[ROWS:].astype(NARROW)
        self.held[3] = value[:ROWS]
        self.row_y = post.send(self.row.at[1], self.gy.at[1], at.row, self.gy.at[1])
        sent = self.to_core(0, at.b_core)
        value = self.part(at.b)
        sent.arrive()
        value = value + self.got[0].astype(WIDE)
        self.held[0] = value[:ROWS]
        self.held[1] = value[ROWS:]

    def second(self):
        at, post = self.at, self.post
        self.far_y.arrive()
        self.side[1] = (self.held[2] + self.gy[0].astype(WIDE)).astype(NARROW)
        self.side_b = post.send(self.side.at[1], self.gx.at[2], at.side, self.gx.at[2])
        self.far_x.arrive()
        self.row[0] = (self.held[3] + self.gx[0].astype(WIDE)).astype(NARROW)
        self.row_a = post.send(self.row.at[0], self.gy.at[2], at.row, self.gy.at[2])

    def third(self):
        self.side_x.arrive()
        self.row_y.arrive()
        self.held[0] = self.held[0] + self.gx[1].astype(WIDE)
        self.held[1] = self.held[1] + self.gy[1].astype(WIDE)
        self.row_a.arrive()
        self.held[0] = self.held[0] + self.gy[2].astype(WIDE)
        self.side_b.arrive()
        self.held[1] = self.held[1] + self.gx[2].astype(WIDE)


class Climb:
    copies, kept = 3, 1

    def __init__(self, post, at, level, out):
        self.post, self.at, self.out = post, at, out
        mine = out.at[:, at.c]
        self.far = post.send(level, mine, at.z2, out.at[:, at.c2])
        self.close = post.send(level, mine, at.z1, out.at[:, at.c1])
        post.keep(level, mine)

    def forward(self):
        at = self.at
        self.far.arrive()
        there = self.out.at[:, at.c2]
        self.last = self.post.send(there, there, at.z1, self.out.at[:, at.c3])

    def finish(self):
        self.close.arrive()
        self.last.arrive()


def call(kernel, name, outs, args, scratch, copies, kept, collective_id):
    sems = [
        pltpu.SemaphoreType.DMA((copies,)),
        pltpu.SemaphoreType.DMA((copies,)),
        pltpu.SemaphoreType.DMA((kept,)),
    ]
    n_in, n_out = len(args), len(outs)

    def inner(*refs):
        post = Post(*refs[len(refs) - 3 :])
        kernel(
            post, Place(), refs[:n_in], refs[n_in : n_in + n_out], refs[n_in + n_out : len(refs) - 3]
        )
        post.close()
        assert post.n <= copies and post.n_local <= kept, (post.n, post.n_local)

    return pl.pallas_call(
        inner,
        out_shape=outs,
        in_specs=[ANYWHERE] * n_in,
        out_specs=[ANYWHERE] * n_out,
        scratch_shapes=scratch + sems,
        compiler_params=pltpu.CompilerParams(
            collective_id=collective_id, has_side_effects=True, vmem_limit_bytes=62 << 20
        ),
        name=name,
    )(*args)


def shape(*dims, dtype=NARROW):
    return jax.ShapeDtypeStruct(dims, dtype)


def gain_row(gains_ref, which):
    return jnp.concatenate([gains_ref[i, which : which + 1, :] for i in range(16)], axis=1)


def normed_rows(values):
    factor = lax.rsqrt(jnp.mean(values * values, axis=-1, keepdims=True) + EPS)
    return values * factor, factor


def start_kernel(post, at, ins, outs, scratch):
    hidden, cot, table, marks, gains, wqkv, wo, w_gate, w_up, w_down = ins
    x_own, cot_own, attn_in, tables, all_marks, all_gains, qkv_all, out_all, gate_lvl, up_lvl, down_lvl = outs
    rows_in, rows_out, gain_buf = scratch
    f, c = at.f, at.c
    bar = pltpu.get_barrier_semaphore()
    partners = (at.side, at.core, at.row, at.cross, at.z1, at.z2)
    for device in partners:
        pl.semaphore_signal(bar, inc=1, device_id=device, device_id_type=MESH)

    @pl.when(f != c)
    def _():
        pl.semaphore_signal(bar, inc=1, device_id=at.swap, device_id_type=MESH)
        pl.semaphore_wait(bar, len(partners) + 1)

    @pl.when(f == c)
    def _():
        pl.semaphore_wait(bar, len(partners))

    moves = []

    def swap(source, target, lands):
        sent = post.make(source, target, at.swap, lands)
        local = pltpu.make_async_copy(source, target, post.local_sems.at[post.n_local])
        post.n_local += 1

        @pl.when(f != c)
        def _():
            sent.copy.start()

        @pl.when(f == c)
        def _():
            local.start()

        moves.append(sent)

        def arrive():
            @pl.when(f != c)
            def _():
                sent.landing.wait_recv()

            @pl.when(f == c)
            def _():
                local.wait()

        return arrive

    halves = [pl.ds(half * ROWS, ROWS) for half in range(2)]
    table_moved = swap(table, tables.at[c], tables.at[f])
    marks_moved = swap(marks, all_marks.at[c], all_marks.at[f])
    x_moved = [swap(hidden.at[half], rows_in.at[half], rows_in.at[half]) for half in halves]

    mine = gain_buf.at[f, c]
    post.keep(gains, mine).wait()
    post.kept.pop()
    gain_step = post.send(mine, mine, at.core, gain_buf.at[at.fs, c])
    heads = wqkv.shape[1] // 4
    span = wo.shape[0] // 4
    first = []
    for device, k, src in (
        (at.row, at.fy, at.fy),
        (at.cross, at.fd, at.fd),
        (at.core, at.fs, at.fs),
    ):
        lane = pl.ds(pl.multiple_of(k * heads, LANES), heads)
        first.append(post.send(wqkv.at[:, lane], qkv_all.at[f, c], device, qkv_all.at[src, c]))
        row = pl.ds(pl.multiple_of(k * span, LANES), span)
        first.append(post.send(wo.at[row], out_all.at[f, c], device, out_all.at[src, c]))
    lane = pl.ds(pl.multiple_of(f * heads, LANES), heads)
    post.keep(wqkv.at[:, lane], qkv_all.at[f, c]).wait()
    row = pl.ds(pl.multiple_of(f * span, LANES), span)
    post.keep(wo.at[row], out_all.at[f, c]).wait()
    post.kept = post.kept[:-2]

    gain_step.arrive()
    pair = gain_buf.at[pl.ds(f // 2 * 2, 2), c]
    gain_step = post.send(pair, pair, at.row, gain_buf.at[pl.ds(at.fy // 2 * 2, 2), c])

    for sent in first:
        sent.arrive()
    levels = []
    for out in (qkv_all, out_all):
        here, there = out.at[:, c], out.at[:, at.c2]
        far = post.send(here, here, at.z2, there)
        close = post.send(here, here, at.z1, out.at[:, at.c1])
        levels.append((far, close, there, out))

    gain_step.arrive()
    gain_step = post.send(gain_buf.at[:, c], gain_buf.at[:, c], at.z1, gain_buf.at[:, at.c1])
    gain_step.arrive()
    pair = gain_buf.at[:, pl.ds(c // 2 * 2, 2)]
    gain_step = post.send(pair, pair, at.z2, gain_buf.at[:, pl.ds(at.c2 // 2 * 2, 2)])
    gain_step.arrive()
    gain = jnp.concatenate(
        [gain_buf[i // 4, i % 4, 0:1, :] for i in range(16)], axis=1
    )
    post.keep(gain_buf, all_gains)

    spread = Spread(post, at, attn_in)
    for half in range(2):
        x_moved[half]()
        normed, _ = normed_rows(rows_in[halves[half]].astype(WIDE))
        rows_out[halves[half]] = (normed * gain).astype(NARROW)
        spread.own(half, rows_out.at[halves[half]])
        post.keep(rows_in.at[halves[half]], x_own.at[halves[half]])

    table_moved()
    marks_moved()
    small = []
    for buf in (tables, all_marks):
        here = buf.at[f]
        small.append((buf, post.send(here, here, at.core, buf.at[at.fs])))
    cot_moved = [swap(cot.at[half], cot_own.at[half], cot_own.at[half]) for half in halves]
    smaller = []
    for buf, sent in small:
        sent.arrive()
        pair = buf.at[pl.ds(f // 2 * 2, 2)]
        smaller.append(post.send(pair, pair, at.row, buf.at[pl.ds(at.fy // 2 * 2, 2)]))

    spread.relay(0)

    part = w_gate.shape[1] // 4
    chunk = part // 4
    later = []
    for device, k, src in (
        (at.row, at.fy, at.fy),
        (at.cross, at.fd, at.fd),
        (at.core, at.fs, at.fs),
        (None, f, f),
    ):
        for j in range(4):
            lane = pl.ds(pl.multiple_of(k * part + j * chunk, LANES), chunk)
            for source, target in (
                (w_gate.at[:, lane], gate_lvl),
                (w_up.at[:, lane], up_lvl),
                (w_down.at[lane], down_lvl),
            ):
                if device is None:
                    post.keep(source, target.at[j, f])
                else:
                    later.append(post.send(source, target.at[j, f], device, target.at[j, src]))

    spread.relay(1)
    forwards = []
    for far, close, there, out in levels:
        far.arrive()
        forwards.append((post.send(there, there, at.z1, out.at[:, at.c3]), close))
    spread.corner()
    for last, close in forwards:
        last.arrive()
        close.arrive()
    spread.finish()
    for sent in smaller + later:
        sent.arrive()
    for arrive in cot_moved:
        arrive()

    @pl.when(f != c)
    def _():
        for sent in moves:
            sent.copy.wait_send()


def rope(values, cos_full, sin_full):
    return values * cos_full + pltpu.roll(values, HALF, 1) * sin_full


def rope_back(values, cos_full, sin_full):
    return values * cos_full - pltpu.roll(values, HALF, 1) * sin_full


def rope_full(table):
    turned_table = pltpu.roll(table, HALF, 1)
    low = lax.broadcasted_iota(jnp.int32, table.shape, 1) < HALF
    return jnp.where(low, table, turned_table), jnp.where(low, -turned_table, table)


def mm(left, right, dims=((1,), (0,))):
    return lax.dot_general(left, right, (dims, ((), ())), preferred_element_type=WIDE)


TILE = 256


def softmax_tile(query, key, id_col, id_row):
    raw = mm(query, key, ((1,), (1,))) * SCALE
    raw = jnp.where(id_row <= id_col, raw, MASKED)
    top = jnp.max(raw, axis=-1, keepdims=True)
    exponent = jnp.exp(raw - top)
    return exponent * (1.0 / jnp.sum(exponent, axis=-1, keepdims=True))


def id_rows(marks, m, tiles):
    return jnp.concatenate([marks[i, m : m + 1, :] for i in range(tiles)], axis=1)


def attend_kernel(jobs, post, at, ins, outs, scratch):
    attn_in, qkv_all, tables_in, marks_in, cot_own = ins[:5]
    levels = jobs(ins[5:])
    queries, keys, values, mixed, dy, *climbed = outs
    rows, weight, tables, marks, q_buf, k_buf, v_buf, mix_buf = scratch
    meet((at.side, at.core, at.row, at.z1, at.z2))
    local = [
        post.keep(tables_in, tables),
        post.keep(marks_in, marks),
        post.keep(qkv_all, weight),
        post.keep(attn_in.at[:, pl.ds(0, ROWS)], rows.at[0]),
        post.keep(attn_in.at[:, pl.ds(ROWS, ROWS)], rows.at[1]),
    ]
    spread = Spread(post, at, dy)
    for half in range(2):
        spread.own(half, cot_own.at[pl.ds(half * ROWS, ROWS)])
    climbs = [Climb(post, at, level, out) for level, out in zip(levels, climbed)]
    for copy in local:
        copy.wait()
        post.kept.remove(copy)
    width = rows.shape[-1]
    columns = weight.shape[-1]
    for m in range(2):
        for i in range(4):
            here = rows[m, 2 * i : 2 * i + 2].reshape(TILE, width)
            projected = mm(here, weight[...].reshape(width, columns))
            cos_full, sin_full = rope_full(tables[i, m])
            place = pl.ds(i * TILE, TILE)
            for g in range(2):
                lane = slice(g * HEAD_DIM, (g + 1) * HEAD_DIM)
                q_buf[m, place, lane] = rope(projected[:, lane], cos_full, sin_full).astype(NARROW)
            k_buf[m, place] = rope(projected[:, 256:384], cos_full, sin_full).astype(NARROW)
            v_buf[m, place] = projected[:, 384:512].astype(NARROW)
    spread.relay(0)
    for m in range(2):
        for i in range(4):
            n = min(i + 2, 4) * TILE
            id_col = marks[i].T[:, m : m + 1]
            id_row = id_rows(marks, m, n // TILE)
            for g in range(2):
                lane = slice(g * HEAD_DIM, (g + 1) * HEAD_DIM)
                prob = softmax_tile(
                    q_buf[m, i * TILE : (i + 1) * TILE, lane], k_buf[m, :n], id_col, id_row
                )
                value = mm(prob.astype(NARROW), v_buf[m, :n]).astype(NARROW)
                for h in range(2):
                    mix_buf[2 * i + h, m * ROWS : (m + 1) * ROWS, lane] = value[
                        h * ROWS : (h + 1) * ROWS
                    ]
        if m == 0:
            spread.relay(1)
            for climb in climbs:
                climb.forward()
    for source, target in ((q_buf, queries), (k_buf, keys), (v_buf, values), (mix_buf, mixed)):
        post.keep(source, target)
    spread.corner()
    spread.finish()
    for climb in climbs:
        climb.finish()


def middle_kernel(jobs, post, at, ins, outs, scratch):
    mixed, out_all, x_own, gains_in = ins[:4]
    levels = jobs(ins[4:])
    mid_own, ffn_in, *climbed = outs
    mix_buf, weight, x_buf, gains, rows_out, *fold_scratch = scratch
    meet((at.side, at.core, at.row, at.z1, at.z2))
    local = [
        post.keep(out_all.at[i // 4, i % 4], weight.at[:, pl.ds(i * LANES, LANES)])
        for i in range(16)
    ]
    local += [post.keep(mixed, mix_buf), post.keep(x_own, x_buf), post.keep(gains_in, gains)]
    for copy in local:
        copy.wait()
        post.kept.remove(copy)
    climbs = [Climb(post, at, level, out) for level, out in zip(levels, climbed)]

    def part(block):
        return mm(mix_buf[block], weight[...])

    fold = Fold(post, at, part, fold_scratch)
    fold.first()
    fold.second()
    fold.third()
    gain = jnp.concatenate([gains[i // 4, i % 4, 1:2, :] for i in range(16)], axis=1)
    spread = Spread(post, at, ffn_in)
    for half in range(2):
        rows = pl.ds(half * ROWS, ROWS)
        value = fold.held[half] + x_buf[rows].astype(WIDE)
        fold.held[half] = value
        normed, _ = normed_rows(value)
        rows_out[half] = (normed * gain).astype(NARROW)
        spread.own(half, rows_out.at[half])
        post.keep(fold.held.at[half], mid_own.at[rows])
    spread.relay(0)
    for climb in climbs:
        climb.forward()
    spread.relay(1)
    spread.corner()
    spread.finish()
    for climb in climbs:
        climb.finish()


class Jobs:
    def __init__(self, *wanted):
        self.wanted = wanted

    def __call__(self, level_refs):
        return [level_refs[a].at[j] for a, j in self.wanted]

    def shapes(self, levels):
        return [
            jax.ShapeDtypeStruct((4, 4) + levels[a].shape[2:], NARROW) for a, j in self.wanted
        ]


def small_arrays(block_ids, positions, attn_gain, ffn_gain):
    micro, _, span = positions.shape
    cos_table, sin_table = rope_tables(positions[:, 0])
    table = jnp.concatenate([cos_table[..., :HALF], sin_table[..., :HALF]], axis=-1)
    ids = lax.dynamic_slice_in_dim(block_ids[:, 0], lax.axis_index("ctx") * span, span, 1)
    marks = jnp.zeros((8, span), WIDE).at[:micro].set(ids.astype(WIDE))
    gains = jnp.zeros((8, LANES), WIDE).at[0].set(attn_gain.astype(WIDE))
    return table, marks, gains.at[1].set(ffn_gain.astype(WIDE))


def rest_by_compiler(
    x_own, cot_own, attn_in, tables, all_marks, all_gains, qkv_all, out_all,
    queries, keys, values, mixed, dy, mid_own, ffn_in, weight_gate, weight_up, weight_down,
):
    fsdp, ctx, tp = lax.axis_size("fsdp"), lax.axis_size("ctx"), lax.axis_size("tp")
    inner = KV_HEADS // tp
    outer = fsdp // inner
    near, far = groups_of(fsdp, inner)
    micro, rows, width = 2, 128, x_own.shape[-1]
    score_scale = SCALE
    swap = [
        ((high * inner + low) * ctx + c, (high * inner + c) * ctx + low)
        for high in range(outer)
        for low in range(inner)
        for c in range(ctx)
    ]

    def rehome(array):
        return lax.ppermute(array, ("fsdp", "ctx"), swap)

    def trade(pieces):
        return lax.all_to_all(pieces, "fsdp", 0, 0, axis_index_groups=near)

    def spread(block):
        both = lax.all_gather(block, "tp")
        return lax.all_gather(both, "fsdp", axis_index_groups=near)

    def fold(parts):
        half = lax.psum_scatter(
            parts.astype(jnp.bfloat16), "fsdp", scatter_dimension=0, axis_index_groups=near
        )
        return lax.psum_scatter(half, "tp", scatter_dimension=0).astype(jnp.float32)

    def scatter_levels(pieces):
        if outer == 1:
            pieces = pieces[0]
        else:
            pieces = lax.psum_scatter(pieces, "fsdp", scatter_dimension=0, axis_index_groups=far)
        return lax.psum_scatter(pieces, "ctx", scatter_dimension=0)

    def return_columns(grad):
        total, cols = grad.shape
        grad = grad.astype(jnp.bfloat16).reshape(outer, inner, ctx, -1, cols)
        mine = trade(scatter_levels(grad.transpose(0, 2, 1, 3, 4)))
        return mine.transpose(1, 0, 2).reshape(mine.shape[1], -1).astype(jnp.float32)

    def return_rows(grad):
        length, total = grad.shape
        grad = grad.astype(jnp.bfloat16).reshape(length, outer, inner, ctx, -1)
        mine = trade(scatter_levels(grad.transpose(1, 3, 2, 0, 4)))
        return mine.reshape(inner * length, -1).astype(jnp.float32)

    def dot(left, right, dims):
        return lax.dot_general(left, right, (dims, ((), ())), preferred_element_type=jnp.float32)

    gain_attn = all_gains[:, :, 0].reshape(-1)
    gain_ffn = all_gains[:, :, 1].reshape(-1)
    ids = all_marks[:, :2].transpose(1, 0, 2).reshape(2, 1024)
    tabs = tables.transpose(1, 0, 2, 3).reshape(2, 1024, 128)
    cos_table = jnp.concatenate([tabs[..., :64]] * 2, axis=-1)
    sin_table = jnp.concatenate([tabs[..., 64:]] * 2, axis=-1)
    cos_heads, sin_heads = cos_table[:, :, None], sin_table[:, :, None]
    weight_qkv = qkv_all.reshape(width, 512)
    weight_out = out_all.transpose(2, 0, 1, 3).reshape(256, width)
    grad_out = cot_own.astype(jnp.float32)
    stream_mid = mid_own
    attn_in = attn_in.reshape(-1, width)
    mixed = mixed.reshape(-1, 256)
    dy = dy.reshape(-1, width)
    ffn_in = ffn_in.reshape(-1, width)
    queries = queries.reshape(2, 1024, 2, 128)
    normed_one, factor_one, _ = norm_rows(x_own.astype(jnp.float32), gain_attn)
    normed_two, factor_two, _ = norm_rows(stream_mid, gain_ffn)
    allowed = (ids[:, None, :] <= ids[:, :, None])[:, None]
    raw = jnp.einsum("blge,bme->bglm", queries, keys, preferred_element_type=jnp.float32)
    scores = jnp.where(allowed, raw * score_scale, MASKED)
    row_max = jnp.max(scores, axis=-1, keepdims=True)
    exponent = jnp.exp(scores - row_max)
    prob = exponent / jnp.sum(exponent, axis=-1, keepdims=True)
    prob_low = prob.astype(jnp.bfloat16)

    def to_heads(flat):
        split = flat.reshape(inner * tp, micro, rows, -1, HEAD_DIM).transpose(1, 0, 2, 3, 4)
        return split.reshape(micro, inner * tp * rows, -1, HEAD_DIM)

    def from_heads(heads):
        split = heads.reshape(micro, inner * tp, rows, -1).transpose(1, 0, 2, 3)
        return split.reshape(inner * tp * micro * rows, -1)

    gate_pre = dot(ffn_in, weight_gate, ((1,), (0,)))
    up_pre = dot(ffn_in, weight_up, ((1,), (0,)))
    gate_sig = jax.nn.sigmoid(gate_pre)
    gate_act = gate_pre * gate_sig
    hidden = (gate_act * up_pre).astype(jnp.bfloat16)
    grad_hidden = dot(dy, weight_down, ((1,), (1,)))
    grad_gate_pre = (
        grad_hidden * up_pre * gate_sig * (1.0 + gate_pre * (1.0 - gate_sig))
    ).astype(jnp.bfloat16)
    grad_up_pre = (grad_hidden * gate_act).astype(jnp.bfloat16)
    grad_ffn_part = dot(grad_gate_pre, weight_gate, ((1,), (1,))) + dot(
        grad_up_pre, weight_up, ((1,), (1,))
    )
    grad_ffn_in = fold(grad_ffn_part.reshape(inner, tp, -1, width))
    down_part = dot(hidden, weight_down, ((1,), (0,)))
    stream_out = stream_mid + fold(down_part.reshape(inner, tp, -1, width))
    grad_down = return_rows(dot(hidden, dy, ((0,), (0,))))
    grad_gate = return_columns(dot(ffn_in, grad_gate_pre, ((0,), (0,))))
    grad_up = return_columns(dot(ffn_in, grad_up_pre, ((0,), (0,))))

    def back_rows(grad, normed, factor, gain_row):
        grad_normed = grad * gain_row
        inner_mean = jnp.mean(grad_normed * normed, axis=-1, keepdims=True)
        return factor * (grad_normed - normed * inner_mean), jnp.sum(grad * normed, axis=0)

    mid_norm, gain_ffn_part = back_rows(grad_ffn_in, normed_two, factor_two, gain_ffn)
    grad_mid = grad_out + mid_norm
    grad_mid_low = spread(grad_mid.astype(jnp.bfloat16)).reshape(-1, width)
    grad_mixed = to_heads(dot(grad_mid_low, weight_out, ((1,), (1,))).astype(jnp.bfloat16))
    grad_wo = return_rows(dot(mixed, grad_mid_low, ((0,), (0,))))
    grad_prob = jnp.einsum("blge,bme->bglm", grad_mixed, values, preferred_element_type=jnp.float32)
    inner_prob = jnp.sum(grad_prob * prob, axis=-1, keepdims=True)
    grad_scores = (score_scale * prob * (grad_prob - inner_prob)).astype(jnp.bfloat16)
    grad_queries = jnp.einsum(
        "bglm,bme->blge", grad_scores, keys, preferred_element_type=jnp.float32
    )
    grad_keys = jnp.einsum(
        "bglm,blge->bme", grad_scores, queries, preferred_element_type=jnp.float32
    )
    grad_values = jnp.einsum(
        "bglm,blge->bme", prob_low, grad_mixed, preferred_element_type=jnp.float32
    )
    grad_turning = jnp.concatenate([grad_queries, grad_keys[:, :, None]], axis=2)
    grad_turning = grad_turning * cos_heads + turned_back(grad_turning * sin_heads)
    grad_projected = jnp.concatenate([grad_turning, grad_values[:, :, None]], axis=2)
    grad_projected = from_heads(grad_projected.astype(jnp.bfloat16))
    grad_attn_in = fold(
        dot(grad_projected, weight_qkv, ((1,), (1,))).reshape(inner, tp, -1, width)
    )
    grad_wqkv = return_columns(dot(attn_in, grad_projected, ((0,), (0,))))
    in_norm, gain_attn_part = back_rows(grad_attn_in, normed_one, factor_one, gain_attn)
    grad_in = (grad_mid + in_norm).astype(jnp.bfloat16)

    gain_parts = jnp.stack([gain_attn_part, gain_ffn_part], axis=1).reshape(fsdp * ctx, -1, 2)
    gain_sums = lax.psum_scatter(gain_parts, ("fsdp", "ctx"), scatter_dimension=0)
    gain_sums = lax.psum(gain_sums, "tp")

    def home(array):
        return rehome(array.reshape(micro, 1, rows, width))

    return (
        home(stream_out.astype(jnp.bfloat16)),
        home(grad_in),
        gain_sums[:, 0],
        grad_wqkv,
        grad_wo,
        gain_sums[:, 1],
        grad_gate,
        grad_up,
        grad_down,
    )


def near_body(
    hidden_in, cotangent, block_ids, positions, attn_gain, wqkv, wo, ffn_gain, w_gate, w_up, w_down
):
    micro, _, rows, width = hidden_in.shape
    own = micro * rows
    ff = w_gate.shape[1]
    chunk = ff // 16
    table, marks, gains = small_arrays(block_ids, positions, attn_gain, ffn_gain)
    (
        x_own, cot_own, attn_in, tables, all_marks, all_gains, qkv_all, out_all, gate_lvl, up_lvl, down_lvl,
    ) = call(
        start_kernel,
        "start",
        [
            shape(own, width), shape(own, width), shape(8, own, width),
            shape(4, *table.shape, dtype=WIDE), shape(4, *marks.shape, dtype=WIDE),
            shape(4, 4, *gains.shape, dtype=WIDE),
            shape(4, 4, LANES, wqkv.shape[1] // 4), shape(4, 4, wo.shape[0] // 4, LANES),
            shape(4, 4, LANES, chunk), shape(4, 4, LANES, chunk), shape(4, 4, chunk, LANES),
        ],
        (
            hidden_in.reshape(own, width), cotangent.reshape(own, width), table, marks, gains,
            wqkv, wo, w_gate, w_up, w_down,
        ),
        [pltpu.VMEM((own, width), NARROW), pltpu.VMEM((own, width), NARROW), pltpu.VMEM((4, 4, 8, LANES), WIDE)],
        80, 32, 1,
    )
    levels = (gate_lvl, up_lvl, down_lvl)
    jobs_a = Jobs((0, 0), (1, 0))
    jobs_b = Jobs((2, 0), (0, 1), (1, 1), (2, 1), (0, 2), (1, 2), (2, 2), (0, 3), (1, 3), (2, 3))
    queries, keys, values, mixed, dy, *climb_a = call(
        functools.partial(attend_kernel, jobs_a),
        "attend",
        [
            shape(2, 1024, 256), shape(2, 1024, 128), shape(2, 1024, 128), shape(8, own, 256),
            shape(8, own, width), *jobs_a.shapes(levels),
        ],
        (attn_in, qkv_all, tables, all_marks, cot_own, *levels),
        [
            pltpu.VMEM((2, 8, ROWS, width), NARROW), pltpu.VMEM(qkv_all.shape, NARROW),
            pltpu.VMEM(tables.shape, WIDE), pltpu.VMEM(all_marks.shape, WIDE),
            pltpu.VMEM((2, 1024, 256), NARROW), pltpu.VMEM((2, 1024, 128), NARROW),
            pltpu.VMEM((2, 1024, 128), NARROW), pltpu.VMEM((8, own, 256), NARROW),
        ],
        40, 24, 2,
    )
    mid_own, ffn_in, *climb_b = call(
        functools.partial(middle_kernel, jobs_b),
        "middle",
        [shape(own, width, dtype=WIDE), shape(8, own, width), *jobs_b.shapes(levels)],
        (mixed, out_all, x_own, all_gains, *levels),
        [
            pltpu.VMEM((8, own, 256), NARROW), pltpu.VMEM((256, width), NARROW),
            pltpu.VMEM((own, width), NARROW), pltpu.VMEM((4, 4, 8, LANES), WIDE),
            pltpu.VMEM((2, ROWS, width), NARROW), *Fold.scratch(width),
        ],
        60, 40, 3,
    )
    have = dict(zip(jobs_a.wanted + jobs_b.wanted, climb_a + climb_b))
    weight_gate = jnp.concatenate([have[0, j].reshape(width, chunk) for j in range(4)], axis=1)
    weight_up = jnp.concatenate([have[1, j].reshape(width, chunk) for j in range(4)], axis=1)
    weight_down = jnp.concatenate(
        [have[2, j].transpose(2, 0, 1, 3).reshape(chunk, width) for j in range(4)], axis=0
    )
    return rest_by_compiler(
        x_own, cot_own, attn_in, tables, all_marks, all_gains, qkv_all, out_all,
        queries, keys, values, mixed, dy, mid_own, ffn_in, weight_gate, weight_up, weight_down,
    )


def body(*shards):
    inner = KV_HEADS // lax.axis_size("tp")
    near = (lax.axis_size("fsdp"), lax.axis_size("ctx"), lax.axis_size("tp"), inner)
    return (near_body if near == (4, 4, 2, 4) else general_body)(*shards)


def solution(mesh):
    return jax.shard_map(
        body,
        mesh=mesh,
        in_specs=(
            P(None, "fsdp", ("ctx", "tp"), None),
            P(None, "fsdp", ("ctx", "tp"), None),
            P(None, "fsdp", None),
            P(None, "fsdp", "ctx"),
            P(("fsdp", "ctx")),
            P(("fsdp", "ctx"), "tp"),
            P("tp", ("fsdp", "ctx")),
            P(("fsdp", "ctx")),
            P(("fsdp", "ctx"), "tp"),
            P(("fsdp", "ctx"), "tp"),
            P("tp", ("fsdp", "ctx")),
        ),
        out_specs=(
            P(None, "fsdp", ("ctx", "tp"), None),
            P(None, "fsdp", ("ctx", "tp"), None),
            P(("fsdp", "ctx")),
            P(("fsdp", "ctx"), "tp"),
            P("tp", ("fsdp", "ctx")),
            P(("fsdp", "ctx")),
            P(("fsdp", "ctx"), "tp"),
            P(("fsdp", "ctx"), "tp"),
            P("tp", ("fsdp", "ctx")),
        ),
        check_vma=False,
    )
```

```python
import functools

import jax
import jax.numpy as jnp
from jax import lax
from jax.sharding import PartitionSpec as P
from jax.experimental import pallas as pl
from jax.experimental.pallas import tpu as pltpu

HEADS = 16
KV_HEADS = 8
HEAD_DIM = 128


EPS = 1e-05
THETA = 1000000.0
MASKED = -1e30


def rope_tables(position_ids):
    half_dim = HEAD_DIM // 2
    inverse = THETA ** (-(jnp.arange(half_dim, dtype=jnp.float32) * 2.0 / HEAD_DIM))
    angles = position_ids.astype(jnp.float32)[..., None] * inverse
    angles = jnp.concatenate([angles, angles], axis=-1)
    return (jnp.cos(angles), jnp.sin(angles))


def turned(values):
    half_dim = values.shape[-1] // 2
    return jnp.concatenate([-values[..., half_dim:], values[..., :half_dim]], axis=-1)


def turned_back(values):
    half_dim = values.shape[-1] // 2
    return jnp.concatenate([values[..., half_dim:], -values[..., :half_dim]], axis=-1)


def norm_rows(stream, gain_row):
    factor = lax.rsqrt(jnp.mean(stream * stream, axis=-1, keepdims=True) + EPS)
    normed = stream * factor
    return (normed, factor, (normed * gain_row).astype(jnp.bfloat16))


def groups_of(fsdp, inner):
    near = [[high * inner + low for low in range(inner)] for high in range(fsdp // inner)]
    far = [[high * inner + low for high in range(fsdp // inner)] for low in range(inner)]
    return near, far


def general_body(
    hidden_in, cotangent, block_ids, positions, attn_gain, wqkv, wo, ffn_gain, w_gate, w_up, w_down
):
    fsdp, ctx, tp = lax.axis_size("fsdp"), lax.axis_size("ctx"), lax.axis_size("tp")
    inner = KV_HEADS // tp
    outer = fsdp // inner
    near, far = groups_of(fsdp, inner)
    micro, _, rows, width = hidden_in.shape
    score_scale = HEAD_DIM ** (-0.5)
    f_at, c_at = lax.axis_index("fsdp"), lax.axis_index("ctx")
    swap = [
        ((high * inner + low) * ctx + c, (high * inner + c) * ctx + low)
        for high in range(outer)
        for low in range(inner)
        for c in range(ctx)
    ]

    def rehome(array):
        return lax.ppermute(array, ("fsdp", "ctx"), swap)

    def trade(pieces):
        return lax.all_to_all(pieces, "fsdp", 0, 0, axis_index_groups=near)

    def spread(block):
        both = lax.all_gather(block, "tp")
        return lax.all_gather(both, "fsdp", axis_index_groups=near)

    def fold(parts):
        half = lax.psum_scatter(
            parts.astype(jnp.bfloat16), "fsdp", scatter_dimension=0, axis_index_groups=near
        )
        return lax.psum_scatter(half, "tp", scatter_dimension=0).astype(jnp.float32)

    def gather_levels(pieces):
        up = lax.all_gather(pieces, "ctx")
        if outer == 1:
            return up[None]
        return lax.all_gather(up, "fsdp", axis_index_groups=far)

    def scatter_levels(pieces):
        if outer == 1:
            pieces = pieces[0]
        else:
            pieces = lax.psum_scatter(pieces, "fsdp", scatter_dimension=0, axis_index_groups=far)
        return lax.psum_scatter(pieces, "ctx", scatter_dimension=0)

    def fetch_columns(shard):
        block, cols = shard.shape
        pieces = trade(shard.reshape(block, inner, cols // inner).transpose(1, 0, 2))
        whole = gather_levels(pieces).transpose(0, 2, 1, 3, 4)
        return whole.reshape(-1, cols // inner)

    def fetch_rows(shard):
        length, block = shard.shape
        pieces = trade(shard.reshape(inner, length // inner, block))
        whole = gather_levels(pieces).transpose(3, 0, 2, 1, 4)
        return whole.reshape(length // inner, -1)

    def return_columns(grad):
        total, cols = grad.shape
        grad = grad.astype(jnp.bfloat16).reshape(outer, inner, ctx, -1, cols)
        mine = trade(scatter_levels(grad.transpose(0, 2, 1, 3, 4)))
        return mine.transpose(1, 0, 2).reshape(mine.shape[1], -1).astype(jnp.float32)

    def return_rows(grad):
        length, total = grad.shape
        grad = grad.astype(jnp.bfloat16).reshape(length, outer, inner, ctx, -1)
        mine = trade(scatter_levels(grad.transpose(1, 3, 2, 0, 4)))
        return mine.reshape(inner * length, -1).astype(jnp.float32)

    def dot(left, right, dims):
        return lax.dot_general(left, right, (dims, ((), ())), preferred_element_type=jnp.float32)

    gains = lax.all_gather(jnp.stack([attn_gain, ffn_gain]), ("fsdp", "ctx"))
    gain_attn = gains[:, 0].reshape(-1).astype(jnp.float32)
    gain_ffn = gains[:, 1].reshape(-1).astype(jnp.float32)
    span = positions.shape[2]
    ids_here = lax.dynamic_slice_in_dim(block_ids[:, 0], c_at * span, span, 1)
    marks = lax.all_gather(jnp.stack([positions[:, 0], ids_here]), ("fsdp", "ctx"))
    my_seq = f_at // inner * inner + c_at
    marks = lax.dynamic_slice_in_dim(marks, my_seq * ctx, ctx, 0)
    marks = marks.transpose(1, 2, 0, 3).reshape(2, micro, ctx * span)
    pos, ids = marks[0], marks[1]

    weight_qkv = fetch_columns(wqkv)
    weight_out = fetch_rows(wo)
    weight_gate = fetch_columns(w_gate)
    weight_up = fetch_columns(w_up)
    weight_down = fetch_rows(w_down)

    stream = rehome(hidden_in).reshape(micro * rows, width).astype(jnp.float32)
    grad_out_low = rehome(cotangent).reshape(micro * rows, width)
    grad_out = grad_out_low.astype(jnp.float32)

    def to_heads(flat):
        split = flat.reshape(inner * tp, micro, rows, -1, HEAD_DIM).transpose(1, 0, 2, 3, 4)
        return split.reshape(micro, inner * tp * rows, -1, HEAD_DIM)

    def from_heads(heads):
        split = heads.reshape(micro, inner * tp, rows, -1).transpose(1, 0, 2, 3)
        return split.reshape(inner * tp * micro * rows, -1)

    normed_one, factor_one, attn_rows = norm_rows(stream, gain_attn)
    attn_in = spread(attn_rows).reshape(-1, width)
    projected = to_heads(dot(attn_in, weight_qkv, ((1,), (0,))))
    group = HEADS // KV_HEADS
    cos_table, sin_table = rope_tables(pos)
    cos_heads, sin_heads = cos_table[:, :, None], sin_table[:, :, None]
    turning = projected[:, :, : group + 1]
    turning = (turning * cos_heads + turned(turning) * sin_heads).astype(jnp.bfloat16)
    queries, keys = turning[:, :, :group], turning[:, :, group]
    values = projected[:, :, group + 1].astype(jnp.bfloat16)
    allowed = (ids[:, None, :] <= ids[:, :, None])[:, None]
    raw = jnp.einsum("blge,bme->bglm", queries, keys, preferred_element_type=jnp.float32)
    scores = jnp.where(allowed, raw * score_scale, MASKED)
    row_max = jnp.max(scores, axis=-1, keepdims=True)
    exponent = jnp.exp(scores - row_max)
    prob = exponent / jnp.sum(exponent, axis=-1, keepdims=True)
    prob_low = prob.astype(jnp.bfloat16)
    mixed = jnp.einsum("bglm,bme->blge", prob_low, values, preferred_element_type=jnp.float32)
    mixed = from_heads(mixed.astype(jnp.bfloat16))
    out_part = dot(mixed, weight_out, ((1,), (0,)))
    stream_mid = stream + fold(out_part.reshape(inner, tp, -1, width))
    normed_two, factor_two, ffn_rows = norm_rows(stream_mid, gain_ffn)
    ffn_in = spread(ffn_rows).reshape(-1, width)
    dy = spread(grad_out_low).reshape(-1, width)

    gate_pre = dot(ffn_in, weight_gate, ((1,), (0,)))
    up_pre = dot(ffn_in, weight_up, ((1,), (0,)))
    gate_sig = jax.nn.sigmoid(gate_pre)
    gate_act = gate_pre * gate_sig
    hidden = (gate_act * up_pre).astype(jnp.bfloat16)
    grad_hidden = dot(dy, weight_down, ((1,), (1,)))
    grad_gate_pre = (
        grad_hidden * up_pre * gate_sig * (1.0 + gate_pre * (1.0 - gate_sig))
    ).astype(jnp.bfloat16)
    grad_up_pre = (grad_hidden * gate_act).astype(jnp.bfloat16)
    grad_ffn_part = dot(grad_gate_pre, weight_gate, ((1,), (1,))) + dot(
        grad_up_pre, weight_up, ((1,), (1,))
    )
    grad_ffn_in = fold(grad_ffn_part.reshape(inner, tp, -1, width))
    down_part = dot(hidden, weight_down, ((1,), (0,)))
    stream_out = stream_mid + fold(down_part.reshape(inner, tp, -1, width))
    grad_down = return_rows(dot(hidden, dy, ((0,), (0,))))
    grad_gate = return_columns(dot(ffn_in, grad_gate_pre, ((0,), (0,))))
    grad_up = return_columns(dot(ffn_in, grad_up_pre, ((0,), (0,))))

    def back_rows(grad, normed, factor, gain_row):
        grad_normed = grad * gain_row
        inner_mean = jnp.mean(grad_normed * normed, axis=-1, keepdims=True)
        return factor * (grad_normed - normed * inner_mean), jnp.sum(grad * normed, axis=0)

    mid_norm, gain_ffn_part = back_rows(grad_ffn_in, normed_two, factor_two, gain_ffn)
    grad_mid = grad_out + mid_norm
    grad_mid_low = spread(grad_mid.astype(jnp.bfloat16)).reshape(-1, width)
    grad_mixed = to_heads(dot(grad_mid_low, weight_out, ((1,), (1,))).astype(jnp.bfloat16))
    grad_wo = return_rows(dot(mixed, grad_mid_low, ((0,), (0,))))
    grad_prob = jnp.einsum("blge,bme->bglm", grad_mixed, values, preferred_element_type=jnp.float32)
    inner_prob = jnp.sum(grad_prob * prob, axis=-1, keepdims=True)
    grad_scores = (score_scale * prob * (grad_prob - inner_prob)).astype(jnp.bfloat16)
    grad_queries = jnp.einsum(
        "bglm,bme->blge", grad_scores, keys, preferred_element_type=jnp.float32
    )
    grad_keys = jnp.einsum(
        "bglm,blge->bme", grad_scores, queries, preferred_element_type=jnp.float32
    )
    grad_values = jnp.einsum(
        "bglm,blge->bme", prob_low, grad_mixed, preferred_element_type=jnp.float32
    )
    grad_turning = jnp.concatenate([grad_queries, grad_keys[:, :, None]], axis=2)
    grad_turning = grad_turning * cos_heads + turned_back(grad_turning * sin_heads)
    grad_projected = jnp.concatenate([grad_turning, grad_values[:, :, None]], axis=2)
    grad_projected = from_heads(grad_projected.astype(jnp.bfloat16))
    grad_attn_in = fold(
        dot(grad_projected, weight_qkv, ((1,), (1,))).reshape(inner, tp, -1, width)
    )
    grad_wqkv = return_columns(dot(attn_in, grad_projected, ((0,), (0,))))
    in_norm, gain_attn_part = back_rows(grad_attn_in, normed_one, factor_one, gain_attn)
    grad_in = (grad_mid + in_norm).astype(jnp.bfloat16)

    gain_parts = jnp.stack([gain_attn_part, gain_ffn_part], axis=1).reshape(fsdp * ctx, -1, 2)
    gain_sums = lax.psum_scatter(gain_parts, ("fsdp", "ctx"), scatter_dimension=0)
    gain_sums = lax.psum(gain_sums, "tp")

    def home(array):
        return rehome(array.reshape(micro, 1, rows, width))

    return (
        home(stream_out.astype(jnp.bfloat16)),
        home(grad_in),
        gain_sums[:, 0],
        grad_wqkv,
        grad_wo,
        gain_sums[:, 1],
        grad_gate,
        grad_up,
        grad_down,
    )


MESH = pl.DeviceIdType.MESH
ROWS = 128
LANES = 128
NARROW = jnp.bfloat16
WIDE = jnp.float32
HALF = HEAD_DIM // 2
SCALE = HEAD_DIM ** (-0.5)
ANYWHERE = pl.BlockSpec(memory_space=pl.ANY)


class Place:
    def __init__(self):
        f, c, t = lax.axis_index("fsdp"), lax.axis_index("ctx"), lax.axis_index("tp")
        self.f, self.c, self.t = f, c, t
        fs, fy = f + 1 - 2 * (f % 2), (f + 2) % 4
        fd = (fs + 2) % 4
        self.fs, self.fy, self.fd = fs, fy, fd
        self.c1, self.c2 = c + 1 - 2 * (c % 2), (c + 2) % 4
        self.c3 = (self.c1 + 2) % 4
        self.side, self.core, self.row = (f, c, 1 - t), (fs, c, t), (fy, c, t)
        self.cross = (fd, c, t)
        self.z1, self.z2 = (f, self.c1, t), (f, self.c2, t)
        self.fr, self.cr = f % 2 * 2 + f // 2, c % 2 * 2 + c // 2
        self.swap = (self.cr, self.fr, t)
        self.b, self.b_side = f * 2 + t, f * 2 + 1 - t
        self.b_row, self.b_far = fy * 2 + t, fy * 2 + 1 - t
        self.b_core, self.b_core_side = fs * 2 + t, fs * 2 + 1 - t
        self.b_core_row, self.b_core_far = fd * 2 + t, fd * 2 + 1 - t


class Sent:
    def __init__(self, copy, landing):
        self.copy, self.landing = copy, landing

    def arrive(self):
        self.landing.wait_recv()

    def leave(self):
        self.copy.wait_send()


class Post:
    def __init__(self, send_sems, recv_sems, local_sems):
        self.sems = send_sems, recv_sems
        self.local_sems = local_sems
        self.n, self.n_local = 0, 0
        self.out, self.kept = [], []

    def make(self, source, target, device, lands):
        sems = dict(
            send_sem=self.sems[0].at[self.n],
            recv_sem=self.sems[1].at[self.n],
            device_id=device,
            device_id_type=MESH,
        )
        self.n += 1
        copy = pltpu.make_async_remote_copy(src_ref=source, dst_ref=target, **sems)
        landing = pltpu.make_async_remote_copy(src_ref=lands, dst_ref=lands, **sems)
        return Sent(copy, landing)

    def send(self, source, target, device, lands):
        sent = self.make(source, target, device, lands)
        sent.copy.start()
        self.out.append(sent)
        return sent

    def keep(self, source, target):
        copy = pltpu.make_async_copy(source, target, self.local_sems.at[self.n_local])
        self.n_local += 1
        copy.start()
        self.kept.append(copy)
        return copy

    def settle(self, copies):
        for copy in copies:
            copy.wait()
        self.kept = [kept for kept in self.kept if not any(kept is copy for copy in copies)]

    def close(self):
        for sent in self.out:
            sent.leave()
        for copy in self.kept:
            copy.wait()
        self.out, self.kept = [], []


def meet(devices):
    bar = pltpu.get_barrier_semaphore()
    for device in devices:
        pl.semaphore_signal(bar, inc=1, device_id=device, device_id_type=MESH)
    pl.semaphore_wait(bar, len(devices))


class Spread:
    def __init__(self, post, at, out):
        self.post, self.at, self.out = post, at, out
        self.sent = {}

    def slot(self, block, half):
        return self.out.at[block, pl.ds(half * ROWS, ROWS)]

    def own(self, half, source):
        at, mine = self.at, self.slot(self.at.b, half)
        self.sent["side", half] = self.post.send(source, mine, at.side, self.slot(at.b_side, half))
        self.sent["row", half] = self.post.send(source, mine, at.row, self.slot(at.b_row, half))
        self.sent["core", half] = self.post.send(source, mine, at.core, self.slot(at.b_core, half))
        self.post.keep(source, mine)

    def pass_on(self, name, half, block, lands):
        here = self.slot(block, half)
        self.sent[name, half] = self.post.send(
            here, here, self.at.core, self.slot(lands, half)
        )

    def relay(self, half):
        at = self.at
        first = ("side", "row") if half == 0 else ("row", "side")
        for name in first:
            self.sent[name, half].arrive()
            block = at.b_side if name == "side" else at.b_row
            here = self.slot(block, half)
            if half == 0 and name == "side":
                self.sent["far", 0] = self.post.send(here, here, at.row, self.slot(at.b_far, 0))
            if half == 1 and name == "row":
                self.sent["far", 1] = self.post.send(here, here, at.side, self.slot(at.b_far, 1))
            lands = at.b_core_side if name == "side" else at.b_core_row
            self.pass_on("core_" + name, half, block, lands)

    def corner(self):
        for half in range(2):
            self.sent["far", half].arrive()
            self.pass_on("core_far", half, self.at.b_far, self.at.b_core_far)

    def finish(self):
        for name in ("core", "core_side", "core_row", "core_far"):
            for half in range(2):
                self.sent[name, half].arrive()


SPREAD_COPIES, SPREAD_KEPT = 14, 2


class Fold:
    copies = 10

    def __init__(self, post, at, part, scratch):
        self.post, self.at, self.part = post, at, part
        self.got, self.give, self.far, self.side, self.row, self.gx, self.gy, self.held = scratch

    @staticmethod
    def scratch(width):
        return [
            pltpu.VMEM((4, 2 * ROWS, width), NARROW),
            pltpu.VMEM((4, 2 * ROWS, width), NARROW),
            pltpu.VMEM((2, ROWS, width), NARROW),
            pltpu.VMEM((2, ROWS, width), NARROW),
            pltpu.VMEM((2, ROWS, width), NARROW),
            pltpu.VMEM((3, ROWS, width), NARROW),
            pltpu.VMEM((3, ROWS, width), NARROW),
            pltpu.VMEM((4, ROWS, width), WIDE),
        ]

    def to_core(self, slot, block):
        self.give[slot] = self.part(block).astype(NARROW)
        return self.post.send(self.give.at[slot], self.got.at[slot], self.at.core, self.got.at[slot])

    def first(self):
        at, post = self.at, self.post
        sent = self.to_core(3, at.b_core_far)
        value = self.part(at.b_far)
        sent.arrive()
        value = (value + self.got[3].astype(WIDE)).astype(NARROW)
        self.far[0] = value[:ROWS]
        self.far[1] = value[ROWS:]
        self.far_x = post.send(self.far.at[0], self.gx.at[0], at.side, self.gx.at[0])
        self.far_y = post.send(self.far.at[1], self.gy.at[0], at.row, self.gy.at[0])
        sent = self.to_core(1, at.b_core_side)
        value = self.part(at.b_side)
        sent.arrive()
        value = value + self.got[1].astype(WIDE)
        self.side[0] = value[:ROWS].astype(NARROW)
        self.held[2] = value[ROWS:]
        self.side_x = post.send(self.side.at[0], self.gx.at[1], at.side, self.gx.at[1])
        sent = self.to_core(2, at.b_core_row)
        value = self.part(at.b_row)
        sent.arrive()
        value = value + self.got[2].astype(WIDE)
        self.row[1] = value[ROWS:].astype(NARROW)
        self.held[3] = value[:ROWS]
        self.row_y = post.send(self.row.at[1], self.gy.at[1], at.row, self.gy.at[1])
        sent = self.to_core(0, at.b_core)
        value = self.part(at.b)
        sent.arrive()
        value = value + self.got[0].astype(WIDE)
        self.held[0] = value[:ROWS]
        self.held[1] = value[ROWS:]

    def second(self):
        at, post = self.at, self.post
        self.far_y.arrive()
        self.side[1] = (self.held[2] + self.gy[0].astype(WIDE)).astype(NARROW)
        self.side_b = post.send(self.side.at[1], self.gx.at[2], at.side, self.gx.at[2])
        self.far_x.arrive()
        self.row[0] = (self.held[3] + self.gx[0].astype(WIDE)).astype(NARROW)
        self.row_a = post.send(self.row.at[0], self.gy.at[2], at.row, self.gy.at[2])

    def third(self):
        self.side_x.arrive()
        self.row_y.arrive()
        self.held[0] = self.held[0] + self.gx[1].astype(WIDE)
        self.held[1] = self.held[1] + self.gy[1].astype(WIDE)
        self.row_a.arrive()
        self.held[0] = self.held[0] + self.gy[2].astype(WIDE)
        self.side_b.arrive()
        self.held[1] = self.held[1] + self.gx[2].astype(WIDE)


class Climb:
    copies, kept = 3, 1

    def __init__(self, post, at, level, out):
        self.post, self.at, self.out = post, at, out
        mine = out.at[:, at.c]
        self.far = post.send(level, mine, at.z2, out.at[:, at.c2])
        self.close = post.send(level, mine, at.z1, out.at[:, at.c1])
        self.own = post.keep(level, mine)

    def forward(self):
        at = self.at
        self.far.arrive()
        there = self.out.at[:, at.c2]
        self.last = self.post.send(there, there, at.z1, self.out.at[:, at.c3])

    def finish(self):
        self.close.arrive()
        self.last.arrive()
        self.post.settle([self.own])


def call(kernel, name, outs, args, scratch, copies, kept, collective_id):
    sems = [
        pltpu.SemaphoreType.DMA((copies,)),
        pltpu.SemaphoreType.DMA((copies,)),
        pltpu.SemaphoreType.DMA((kept,)),
    ]
    n_in, n_out = len(args), len(outs)

    def inner(*refs):
        post = Post(*refs[len(refs) - 3 :])
        kernel(
            post, Place(), refs[:n_in], refs[n_in : n_in + n_out], refs[n_in + n_out : len(refs) - 3]
        )
        post.close()
        assert post.n <= copies and post.n_local <= kept, (post.n, post.n_local)

    return pl.pallas_call(
        inner,
        out_shape=outs,
        in_specs=[ANYWHERE] * n_in,
        out_specs=[ANYWHERE] * n_out,
        scratch_shapes=scratch + sems,
        compiler_params=pltpu.CompilerParams(
            collective_id=collective_id, has_side_effects=True, vmem_limit_bytes=62 << 20
        ),
        name=name,
    )(*args)


def shape(*dims, dtype=NARROW):
    return jax.ShapeDtypeStruct(dims, dtype)


def gain_row(gains_ref, which):
    return jnp.concatenate([gains_ref[i, which : which + 1, :] for i in range(16)], axis=1)


def normed_rows(values):
    factor = lax.rsqrt(jnp.mean(values * values, axis=-1, keepdims=True) + EPS)
    return values * factor, factor


class Swap:
    def __init__(self, post, at):
        self.post, self.at, self.moves = post, at, []

    def __call__(self, source, target, lands):
        post, at = self.post, self.at
        sent = post.make(source, target, at.swap, lands)
        local = pltpu.make_async_copy(source, target, post.local_sems.at[post.n_local])
        post.n_local += 1

        @pl.when(at.f != at.cr)
        def _():
            sent.copy.start()

        @pl.when(at.f == at.cr)
        def _():
            local.start()

        self.moves.append(sent)

        def arrive():
            @pl.when(at.f != at.cr)
            def _():
                sent.landing.wait_recv()

            @pl.when(at.f == at.cr)
            def _():
                local.wait()

        return arrive

    def finish(self):
        @pl.when(self.at.f != self.at.cr)
        def _():
            for sent in self.moves:
                sent.copy.wait_send()


def meet_swap(at):
    bar = pltpu.get_barrier_semaphore()
    partners = (at.side, at.core, at.row, at.cross, at.z1, at.z2)
    for device in partners:
        pl.semaphore_signal(bar, inc=1, device_id=device, device_id_type=MESH)

    @pl.when(at.f != at.cr)
    def _():
        pl.semaphore_signal(bar, inc=1, device_id=at.swap, device_id_type=MESH)
        pl.semaphore_wait(bar, len(partners) + 1)

    @pl.when(at.f == at.cr)
    def _():
        pl.semaphore_wait(bar, len(partners))


HALVES = [pl.ds(half * ROWS, ROWS) for half in range(2)]


def start_kernel(post, at, ins, outs, scratch):
    hidden, cot, table, marks, gains, wqkv, wo, w_gate, w_up, w_down = ins
    x_own, cot_own, attn_in, tables, all_marks, all_gains, qkv_all, out_all, gate_lvl, up_lvl, down_lvl = outs
    rows_in, rows_out, gain_buf = scratch
    f, c = at.f, at.c
    meet_swap(at)
    swap = Swap(post, at)
    x_moved = [swap(hidden.at[half], rows_in.at[half], rows_in.at[half]) for half in HALVES]
    heads = wqkv.shape[1] // 4
    span = wo.shape[0] // 4
    first = []
    for device, k in ((at.row, at.fy), (at.cross, at.fd), (at.core, at.fs)):
        lane = pl.ds(pl.multiple_of(k * heads, LANES), heads)
        first.append(post.send(wqkv.at[:, lane], qkv_all.at[f, c], device, qkv_all.at[k, c]))
        row = pl.ds(pl.multiple_of(k * span, LANES), span)
        first.append(post.send(wo.at[row], out_all.at[f, c], device, out_all.at[k, c]))
    lane = pl.ds(pl.multiple_of(f * heads, LANES), heads)
    own = [post.keep(wqkv.at[:, lane], qkv_all.at[f, c])]
    row = pl.ds(pl.multiple_of(f * span, LANES), span)
    own.append(post.keep(wo.at[row], out_all.at[f, c]))
    table_moved = swap(table, tables.at[at.cr], tables.at[f])
    marks_moved = swap(marks, all_marks.at[at.cr], all_marks.at[f])

    mine = gain_buf.at[f, c]
    post.settle([post.keep(gains, mine)])
    step = post.send(mine, mine, at.core, gain_buf.at[at.fs, c])
    step.arrive()
    pair = gain_buf.at[pl.ds(f // 2 * 2, 2), c]
    step = post.send(pair, pair, at.row, gain_buf.at[pl.ds(at.fy // 2 * 2, 2), c])
    step.arrive()
    step = post.send(gain_buf.at[:, c], gain_buf.at[:, c], at.z1, gain_buf.at[:, at.c1])
    step.arrive()
    pair = gain_buf.at[:, pl.ds(c // 2 * 2, 2)]
    step = post.send(pair, pair, at.z2, gain_buf.at[:, pl.ds(at.c2 // 2 * 2, 2)])
    step.arrive()
    gain = jnp.concatenate([gain_buf[i // 4, i % 4, 0:1, :] for i in range(16)], axis=1)
    post.keep(gain_buf, all_gains)

    post.settle(own)
    for sent in first:
        sent.arrive()

    spread = Spread(post, at, attn_in)
    levels = []

    def climb():
        for out in (qkv_all, out_all):
            here, there = out.at[:, c], out.at[:, at.c2]
            far = post.send(here, here, at.z2, there)
            close = post.send(here, here, at.z1, out.at[:, at.c1])
            levels.append((far, close, there, out))

    for half in range(2):
        x_moved[half]()
        if half == 1:
            climb()
        normed, _ = normed_rows(rows_in[HALVES[half]].astype(WIDE))
        rows_out[HALVES[half]] = (normed * gain).astype(NARROW)
        spread.own(half, rows_out.at[HALVES[half]])
        post.keep(rows_in.at[HALVES[half]], x_own.at[HALVES[half]])

    table_moved()
    marks_moved()
    small = []
    for buf in (tables, all_marks):
        here = buf.at[f]
        small.append((buf, post.send(here, here, at.core, buf.at[at.fs])))
    smaller = []
    for buf, sent in small:
        sent.arrive()
        pair = buf.at[pl.ds(f // 2 * 2, 2)]
        smaller.append(post.send(pair, pair, at.row, buf.at[pl.ds(at.fy // 2 * 2, 2)]))

    spread.relay(0)
    spread.relay(1)

    part = w_gate.shape[1] // 4
    chunk = part // 4
    later = []
    for device, k in ((at.row, at.fy), (at.cross, at.fd), (at.core, at.fs), (None, f)):
        for j in range(4):
            lane = pl.ds(pl.multiple_of(k * part + j * chunk, LANES), chunk)
            for source, target in (
                (w_gate.at[:, lane], gate_lvl),
                (w_up.at[:, lane], up_lvl),
                (w_down.at[lane], down_lvl),
            ):
                if device is None:
                    post.keep(source, target.at[j, f])
                else:
                    later.append(post.send(source, target.at[j, f], device, target.at[j, k]))

    forwards = []
    for far, close, there, out in levels:
        far.arrive()
        forwards.append((post.send(there, there, at.z1, out.at[:, at.c3]), close))
    cot_moved = [swap(cot.at[half], cot_own.at[half], cot_own.at[half]) for half in HALVES]
    spread.corner()
    for last, close in forwards:
        last.arrive()
        close.arrive()
    spread.finish()
    for sent in smaller + later:
        sent.arrive()
    for arrive in cot_moved:
        arrive()
    swap.finish()


def rope(values, cos_full, sin_full):
    return values * cos_full + pltpu.roll(values, HALF, 1) * sin_full


def rope_back(values, cos_full, sin_full):
    return values * cos_full - pltpu.roll(values, HALF, 1) * sin_full


def rope_full(table):
    turned_table = pltpu.roll(table, HALF, 1)
    low = lax.broadcasted_iota(jnp.int32, table.shape, 1) < HALF
    return jnp.where(low, table, turned_table), jnp.where(low, -turned_table, table)


def mm(left, right, dims=((1,), (0,))):
    return lax.dot_general(left, right, (dims, ((), ())), preferred_element_type=WIDE)


TILE = 256
QUARTER = (0, 2, 1, 3)


def softmax_tile(query, key, id_col, id_row):
    raw = mm(query, key, ((1,), (1,))) * SCALE
    raw = jnp.where(id_row <= id_col, raw, MASKED)
    top = jnp.max(raw, axis=-1, keepdims=True)
    exponent = jnp.exp(raw - top)
    return exponent * (1.0 / jnp.sum(exponent, axis=-1, keepdims=True))


def id_rows(marks, m, tiles):
    return jnp.concatenate([marks[QUARTER[i], m : m + 1, :] for i in range(tiles)], axis=1)


def attend_kernel(jobs, post, at, ins, outs, scratch):
    attn_in, qkv_all, tables_in, marks_in, cot_own = ins[:5]
    levels = jobs(ins[5:])
    queries, keys, values, mixed, dy, *climbed = outs
    rows, weight, tables, marks, q_buf, k_buf, v_buf, mix_buf = scratch
    meet((at.side, at.core, at.row, at.z1, at.z2))
    local = [
        post.keep(tables_in, tables),
        post.keep(marks_in, marks),
        post.keep(qkv_all, weight),
        post.keep(attn_in.at[:, pl.ds(0, ROWS)], rows.at[0]),
        post.keep(attn_in.at[:, pl.ds(ROWS, ROWS)], rows.at[1]),
    ]
    spread = Spread(post, at, dy)
    for half in range(2):
        spread.own(half, cot_own.at[pl.ds(half * ROWS, ROWS)])
    climbs = [Climb(post, at, level, out) for level, out in zip(levels, climbed)]
    post.settle(local)
    width = rows.shape[-1]
    columns = weight.shape[-1]
    for m in range(2):
        for i in range(4):
            q = QUARTER[i]
            here = rows[m, 2 * q : 2 * q + 2].reshape(TILE, width)
            projected = mm(here, weight[...].reshape(width, columns))
            cos_full, sin_full = rope_full(tables[q, m])
            place = pl.ds(i * TILE, TILE)
            for g in range(2):
                lane = slice(g * HEAD_DIM, (g + 1) * HEAD_DIM)
                q_buf[m, place, lane] = rope(projected[:, lane], cos_full, sin_full).astype(NARROW)
            k_buf[m, place] = rope(projected[:, 256:384], cos_full, sin_full).astype(NARROW)
            v_buf[m, place] = projected[:, 384:512].astype(NARROW)
    spread.relay(0)
    for m in range(2):
        for i in range(4):
            n = min(i + 2, 4) * TILE
            q = QUARTER[i]
            id_col = marks[q].T[:, m : m + 1]
            id_row = id_rows(marks, m, n // TILE)
            for g in range(2):
                lane = slice(g * HEAD_DIM, (g + 1) * HEAD_DIM)
                prob = softmax_tile(
                    q_buf[m, i * TILE : (i + 1) * TILE, lane], k_buf[m, :n], id_col, id_row
                )
                value = mm(prob.astype(NARROW), v_buf[m, :n]).astype(NARROW)
                for h in range(2):
                    mix_buf[2 * q + h, m * ROWS : (m + 1) * ROWS, lane] = value[
                        h * ROWS : (h + 1) * ROWS
                    ]
        if m == 0:
            spread.relay(1)
            for climb in climbs:
                climb.forward()
    for source, target in ((q_buf, queries), (k_buf, keys), (v_buf, values), (mix_buf, mixed)):
        post.keep(source, target)
    spread.corner()
    spread.finish()
    for climb in climbs:
        climb.finish()


def middle_kernel(jobs, post, at, ins, outs, scratch):
    mixed, out_all, x_own, gains_in = ins[:4]
    levels = jobs(ins[4:])
    mid_own, ffn_in, *climbed = outs
    mix_buf, weight, x_buf, gains, rows_out, *fold_scratch = scratch
    meet((at.side, at.core, at.row, at.z1, at.z2))
    local = [
        post.keep(out_all.at[i // 4, i % 4], weight.at[:, pl.ds(i * LANES, LANES)])
        for i in range(16)
    ]
    local += [post.keep(mixed, mix_buf), post.keep(x_own, x_buf), post.keep(gains_in, gains)]
    post.settle(local)
    climbs = [Climb(post, at, level, out) for level, out in zip(levels, climbed)]

    def part(block):
        return mm(mix_buf[block], weight[...])

    fold = Fold(post, at, part, fold_scratch)
    fold.first()
    fold.second()
    fold.third()
    gain = jnp.concatenate([gains[i // 4, i % 4, 1:2, :] for i in range(16)], axis=1)
    spread = Spread(post, at, ffn_in)
    for half in range(2):
        rows = pl.ds(half * ROWS, ROWS)
        value = fold.held[half] + x_buf[rows].astype(WIDE)
        fold.held[half] = value
        normed, _ = normed_rows(value)
        rows_out[half] = (normed * gain).astype(NARROW)
        spread.own(half, rows_out.at[half])
        post.keep(fold.held.at[half], mid_own.at[rows])
    spread.relay(0)
    for climb in climbs:
        climb.forward()
    spread.relay(1)
    spread.corner()
    spread.finish()
    for climb in climbs:
        climb.finish()


class Jobs:
    def __init__(self, *wanted):
        self.wanted = wanted

    def __call__(self, level_refs):
        return [level_refs[a].at[j] for a, j in self.wanted]

    def shapes(self, levels):
        return [
            jax.ShapeDtypeStruct((4, 4) + levels[a].shape[2:], NARROW) for a, j in self.wanted
        ]


def small_arrays(block_ids, positions, attn_gain, ffn_gain):
    micro, _, span = positions.shape
    cos_table, sin_table = rope_tables(positions[:, 0])
    table = jnp.concatenate([cos_table[..., :HALF], sin_table[..., :HALF]], axis=-1)
    ids = lax.dynamic_slice_in_dim(block_ids[:, 0], lax.axis_index("ctx") * span, span, 1)
    marks = jnp.zeros((8, span), WIDE).at[:micro].set(ids.astype(WIDE))
    gains = jnp.zeros((8, LANES), WIDE).at[0].set(attn_gain.astype(WIDE))
    return table, marks, gains.at[1].set(ffn_gain.astype(WIDE))


def ffn_kernel(jobs, post, at, ins, outs, scratch):
    ffn_in, dy = ins[:2]
    ready = ins[2:8]
    levels = jobs(ins[8:])
    hidden, grads_pre, parts, *climbed = outs
    x_buf, dy_buf, gate_buf, up_buf, down_buf, act, act_t, staged = scratch
    meet((at.z1, at.z2))
    climbs = [Climb(post, at, level, out) for level, out in zip(levels, climbed)]
    local = [post.keep(ffn_in, x_buf), post.keep(dy, dy_buf)]
    weights = list(ready) + list(climbed)

    def load(j):
        slot = j % 2
        gate, up, down = weights[3 * j : 3 * j + 3]
        copies = [post.keep(gate, gate_buf.at[slot]), post.keep(up, up_buf.at[slot])]
        for i in range(16):
            copies.append(
                post.keep(down.at[i // 4, i % 4], down_buf.at[slot, :, pl.ds(i * LANES, LANES)])
            )
        return copies

    loading = load(0)
    post.settle(local)
    width = x_buf.shape[-1]
    saved = []
    for j in range(4):
        slot = j % 2
        if loading is None:
            for climb in climbs[3 * (j - 2) : 3 * (j - 1)]:
                climb.finish()
            loading = load(j)
        post.settle(loading)
        loading = load(1) if j == 0 else None
        post.settle(saved)

        def rows(i, carry):
            x, grad = x_buf[i], dy_buf[i]
            gate = mm(x, gate_buf[slot].reshape(width, -1))
            up = mm(x, up_buf[slot].reshape(width, -1))
            grad_hidden = mm(grad, down_buf[slot], ((1,), (1,)))
            sig = 1.0 / (1.0 + jnp.exp(-gate))
            silu = gate * sig
            values = (
                grad_hidden * up * sig * (1.0 + gate * (1.0 - sig)),
                grad_hidden * silu,
                silu * up,
            )
            place = pl.ds(pl.multiple_of(i * TILE, TILE), TILE)
            for k in range(3):
                act[k, i] = values[k].astype(NARROW)
                act_t[k, :, place] = values[k].T.astype(NARROW)
            return carry

        lax.fori_loop(0, 8, rows, 0)
        chunk = act.shape[-1]
        lane = pl.ds(j * chunk, chunk)
        saved = [
            post.keep(act.at[0], grads_pre.at[:, :, lane]),
            post.keep(act.at[1], grads_pre.at[:, :, pl.ds((4 + j) * chunk, chunk)]),
            post.keep(act.at[2], hidden.at[:, :, lane]),
        ]
        if j < 2:
            for climb in climbs[3 * j : 3 * j + 3]:
                climb.forward()

        def sums(n, carry):
            place = pl.ds(pl.multiple_of(n * TILE, TILE), TILE)
            x = x_buf[:, :, place].reshape(8 * TILE, TILE)
            grad = dy_buf[:, :, place].reshape(8 * TILE, TILE)
            for k in range(3):
                value = mm(act_t[k], grad if k == 2 else x).astype(NARROW)
                staged[k, 2 * n] = value[:, :LANES]
                staged[k, 2 * n + 1] = value[:, LANES:]
            return carry

        lax.fori_loop(0, 8, sums, 0)
        for k in range(3):
            for fl in range(4):
                saved.append(post.keep(staged.at[k, pl.ds(4 * fl, 4)], parts.at[3 * j + k, fl]))


class Descend:
    def __init__(self, post, at, pieces, got):
        self.near = post.send(pieces.at[:, at.c1], got.at[0], at.z1, got.at[0])
        self.next = post.send(pieces.at[:, at.c3], got.at[1], at.z1, got.at[1])

    def finish(self):
        self.near.arrive()
        self.next.arrive()


def norm_back_rows(grad, values, gain):
    normed, factor = normed_rows(values)
    scaled = grad * gain
    inner_mean = jnp.mean(scaled * normed, axis=-1, keepdims=True)
    return factor * (scaled - normed * inner_mean), jnp.sum(grad * normed, axis=0, keepdims=True)


def back_kernel(first, count, post, at, ins, outs, scratch):
    grads_pre, mid_own, cot_own, gains_in, parts, *weights = ins
    grad_mid_own, grad_mid, gain_part, got = outs
    pre_buf, weight, mid_buf, cot_buf, gains, rows_out, gain_out, *fold_scratch = scratch
    meet((at.side, at.core, at.row, at.z1, at.z2))
    downs = [Descend(post, at, parts.at[first + q], got.at[q]) for q in range(count)]
    chunk = pre_buf.shape[-1] // 8
    local = [post.keep(grads_pre, pre_buf)]
    for a in range(2):
        for j in range(4):
            place = pl.ds((4 * a + j) * chunk, chunk)
            local.append(post.keep(weights[4 * a + j], weight.at[:, :, :, place]))
    local += [post.keep(mid_own, mid_buf), post.keep(cot_own, cot_buf), post.keep(gains_in, gains)]
    post.settle(local)
    width = mid_buf.shape[-1]

    def part(block):
        return mm(pre_buf[block], weight[...].reshape(width, -1), ((1,), (1,)))

    fold = Fold(post, at, part, fold_scratch)
    fold.first()
    fold.second()
    fold.third()
    gain = jnp.concatenate([gains[i // 4, i % 4, 1:2, :] for i in range(16)], axis=1)
    spread = Spread(post, at, grad_mid)
    total = jnp.zeros((1, width), WIDE)
    for half in range(2):
        rows = HALVES[half]
        back, piece = norm_back_rows(fold.held[half], mid_buf[rows], gain)
        total = total + piece
        value = cot_buf[rows].astype(WIDE) + back
        fold.held[half] = value
        rows_out[half] = value.astype(NARROW)
        spread.own(half, rows_out.at[half])
        post.keep(fold.held.at[half], grad_mid_own.at[rows])
    gain_out[...] = jnp.broadcast_to(total, gain_out.shape)
    post.keep(gain_out, gain_part)
    spread.relay(0)
    spread.relay(1)
    spread.corner()
    spread.finish()
    for down in downs:
        down.finish()


def attend_back_kernel(first, count, post, at, ins, outs, scratch):
    (
        grad_mid, queries, keys, values, marks_in, tables_in, out_all, mixed, attn_in, hidden, mid_own, parts, *downs_in
    ) = ins
    grad_proj, parts_attn, hidden_out, got = outs
    (
        gm_buf, q_buf, k_buf, v_buf, marks, tables, weight, mix_buf, hid_buf, down_buf, gp_buf, gk_buf, gv_buf,
        mix_t, gp_t, column, staged, mid_buf, out_buf, *fold_scratch
    ) = scratch
    meet((at.side, at.core, at.row, at.z1, at.z2))
    steps = [Descend(post, at, parts.at[first + q], got.at[q]) for q in range(count)]

    chunk = hid_buf.shape[-1] // 4
    early = [post.keep(hidden, hid_buf)]
    for j in range(4):
        for i in range(16):
            target = down_buf.at[pl.ds(j * chunk, chunk), pl.ds(i * LANES, LANES)]
            early.append(post.keep(downs_in[j].at[i // 4, i % 4], target))
    late = [
        post.keep(source, target)
        for source, target in (
            (grad_mid, gm_buf), (queries, q_buf), (keys, k_buf), (values, v_buf), (marks_in, marks),
            (tables_in, tables), (mixed, mix_buf), (mid_own, mid_buf),
        )
    ]
    late += [
        post.keep(out_all.at[i // 4, i % 4], weight.at[:, pl.ds(i * LANES, LANES)])
        for i in range(16)
    ]
    post.settle(early)
    fold = Fold(post, at, lambda block: mm(hid_buf[block], down_buf[...]), fold_scratch)
    fold.first()
    post.settle(late)

    def fetch(n):
        place = pl.ds(n * TILE, TILE)
        return post.keep(attn_in.at[:, :, place], column.at[n % 2])

    fetched = fetch(0)
    width = gm_buf.shape[-1]
    for m in range(2):
        for i in range(4):
            q = QUARTER[i]
            n = min(i + 2, 4) * TILE
            place = slice(i * TILE, (i + 1) * TILE)
            id_col = marks[q].T[:, m : m + 1]
            id_row = id_rows(marks, m, n // TILE)
            cos_full, sin_full = rope_full(tables[q, m])
            rows = gm_buf[2 * q : 2 * q + 2, m * ROWS : (m + 1) * ROWS].reshape(TILE, width)
            grad_mixed = mm(rows, weight[...], ((1,), (1,))).astype(NARROW)
            for g in range(2):
                lane = slice(g * HEAD_DIM, (g + 1) * HEAD_DIM)
                query = q_buf[m, place, lane]
                prob = softmax_tile(query, k_buf[m, :n], id_col, id_row)
                grad = grad_mixed[:, lane]
                grad_prob = mm(grad, v_buf[m, :n], ((1,), (1,)))
                inner = jnp.sum(grad_prob * prob, axis=-1, keepdims=True)
                grad_scores = (SCALE * prob * (grad_prob - inner)).astype(NARROW)
                grad_query = mm(grad_scores, k_buf[m, :n])
                grad_key = mm(grad_scores, query, ((0,), (0,)))
                grad_value = mm(prob.astype(NARROW), grad, ((0,), (0,)))
                if i == 0 and g == 0:
                    gk_buf[:n], gv_buf[:n] = grad_key, grad_value
                    gk_buf[n:], gv_buf[n:] = (jnp.zeros_like(gk_buf[n:]),) * 2
                else:
                    gk_buf[:n] = gk_buf[:n] + grad_key
                    gv_buf[:n] = gv_buf[:n] + grad_value
                done = rope_back(grad_query, cos_full, sin_full).astype(NARROW)
                for h in range(2):
                    gp_buf[2 * q + h, m * ROWS : (m + 1) * ROWS, lane] = done[h * ROWS : (h + 1) * ROWS]
        for i in range(4):
            q = QUARTER[i]
            place = slice(i * TILE, (i + 1) * TILE)
            cos_full, sin_full = rope_full(tables[q, m])
            done = (
                rope_back(gk_buf[place], cos_full, sin_full).astype(NARROW),
                gv_buf[place].astype(NARROW),
            )
            for k in range(2):
                lane = slice((2 + k) * HEAD_DIM, (3 + k) * HEAD_DIM)
                for h in range(2):
                    gp_buf[2 * q + h, m * ROWS : (m + 1) * ROWS, lane] = done[k][h * ROWS : (h + 1) * ROWS]
        if m == 0:
            fold.second()
    post.keep(gp_buf, grad_proj)
    fold.third()
    for half in range(2):
        out_buf[HALVES[half]] = (fold.held[half] + mid_buf[HALVES[half]]).astype(NARROW)
    post.keep(out_buf, hidden_out)
    for i in range(8):
        place = slice(i * TILE, (i + 1) * TILE)
        mix_t[:, place] = mix_buf[i].astype(WIDE).T.astype(NARROW)
        gp_t[:, place] = gp_buf[i].astype(WIDE).T.astype(NARROW)
    span = mix_t.shape[0]
    for n in range(8):
        post.settle([fetched])
        if n < 7:
            fetched = fetch(n + 1)
        place = slice(n * TILE, (n + 1) * TILE)
        value = mm(mix_t[...], gm_buf[:, :, place].reshape(8 * TILE, TILE)).astype(NARROW)
        other = mm(gp_t[...], column[n % 2].reshape(8 * TILE, TILE)).astype(NARROW)
        for h in range(2):
            block = 2 * n + h
            lane = slice(h * LANES, (h + 1) * LANES)
            staged[block // 4, block % 4, :span] = value[:, lane]
            staged[block // 4, block % 4, span:] = other[:, lane]
    post.keep(staged, parts_attn)
    for step in steps:
        step.finish()


def end_kernel(post, at, ins, outs, scratch):
    (
        grad_proj, qkv_all, x_own, gains_in, grad_mid_own, hidden_out, gain_ffn_part, parts, got_a, got_b, parts_attn
    ) = ins
    out_home, grad_home, gain_sums, ffn_sums, attn_sums = outs
    (
        gp_buf, weight, x_buf, gains, mid_buf, rows_out, gain_buf, gain_got,
        own_ffn, far_ffn, one_ffn, two_ffn, end_ffn, own_attn, far_attn, got_attn, end_attn, *fold_scratch
    ) = scratch
    f, c = at.f, at.c
    meet_swap(at)
    step_attn = Descend(post, at, parts_attn, got_attn)
    swap = Swap(post, at)
    moved = [swap(hidden_out.at[half], out_home.at[half], out_home.at[half]) for half in HALVES]

    n_a = got_a.shape[0]
    n_all = parts.shape[0]
    a, b = pl.ds(0, n_a), pl.ds(n_a, n_all - n_a)
    sums = [
        post.keep(parts.at[:, :, at.c2], far_ffn),
        post.keep(got_a.at[:, 1], two_ffn.at[a]),
        post.keep(got_b.at[:, 1], two_ffn.at[b]),
    ]
    fold_in = [
        post.keep(grad_proj, gp_buf), post.keep(qkv_all, weight), post.keep(x_own, x_buf),
        post.keep(gains_in, gains), post.keep(grad_mid_own, mid_buf),
        post.keep(gain_ffn_part, gain_buf),
    ]
    later = [
        post.keep(parts.at[:, :, c], own_ffn),
        post.keep(got_a.at[:, 0], one_ffn.at[a]),
        post.keep(got_b.at[:, 0], one_ffn.at[b]),
        post.keep(parts_attn.at[:, c], own_attn), post.keep(parts_attn.at[:, at.c2], far_attn),
    ]
    post.settle(sums)

    def add(left, right):
        return (left.astype(WIDE) + right.astype(WIDE)).astype(NARROW)

    def add_far(q, carry):
        far_ffn[q] = add(far_ffn[q], two_ffn[q])
        return carry

    lax.fori_loop(0, n_all, add_far, 0)
    far_sent = post.send(far_ffn, end_ffn, at.z2, end_ffn)
    post.settle(fold_in)
    width = x_buf.shape[-1]

    def part(block):
        return mm(gp_buf[block], weight[...].reshape(width, -1), ((1,), (1,)))

    fold = Fold(post, at, part, fold_scratch)
    fold.first()
    fold.second()
    fold.third()
    gain = jnp.concatenate([gains[i // 4, i % 4, 0:1, :] for i in range(16)], axis=1)
    total = jnp.zeros((1, width), WIDE)
    for half in range(2):
        rows = HALVES[half]
        back, piece = norm_back_rows(fold.held[half], x_buf[rows].astype(WIDE), gain)
        total = total + piece
        rows_out[rows] = (mid_buf[rows] + back).astype(NARROW)
        moved.append(swap(rows_out.at[rows], grad_home.at[rows], grad_home.at[rows]))
    gain_buf[0:1] = total
    post.settle(later)
    step_attn.finish()
    for k in range(4):
        far_attn[k] = add(far_attn[k], got_attn[1, k])
    far_attn_sent = post.send(far_attn, end_attn, at.z2, end_attn)
    for k, device in enumerate((at.core, at.row, at.side, at.z1, at.z2)):
        gain_sent = post.send(gain_buf, gain_got.at[k], device, gain_got.at[k])
        gain_sent.arrive()
        gain_sent.leave()
        post.out.pop()
        gain_buf[...] = gain_buf[...] + gain_got[k]
    place = pl.ds(pl.multiple_of((f * 4 + c) * LANES, LANES), LANES)
    post.keep(gain_buf.at[:, place], gain_sums)

    far_sent.arrive()

    def add_own(q, carry):
        value = own_ffn[q].astype(WIDE) + one_ffn[q].astype(WIDE) + end_ffn[q].astype(WIDE)
        own_ffn[q] = value.astype(NARROW)
        return carry

    lax.fori_loop(0, n_all, add_own, 0)
    trades = []
    places = ((at.row, at.fy), (at.cross, at.fd), (at.core, at.fs))

    def trade(mine, out):
        post.keep(mine(f), out.at[f])
        for device, k in places:
            trades.append(post.send(mine(k), out.at[f], device, out.at[k]))

    trade(lambda k: own_ffn.at[:, k], ffn_sums)
    far_attn_sent.arrive()
    for k in range(4):
        value = own_attn[k].astype(WIDE) + got_attn[0, k].astype(WIDE) + end_attn[k].astype(WIDE)
        own_attn[k] = value.astype(NARROW)
    trade(lambda k: own_attn.at[k], attn_sums)
    for sent in trades:
        sent.arrive()
    for arrive in moved:
        arrive()
    swap.finish()


def near_body(
    hidden_in, cotangent, block_ids, positions, attn_gain, wqkv, wo, ffn_gain, w_gate, w_up, w_down
):
    micro, _, rows, width = hidden_in.shape
    own = micro * rows
    ff = w_gate.shape[1]
    chunk = ff // 16
    table, marks, gains = small_arrays(block_ids, positions, attn_gain, ffn_gain)
    (
        x_own, cot_own, attn_in, tables, all_marks, all_gains, qkv_all, out_all, gate_lvl, up_lvl, down_lvl,
    ) = call(
        start_kernel,
        "start",
        [
            shape(own, width), shape(own, width), shape(8, own, width),
            shape(4, *table.shape, dtype=WIDE), shape(4, *marks.shape, dtype=WIDE),
            shape(4, 4, *gains.shape, dtype=WIDE),
            shape(4, 4, LANES, wqkv.shape[1] // 4), shape(4, 4, wo.shape[0] // 4, LANES),
            shape(4, 4, LANES, chunk), shape(4, 4, LANES, chunk), shape(4, 4, chunk, LANES),
        ],
        (
            hidden_in.reshape(own, width), cotangent.reshape(own, width), table, marks, gains,
            wqkv, wo, w_gate, w_up, w_down,
        ),
        [pltpu.VMEM((own, width), NARROW), pltpu.VMEM((own, width), NARROW), pltpu.VMEM((4, 4, 8, LANES), WIDE)],
        80, 32, 1,
    )
    levels = (gate_lvl, up_lvl, down_lvl)
    jobs_a = Jobs((0, 0), (1, 0))
    jobs_b = Jobs((2, 0), (0, 1), (1, 1), (2, 1))
    jobs_c = Jobs(*((a, j) for j in (2, 3) for a in range(3)))
    queries, keys, values, mixed, dy, *climb_a = call(
        functools.partial(attend_kernel, jobs_a),
        "attend",
        [
            shape(2, 1024, 256), shape(2, 1024, 128), shape(2, 1024, 128), shape(8, own, 256),
            shape(8, own, width), *jobs_a.shapes(levels),
        ],
        (attn_in, qkv_all, tables, all_marks, cot_own, *levels),
        [
            pltpu.VMEM((2, 8, ROWS, width), NARROW), pltpu.VMEM(qkv_all.shape, NARROW),
            pltpu.VMEM(tables.shape, WIDE), pltpu.VMEM(all_marks.shape, WIDE),
            pltpu.VMEM((2, 1024, 256), NARROW), pltpu.VMEM((2, 1024, 128), NARROW),
            pltpu.VMEM((2, 1024, 128), NARROW), pltpu.VMEM((8, own, 256), NARROW),
        ],
        40, 24, 2,
    )
    mid_own, ffn_in, *climb_b = call(
        functools.partial(middle_kernel, jobs_b),
        "middle",
        [shape(own, width, dtype=WIDE), shape(8, own, width), *jobs_b.shapes(levels)],
        (mixed, out_all, x_own, all_gains, *levels),
        [
            pltpu.VMEM((8, own, 256), NARROW), pltpu.VMEM((256, width), NARROW),
            pltpu.VMEM((own, width), NARROW), pltpu.VMEM((4, 4, 8, LANES), WIDE),
            pltpu.VMEM((2, ROWS, width), NARROW), *Fold.scratch(width),
        ],
        60, 40, 3,
    )
    have = dict(zip(jobs_a.wanted + jobs_b.wanted, climb_a + climb_b))
    hidden, grads_pre, parts, *climb_c = call(
        functools.partial(ffn_kernel, jobs_c),
        "ffn",
        [
            shape(8, own, ff // 4), shape(8, own, ff // 2), shape(12, 4, 4, chunk, LANES),
            *jobs_c.shapes(levels),
        ],
        (ffn_in, dy, *(have[a, j] for j in range(2) for a in range(3)), *levels),
        [
            pltpu.VMEM((8, own, width), NARROW), pltpu.VMEM((8, own, width), NARROW),
            pltpu.VMEM((2, 4, 4, LANES, chunk), NARROW), pltpu.VMEM((2, 4, 4, LANES, chunk), NARROW),
            pltpu.VMEM((2, chunk, width), NARROW), pltpu.VMEM((3, 8, own, chunk), NARROW),
            pltpu.VMEM((3, chunk, 8 * own), NARROW), pltpu.VMEM((3, 16, chunk, LANES), NARROW),
        ],
        24, 160, 4,
    )
    have.update(zip(jobs_c.wanted, climb_c))
    count_a = 7
    fold_scratch = Fold.scratch(width)
    grad_mid_own, grad_mid, gain_ffn_part, got_a = call(
        functools.partial(back_kernel, 0, count_a),
        "back",
        [
            shape(own, width, dtype=WIDE), shape(8, own, width), shape(8, width, dtype=WIDE),
            shape(count_a, 2, 4, chunk, LANES),
        ],
        (
            grads_pre, mid_own, cot_own, all_gains, parts,
            *(have[a, j] for a in range(2) for j in range(4)),
        ),
        [
            pltpu.VMEM((8, own, ff // 2), NARROW), pltpu.VMEM((4, 4, LANES, ff // 2), NARROW),
            pltpu.VMEM((own, width), WIDE), pltpu.VMEM((own, width), NARROW),
            pltpu.VMEM((4, 4, 8, LANES), WIDE), pltpu.VMEM((2, ROWS, width), NARROW),
            pltpu.VMEM((8, width), WIDE), *fold_scratch,
        ],
        48, 32, 5,
    )
    grad_proj, parts_attn, hidden_out, got_b = call(
        functools.partial(attend_back_kernel, count_a, 12 - count_a),
        "attend_back",
        [
            shape(8, own, 512), shape(4, 4, 768, LANES), shape(own, width),
            shape(12 - count_a, 2, 4, chunk, LANES),
        ],
        (
            grad_mid, queries, keys, values, all_marks, tables, out_all, mixed, attn_in, hidden, mid_own, parts,
            *(have[2, j] for j in range(4)),
        ),
        [
            pltpu.VMEM((8, own, width), NARROW), pltpu.VMEM((2, 1024, 256), NARROW),
            pltpu.VMEM((2, 1024, 128), NARROW), pltpu.VMEM((2, 1024, 128), NARROW),
            pltpu.VMEM(all_marks.shape, WIDE), pltpu.VMEM(tables.shape, WIDE),
            pltpu.VMEM((256, width), NARROW), pltpu.VMEM((8, own, 256), NARROW),
            pltpu.VMEM((8, own, ff // 4), NARROW), pltpu.VMEM((ff // 4, width), NARROW),
            pltpu.VMEM((8, own, 512), NARROW), pltpu.VMEM((1024, 128), WIDE),
            pltpu.VMEM((1024, 128), WIDE), pltpu.VMEM((256, 8 * own), NARROW),
            pltpu.VMEM((512, 8 * own), NARROW), pltpu.VMEM((2, 8, own, TILE), NARROW),
            pltpu.VMEM((4, 4, 768, LANES), NARROW), pltpu.VMEM((own, width), WIDE),
            pltpu.VMEM((own, width), NARROW), *fold_scratch,
        ],
        32, 128, 6,
    )
    out_home, grad_home, gain_sums, ffn_sums, attn_sums = call(
        end_kernel,
        "end",
        [
            shape(own, width), shape(own, width), shape(8, LANES, dtype=WIDE),
            shape(4, 12, chunk, LANES), shape(4, 768, LANES),
        ],
        (
            grad_proj, qkv_all, x_own, all_gains, grad_mid_own, hidden_out, gain_ffn_part, parts, got_a, got_b, parts_attn
        ),
        [
            pltpu.VMEM((8, own, 512), NARROW), pltpu.VMEM(qkv_all.shape, NARROW),
            pltpu.VMEM((own, width), NARROW), pltpu.VMEM((4, 4, 8, LANES), WIDE),
            pltpu.VMEM((own, width), WIDE), pltpu.VMEM((own, width), NARROW),
            pltpu.VMEM((8, width), WIDE), pltpu.VMEM((5, 8, width), WIDE),
            *[pltpu.VMEM((12, 4, chunk, LANES), NARROW)] * 5,
            pltpu.VMEM((4, 768, LANES), NARROW), pltpu.VMEM((4, 768, LANES), NARROW),
            pltpu.VMEM((2, 4, 768, LANES), NARROW), pltpu.VMEM((4, 768, LANES), NARROW),
            *fold_scratch,
        ],
        40, 40, 7,
    )
    grads = ffn_sums.reshape(4, 4, 3, chunk, LANES).transpose(2, 0, 1, 3, 4)
    grads = grads.reshape(3, ff, LANES)
    grad_qkv = attn_sums[:, 256:].reshape(-1, LANES)
    grad_out = attn_sums[:, :256].reshape(-1, LANES)
    return (
        out_home.reshape(hidden_in.shape),
        grad_home.reshape(hidden_in.shape),
        gain_sums[0],
        grad_qkv.T.astype(WIDE),
        grad_out.astype(WIDE),
        gain_sums[1],
        grads[0].T.astype(WIDE),
        grads[1].T.astype(WIDE),
        grads[2].astype(WIDE),
    )


def body(*shards):
    inner = KV_HEADS // lax.axis_size("tp")
    near = (lax.axis_size("fsdp"), lax.axis_size("ctx"), lax.axis_size("tp"), inner)
    return (near_body if near == (4, 4, 2, 4) else general_body)(*shards)


def solution(mesh):
    return jax.shard_map(
        body,
        mesh=mesh,
        in_specs=(
            P(None, "fsdp", ("ctx", "tp"), None),
            P(None, "fsdp", ("ctx", "tp"), None),
            P(None, "fsdp", None),
            P(None, "fsdp", "ctx"),
            P(("fsdp", "ctx")),
            P(("fsdp", "ctx"), "tp"),
            P("tp", ("fsdp", "ctx")),
            P(("fsdp", "ctx")),
            P(("fsdp", "ctx"), "tp"),
            P(("fsdp", "ctx"), "tp"),
            P("tp", ("fsdp", "ctx")),
        ),
        out_specs=(
            P(None, "fsdp", ("ctx", "tp"), None),
            P(None, "fsdp", ("ctx", "tp"), None),
            P(("fsdp", "ctx")),
            P(("fsdp", "ctx"), "tp"),
            P("tp", ("fsdp", "ctx")),
            P(("fsdp", "ctx")),
            P(("fsdp", "ctx"), "tp"),
            P(("fsdp", "ctx"), "tp"),
            P("tp", ("fsdp", "ctx")),
        ),
        check_vma=False,
    )
```

```python
import functools
import math

import jax
import jax.numpy as jnp
from jax import lax
from jax.sharding import PartitionSpec as P
from jax.experimental import pallas as pl
from jax.experimental.pallas import tpu as pltpu

HEADS = 16
KV_HEADS = 8
HEAD_DIM = 128


EPS = 1e-05
THETA = 1000000.0
MASKED = -1e30


def rope_tables(position_ids):
    half_dim = HEAD_DIM // 2
    inverse = THETA ** (-(jnp.arange(half_dim, dtype=jnp.float32) * 2.0 / HEAD_DIM))
    angles = position_ids.astype(jnp.float32)[..., None] * inverse
    angles = jnp.concatenate([angles, angles], axis=-1)
    return (jnp.cos(angles), jnp.sin(angles))


def turned(values):
    half_dim = values.shape[-1] // 2
    return jnp.concatenate([-values[..., half_dim:], values[..., :half_dim]], axis=-1)


def turned_back(values):
    half_dim = values.shape[-1] // 2
    return jnp.concatenate([values[..., half_dim:], -values[..., :half_dim]], axis=-1)


def norm_rows(stream, gain_row):
    factor = lax.rsqrt(jnp.mean(stream * stream, axis=-1, keepdims=True) + EPS)
    normed = stream * factor
    return (normed, factor, (normed * gain_row).astype(jnp.bfloat16))


def groups_of(fsdp, inner):
    near = [[high * inner + low for low in range(inner)] for high in range(fsdp // inner)]
    far = [[high * inner + low for high in range(fsdp // inner)] for low in range(inner)]
    return near, far


def general_body(
    hidden_in, cotangent, block_ids, positions, attn_gain, wqkv, wo, ffn_gain, w_gate, w_up, w_down
):
    fsdp, ctx, tp = lax.axis_size("fsdp"), lax.axis_size("ctx"), lax.axis_size("tp")
    inner = KV_HEADS // tp
    outer = fsdp // inner
    near, far = groups_of(fsdp, inner)
    micro, _, rows, width = hidden_in.shape
    score_scale = HEAD_DIM ** (-0.5)
    f_at, c_at = lax.axis_index("fsdp"), lax.axis_index("ctx")
    swap = [
        ((high * inner + low) * ctx + c, (high * inner + c) * ctx + low)
        for high in range(outer)
        for low in range(inner)
        for c in range(ctx)
    ]

    def rehome(array):
        return lax.ppermute(array, ("fsdp", "ctx"), swap)

    def trade(pieces):
        return lax.all_to_all(pieces, "fsdp", 0, 0, axis_index_groups=near)

    def spread(block):
        both = lax.all_gather(block, "tp")
        return lax.all_gather(both, "fsdp", axis_index_groups=near)

    def fold(parts):
        half = lax.psum_scatter(
            parts.astype(jnp.bfloat16), "fsdp", scatter_dimension=0, axis_index_groups=near
        )
        return lax.psum_scatter(half, "tp", scatter_dimension=0).astype(jnp.float32)

    def gather_levels(pieces):
        up = lax.all_gather(pieces, "ctx")
        if outer == 1:
            return up[None]
        return lax.all_gather(up, "fsdp", axis_index_groups=far)

    def scatter_levels(pieces):
        if outer == 1:
            pieces = pieces[0]
        else:
            pieces = lax.psum_scatter(pieces, "fsdp", scatter_dimension=0, axis_index_groups=far)
        return lax.psum_scatter(pieces, "ctx", scatter_dimension=0)

    def fetch_columns(shard):
        block, cols = shard.shape
        pieces = trade(shard.reshape(block, inner, cols // inner).transpose(1, 0, 2))
        whole = gather_levels(pieces).transpose(0, 2, 1, 3, 4)
        return whole.reshape(-1, cols // inner)

    def fetch_rows(shard):
        length, block = shard.shape
        pieces = trade(shard.reshape(inner, length // inner, block))
        whole = gather_levels(pieces).transpose(3, 0, 2, 1, 4)
        return whole.reshape(length // inner, -1)

    def return_columns(grad):
        total, cols = grad.shape
        grad = grad.astype(jnp.bfloat16).reshape(outer, inner, ctx, -1, cols)
        mine = trade(scatter_levels(grad.transpose(0, 2, 1, 3, 4)))
        return mine.transpose(1, 0, 2).reshape(mine.shape[1], -1).astype(jnp.float32)

    def return_rows(grad):
        length, total = grad.shape
        grad = grad.astype(jnp.bfloat16).reshape(length, outer, inner, ctx, -1)
        mine = trade(scatter_levels(grad.transpose(1, 3, 2, 0, 4)))
        return mine.reshape(inner * length, -1).astype(jnp.float32)

    def dot(left, right, dims):
        return lax.dot_general(left, right, (dims, ((), ())), preferred_element_type=jnp.float32)

    gains = lax.all_gather(jnp.stack([attn_gain, ffn_gain]), ("fsdp", "ctx"))
    gain_attn = gains[:, 0].reshape(-1).astype(jnp.float32)
    gain_ffn = gains[:, 1].reshape(-1).astype(jnp.float32)
    span = positions.shape[2]
    ids_here = lax.dynamic_slice_in_dim(block_ids[:, 0], c_at * span, span, 1)
    marks = lax.all_gather(jnp.stack([positions[:, 0], ids_here]), ("fsdp", "ctx"))
    my_seq = f_at // inner * inner + c_at
    marks = lax.dynamic_slice_in_dim(marks, my_seq * ctx, ctx, 0)
    marks = marks.transpose(1, 2, 0, 3).reshape(2, micro, ctx * span)
    pos, ids = marks[0], marks[1]

    weight_qkv = fetch_columns(wqkv)
    weight_out = fetch_rows(wo)
    weight_gate = fetch_columns(w_gate)
    weight_up = fetch_columns(w_up)
    weight_down = fetch_rows(w_down)

    stream = rehome(hidden_in).reshape(micro * rows, width).astype(jnp.float32)
    grad_out_low = rehome(cotangent).reshape(micro * rows, width)
    grad_out = grad_out_low.astype(jnp.float32)

    def to_heads(flat):
        split = flat.reshape(inner * tp, micro, rows, -1, HEAD_DIM).transpose(1, 0, 2, 3, 4)
        return split.reshape(micro, inner * tp * rows, -1, HEAD_DIM)

    def from_heads(heads):
        split = heads.reshape(micro, inner * tp, rows, -1).transpose(1, 0, 2, 3)
        return split.reshape(inner * tp * micro * rows, -1)

    normed_one, factor_one, attn_rows = norm_rows(stream, gain_attn)
    attn_in = spread(attn_rows).reshape(-1, width)
    projected = to_heads(dot(attn_in, weight_qkv, ((1,), (0,))))
    group = HEADS // KV_HEADS
    cos_table, sin_table = rope_tables(pos)
    cos_heads, sin_heads = cos_table[:, :, None], sin_table[:, :, None]
    turning = projected[:, :, : group + 1]
    turning = (turning * cos_heads + turned(turning) * sin_heads).astype(jnp.bfloat16)
    queries, keys = turning[:, :, :group], turning[:, :, group]
    values = projected[:, :, group + 1].astype(jnp.bfloat16)
    allowed = (ids[:, None, :] <= ids[:, :, None])[:, None]
    raw = jnp.einsum("blge,bme->bglm", queries, keys, preferred_element_type=jnp.float32)
    scores = jnp.where(allowed, raw * score_scale, MASKED)
    row_max = jnp.max(scores, axis=-1, keepdims=True)
    exponent = jnp.exp(scores - row_max)
    prob = exponent / jnp.sum(exponent, axis=-1, keepdims=True)
    prob_low = prob.astype(jnp.bfloat16)
    mixed = jnp.einsum("bglm,bme->blge", prob_low, values, preferred_element_type=jnp.float32)
    mixed = from_heads(mixed.astype(jnp.bfloat16))
    out_part = dot(mixed, weight_out, ((1,), (0,)))
    stream_mid = stream + fold(out_part.reshape(inner, tp, -1, width))
    normed_two, factor_two, ffn_rows = norm_rows(stream_mid, gain_ffn)
    ffn_in = spread(ffn_rows).reshape(-1, width)
    dy = spread(grad_out_low).reshape(-1, width)

    gate_pre = dot(ffn_in, weight_gate, ((1,), (0,)))
    up_pre = dot(ffn_in, weight_up, ((1,), (0,)))
    gate_sig = jax.nn.sigmoid(gate_pre)
    gate_act = gate_pre * gate_sig
    hidden = (gate_act * up_pre).astype(jnp.bfloat16)
    grad_hidden = dot(dy, weight_down, ((1,), (1,)))
    grad_gate_pre = (
        grad_hidden * up_pre * gate_sig * (1.0 + gate_pre * (1.0 - gate_sig))
    ).astype(jnp.bfloat16)
    grad_up_pre = (grad_hidden * gate_act).astype(jnp.bfloat16)
    grad_ffn_part = dot(grad_gate_pre, weight_gate, ((1,), (1,))) + dot(
        grad_up_pre, weight_up, ((1,), (1,))
    )
    grad_ffn_in = fold(grad_ffn_part.reshape(inner, tp, -1, width))
    down_part = dot(hidden, weight_down, ((1,), (0,)))
    stream_out = stream_mid + fold(down_part.reshape(inner, tp, -1, width))
    grad_down = return_rows(dot(hidden, dy, ((0,), (0,))))
    grad_gate = return_columns(dot(ffn_in, grad_gate_pre, ((0,), (0,))))
    grad_up = return_columns(dot(ffn_in, grad_up_pre, ((0,), (0,))))

    def back_rows(grad, normed, factor, gain_row):
        grad_normed = grad * gain_row
        inner_mean = jnp.mean(grad_normed * normed, axis=-1, keepdims=True)
        return factor * (grad_normed - normed * inner_mean), jnp.sum(grad * normed, axis=0)

    mid_norm, gain_ffn_part = back_rows(grad_ffn_in, normed_two, factor_two, gain_ffn)
    grad_mid = grad_out + mid_norm
    grad_mid_low = spread(grad_mid.astype(jnp.bfloat16)).reshape(-1, width)
    grad_mixed = to_heads(dot(grad_mid_low, weight_out, ((1,), (1,))).astype(jnp.bfloat16))
    grad_wo = return_rows(dot(mixed, grad_mid_low, ((0,), (0,))))
    grad_prob = jnp.einsum("blge,bme->bglm", grad_mixed, values, preferred_element_type=jnp.float32)
    inner_prob = jnp.sum(grad_prob * prob, axis=-1, keepdims=True)
    grad_scores = (score_scale * prob * (grad_prob - inner_prob)).astype(jnp.bfloat16)
    grad_queries = jnp.einsum(
        "bglm,bme->blge", grad_scores, keys, preferred_element_type=jnp.float32
    )
    grad_keys = jnp.einsum(
        "bglm,blge->bme", grad_scores, queries, preferred_element_type=jnp.float32
    )
    grad_values = jnp.einsum(
        "bglm,blge->bme", prob_low, grad_mixed, preferred_element_type=jnp.float32
    )
    grad_turning = jnp.concatenate([grad_queries, grad_keys[:, :, None]], axis=2)
    grad_turning = grad_turning * cos_heads + turned_back(grad_turning * sin_heads)
    grad_projected = jnp.concatenate([grad_turning, grad_values[:, :, None]], axis=2)
    grad_projected = from_heads(grad_projected.astype(jnp.bfloat16))
    grad_attn_in = fold(
        dot(grad_projected, weight_qkv, ((1,), (1,))).reshape(inner, tp, -1, width)
    )
    grad_wqkv = return_columns(dot(attn_in, grad_projected, ((0,), (0,))))
    in_norm, gain_attn_part = back_rows(grad_attn_in, normed_one, factor_one, gain_attn)
    grad_in = (grad_mid + in_norm).astype(jnp.bfloat16)

    gain_parts = jnp.stack([gain_attn_part, gain_ffn_part], axis=1).reshape(fsdp * ctx, -1, 2)
    gain_sums = lax.psum_scatter(gain_parts, ("fsdp", "ctx"), scatter_dimension=0)
    gain_sums = lax.psum(gain_sums, "tp")

    def home(array):
        return rehome(array.reshape(micro, 1, rows, width))

    return (
        home(stream_out.astype(jnp.bfloat16)),
        home(grad_in),
        gain_sums[:, 0],
        grad_wqkv,
        grad_wo,
        gain_sums[:, 1],
        grad_gate,
        grad_up,
        grad_down,
    )


MESH = pl.DeviceIdType.MESH
ROWS = 128
LANES = 128
NARROW = jnp.bfloat16
WIDE = jnp.float32
HALF = HEAD_DIM // 2
SCALE = HEAD_DIM ** (-0.5)
ANYWHERE = pl.BlockSpec(memory_space=pl.ANY)


class Place:
    def __init__(self):
        f, c, t = lax.axis_index("fsdp"), lax.axis_index("ctx"), lax.axis_index("tp")
        self.f, self.c, self.t = f, c, t
        fs, fy = f + 1 - 2 * (f % 2), (f + 2) % 4
        fd = (fs + 2) % 4
        self.fs, self.fy, self.fd = fs, fy, fd
        self.c1, self.c2 = c + 1 - 2 * (c % 2), (c + 2) % 4
        self.c3 = (self.c1 + 2) % 4
        self.side, self.core, self.row = (f, c, 1 - t), (fs, c, t), (fy, c, t)
        self.cross = (fd, c, t)
        self.z1, self.z2 = (f, self.c1, t), (f, self.c2, t)
        self.is_end, self.is_mid = c * (3 - c) == 0, c * (3 - c) != 0
        self.c_near, self.c_mate, self.c_outer = 1 + c // 3, 3 - c, 3 * c - 3
        self.z3 = (f, 3 - c, t)
        y, k, high, low = f // 2, f % 2, c // 2, c % 2
        self.to_f, to_c = (low + y) % 2 * 2 + high, k * 2 + y
        self.to = (self.to_f, to_c, t)
        self.whence = (low * 2 + high, k * 2 + (y + low) % 2, t)
        self.away = (self.to_f - f) * (self.to_f - f) + (to_c - c) * (to_c - c)
        self.b, self.b_side = f * 2 + t, f * 2 + 1 - t
        self.b_row, self.b_far = fy * 2 + t, fy * 2 + 1 - t
        self.b_core, self.b_core_side = fs * 2 + t, fs * 2 + 1 - t
        self.b_core_row, self.b_core_far = fd * 2 + t, fd * 2 + 1 - t


class Sent:
    def __init__(self, copy, landing):
        self.copy, self.landing = copy, landing

    def arrive(self):
        self.landing.wait_recv()

    def leave(self):
        self.copy.wait_send()


class Post:
    def __init__(self, send_sems, recv_sems, local_sems):
        self.sems = send_sems, recv_sems
        self.local_sems = local_sems
        self.n, self.n_local = 0, 0
        self.out, self.kept = [], []
        self.gates = []

    def make(self, source, target, device, lands):
        sems = dict(
            send_sem=self.sems[0].at[self.n],
            recv_sem=self.sems[1].at[self.n],
            device_id=device,
            device_id_type=MESH,
        )
        self.n += 1
        copy = pltpu.make_async_remote_copy(src_ref=source, dst_ref=target, **sems)
        landing = pltpu.make_async_remote_copy(src_ref=lands, dst_ref=lands, **sems)
        return Sent(copy, landing)

    def send(self, source, target, device, lands):
        sent = self.make(source, target, device, lands)
        sent.copy.start()
        self.out.append(sent)
        return sent

    def keep(self, source, target):
        copy = pltpu.make_async_copy(source, target, self.local_sems.at[self.n_local])
        self.n_local += 1
        copy.start()
        self.kept.append(copy)
        return copy

    def settle(self, copies):
        for copy in copies:
            copy.wait()
        self.kept = [kept for kept in self.kept if not any(kept is copy for copy in copies)]

    def close(self):
        for sent in self.out:
            sent.leave()
        for copy in self.kept:
            copy.wait()
        for gate in self.gates:
            gate.leave()
        self.out, self.kept, self.gates = [], [], []


class Gate:
    def __init__(self, post, sends, gets, what, lands):
        self.post, self.sends, self.gets, self.what, self.lands = post, sends, gets, what, lands
        self.n = post.n
        post.n += 1

    def copy(self, source, target, device):
        return pltpu.make_async_remote_copy(
            src_ref=source,
            dst_ref=target,
            send_sem=self.post.sems[0].at[self.n],
            recv_sem=self.post.sems[1].at[self.n],
            device_id=device,
            device_id_type=MESH,
        )

    def start(self):
        @pl.when(self.sends)
        def _():
            self.copy(*self.what()).start()

        self.post.gates.append(self)
        return self

    def arrive(self):
        @pl.when(self.gets)
        def _():
            there = self.lands()
            self.copy(there, there, self.post.anyone).wait_recv()

    def leave(self):
        @pl.when(self.sends)
        def _():
            self.copy(*self.what()).wait_send()


def meet(devices):
    bar = pltpu.get_barrier_semaphore()
    for device in devices:
        pl.semaphore_signal(bar, inc=1, device_id=device, device_id_type=MESH)
    pl.semaphore_wait(bar, len(devices))


class Spread:
    def __init__(self, post, at, out):
        self.post, self.at, self.out = post, at, out
        self.sent = {}

    def slot(self, block, half):
        return self.out.at[block, pl.ds(half * ROWS, ROWS)]

    def own(self, half, source):
        at, mine = self.at, self.slot(self.at.b, half)
        self.sent["side", half] = self.post.send(source, mine, at.side, self.slot(at.b_side, half))
        self.sent["row", half] = self.post.send(source, mine, at.row, self.slot(at.b_row, half))
        self.sent["core", half] = self.post.send(source, mine, at.core, self.slot(at.b_core, half))
        self.post.keep(source, mine)

    def pass_on(self, name, half, block, lands):
        here = self.slot(block, half)
        self.sent[name, half] = self.post.send(
            here, here, self.at.core, self.slot(lands, half)
        )

    def relay(self, half):
        at = self.at
        first = ("side", "row") if half == 0 else ("row", "side")
        for name in first:
            self.sent[name, half].arrive()
            block = at.b_side if name == "side" else at.b_row
            here = self.slot(block, half)
            if half == 0 and name == "side":
                self.sent["far", 0] = self.post.send(here, here, at.row, self.slot(at.b_far, 0))
            if half == 1 and name == "row":
                self.sent["far", 1] = self.post.send(here, here, at.side, self.slot(at.b_far, 1))
            lands = at.b_core_side if name == "side" else at.b_core_row
            self.pass_on("core_" + name, half, block, lands)

    def corner(self):
        for half in range(2):
            self.sent["far", half].arrive()
            self.pass_on("core_far", half, self.at.b_far, self.at.b_core_far)

    def finish(self):
        for name in ("core", "core_side", "core_row", "core_far"):
            for half in range(2):
                self.sent[name, half].arrive()


SPREAD_COPIES, SPREAD_KEPT = 14, 2


class Fold:
    copies = 10

    def __init__(self, post, at, part, scratch):
        self.post, self.at, self.part = post, at, part
        self.got, self.give, self.far, self.side, self.row, self.gx, self.gy, self.held = scratch

    @staticmethod
    def scratch(width):
        return [
            pltpu.VMEM((4, 2 * ROWS, width), NARROW),
            pltpu.VMEM((4, 2 * ROWS, width), NARROW),
            pltpu.VMEM((2, ROWS, width), NARROW),
            pltpu.VMEM((2, ROWS, width), NARROW),
            pltpu.VMEM((2, ROWS, width), NARROW),
            pltpu.VMEM((3, ROWS, width), NARROW),
            pltpu.VMEM((3, ROWS, width), NARROW),
            pltpu.VMEM((4, ROWS, width), WIDE),
        ]

    def to_core(self, slot, block):
        self.give[slot] = self.part(block).astype(NARROW)
        return self.post.send(self.give.at[slot], self.got.at[slot], self.at.core, self.got.at[slot])

    def first(self):
        at, post = self.at, self.post
        sent = self.to_core(3, at.b_core_far)
        value = self.part(at.b_far)
        sent.arrive()
        value = (value + self.got[3].astype(WIDE)).astype(NARROW)
        self.far[0] = value[:ROWS]
        self.far[1] = value[ROWS:]
        self.far_x = post.send(self.far.at[0], self.gx.at[0], at.side, self.gx.at[0])
        self.far_y = post.send(self.far.at[1], self.gy.at[0], at.row, self.gy.at[0])
        sent = self.to_core(1, at.b_core_side)
        value = self.part(at.b_side)
        sent.arrive()
        value = value + self.got[1].astype(WIDE)
        self.side[0] = value[:ROWS].astype(NARROW)
        self.held[2] = value[ROWS:]
        self.side_x = post.send(self.side.at[0], self.gx.at[1], at.side, self.gx.at[1])
        sent = self.to_core(2, at.b_core_row)
        value = self.part(at.b_row)
        sent.arrive()
        value = value + self.got[2].astype(WIDE)
        self.row[1] = value[ROWS:].astype(NARROW)
        self.held[3] = value[:ROWS]
        self.row_y = post.send(self.row.at[1], self.gy.at[1], at.row, self.gy.at[1])
        sent = self.to_core(0, at.b_core)
        value = self.part(at.b)
        sent.arrive()
        value = value + self.got[0].astype(WIDE)
        self.held[0] = value[:ROWS]
        self.held[1] = value[ROWS:]

    def second(self):
        at, post = self.at, self.post
        self.far_y.arrive()
        self.side[1] = (self.held[2] + self.gy[0].astype(WIDE)).astype(NARROW)
        self.side_b = post.send(self.side.at[1], self.gx.at[2], at.side, self.gx.at[2])
        self.far_x.arrive()
        self.row[0] = (self.held[3] + self.gx[0].astype(WIDE)).astype(NARROW)
        self.row_a = post.send(self.row.at[0], self.gy.at[2], at.row, self.gy.at[2])

    def third(self):
        self.side_x.arrive()
        self.row_y.arrive()
        self.held[0] = self.held[0] + self.gx[1].astype(WIDE)
        self.held[1] = self.held[1] + self.gy[1].astype(WIDE)
        self.row_a.arrive()
        self.held[0] = self.held[0] + self.gy[2].astype(WIDE)
        self.side_b.arrive()
        self.held[1] = self.held[1] + self.gx[2].astype(WIDE)


class Climb:
    copies, kept = 3, 1

    def __init__(self, post, at, level, out):
        self.post, self.at, self.out = post, at, out
        mine = out.at[:, at.c]
        self.far = post.send(level, mine, at.z2, out.at[:, at.c2])
        self.close = post.send(level, mine, at.z1, out.at[:, at.c1])
        self.own = post.keep(level, mine)

    def forward(self):
        at = self.at
        self.far.arrive()
        there = self.out.at[:, at.c2]
        self.last = self.post.send(there, there, at.z1, self.out.at[:, at.c3])

    def finish(self):
        self.close.arrive()
        self.last.arrive()
        self.post.settle([self.own])


class LineClimb:
    def __init__(self, post, at, level, out):
        self.post = post
        line = lambda c: (at.f, c, at.t)
        slot = lambda c: out.at[:, c]
        near, mate, outer = at.c_near, at.c_mate, at.c_outer
        end, mid = at.is_end, at.is_mid
        self.t0 = Gate(post, end, mid, lambda: (level, slot(at.c), line(near)), lambda: slot(outer))
        self.t1 = Gate(post, mid, end, lambda: (level, slot(at.c), line(outer)), lambda: slot(near))
        self.t2 = Gate(post, mid, mid, lambda: (level, slot(at.c), line(mate)), lambda: slot(mate))
        self.t3 = Gate(
            post, mid, mid, lambda: (slot(outer), slot(outer), line(mate)), lambda: slot(3 - outer)
        )
        self.t4 = Gate(
            post, mid, end, lambda: (slot(mate), slot(mate), line(outer)), lambda: slot(3 - near)
        )
        self.t5 = Gate(
            post, mid, end, lambda: (slot(3 - outer), slot(3 - outer), line(outer)), lambda: slot(3 - at.c)
        )
        for gate in (self.t0, self.t1, self.t2):
            gate.start()
        self.own = post.keep(level, slot(at.c))

    def forward(self):
        self.t2.arrive()
        self.t4.start()
        self.t0.arrive()
        self.t3.start()

    def last(self):
        self.t3.arrive()
        self.t5.start()

    def finish(self):
        for gate in (self.t1, self.t4, self.t5):
            gate.arrive()
        self.post.settle([self.own])


class Ends:
    def __init__(self, post, at, parts, first, got):
        self.gates = [
            Gate(
                post, at.is_end, at.is_mid,
                lambda q=q: (
                    parts.at[first + q, :, pl.ds((3 - at.c) // 3, 3)], got.at[q], (at.f, at.c_near, at.t)
                ),
                lambda q=q: got.at[q],
            ).start()
            for q in range(got.shape[0])
        ]

    def finish(self):
        for gate in self.gates:
            gate.arrive()


class Middle:
    def __init__(self, post, at, step, parts, first, came, out, own, more):
        self.post, self.at, self.out, self.own, self.more = post, at, out, own, more
        self.step, self.n = step, out.shape[0]
        self.sems = [post.local_sems.at[post.n_local + k] for k in range(2)]
        post.n_local += 2
        rows = pl.ds(first, self.n)

        def sources():
            if step == 1:
                return (
                    parts.at[rows, :, pl.ds(2 * (2 - at.c), 2)], came.at[:, :, pl.ds(2 - at.c, 2)]
                )
            return parts.at[rows, :, 3 * (at.c - 1)], came.at[:, :, at.c - 1]

        self.sources = sources

        @pl.when(at.is_mid)
        def _():
            for source, target, sem in zip(sources(), (own, more), self.sems):
                pltpu.make_async_copy(source, target, sem).start()

    def send(self):
        at, own, more = self.at, self.own, self.more

        @pl.when(at.is_mid)
        def _():
            for source, target, sem in zip(self.sources(), (own, more), self.sems):
                pltpu.make_async_copy(source, target, sem).wait()

            def add(q, carry):
                own[q] = (own[q].astype(WIDE) + more[q].astype(WIDE)).astype(NARROW)
                return carry

            lax.fori_loop(0, self.n, add, 0)

        c_to = at.c_mate if self.step == 1 else at.c_outer
        self.gate = Gate(
            self.post, at.is_mid, at.is_mid if self.step == 1 else at.is_end,
            lambda: (own, self.out, (at.f, c_to, at.t)), lambda: self.out,
        ).start()

    def finish(self):
        self.gate.arrive()


def middle_scratch(step, n):
    dims = (n, 4, 2, 256, LANES) if step == 1 else (n, 4, 256, LANES)
    return [pltpu.VMEM(dims, NARROW)] * 2


def call(kernel, name, outs, args, scratch, copies, kept, collective_id):
    sems = [
        pltpu.SemaphoreType.DMA((copies,)),
        pltpu.SemaphoreType.DMA((copies,)),
        pltpu.SemaphoreType.DMA((kept,)),
    ]
    n_in, n_out = len(args), len(outs)

    def inner(*refs):
        post, at = Post(*refs[len(refs) - 3 :]), Place()
        post.anyone = at.z1
        kernel(
            post, at, refs[:n_in], refs[n_in : n_in + n_out], refs[n_in + n_out : len(refs) - 3]
        )
        post.close()
        assert post.n <= copies and post.n_local <= kept, (post.n, post.n_local)

    return pl.pallas_call(
        inner,
        out_shape=outs,
        in_specs=[ANYWHERE] * n_in,
        out_specs=[ANYWHERE] * n_out,
        scratch_shapes=scratch + sems,
        compiler_params=pltpu.CompilerParams(
            collective_id=collective_id, has_side_effects=True, vmem_limit_bytes=62 << 20
        ),
        name=name,
    )(*args)


def shape(*dims, dtype=NARROW):
    return jax.ShapeDtypeStruct(dims, dtype)


def gain_row(gains_ref, which):
    return jnp.concatenate([gains_ref[i, which : which + 1, :] for i in range(16)], axis=1)


def normed_rows(values):
    factor = lax.rsqrt(jnp.mean(values * values, axis=-1, keepdims=True) + EPS)
    return values * factor, factor


class Swap:
    def __init__(self, post, at, home=False):
        self.post, self.at, self.moves = post, at, []
        self.device = at.whence if home else at.to

    def __call__(self, source, target, lands):
        post, at = self.post, self.at
        sent = post.make(source, target, self.device, lands)
        local = pltpu.make_async_copy(source, target, post.local_sems.at[post.n_local])
        post.n_local += 1

        @pl.when(at.away != 0)
        def _():
            sent.copy.start()

        @pl.when(at.away == 0)
        def _():
            local.start()

        self.moves.append(sent)

        def arrive():
            @pl.when(at.away != 0)
            def _():
                sent.landing.wait_recv()

            @pl.when(at.away == 0)
            def _():
                local.wait()

        return arrive

    def finish(self):
        @pl.when(self.at.away != 0)
        def _():
            for sent in self.moves:
                sent.copy.wait_send()


def meet_swap(at):
    bar = pltpu.get_barrier_semaphore()
    partners = (at.side, at.core, at.row, at.cross, at.z1, at.z2, at.z3)
    for device in partners:
        pl.semaphore_signal(bar, inc=1, device_id=device, device_id_type=MESH)

    @pl.when(at.away != 0)
    def _():
        for device in (at.to, at.whence):
            pl.semaphore_signal(bar, inc=1, device_id=device, device_id_type=MESH)
        pl.semaphore_wait(bar, len(partners) + 2)

    @pl.when(at.away == 0)
    def _():
        pl.semaphore_wait(bar, len(partners))


class Deal:
    def __init__(self, post, at, shards, j, outs):
        self.post, self.sent, self.kept = post, [], []
        gate, up, down = shards
        part = gate.shape[1] // 4
        chunk = part // 4
        for device, k in ((at.row, at.fy), (at.cross, at.fd), (at.core, at.fs), (None, at.f)):
            lane = pl.ds(pl.multiple_of(k * part + j * chunk, LANES), chunk)
            for source, out in zip((gate.at[:, lane], up.at[:, lane], down.at[lane]), outs):
                if device is None:
                    self.kept.append(post.keep(source, out.at[at.f]))
                else:
                    self.sent.append(post.send(source, out.at[at.f], device, out.at[k]))

    def finish(self):
        for sent in self.sent:
            sent.arrive()


HALVES = [pl.ds(half * ROWS, ROWS) for half in range(2)]


def start_kernel(post, at, ins, outs, scratch):
    hidden, cot, marks, gains, wqkv, wo, *shards = ins
    x_own, cot_own, attn_in, all_marks, all_gains, qkv_all, out_all, *levels_out = outs
    rows_in, rows_out, gain_buf = scratch
    f, c = at.f, at.c
    meet_swap(at)
    swap = Swap(post, at)
    x_moved = [swap(hidden.at[half], rows_in.at[half], rows_in.at[half]) for half in HALVES]
    heads = wqkv.shape[1] // 4
    span = wo.shape[0] // 4
    first = []
    for device, k in ((at.row, at.fy), (at.cross, at.fd), (at.core, at.fs)):
        lane = pl.ds(pl.multiple_of(k * heads, LANES), heads)
        first.append(post.send(wqkv.at[:, lane], qkv_all.at[f, c], device, qkv_all.at[k, c]))
        row = pl.ds(pl.multiple_of(k * span, LANES), span)
        first.append(post.send(wo.at[row], out_all.at[f, c], device, out_all.at[k, c]))
    lane = pl.ds(pl.multiple_of(f * heads, LANES), heads)
    own = [post.keep(wqkv.at[:, lane], qkv_all.at[f, c])]
    row = pl.ds(pl.multiple_of(f * span, LANES), span)
    own.append(post.keep(wo.at[row], out_all.at[f, c]))
    marks_moved = swap(marks, all_marks.at[at.to_f], all_marks.at[f])

    mine = gain_buf.at[f, c]
    post.settle([post.keep(gains, mine)])
    step = post.send(mine, mine, at.core, gain_buf.at[at.fs, c])
    step.arrive()
    pair = gain_buf.at[pl.ds(f // 2 * 2, 2), c]
    step = post.send(pair, pair, at.row, gain_buf.at[pl.ds(at.fy // 2 * 2, 2), c])
    step.arrive()
    step = post.send(gain_buf.at[:, c], gain_buf.at[:, c], at.z1, gain_buf.at[:, at.c1])
    step.arrive()
    pair = gain_buf.at[:, pl.ds(c // 2 * 2, 2)]
    step = post.send(pair, pair, at.z2, gain_buf.at[:, pl.ds(at.c2 // 2 * 2, 2)])
    step.arrive()
    gain = jnp.concatenate([gain_buf[i // 4, i % 4, 0:1, :] for i in range(16)], axis=1)
    post.keep(gain_buf, all_gains)

    post.settle(own)
    for sent in first:
        sent.arrive()

    spread = Spread(post, at, attn_in)
    levels = []

    def climb():
        for out in (qkv_all, out_all):
            here, there = out.at[:, c], out.at[:, at.c2]
            far = post.send(here, here, at.z2, there)
            close = post.send(here, here, at.z1, out.at[:, at.c1])
            levels.append((far, close, there, out))

    for half in range(2):
        x_moved[half]()
        if half == 1:
            climb()
        normed, _ = normed_rows(rows_in[HALVES[half]].astype(WIDE))
        rows_out[HALVES[half]] = (normed * gain).astype(NARROW)
        spread.own(half, rows_out.at[HALVES[half]])
        post.keep(rows_in.at[HALVES[half]], x_own.at[HALVES[half]])

    marks_moved()
    here = all_marks.at[f]
    small = post.send(here, here, at.core, all_marks.at[at.fs])
    spread.relay(0)
    small.arrive()
    pair = all_marks.at[pl.ds(f // 2 * 2, 2)]
    smaller = post.send(pair, pair, at.row, all_marks.at[pl.ds(at.fy // 2 * 2, 2)])
    spread.relay(1)
    forwards = []
    for far, close, there, out in levels:
        far.arrive()
        forwards.append((post.send(there, there, at.z1, out.at[:, at.c3]), close))
    cot_moved = [swap(cot.at[half], cot_own.at[half], cot_own.at[half]) for half in HALVES]
    deals = [Deal(post, at, shards, j, levels_out[3 * j : 3 * j + 3]) for j in range(2)]
    spread.corner()
    for last, close in forwards:
        last.arrive()
        close.arrive()
    spread.finish()
    smaller.arrive()
    for deal in deals:
        deal.finish()
    for arrive in cot_moved:
        arrive()
    swap.finish()


def rope(values, cos_full, sin_full):
    return values * cos_full + pltpu.roll(values, HALF, 1) * sin_full


def rope_back(values, cos_full, sin_full):
    return values * cos_full - pltpu.roll(values, HALF, 1) * sin_full


def rope_full(marks, m, inverse):
    angle = marks.T[:, 2 + m : 3 + m] * inverse
    low = lax.broadcasted_iota(jnp.int32, angle.shape, 1) < HALF
    turns = jnp.floor(angle * (2.0 / math.pi) + 0.5)
    rest = ((angle - turns * 1.5703125) - turns * 4.837512969970703125e-4) - turns * 7.54978995489188e-8
    square = rest * rest
    sine = rest + rest * square * (
        -1.6666654611e-1 + square * (8.3321608736e-3 - square * 1.9515295891e-4)
    )
    cosine = 1.0 - 0.5 * square + square * square * (
        4.166664568298827e-2 + square * (-1.388731625493765e-3 + square * 2.443315711809948e-5)
    )
    quadrant = turns + jnp.where(low, 1.0, 0.0)
    half = jnp.floor(quadrant * 0.5)
    odd = quadrant - 2.0 * half > 0.5
    negative = half - 2.0 * jnp.floor(half * 0.5) > 0.5
    table = jnp.where(odd, cosine, sine)
    table = jnp.where(negative, -table, table)
    turned_table = pltpu.roll(table, HALF, 1)
    return jnp.where(low, table, turned_table), jnp.where(low, -turned_table, table)


def quarter(at, i):
    return (i + at.c) % 2 * 2 + i // 2


def mm(left, right, dims=((1,), (0,))):
    return lax.dot_general(left, right, (dims, ((), ())), preferred_element_type=WIDE)


TILE = 256

def softmax_tile(query, key, id_col, id_row):
    raw = mm(query, key, ((1,), (1,))) * SCALE
    raw = jnp.where(id_row <= id_col, raw, MASKED)
    top = jnp.max(raw, axis=-1, keepdims=True)
    exponent = jnp.exp(raw - top)
    return exponent * (1.0 / jnp.sum(exponent, axis=-1, keepdims=True))


def id_rows(at, marks, m, tiles):
    return jnp.concatenate([marks[quarter(at, i), m : m + 1, :] for i in range(tiles)], axis=1)


def attend_kernel(post, at, ins, outs, scratch):
    attn_in, qkv_all, inverse_in, marks_in, cot_own, *shards = ins[:8]
    levels = ins[8:]
    queries, keys, values, mixed, dy, *more = outs
    climbed, dealt = more[: len(levels)], more[len(levels) :]
    rows, weight, inverse, marks, q_buf, k_buf, v_buf, mix_buf = scratch
    meet((at.side, at.core, at.row, at.cross, at.z1, at.z2))
    local = [
        post.keep(inverse_in, inverse),
        post.keep(marks_in, marks),
        post.keep(qkv_all, weight),
        post.keep(attn_in.at[:, pl.ds(0, ROWS)], rows.at[0]),
        post.keep(attn_in.at[:, pl.ds(ROWS, ROWS)], rows.at[1]),
    ]
    spread = Spread(post, at, dy)
    for half in range(2):
        spread.own(half, cot_own.at[pl.ds(half * ROWS, ROWS)])
    climbs = [Climb(post, at, level, out) for level, out in zip(levels, climbed)]
    deal = Deal(post, at, shards, 2, dealt)
    post.settle(local)
    width = rows.shape[-1]
    columns = weight.shape[-1]
    for m in range(2):
        for i in range(4):
            q = quarter(at, i)
            here = rows[m, pl.ds(2 * q, 2)].reshape(TILE, width)
            projected = mm(here, weight[...].reshape(width, columns))
            cos_full, sin_full = rope_full(marks[q], m, inverse[0:1])
            place = pl.ds(i * TILE, TILE)
            for g in range(2):
                lane = slice(g * HEAD_DIM, (g + 1) * HEAD_DIM)
                q_buf[m, place, lane] = rope(projected[:, lane], cos_full, sin_full).astype(NARROW)
            k_buf[m, place] = rope(projected[:, 256:384], cos_full, sin_full).astype(NARROW)
            v_buf[m, place] = projected[:, 384:512].astype(NARROW)
    spread.relay(0)
    for m in range(2):
        for i in range(4):
            n = min(i + 2, 4) * TILE
            q = quarter(at, i)
            id_col = marks[q].T[:, m : m + 1]
            id_row = id_rows(at, marks, m, n // TILE)
            for g in range(2):
                lane = slice(g * HEAD_DIM, (g + 1) * HEAD_DIM)
                prob = softmax_tile(
                    q_buf[m, i * TILE : (i + 1) * TILE, lane], k_buf[m, :n], id_col, id_row
                )
                value = mm(prob.astype(NARROW), v_buf[m, :n]).astype(NARROW)
                for h in range(2):
                    mix_buf[2 * q + h, m * ROWS : (m + 1) * ROWS, lane] = value[
                        h * ROWS : (h + 1) * ROWS
                    ]
        if m == 0:
            spread.relay(1)
            for climb in climbs:
                climb.forward()
    for source, target in ((q_buf, queries), (k_buf, keys), (v_buf, values), (mix_buf, mixed)):
        post.keep(source, target)
    spread.corner()
    spread.finish()
    for climb in climbs:
        climb.finish()
    deal.finish()


def middle_kernel(post, at, ins, outs, scratch):
    mixed, out_all, x_own, gains_in, *shards = ins[:7]
    levels = ins[7:]
    mid_own, ffn_in, *more = outs
    climbed, dealt = more[: len(levels)], more[len(levels) :]
    mix_buf, weight, x_buf, gains, rows_out, *fold_scratch = scratch
    meet((at.side, at.core, at.row, at.cross, at.z1, at.z2))
    local = [
        post.keep(out_all.at[i // 4, i % 4], weight.at[:, pl.ds(i * LANES, LANES)])
        for i in range(16)
    ]
    local += [post.keep(mixed, mix_buf), post.keep(x_own, x_buf), post.keep(gains_in, gains)]
    post.settle(local)
    climbs = [Climb(post, at, level, out) for level, out in zip(levels, climbed)]

    def part(block):
        return mm(mix_buf[block], weight[...])

    fold = Fold(post, at, part, fold_scratch)
    fold.first()
    fold.second()
    deal = Deal(post, at, shards, 3, dealt)
    fold.third()
    gain = jnp.concatenate([gains[i // 4, i % 4, 1:2, :] for i in range(16)], axis=1)
    spread = Spread(post, at, ffn_in)
    for half in range(2):
        rows = pl.ds(half * ROWS, ROWS)
        value = fold.held[half] + x_buf[rows].astype(WIDE)
        fold.held[half] = value
        normed, _ = normed_rows(value)
        rows_out[half] = (normed * gain).astype(NARROW)
        spread.own(half, rows_out.at[half])
        post.keep(fold.held.at[half], mid_own.at[rows])
    spread.relay(0)
    for climb in climbs:
        climb.forward()
    spread.relay(1)
    spread.corner()
    spread.finish()
    for climb in climbs:
        climb.finish()
    deal.finish()


def small_arrays(block_ids, positions, attn_gain, ffn_gain):
    micro, _, span = positions.shape
    ids = lax.dynamic_slice_in_dim(block_ids[:, 0], lax.axis_index("ctx") * span, span, 1)
    rows = jnp.concatenate([ids, positions[:, 0]]).astype(WIDE)
    marks = jnp.pad(rows, ((0, 8 - 2 * micro), (0, 0)))
    gains = jnp.pad(jnp.stack([attn_gain, ffn_gain]).astype(WIDE), ((0, 6), (0, 0)))
    return marks, gains


def ffn_kernel(post, at, ins, outs, scratch):
    ffn_in, dy = ins[:2]
    ready = ins[2:9]
    levels = ins[9:]
    hidden, grads_pre, parts, ends_a, ends_b, mates, *climbed = outs
    x_buf, dy_buf, gate_buf, up_buf, down_buf, act, act_t, staged, *sum_bufs = scratch
    meet((at.z1, at.z3))
    climbs = [LineClimb(post, at, level, out) for level, out in zip(levels, climbed)]
    local = [post.keep(ffn_in, x_buf), post.keep(dy, dy_buf)]
    weights = list(ready) + list(climbed)

    def load(j):
        slot = j % 2
        gate, up, down = weights[3 * j : 3 * j + 3]
        copies = [post.keep(gate, gate_buf.at[slot]), post.keep(up, up_buf.at[slot])]
        for i in range(16):
            copies.append(
                post.keep(down.at[i // 4, i % 4], down_buf.at[slot, :, pl.ds(i * LANES, LANES)])
            )
        return copies

    loading = load(0)
    post.settle(local)
    width = x_buf.shape[-1]
    saved, sums_0 = [], []
    for j in range(4):
        slot = j % 2
        if loading is None:
            for climb in climbs[:2] if j == 2 else climbs[2:]:
                climb.finish()
            loading = load(j)
        post.settle(loading)
        loading = load(1) if j == 0 else None
        post.settle(saved)

        def rows(i, carry):
            x, grad = x_buf[i], dy_buf[i]
            gate = mm(x, gate_buf[slot].reshape(width, -1))
            up = mm(x, up_buf[slot].reshape(width, -1))
            grad_hidden = mm(grad, down_buf[slot], ((1,), (1,)))
            sig = jax.nn.sigmoid(gate)
            silu = gate * sig
            values = (
                grad_hidden * up * sig * (1.0 + gate * (1.0 - sig)),
                grad_hidden * silu,
                silu * up,
            )
            place = pl.ds(pl.multiple_of(i * TILE, TILE), TILE)
            for k in range(3):
                act[k, i] = values[k].astype(NARROW)
                act_t[k, :, place] = values[k].T.astype(NARROW)
            return carry

        lax.fori_loop(0, 8, rows, 0)
        chunk = act.shape[-1]
        lane = pl.ds(j * chunk, chunk)
        saved = [
            post.keep(act.at[0], grads_pre.at[:, :, lane]),
            post.keep(act.at[1], grads_pre.at[:, :, pl.ds((4 + j) * chunk, chunk)]),
            post.keep(act.at[2], hidden.at[:, :, lane]),
        ]
        for climb in climbs[:2] if j == 1 else climbs[2:] if j == 2 else ():
            climb.last()
        for climb in climbs[:2] if j == 0 else climbs[2:] if j == 1 else ():
            climb.forward()

        def sums(n, carry):
            place = pl.ds(pl.multiple_of(n * TILE, TILE), TILE)
            x = x_buf[:, :, place].reshape(8 * TILE, TILE)
            grad = dy_buf[:, :, place].reshape(8 * TILE, TILE)
            for k in range(3):
                value = mm(act_t[k], grad if k == 2 else x).astype(NARROW)
                staged[k, 2 * n] = value[:, :LANES]
                staged[k, 2 * n + 1] = value[:, LANES:]
            return carry

        lax.fori_loop(0, 8, sums, 0)
        stored = [
            post.keep(staged.at[k, pl.ds(4 * fl, 4)], parts.at[3 * j + k, fl])
            for k in range(3)
            for fl in range(4)
        ]
        if j < 2:
            post.settle(stored)
            sums_0.append(Ends(post, at, parts, 3 * j, (ends_a, ends_b)[j]))
        else:
            saved += stored
        if j == 2:
            sums_0[0].finish()
            sums_1 = Middle(post, at, 1, parts, 0, ends_a, mates, *sum_bufs)
            sums_1.send()
    sums_0[1].finish()
    sums_1.finish()


class Descend:
    def __init__(self, post, at, pieces, got):
        self.near = post.send(pieces.at[:, at.c1], got.at[0], at.z1, got.at[0])
        self.next = post.send(pieces.at[:, at.c3], got.at[1], at.z1, got.at[1])

    def finish(self):
        self.near.arrive()
        self.next.arrive()


def norm_back_rows(grad, values, gain):
    normed, factor = normed_rows(values)
    scaled = grad * gain
    inner_mean = jnp.mean(scaled * normed, axis=-1, keepdims=True)
    return factor * (scaled - normed * inner_mean), jnp.sum(grad * normed, axis=0, keepdims=True)


def back_kernel(post, at, ins, outs, scratch):
    grads_pre, mid_own, cot_own, gains_in, parts, ends_b, mates_a, *weights = ins
    grad_mid_own, grad_mid, gain_part, ends_c, mates_b, outer_a = outs
    pre_buf, weight, mid_buf, cot_buf, gains, rows_out, gain_out = scratch[:7]
    bufs_1, bufs_2, fold_scratch = scratch[7:9], scratch[9:11], scratch[11:]
    meet((at.side, at.core, at.row, at.z1, at.z3))
    downs = [
        Middle(post, at, 1, parts, 3, ends_b, mates_b, *bufs_1),
        Middle(post, at, 2, parts, 0, mates_a, outer_a, *bufs_2),
        Ends(post, at, parts, 6, ends_c),
    ]
    chunk = pre_buf.shape[-1] // 8
    local = [post.keep(grads_pre, pre_buf)]
    for a in range(2):
        for j in range(4):
            place = pl.ds((4 * a + j) * chunk, chunk)
            local.append(post.keep(weights[4 * a + j], weight.at[:, :, :, place]))
    local += [post.keep(mid_own, mid_buf), post.keep(cot_own, cot_buf), post.keep(gains_in, gains)]
    post.settle(local)
    width = mid_buf.shape[-1]

    def part(block):
        return mm(pre_buf[block], weight[...].reshape(width, -1), ((1,), (1,)))

    for down in downs[:2]:
        down.send()
    fold = Fold(post, at, part, fold_scratch)
    fold.first()
    fold.second()
    fold.third()
    gain = jnp.concatenate([gains[i // 4, i % 4, 1:2, :] for i in range(16)], axis=1)
    spread = Spread(post, at, grad_mid)
    total = jnp.zeros((1, width), WIDE)
    for half in range(2):
        rows = HALVES[half]
        back, piece = norm_back_rows(fold.held[half], mid_buf[rows], gain)
        total = total + piece
        value = cot_buf[rows].astype(WIDE) + back
        fold.held[half] = value
        rows_out[half] = value.astype(NARROW)
        spread.own(half, rows_out.at[half])
        post.keep(fold.held.at[half], grad_mid_own.at[rows])
    gain_out[...] = jnp.broadcast_to(total, gain_out.shape)
    post.keep(gain_out, gain_part)
    spread.relay(0)
    spread.relay(1)
    spread.corner()
    spread.finish()
    for down in downs:
        down.finish()


def attend_back_kernel(post, at, ins, outs, scratch):
    (
        grad_mid, queries, keys, values, marks_in, inverse_in, out_all, mixed, attn_in, hidden, mid_own, parts,
        ends_c, mates_b, *downs_in
    ) = ins
    grad_proj, parts_attn, hidden_out, ends_d, mates_c, outer_b = outs
    (
        gm_buf, q_buf, k_buf, v_buf, marks, inverse, weight, mix_buf, hid_buf, down_buf, gp_buf, gk_buf, gv_buf,
        staged, mid_buf, out_buf
    ) = scratch[:16]
    bufs_1, bufs_2, fold_scratch = scratch[16:18], scratch[18:20], scratch[20:]
    meet((at.side, at.core, at.row, at.z1, at.z3))
    steps = [
        Middle(post, at, 1, parts, 6, ends_c, mates_c, *bufs_1),
        Middle(post, at, 2, parts, 3, mates_b, outer_b, *bufs_2),
        Ends(post, at, parts, 11, ends_d),
    ]

    chunk = hid_buf.shape[-1] // 4
    early = [post.keep(hidden, hid_buf)]
    for j in range(4):
        for i in range(16):
            target = down_buf.at[pl.ds(j * chunk, chunk), pl.ds(i * LANES, LANES)]
            early.append(post.keep(downs_in[j].at[i // 4, i % 4], target))
    late = [
        post.keep(source, target)
        for source, target in (
            (grad_mid, gm_buf), (queries, q_buf), (keys, k_buf), (values, v_buf), (marks_in, marks),
            (inverse_in, inverse), (mixed, mix_buf), (mid_own, mid_buf),
        )
    ]
    late += [
        post.keep(out_all.at[i // 4, i % 4], weight.at[:, pl.ds(i * LANES, LANES)])
        for i in range(16)
    ]
    post.settle(early)
    for step in steps[:2]:
        step.send()
    fold = Fold(post, at, lambda block: mm(hid_buf[block], down_buf[...]), fold_scratch)
    fold.first()
    post.settle(late)

    def fetch(n):
        place = pl.ds(n * TILE, TILE)
        return post.keep(attn_in.at[:, :, place], column(n))

    def column(n):
        return hid_buf.at[:, :, pl.ds(n % 2 * TILE, TILE)]

    mix_t, gp_t = down_buf.at[pl.ds(512, 256)], down_buf.at[pl.ds(0, 512)]
    fetched = fetch(0)
    width = gm_buf.shape[-1]
    for m in range(2):
        for i in range(4):
            q = quarter(at, i)
            n = min(i + 2, 4) * TILE
            place = slice(i * TILE, (i + 1) * TILE)
            id_col = marks[q].T[:, m : m + 1]
            id_row = id_rows(at, marks, m, n // TILE)
            cos_full, sin_full = rope_full(marks[q], m, inverse[0:1])
            rows = gm_buf[pl.ds(2 * q, 2), m * ROWS : (m + 1) * ROWS].reshape(TILE, width)
            grad_mixed = mm(rows, weight[...], ((1,), (1,))).astype(NARROW)
            for g in range(2):
                lane = slice(g * HEAD_DIM, (g + 1) * HEAD_DIM)
                query = q_buf[m, place, lane]
                prob = softmax_tile(query, k_buf[m, :n], id_col, id_row)
                grad = grad_mixed[:, lane]
                grad_prob = mm(grad, v_buf[m, :n], ((1,), (1,)))
                inner = jnp.sum(grad_prob * prob, axis=-1, keepdims=True)
                grad_scores = (SCALE * prob * (grad_prob - inner)).astype(NARROW)
                grad_query = mm(grad_scores, k_buf[m, :n])
                grad_key = mm(grad_scores, query, ((0,), (0,)))
                grad_value = mm(prob.astype(NARROW), grad, ((0,), (0,)))
                if i == 0 and g == 0:
                    gk_buf[:n], gv_buf[:n] = grad_key, grad_value
                    gk_buf[n:], gv_buf[n:] = (jnp.zeros_like(gk_buf[n:]),) * 2
                else:
                    gk_buf[:n] = gk_buf[:n] + grad_key
                    gv_buf[:n] = gv_buf[:n] + grad_value
                done = rope_back(grad_query, cos_full, sin_full).astype(NARROW)
                for h in range(2):
                    gp_buf[2 * q + h, m * ROWS : (m + 1) * ROWS, lane] = done[h * ROWS : (h + 1) * ROWS]
        for i in range(4):
            q = quarter(at, i)
            place = slice(i * TILE, (i + 1) * TILE)
            cos_full, sin_full = rope_full(marks[q], m, inverse[0:1])
            done = (
                rope_back(gk_buf[place], cos_full, sin_full).astype(NARROW),
                gv_buf[place].astype(NARROW),
            )
            for k in range(2):
                lane = slice((2 + k) * HEAD_DIM, (3 + k) * HEAD_DIM)
                for h in range(2):
                    gp_buf[2 * q + h, m * ROWS : (m + 1) * ROWS, lane] = done[k][h * ROWS : (h + 1) * ROWS]
        if m == 0:
            fold.second()
    post.keep(gp_buf, grad_proj)
    fold.third()
    for half in range(2):
        out_buf[HALVES[half]] = (fold.held[half] + mid_buf[HALVES[half]]).astype(NARROW)
    post.keep(out_buf, hidden_out)
    for i in range(8):
        place = slice(i * TILE, (i + 1) * TILE)
        mix_t[:, place] = mix_buf[i].astype(WIDE).T.astype(NARROW)
        gp_t[:, place] = gp_buf[i].astype(WIDE).T.astype(NARROW)
    span = mix_t.shape[0]
    for n in range(8):
        post.settle([fetched])
        if n < 7:
            fetched = fetch(n + 1)
        place = slice(n * TILE, (n + 1) * TILE)
        value = mm(mix_t[...], gm_buf[:, :, place].reshape(8 * TILE, TILE)).astype(NARROW)
        other = mm(gp_t[...], column(n)[...].reshape(8 * TILE, TILE)).astype(NARROW)
        for h in range(2):
            block = 2 * n + h
            lane = slice(h * LANES, (h + 1) * LANES)
            staged[block // 4, block % 4, :span] = value[:, lane]
            staged[block // 4, block % 4, span:] = other[:, lane]
    post.keep(staged, parts_attn)
    for step in steps:
        step.finish()


def end_kernel(post, at, ins, outs, scratch):
    (
        grad_proj, qkv_all, x_own, gains_in, grad_mid_own, hidden_out, gain_ffn_part, parts, parts_attn,
        ends_a, ends_b, ends_c, ends_d, mates_a, mates_b, mates_c, outer_a, outer_b
    ) = ins
    out_home, grad_home, gain_sums, mates_d, *home_sums = outs
    (
        gp_buf, weight, x_buf, gains, mid_buf, rows_out, gain_buf, gain_got,
        own_ffn, one_ffn, two_ffn, outer_c, outer_d, own_attn, far_attn, got_attn, end_attn
    ) = scratch[:17]
    bufs_1, bufs_2, bufs_3, fold_scratch = scratch[17:19], scratch[19:21], scratch[21:23], scratch[23:]
    f, c = at.f, at.c
    meet_swap(at)
    step_attn = Descend(post, at, parts_attn, got_attn)
    steps = [
        Middle(post, at, 1, parts, 11, ends_d, mates_d, *bufs_1),
        Middle(post, at, 2, parts, 6, mates_c, outer_c, *bufs_2),
    ]
    swap = Swap(post, at, home=True)
    moved = [swap(hidden_out.at[half], out_home.at[half], out_home.at[half]) for half in HALVES]
    fold_in = [
        post.keep(grad_proj, gp_buf), post.keep(qkv_all, weight), post.keep(x_own, x_buf),
        post.keep(gains_in, gains), post.keep(grad_mid_own, mid_buf),
        post.keep(gain_ffn_part, gain_buf),
    ]
    later = [
        post.keep(parts.at[:, :, c], own_ffn),
        post.keep(parts_attn.at[:, c], own_attn), post.keep(parts_attn.at[:, at.c2], far_attn),
    ]
    sum_sems = [post.local_sems.at[post.n_local + k] for k in range(7)]
    post.n_local += 7

    def mid_loads():
        pieces = [
            (ends_a.at[:, :, 2 * (c - 1)], one_ffn.at[pl.ds(0, 3)]),
            (ends_b.at[:, :, 2 * (c - 1)], one_ffn.at[pl.ds(3, 3)]),
            (ends_c.at[:, :, 2 * (c - 1)], one_ffn.at[pl.ds(6, 5)]),
            (ends_d.at[:, :, 2 * (c - 1)], one_ffn.at[pl.ds(11, 1)]),
            (mates_a.at[:, :, 2 - c], two_ffn.at[pl.ds(0, 3)]),
            (mates_b.at[:, :, 2 - c], two_ffn.at[pl.ds(3, 3)]),
            (mates_c.at[:, :, 2 - c], two_ffn.at[pl.ds(6, 5)]),
        ]
        return [pltpu.make_async_copy(*piece, sem) for piece, sem in zip(pieces, sum_sems)]

    def end_loads():
        pieces = [(outer_a, two_ffn.at[pl.ds(0, 3)]), (outer_b, two_ffn.at[pl.ds(3, 3)])]
        return [pltpu.make_async_copy(*piece, sem) for piece, sem in zip(pieces, sum_sems)]

    @pl.when(at.is_mid)
    def _():
        for copy in mid_loads():
            copy.start()

    @pl.when(at.is_end)
    def _():
        for copy in end_loads():
            copy.start()

    for step in steps:
        step.send()

    def add(left, right):
        return (left.astype(WIDE) + right.astype(WIDE)).astype(NARROW)

    post.settle(fold_in)
    width = x_buf.shape[-1]

    def part(block):
        return mm(gp_buf[block], weight[...].reshape(width, -1), ((1,), (1,)))

    fold = Fold(post, at, part, fold_scratch)
    fold.first()
    fold.second()
    fold.third()
    gain = jnp.concatenate([gains[i // 4, i % 4, 0:1, :] for i in range(16)], axis=1)
    total = jnp.zeros((1, width), WIDE)
    for half in range(2):
        rows = HALVES[half]
        back, piece = norm_back_rows(fold.held[half], x_buf[rows].astype(WIDE), gain)
        total = total + piece
        rows_out[rows] = (mid_buf[rows] + back).astype(NARROW)
        moved.append(swap(rows_out.at[rows], grad_home.at[rows], grad_home.at[rows]))
    gain_buf[0:1] = total
    post.settle(later)
    steps[0].finish()
    steps.append(Middle(post, at, 2, parts, 11, mates_d, outer_d, *bufs_3))
    step_attn.finish()
    for k in range(4):
        far_attn[k] = add(far_attn[k], got_attn[1, k])
    far_attn_sent = post.send(far_attn, end_attn, at.z2, end_attn)
    steps[2].send()
    for k, device in enumerate((at.core, at.row, at.side, at.z1, at.z2)):
        gain_sent = post.send(gain_buf, gain_got.at[k], device, gain_got.at[k])
        gain_sent.arrive()
        gain_sent.leave()
        post.out.pop()
        gain_buf[...] = gain_buf[...] + gain_got[k]
    place = pl.ds(pl.multiple_of((f * 4 + c) * LANES, LANES), LANES)
    post.keep(gain_buf.at[:, place], gain_sums)

    @pl.when(at.is_mid)
    def _():
        copies = mid_loads()
        for copy in copies:
            copy.wait()
        last = pltpu.make_async_copy(mates_d.at[:, :, 2 - c], two_ffn.at[pl.ds(11, 1)], sum_sems[0])
        last.start()
        last.wait()

        def add_own(p, carry):
            value = own_ffn[p].astype(WIDE) + one_ffn[p].astype(WIDE) + two_ffn[p].astype(WIDE)
            own_ffn[p] = value.astype(NARROW)
            return carry

        lax.fori_loop(0, 12, add_own, 0)

    for step in steps[1:]:
        step.finish()

    @pl.when(at.is_end)
    def _():
        for copy in end_loads():
            copy.wait()

        def add_own(first, other):
            def body(q, carry):
                own_ffn[first + q] = add(own_ffn[first + q], other[q])
                return carry

            return body

        lax.fori_loop(0, 6, add_own(0, two_ffn), 0)
        lax.fori_loop(0, 5, add_own(6, outer_c), 0)
        lax.fori_loop(0, 1, add_own(11, outer_d), 0)

    trades = []
    places = ((at.row, at.fy), (at.cross, at.fd), (at.core, at.fs))

    def trade(mine, out):
        post.keep(mine(f), out.at[f])
        for device, k in places:
            trades.append(post.send(mine(k), out.at[f], device, out.at[k]))

    def trade_chunks(n):
        for j in range(4):
            post.keep(own_ffn.at[3 * j + n, f], home_sums[n].at[f, j])
            for device, k in places:
                trades.append(
                    post.send(own_ffn.at[3 * j + n, k], home_sums[n].at[f, j], device, home_sums[n].at[k, j])
                )

    for n in range(3):
        trade_chunks(n)
    far_attn_sent.arrive()
    for k in range(4):
        value = own_attn[k].astype(WIDE) + got_attn[0, k].astype(WIDE) + end_attn[k].astype(WIDE)
        own_attn[k] = value.astype(NARROW)
    span = home_sums[3].shape[1]
    trade(lambda k: own_attn.at[k, pl.ds(0, span)], home_sums[3])
    trade(lambda k: own_attn.at[k, pl.ds(span, home_sums[4].shape[1])], home_sums[4])
    for sent in trades:
        sent.arrive()
    for arrive in moved:
        arrive()
    swap.finish()


def home_kernel(gate, up, down, qkv, out, gate_out, up_out, down_out, qkv_out, out_out):
    for source, target in ((gate, gate_out), (up, up_out), (qkv, qkv_out)):
        for n in range(source.shape[0] // 512):
            place = pl.ds(n * 512, 512)
            target[:, place] = source[place, :].astype(WIDE).T
    down_out[...] = down[...].astype(WIDE)
    out_out[...] = out[...].astype(WIDE)


def near_body(
    hidden_in, cotangent, block_ids, positions, attn_gain, wqkv, wo, ffn_gain, w_gate, w_up, w_down
):
    micro, _, rows, width = hidden_in.shape
    own = micro * rows
    ff = w_gate.shape[1]
    chunk = ff // 16
    shards = (w_gate, w_up, w_down)
    marks, gains = small_arrays(block_ids, positions, attn_gain, ffn_gain)
    inverse = THETA ** (-(jnp.arange(HALF, dtype=WIDE) * 2.0 / HEAD_DIM))
    inverse = jnp.broadcast_to(jnp.concatenate([inverse, inverse]), (8, HEAD_DIM))
    level_shapes = [shape(4, LANES, chunk), shape(4, LANES, chunk), shape(4, chunk, LANES)]
    whole_shapes = [shape(4, 4, LANES, chunk), shape(4, 4, LANES, chunk), shape(4, 4, chunk, LANES)]
    gains_shape = (4, 4, *gains.shape)
    x_own, cot_own, attn_in, all_marks, all_gains, qkv_all, out_all, *level = call(
        start_kernel,
        "start",
        [
            shape(own, width), shape(own, width), shape(8, own, width),
            shape(4, *marks.shape, dtype=WIDE), shape(*gains_shape, dtype=WIDE),
            shape(4, 4, LANES, wqkv.shape[1] // 4), shape(4, 4, wo.shape[0] // 4, LANES),
            *level_shapes, *level_shapes,
        ],
        (hidden_in.reshape(own, width), cotangent.reshape(own, width), marks, gains, wqkv, wo, *shards),
        [pltpu.VMEM((own, width), NARROW), pltpu.VMEM((own, width), NARROW), pltpu.VMEM(gains_shape, WIDE)],
        72, 24, 1,
    )
    queries, keys, values, mixed, dy, *more = call(
        attend_kernel,
        "attend",
        [
            shape(2, 1024, 256), shape(2, 1024, 128), shape(2, 1024, 128), shape(8, own, 256),
            shape(8, own, width), *whole_shapes, *level_shapes,
        ],
        (attn_in, qkv_all, inverse, all_marks, cot_own, *shards, *level[:3]),
        [
            pltpu.VMEM((2, 8, ROWS, width), NARROW), pltpu.VMEM(qkv_all.shape, NARROW),
            pltpu.VMEM(inverse.shape, WIDE), pltpu.VMEM(all_marks.shape, WIDE),
            pltpu.VMEM((2, 1024, 256), NARROW), pltpu.VMEM((2, 1024, 128), NARROW),
            pltpu.VMEM((2, 1024, 128), NARROW), pltpu.VMEM((8, own, 256), NARROW),
        ],
        40, 24, 2,
    )
    whole, level = more[:3], level + more[3:]
    mid_own, ffn_in, *more = call(
        middle_kernel,
        "middle",
        [
            shape(own, width, dtype=WIDE), shape(8, own, width), *whole_shapes, whole_shapes[0], *level_shapes,
        ],
        (mixed, out_all, x_own, all_gains, *shards, *level[3:7]),
        [
            pltpu.VMEM((8, own, 256), NARROW), pltpu.VMEM((256, width), NARROW),
            pltpu.VMEM((own, width), NARROW), pltpu.VMEM(gains_shape, WIDE),
            pltpu.VMEM((2, ROWS, width), NARROW), *Fold.scratch(width),
        ],
        52, 32, 3,
    )
    whole, level = whole + more[:4], level + more[4:]
    hidden, grads_pre, parts, ends_a, ends_b, mates_a, *more = call(
        ffn_kernel,
        "ffn",
        [
            shape(8, own, ff // 4), shape(8, own, ff // 2), shape(12, 4, 4, chunk, LANES),
            shape(3, 4, 3, chunk, LANES), shape(3, 4, 3, chunk, LANES), shape(3, 4, 2, chunk, LANES),
            *whole_shapes[1:], *whole_shapes,
        ],
        (ffn_in, dy, *whole, *level[7:]),
        [
            pltpu.VMEM((8, own, width), NARROW), pltpu.VMEM((8, own, width), NARROW),
            pltpu.VMEM((2, 4, 4, LANES, chunk), NARROW), pltpu.VMEM((2, 4, 4, LANES, chunk), NARROW),
            pltpu.VMEM((2, chunk, width), NARROW), pltpu.VMEM((3, 8, own, chunk), NARROW),
            pltpu.VMEM((3, chunk, 8 * own), NARROW), pltpu.VMEM((3, 16, chunk, LANES), NARROW),
            *middle_scratch(1, 3),
        ],
        48, 160, 4,
    )
    whole = whole + more
    fold_scratch = Fold.scratch(width)
    grad_mid_own, grad_mid, gain_ffn_part, ends_c, mates_b, outer_a = call(
        back_kernel,
        "back",
        [
            shape(own, width, dtype=WIDE), shape(8, own, width), shape(8, width, dtype=WIDE),
            shape(5, 4, 3, chunk, LANES), shape(3, 4, 2, chunk, LANES), shape(3, 4, chunk, LANES),
        ],
        (grads_pre, mid_own, cot_own, all_gains, parts, ends_b, mates_a, *whole[0::3], *whole[1::3]),
        [
            pltpu.VMEM((8, own, ff // 2), NARROW), pltpu.VMEM((4, 4, LANES, ff // 2), NARROW),
            pltpu.VMEM((own, width), WIDE), pltpu.VMEM((own, width), NARROW),
            pltpu.VMEM(gains_shape, WIDE), pltpu.VMEM((2, ROWS, width), NARROW),
            pltpu.VMEM((8, width), WIDE), *middle_scratch(1, 3), *middle_scratch(2, 3), *fold_scratch,
        ],
        48, 32, 5,
    )
    grad_proj, parts_attn, hidden_out, ends_d, mates_c, outer_b = call(
        attend_back_kernel,
        "attend_back",
        [
            shape(8, own, 512), shape(4, 4, 768, LANES), shape(own, width),
            shape(1, 4, 3, chunk, LANES), shape(5, 4, 2, chunk, LANES), shape(3, 4, chunk, LANES),
        ],
        (
            grad_mid, queries, keys, values, all_marks, inverse, out_all, mixed, attn_in, hidden, mid_own, parts,
            ends_c, mates_b, *whole[2::3],
        ),
        [
            pltpu.VMEM((8, own, width), NARROW), pltpu.VMEM((2, 1024, 256), NARROW),
            pltpu.VMEM((2, 1024, 128), NARROW), pltpu.VMEM((2, 1024, 128), NARROW),
            pltpu.VMEM(all_marks.shape, WIDE), pltpu.VMEM(inverse.shape, WIDE),
            pltpu.VMEM((256, width), NARROW), pltpu.VMEM((8, own, 256), NARROW),
            pltpu.VMEM((8, own, ff // 4), NARROW), pltpu.VMEM((ff // 4, width), NARROW),
            pltpu.VMEM((8, own, 512), NARROW), pltpu.VMEM((1024, 128), WIDE),
            pltpu.VMEM((1024, 128), WIDE),
            pltpu.VMEM((4, 4, 768, LANES), NARROW), pltpu.VMEM((own, width), WIDE),
            pltpu.VMEM((own, width), NARROW), *middle_scratch(1, 5), *middle_scratch(2, 3), *fold_scratch,
        ],
        32, 128, 6,
    )
    out_home, grad_home, gain_sums, _, *sums = call(
        end_kernel,
        "end",
        [
            shape(own, width), shape(own, width), shape(8, LANES, dtype=WIDE),
            shape(1, 4, 2, chunk, LANES), *[shape(4, 4, chunk, LANES)] * 3, shape(4, 256, LANES), shape(4, 512, LANES),
        ],
        (
            grad_proj, qkv_all, x_own, all_gains, grad_mid_own, hidden_out, gain_ffn_part, parts, parts_attn,
            ends_a, ends_b, ends_c, ends_d, mates_a, mates_b, mates_c, outer_a, outer_b,
        ),
        [
            pltpu.VMEM((8, own, 512), NARROW), pltpu.VMEM(qkv_all.shape, NARROW),
            pltpu.VMEM((own, width), NARROW), pltpu.VMEM(gains_shape, WIDE),
            pltpu.VMEM((own, width), WIDE), pltpu.VMEM((own, width), NARROW),
            pltpu.VMEM((8, width), WIDE), pltpu.VMEM((5, 8, width), WIDE),
            *[pltpu.VMEM((12, 4, chunk, LANES), NARROW)] * 3,
            pltpu.VMEM((5, 4, chunk, LANES), NARROW), pltpu.VMEM((1, 4, chunk, LANES), NARROW),
            pltpu.VMEM((4, 768, LANES), NARROW), pltpu.VMEM((4, 768, LANES), NARROW),
            pltpu.VMEM((2, 4, 768, LANES), NARROW), pltpu.VMEM((4, 768, LANES), NARROW),
            *middle_scratch(1, 1), *middle_scratch(2, 5), *middle_scratch(2, 1), *fold_scratch,
        ],
        80, 64, 7,
    )
    gate, up, down, out, qkv = (array.reshape(-1, LANES) for array in sums)
    grad_gate, grad_up, grad_down, grad_qkv, grad_out = pl.pallas_call(
        home_kernel,
        out_shape=[
            jax.ShapeDtypeStruct(array.shape, WIDE) for array in (w_gate, w_up, w_down, wqkv, wo)
        ],
        compiler_params=pltpu.CompilerParams(vmem_limit_bytes=48 << 20),
        name="home",
    )(gate, up, down, qkv, out)
    return (
        out_home.reshape(hidden_in.shape),
        grad_home.reshape(hidden_in.shape),
        gain_sums[0],
        grad_qkv,
        grad_out,
        gain_sums[1],
        grad_gate,
        grad_up,
        grad_down,
    )


def body(*shards):
    inner = KV_HEADS // lax.axis_size("tp")
    near = (lax.axis_size("fsdp"), lax.axis_size("ctx"), lax.axis_size("tp"), inner)
    return (near_body if near == (4, 4, 2, 4) else general_body)(*shards)


def solution(mesh):
    return jax.shard_map(
        body,
        mesh=mesh,
        in_specs=(
            P(None, "fsdp", ("ctx", "tp"), None),
            P(None, "fsdp", ("ctx", "tp"), None),
            P(None, "fsdp", None),
            P(None, "fsdp", "ctx"),
            P(("fsdp", "ctx")),
            P(("fsdp", "ctx"), "tp"),
            P("tp", ("fsdp", "ctx")),
            P(("fsdp", "ctx")),
            P(("fsdp", "ctx"), "tp"),
            P(("fsdp", "ctx"), "tp"),
            P("tp", ("fsdp", "ctx")),
        ),
        out_specs=(
            P(None, "fsdp", ("ctx", "tp"), None),
            P(None, "fsdp", ("ctx", "tp"), None),
            P(("fsdp", "ctx")),
            P(("fsdp", "ctx"), "tp"),
            P("tp", ("fsdp", "ctx")),
            P(("fsdp", "ctx")),
            P(("fsdp", "ctx"), "tp"),
            P(("fsdp", "ctx"), "tp"),
            P("tp", ("fsdp", "ctx")),
        ),
        check_vma=False,
    )
```

```python
import functools
import math

import jax
import jax.numpy as jnp
from jax import lax
from jax.sharding import PartitionSpec as P
from jax.experimental import pallas as pl
from jax.experimental.pallas import tpu as pltpu

HEADS = 16
KV_HEADS = 8
HEAD_DIM = 128


EPS = 1e-05
THETA = 1000000.0
MASKED = -1e30


def rope_tables(position_ids):
    half_dim = HEAD_DIM // 2
    inverse = THETA ** (-(jnp.arange(half_dim, dtype=jnp.float32) * 2.0 / HEAD_DIM))
    angles = position_ids.astype(jnp.float32)[..., None] * inverse
    angles = jnp.concatenate([angles, angles], axis=-1)
    return (jnp.cos(angles), jnp.sin(angles))


def turned(values):
    half_dim = values.shape[-1] // 2
    return jnp.concatenate([-values[..., half_dim:], values[..., :half_dim]], axis=-1)


def turned_back(values):
    half_dim = values.shape[-1] // 2
    return jnp.concatenate([values[..., half_dim:], -values[..., :half_dim]], axis=-1)


def norm_rows(stream, gain_row):
    factor = lax.rsqrt(jnp.mean(stream * stream, axis=-1, keepdims=True) + EPS)
    normed = stream * factor
    return (normed, factor, (normed * gain_row).astype(jnp.bfloat16))


def groups_of(fsdp, inner):
    near = [[high * inner + low for low in range(inner)] for high in range(fsdp // inner)]
    far = [[high * inner + low for high in range(fsdp // inner)] for low in range(inner)]
    return near, far


def general_body(
    hidden_in, cotangent, block_ids, positions, attn_gain, wqkv, wo, ffn_gain, w_gate, w_up, w_down
):
    fsdp, ctx, tp = lax.axis_size("fsdp"), lax.axis_size("ctx"), lax.axis_size("tp")
    inner = KV_HEADS // tp
    outer = fsdp // inner
    near, far = groups_of(fsdp, inner)
    micro, _, rows, width = hidden_in.shape
    score_scale = HEAD_DIM ** (-0.5)
    f_at, c_at = lax.axis_index("fsdp"), lax.axis_index("ctx")
    swap = [
        ((high * inner + low) * ctx + c, (high * inner + c) * ctx + low)
        for high in range(outer)
        for low in range(inner)
        for c in range(ctx)
    ]

    def rehome(array):
        return lax.ppermute(array, ("fsdp", "ctx"), swap)

    def trade(pieces):
        return lax.all_to_all(pieces, "fsdp", 0, 0, axis_index_groups=near)

    def spread(block):
        both = lax.all_gather(block, "tp")
        return lax.all_gather(both, "fsdp", axis_index_groups=near)

    def fold(parts):
        half = lax.psum_scatter(
            parts.astype(jnp.bfloat16), "fsdp", scatter_dimension=0, axis_index_groups=near
        )
        return lax.psum_scatter(half, "tp", scatter_dimension=0).astype(jnp.float32)

    def gather_levels(pieces):
        up = lax.all_gather(pieces, "ctx")
        if outer == 1:
            return up[None]
        return lax.all_gather(up, "fsdp", axis_index_groups=far)

    def scatter_levels(pieces):
        if outer == 1:
            pieces = pieces[0]
        else:
            pieces = lax.psum_scatter(pieces, "fsdp", scatter_dimension=0, axis_index_groups=far)
        return lax.psum_scatter(pieces, "ctx", scatter_dimension=0)

    def fetch_columns(shard):
        block, cols = shard.shape
        pieces = trade(shard.reshape(block, inner, cols // inner).transpose(1, 0, 2))
        whole = gather_levels(pieces).transpose(0, 2, 1, 3, 4)
        return whole.reshape(-1, cols // inner)

    def fetch_rows(shard):
        length, block = shard.shape
        pieces = trade(shard.reshape(inner, length // inner, block))
        whole = gather_levels(pieces).transpose(3, 0, 2, 1, 4)
        return whole.reshape(length // inner, -1)

    def return_columns(grad):
        total, cols = grad.shape
        grad = grad.astype(jnp.bfloat16).reshape(outer, inner, ctx, -1, cols)
        mine = trade(scatter_levels(grad.transpose(0, 2, 1, 3, 4)))
        return mine.transpose(1, 0, 2).reshape(mine.shape[1], -1).astype(jnp.float32)

    def return_rows(grad):
        length, total = grad.shape
        grad = grad.astype(jnp.bfloat16).reshape(length, outer, inner, ctx, -1)
        mine = trade(scatter_levels(grad.transpose(1, 3, 2, 0, 4)))
        return mine.reshape(inner * length, -1).astype(jnp.float32)

    def dot(left, right, dims):
        return lax.dot_general(left, right, (dims, ((), ())), preferred_element_type=jnp.float32)

    gains = lax.all_gather(jnp.stack([attn_gain, ffn_gain]), ("fsdp", "ctx"))
    gain_attn = gains[:, 0].reshape(-1).astype(jnp.float32)
    gain_ffn = gains[:, 1].reshape(-1).astype(jnp.float32)
    span = positions.shape[2]
    ids_here = lax.dynamic_slice_in_dim(block_ids[:, 0], c_at * span, span, 1)
    marks = lax.all_gather(jnp.stack([positions[:, 0], ids_here]), ("fsdp", "ctx"))
    my_seq = f_at // inner * inner + c_at
    marks = lax.dynamic_slice_in_dim(marks, my_seq * ctx, ctx, 0)
    marks = marks.transpose(1, 2, 0, 3).reshape(2, micro, ctx * span)
    pos, ids = marks[0], marks[1]

    weight_qkv = fetch_columns(wqkv)
    weight_out = fetch_rows(wo)
    weight_gate = fetch_columns(w_gate)
    weight_up = fetch_columns(w_up)
    weight_down = fetch_rows(w_down)

    stream = rehome(hidden_in).reshape(micro * rows, width).astype(jnp.float32)
    grad_out_low = rehome(cotangent).reshape(micro * rows, width)
    grad_out = grad_out_low.astype(jnp.float32)

    def to_heads(flat):
        split = flat.reshape(inner * tp, micro, rows, -1, HEAD_DIM).transpose(1, 0, 2, 3, 4)
        return split.reshape(micro, inner * tp * rows, -1, HEAD_DIM)

    def from_heads(heads):
        split = heads.reshape(micro, inner * tp, rows, -1).transpose(1, 0, 2, 3)
        return split.reshape(inner * tp * micro * rows, -1)

    normed_one, factor_one, attn_rows = norm_rows(stream, gain_attn)
    attn_in = spread(attn_rows).reshape(-1, width)
    projected = to_heads(dot(attn_in, weight_qkv, ((1,), (0,))))
    group = HEADS // KV_HEADS
    cos_table, sin_table = rope_tables(pos)
    cos_heads, sin_heads = cos_table[:, :, None], sin_table[:, :, None]
    turning = projected[:, :, : group + 1]
    turning = (turning * cos_heads + turned(turning) * sin_heads).astype(jnp.bfloat16)
    queries, keys = turning[:, :, :group], turning[:, :, group]
    values = projected[:, :, group + 1].astype(jnp.bfloat16)
    allowed = (ids[:, None, :] <= ids[:, :, None])[:, None]
    raw = jnp.einsum("blge,bme->bglm", queries, keys, preferred_element_type=jnp.float32)
    scores = jnp.where(allowed, raw * score_scale, MASKED)
    row_max = jnp.max(scores, axis=-1, keepdims=True)
    exponent = jnp.exp(scores - row_max)
    prob = exponent / jnp.sum(exponent, axis=-1, keepdims=True)
    prob_low = prob.astype(jnp.bfloat16)
    mixed = jnp.einsum("bglm,bme->blge", prob_low, values, preferred_element_type=jnp.float32)
    mixed = from_heads(mixed.astype(jnp.bfloat16))
    out_part = dot(mixed, weight_out, ((1,), (0,)))
    stream_mid = stream + fold(out_part.reshape(inner, tp, -1, width))
    normed_two, factor_two, ffn_rows = norm_rows(stream_mid, gain_ffn)
    ffn_in = spread(ffn_rows).reshape(-1, width)
    dy = spread(grad_out_low).reshape(-1, width)

    gate_pre = dot(ffn_in, weight_gate, ((1,), (0,)))
    up_pre = dot(ffn_in, weight_up, ((1,), (0,)))
    gate_sig = jax.nn.sigmoid(gate_pre)
    gate_act = gate_pre * gate_sig
    hidden = (gate_act * up_pre).astype(jnp.bfloat16)
    grad_hidden = dot(dy, weight_down, ((1,), (1,)))
    grad_gate_pre = (
        grad_hidden * up_pre * gate_sig * (1.0 + gate_pre * (1.0 - gate_sig))
    ).astype(jnp.bfloat16)
    grad_up_pre = (grad_hidden * gate_act).astype(jnp.bfloat16)
    grad_ffn_part = dot(grad_gate_pre, weight_gate, ((1,), (1,))) + dot(
        grad_up_pre, weight_up, ((1,), (1,))
    )
    grad_ffn_in = fold(grad_ffn_part.reshape(inner, tp, -1, width))
    down_part = dot(hidden, weight_down, ((1,), (0,)))
    stream_out = stream_mid + fold(down_part.reshape(inner, tp, -1, width))
    grad_down = return_rows(dot(hidden, dy, ((0,), (0,))))
    grad_gate = return_columns(dot(ffn_in, grad_gate_pre, ((0,), (0,))))
    grad_up = return_columns(dot(ffn_in, grad_up_pre, ((0,), (0,))))

    def back_rows(grad, normed, factor, gain_row):
        grad_normed = grad * gain_row
        inner_mean = jnp.mean(grad_normed * normed, axis=-1, keepdims=True)
        return factor * (grad_normed - normed * inner_mean), jnp.sum(grad * normed, axis=0)

    mid_norm, gain_ffn_part = back_rows(grad_ffn_in, normed_two, factor_two, gain_ffn)
    grad_mid = grad_out + mid_norm
    grad_mid_low = spread(grad_mid.astype(jnp.bfloat16)).reshape(-1, width)
    grad_mixed = to_heads(dot(grad_mid_low, weight_out, ((1,), (1,))).astype(jnp.bfloat16))
    grad_wo = return_rows(dot(mixed, grad_mid_low, ((0,), (0,))))
    grad_prob = jnp.einsum("blge,bme->bglm", grad_mixed, values, preferred_element_type=jnp.float32)
    inner_prob = jnp.sum(grad_prob * prob, axis=-1, keepdims=True)
    grad_scores = (score_scale * prob * (grad_prob - inner_prob)).astype(jnp.bfloat16)
    grad_queries = jnp.einsum(
        "bglm,bme->blge", grad_scores, keys, preferred_element_type=jnp.float32
    )
    grad_keys = jnp.einsum(
        "bglm,blge->bme", grad_scores, queries, preferred_element_type=jnp.float32
    )
    grad_values = jnp.einsum(
        "bglm,blge->bme", prob_low, grad_mixed, preferred_element_type=jnp.float32
    )
    grad_turning = jnp.concatenate([grad_queries, grad_keys[:, :, None]], axis=2)
    grad_turning = grad_turning * cos_heads + turned_back(grad_turning * sin_heads)
    grad_projected = jnp.concatenate([grad_turning, grad_values[:, :, None]], axis=2)
    grad_projected = from_heads(grad_projected.astype(jnp.bfloat16))
    grad_attn_in = fold(
        dot(grad_projected, weight_qkv, ((1,), (1,))).reshape(inner, tp, -1, width)
    )
    grad_wqkv = return_columns(dot(attn_in, grad_projected, ((0,), (0,))))
    in_norm, gain_attn_part = back_rows(grad_attn_in, normed_one, factor_one, gain_attn)
    grad_in = (grad_mid + in_norm).astype(jnp.bfloat16)

    gain_parts = jnp.stack([gain_attn_part, gain_ffn_part], axis=1).reshape(fsdp * ctx, -1, 2)
    gain_sums = lax.psum_scatter(gain_parts, ("fsdp", "ctx"), scatter_dimension=0)
    gain_sums = lax.psum(gain_sums, "tp")

    def home(array):
        return rehome(array.reshape(micro, 1, rows, width))

    return (
        home(stream_out.astype(jnp.bfloat16)),
        home(grad_in),
        gain_sums[:, 0],
        grad_wqkv,
        grad_wo,
        gain_sums[:, 1],
        grad_gate,
        grad_up,
        grad_down,
    )


MESH = pl.DeviceIdType.MESH
ROWS = 128
LANES = 128
NARROW = jnp.bfloat16
WIDE = jnp.float32
HALF = HEAD_DIM // 2
SCALE = HEAD_DIM ** (-0.5)
ANYWHERE = pl.BlockSpec(memory_space=pl.ANY)


class Place:
    def __init__(self):
        f, c, t = lax.axis_index("fsdp"), lax.axis_index("ctx"), lax.axis_index("tp")
        self.f, self.c, self.t = f, c, t
        fs, fy = f + 1 - 2 * (f % 2), (f + 2) % 4
        fd = (fs + 2) % 4
        self.fs, self.fy, self.fd = fs, fy, fd
        self.c1, self.c2 = c + 1 - 2 * (c % 2), (c + 2) % 4
        self.c3 = (self.c1 + 2) % 4
        self.side, self.core, self.row = (f, c, 1 - t), (fs, c, t), (fy, c, t)
        self.cross = (fd, c, t)
        self.z1, self.z2 = (f, self.c1, t), (f, self.c2, t)
        self.is_end, self.is_mid = c * (3 - c) == 0, c * (3 - c) != 0
        self.c_near, self.c_mate, self.c_outer = 1 + c // 3, 3 - c, 3 * c - 3
        self.z3 = (f, 3 - c, t)
        self.core_side, self.row_side = (fs, c, 1 - t), (fy, c, 1 - t)
        self.cross_side = (fd, c, 1 - t)
        self.level = (
            self.side, self.core, self.row, self.cross, self.core_side, self.row_side, self.cross_side
        )
        y, k, high, low = f // 2, f % 2, c // 2, c % 2
        self.to_f, to_c = (low + y) % 2 * 2 + high, k * 2 + y
        self.to = (self.to_f, to_c, t)
        self.whence = (low * 2 + high, k * 2 + (y + low) % 2, t)
        self.away = (self.to_f - f) * (self.to_f - f) + (to_c - c) * (to_c - c)
        self.b, self.b_side = f * 2 + t, f * 2 + 1 - t
        self.b_row, self.b_far = fy * 2 + t, fy * 2 + 1 - t
        self.b_core, self.b_core_side = fs * 2 + t, fs * 2 + 1 - t
        self.b_core_row, self.b_core_far = fd * 2 + t, fd * 2 + 1 - t


class Sent:
    def __init__(self, copy, landing):
        self.copy, self.landing = copy, landing

    def arrive(self):
        self.landing.wait_recv()

    def leave(self):
        self.copy.wait_send()


class Post:
    def __init__(self, send_sems, recv_sems, local_sems):
        self.sems = send_sems, recv_sems
        self.local_sems = local_sems
        self.n, self.n_local = 0, 0
        self.out, self.kept = [], []
        self.gates = []

    def make(self, source, target, device, lands):
        sems = dict(
            send_sem=self.sems[0].at[self.n],
            recv_sem=self.sems[1].at[self.n],
            device_id=device,
            device_id_type=MESH,
        )
        self.n += 1
        copy = pltpu.make_async_remote_copy(src_ref=source, dst_ref=target, **sems)
        landing = pltpu.make_async_remote_copy(src_ref=lands, dst_ref=lands, **sems)
        return Sent(copy, landing)

    def send(self, source, target, device, lands):
        sent = self.make(source, target, device, lands)
        sent.copy.start()
        self.out.append(sent)
        return sent

    def keep(self, source, target):
        copy = pltpu.make_async_copy(source, target, self.local_sems.at[self.n_local])
        self.n_local += 1
        copy.start()
        self.kept.append(copy)
        return copy

    def settle(self, copies):
        for copy in copies:
            copy.wait()
        self.kept = [kept for kept in self.kept if not any(kept is copy for copy in copies)]

    def close(self):
        for sent in self.out:
            sent.leave()
        for copy in self.kept:
            copy.wait()
        for gate in self.gates:
            gate.leave()
        self.out, self.kept, self.gates = [], [], []


class Gate:
    def __init__(self, post, sends, gets, what, lands):
        self.post, self.sends, self.gets, self.what, self.lands = post, sends, gets, what, lands
        self.n = post.n
        post.n += 1

    def copy(self, source, target, device):
        return pltpu.make_async_remote_copy(
            src_ref=source,
            dst_ref=target,
            send_sem=self.post.sems[0].at[self.n],
            recv_sem=self.post.sems[1].at[self.n],
            device_id=device,
            device_id_type=MESH,
        )

    def start(self):
        @pl.when(self.sends)
        def _():
            self.copy(*self.what()).start()

        self.post.gates.append(self)
        return self

    def arrive(self):
        @pl.when(self.gets)
        def _():
            there = self.lands()
            self.copy(there, there, self.post.anyone).wait_recv()

    def leave(self):
        @pl.when(self.sends)
        def _():
            self.copy(*self.what()).wait_send()


def meet(devices):
    bar = pltpu.get_barrier_semaphore()
    for device in devices:
        pl.semaphore_signal(bar, inc=1, device_id=device, device_id_type=MESH)
    pl.semaphore_wait(bar, len(devices))


class Spread:
    def __init__(self, post, at, out):
        self.post, self.at, self.out = post, at, out
        self.sent = {}

    def slot(self, block, half):
        return self.out.at[block, pl.ds(half * ROWS, ROWS)]

    def own(self, half, source):
        at, mine = self.at, self.slot(self.at.b, half)
        self.sent["side", half] = self.post.send(source, mine, at.side, self.slot(at.b_side, half))
        self.sent["row", half] = self.post.send(source, mine, at.row, self.slot(at.b_row, half))
        self.sent["core", half] = self.post.send(source, mine, at.core, self.slot(at.b_core, half))
        self.post.keep(source, mine)

    def pass_on(self, name, half, block, lands):
        here = self.slot(block, half)
        self.sent[name, half] = self.post.send(
            here, here, self.at.core, self.slot(lands, half)
        )

    def relay(self, half):
        at = self.at
        first = ("side", "row") if half == 0 else ("row", "side")
        for name in first:
            self.sent[name, half].arrive()
            block = at.b_side if name == "side" else at.b_row
            here = self.slot(block, half)
            if half == 0 and name == "side":
                self.sent["far", 0] = self.post.send(here, here, at.row, self.slot(at.b_far, 0))
            if half == 1 and name == "row":
                self.sent["far", 1] = self.post.send(here, here, at.side, self.slot(at.b_far, 1))
            lands = at.b_core_side if name == "side" else at.b_core_row
            self.pass_on("core_" + name, half, block, lands)

    def corner(self):
        for half in range(2):
            self.sent["far", half].arrive()
            self.pass_on("core_far", half, self.at.b_far, self.at.b_core_far)

    def finish(self):
        for name in ("core", "core_side", "core_row", "core_far"):
            for half in range(2):
                self.sent[name, half].arrive()


SPREAD_COPIES, SPREAD_KEPT = 14, 2


class Fold:
    copies = 10

    def __init__(self, post, at, part, scratch):
        self.post, self.at, self.part = post, at, part
        self.got, self.give, self.far, self.side, self.row, self.gx, self.gy, self.held = scratch

    @staticmethod
    def scratch(width):
        return [
            pltpu.VMEM((4, 2 * ROWS, width), NARROW),
            pltpu.VMEM((4, 2 * ROWS, width), NARROW),
            pltpu.VMEM((2, ROWS, width), NARROW),
            pltpu.VMEM((2, ROWS, width), NARROW),
            pltpu.VMEM((2, ROWS, width), NARROW),
            pltpu.VMEM((3, ROWS, width), NARROW),
            pltpu.VMEM((3, ROWS, width), NARROW),
            pltpu.VMEM((4, ROWS, width), WIDE),
        ]

    def pair(self, slot, for_core, for_own):
        both = self.part(for_core, for_own)
        self.give[slot] = both[: 2 * ROWS].astype(NARROW)
        sent = self.post.send(
            self.give.at[slot], self.got.at[slot], self.at.core, self.got.at[slot]
        )
        return sent, both[2 * ROWS :]

    def add_core(self, slot, pair):
        sent, value = pair
        sent.arrive()
        return value + self.got[slot].astype(WIDE)

    def first(self):
        at, post = self.at, self.post
        far = self.pair(3, at.b_core_far, at.b_far)
        side = self.pair(1, at.b_core_side, at.b_side)
        value = self.add_core(3, far).astype(NARROW)
        self.far[0] = value[:ROWS]
        self.far[1] = value[ROWS:]
        self.far_x = post.send(self.far.at[0], self.gx.at[0], at.side, self.gx.at[0])
        self.far_y = post.send(self.far.at[1], self.gy.at[0], at.row, self.gy.at[0])
        row = self.pair(2, at.b_core_row, at.b_row)
        value = self.add_core(1, side)
        self.side[0] = value[:ROWS].astype(NARROW)
        self.held[2] = value[ROWS:]
        self.side_x = post.send(self.side.at[0], self.gx.at[1], at.side, self.gx.at[1])
        own = self.pair(0, at.b_core, at.b)
        value = self.add_core(2, row)
        self.row[1] = value[ROWS:].astype(NARROW)
        self.held[3] = value[:ROWS]
        self.row_y = post.send(self.row.at[1], self.gy.at[1], at.row, self.gy.at[1])
        value = self.add_core(0, own)
        self.held[0] = value[:ROWS]
        self.held[1] = value[ROWS:]

    def second(self):
        at, post = self.at, self.post
        self.far_y.arrive()
        self.side[1] = (self.held[2] + self.gy[0].astype(WIDE)).astype(NARROW)
        self.side_b = post.send(self.side.at[1], self.gx.at[2], at.side, self.gx.at[2])
        self.far_x.arrive()
        self.row[0] = (self.held[3] + self.gx[0].astype(WIDE)).astype(NARROW)
        self.row_a = post.send(self.row.at[0], self.gy.at[2], at.row, self.gy.at[2])

    def third(self):
        self.side_x.arrive()
        self.row_y.arrive()
        self.held[0] = self.held[0] + self.gx[1].astype(WIDE)
        self.held[1] = self.held[1] + self.gy[1].astype(WIDE)
        self.row_a.arrive()
        self.held[0] = self.held[0] + self.gy[2].astype(WIDE)
        self.side_b.arrive()
        self.held[1] = self.held[1] + self.gx[2].astype(WIDE)


class Climb:
    copies, kept = 3, 1

    def __init__(self, post, at, level, out):
        self.post, self.at, self.out = post, at, out
        mine = out.at[:, at.c]
        self.far = post.send(level, mine, at.z2, out.at[:, at.c2])
        self.close = post.send(level, mine, at.z1, out.at[:, at.c1])
        self.own = post.keep(level, mine)

    def forward(self):
        at = self.at
        self.far.arrive()
        there = self.out.at[:, at.c2]
        self.last = self.post.send(there, there, at.z1, self.out.at[:, at.c3])

    def finish(self):
        self.close.arrive()
        self.last.arrive()
        self.post.settle([self.own])


class LineClimb:
    def __init__(self, post, at, level, out):
        self.post = post
        line = lambda c: (at.f, c, at.t)
        slot = lambda c: out.at[:, c]
        near, mate, outer = at.c_near, at.c_mate, at.c_outer
        end, mid = at.is_end, at.is_mid
        self.t0 = Gate(post, end, mid, lambda: (level, slot(at.c), line(near)), lambda: slot(outer))
        self.t1 = Gate(post, mid, end, lambda: (level, slot(at.c), line(outer)), lambda: slot(near))
        self.t2 = Gate(post, mid, mid, lambda: (level, slot(at.c), line(mate)), lambda: slot(mate))
        self.t3 = Gate(
            post, mid, mid, lambda: (slot(outer), slot(outer), line(mate)), lambda: slot(3 - outer)
        )
        self.t4 = Gate(
            post, mid, end, lambda: (slot(mate), slot(mate), line(outer)), lambda: slot(3 - near)
        )
        self.t5 = Gate(
            post, mid, end, lambda: (slot(3 - outer), slot(3 - outer), line(outer)), lambda: slot(3 - at.c)
        )
        for gate in (self.t0, self.t1, self.t2):
            gate.start()
        self.own = post.keep(level, slot(at.c))

    def forward(self):
        self.t2.arrive()
        self.t4.start()
        self.t0.arrive()
        self.t3.start()

    def last(self):
        self.t3.arrive()
        self.t5.start()

    def finish(self):
        for gate in (self.t1, self.t4, self.t5):
            gate.arrive()
        self.post.settle([self.own])


class Ends:
    def __init__(self, post, at, parts, first, got, start=0, count=None):
        count = got.shape[0] if count is None else count
        self.gates = [
            Gate(
                post, at.is_end, at.is_mid,
                lambda q=q: (
                    parts.at[first + q, :, pl.ds((3 - at.c) // 3, 3)], got.at[q], (at.f, at.c_near, at.t)
                ),
                lambda q=q: got.at[q],
            ).start()
            for q in range(start, start + count)
        ]

    def finish(self):
        for gate in self.gates:
            gate.arrive()


class Middle:
    def __init__(self, post, at, step, parts, first, came, out, own, more):
        self.post, self.at, self.out, self.own, self.more = post, at, out, own, more
        self.step, self.n = step, out.shape[0]
        self.sems = [post.local_sems.at[post.n_local + k] for k in range(2)]
        post.n_local += 2
        rows = pl.ds(first, self.n)

        def sources():
            if step == 1:
                return (
                    parts.at[rows, :, pl.ds(2 * (2 - at.c), 2)], came.at[:, :, pl.ds(2 - at.c, 2)]
                )
            return parts.at[rows, :, 3 * (at.c - 1)], came.at[:, :, at.c - 1]

        self.sources = sources

        @pl.when(at.is_mid)
        def _():
            for source, target, sem in zip(sources(), (own, more), self.sems):
                pltpu.make_async_copy(source, target, sem).start()

    def send(self):
        at, own, more = self.at, self.own, self.more

        @pl.when(at.is_mid)
        def _():
            for source, target, sem in zip(self.sources(), (own, more), self.sems):
                pltpu.make_async_copy(source, target, sem).wait()

            def add(q, carry):
                own[q] = (own[q].astype(WIDE) + more[q].astype(WIDE)).astype(NARROW)
                return carry

            lax.fori_loop(0, self.n, add, 0)

        c_to = at.c_mate if self.step == 1 else at.c_outer
        self.gate = Gate(
            self.post, at.is_mid, at.is_mid if self.step == 1 else at.is_end,
            lambda: (own, self.out, (at.f, c_to, at.t)), lambda: self.out,
        ).start()

    def finish(self):
        self.gate.arrive()


def middle_scratch(step, n):
    dims = (n, 4, 2, 256, LANES) if step == 1 else (n, 4, 256, LANES)
    return [pltpu.VMEM(dims, NARROW)] * 2


def call(kernel, name, outs, args, scratch, copies, kept, collective_id):
    sems = [
        pltpu.SemaphoreType.DMA((copies,)),
        pltpu.SemaphoreType.DMA((copies,)),
        pltpu.SemaphoreType.DMA((kept,)),
    ]
    n_in, n_out = len(args), len(outs)

    def inner(*refs):
        post, at = Post(*refs[len(refs) - 3 :]), Place()
        post.anyone = at.z1
        kernel(
            post, at, refs[:n_in], refs[n_in : n_in + n_out], refs[n_in + n_out : len(refs) - 3]
        )
        post.close()
        assert post.n <= copies and post.n_local <= kept, (post.n, post.n_local)

    return pl.pallas_call(
        inner,
        out_shape=outs,
        in_specs=[ANYWHERE] * n_in,
        out_specs=[ANYWHERE] * n_out,
        scratch_shapes=scratch + sems,
        compiler_params=pltpu.CompilerParams(
            collective_id=collective_id, has_side_effects=True, vmem_limit_bytes=62 << 20
        ),
        name=name,
    )(*args)


def shape(*dims, dtype=NARROW):
    return jax.ShapeDtypeStruct(dims, dtype)


def gain_row(gains_ref, which):
    return jnp.concatenate([gains_ref[i, which : which + 1, :] for i in range(16)], axis=1)


def normed_rows(values):
    factor = lax.rsqrt(jnp.mean(values * values, axis=-1, keepdims=True) + EPS)
    return values * factor, factor


class Swap:
    def __init__(self, post, at, home=False):
        self.post, self.at, self.moves = post, at, []
        self.device = at.whence if home else at.to

    def __call__(self, source, target, lands):
        post, at = self.post, self.at
        sent = post.make(source, target, self.device, lands)
        local = pltpu.make_async_copy(source, target, post.local_sems.at[post.n_local])
        post.n_local += 1

        @pl.when(at.away != 0)
        def _():
            sent.copy.start()

        @pl.when(at.away == 0)
        def _():
            local.start()

        self.moves.append(sent)

        def arrive():
            @pl.when(at.away != 0)
            def _():
                sent.landing.wait_recv()

            @pl.when(at.away == 0)
            def _():
                local.wait()

        return arrive

    def finish(self):
        @pl.when(self.at.away != 0)
        def _():
            for sent in self.moves:
                sent.copy.wait_send()


def meet_swap(at):
    bar = pltpu.get_barrier_semaphore()
    partners = (*at.level, at.z1, at.z2, at.z3)
    for device in partners:
        pl.semaphore_signal(bar, inc=1, device_id=device, device_id_type=MESH)

    @pl.when(at.away != 0)
    def _():
        for device in (at.to, at.whence):
            pl.semaphore_signal(bar, inc=1, device_id=device, device_id_type=MESH)
        pl.semaphore_wait(bar, len(partners) + 2)

    @pl.when(at.away == 0)
    def _():
        pl.semaphore_wait(bar, len(partners))


class Deal:
    def __init__(self, post, at, shards, j, outs):
        self.post, self.sent, self.kept = post, [], []
        gate, up, down = shards
        part = gate.shape[1] // 4
        chunk = part // 4
        for device, k in ((at.row, at.fy), (at.cross, at.fd), (at.core, at.fs), (None, at.f)):
            lane = pl.ds(pl.multiple_of(k * part + j * chunk, LANES), chunk)
            for source, out in zip((gate.at[:, lane], up.at[:, lane], down.at[lane]), outs):
                if device is None:
                    self.kept.append(post.keep(source, out.at[at.f]))
                else:
                    self.sent.append(post.send(source, out.at[at.f], device, out.at[k]))

    def finish(self):
        for sent in self.sent:
            sent.arrive()


HALVES = [pl.ds(half * ROWS, ROWS) for half in range(2)]


def start_kernel(post, at, ins, outs, scratch):
    hidden, marks, gains, wqkv, wo, *shards = ins
    x_own, attn_in, all_marks, all_gains, qkv_all, out_all, *levels_out = outs
    rows_in, rows_out, gain_buf = scratch
    f, c = at.f, at.c
    meet_swap(at)
    swap = Swap(post, at)
    x_moved = [swap(hidden.at[half], rows_in.at[half], rows_in.at[half]) for half in HALVES]
    heads = wqkv.shape[1] // 4
    span = wo.shape[0] // 4
    first = []
    for device, k in ((at.row, at.fy), (at.cross, at.fd), (at.core, at.fs)):
        lane = pl.ds(pl.multiple_of(k * heads, LANES), heads)
        first.append(post.send(wqkv.at[:, lane], qkv_all.at[f, c], device, qkv_all.at[k, c]))
        row = pl.ds(pl.multiple_of(k * span, LANES), span)
        first.append(post.send(wo.at[row], out_all.at[f, c], device, out_all.at[k, c]))
    lane = pl.ds(pl.multiple_of(f * heads, LANES), heads)
    own = [post.keep(wqkv.at[:, lane], qkv_all.at[f, c])]
    row = pl.ds(pl.multiple_of(f * span, LANES), span)
    own.append(post.keep(wo.at[row], out_all.at[f, c]))
    marks_moved = swap(marks, all_marks.at[at.to_f], all_marks.at[f])

    mine = gain_buf.at[f, c]
    post.settle([post.keep(gains, mine)])
    step = post.send(mine, mine, at.core, gain_buf.at[at.fs, c])
    step.arrive()
    pair = gain_buf.at[pl.ds(f // 2 * 2, 2), c]
    step = post.send(pair, pair, at.row, gain_buf.at[pl.ds(at.fy // 2 * 2, 2), c])
    step.arrive()
    step = post.send(gain_buf.at[:, c], gain_buf.at[:, c], at.z1, gain_buf.at[:, at.c1])
    step.arrive()
    pair = gain_buf.at[:, pl.ds(c // 2 * 2, 2)]
    step = post.send(pair, pair, at.z2, gain_buf.at[:, pl.ds(at.c2 // 2 * 2, 2)])
    step.arrive()
    gain = jnp.concatenate([gain_buf[i // 4, i % 4, 0:1, :] for i in range(16)], axis=1)
    post.keep(gain_buf, all_gains)

    post.settle(own)
    for sent in first:
        sent.arrive()

    spread = Spread(post, at, attn_in)
    levels = []

    def climb():
        for out in (qkv_all, out_all):
            here, there = out.at[:, c], out.at[:, at.c2]
            far = post.send(here, here, at.z2, there)
            close = post.send(here, here, at.z1, out.at[:, at.c1])
            levels.append((far, close, there, out))

    for half in range(2):
        x_moved[half]()
        if half == 1:
            climb()
        normed, _ = normed_rows(rows_in[HALVES[half]].astype(WIDE))
        rows_out[HALVES[half]] = (normed * gain).astype(NARROW)
        spread.own(half, rows_out.at[HALVES[half]])
        post.keep(rows_in.at[HALVES[half]], x_own.at[HALVES[half]])

    marks_moved()
    here = all_marks.at[f]
    small = post.send(here, here, at.core, all_marks.at[at.fs])
    spread.relay(0)
    small.arrive()
    pair = all_marks.at[pl.ds(f // 2 * 2, 2)]
    smaller = post.send(pair, pair, at.row, all_marks.at[pl.ds(at.fy // 2 * 2, 2)])
    spread.relay(1)
    forwards = []
    for far, close, there, out in levels:
        far.arrive()
        forwards.append((post.send(there, there, at.z1, out.at[:, at.c3]), close))
    deals = [Deal(post, at, shards, j, levels_out[3 * j : 3 * j + 3]) for j in range(2)]
    spread.corner()
    for last, close in forwards:
        last.arrive()
        close.arrive()
    spread.finish()
    smaller.arrive()
    for deal in deals:
        deal.finish()
    swap.finish()


def rope(values, cos_full, sin_full):
    return values * cos_full + pltpu.roll(values, HALF, 1) * sin_full


def rope_back(values, cos_full, sin_full):
    return values * cos_full - pltpu.roll(values, HALF, 1) * sin_full


def rope_full(marks, m, inverse):
    angle = marks.T[:, 2 + m : 3 + m] * inverse
    low = lax.broadcasted_iota(jnp.int32, angle.shape, 1) < HALF
    turns = jnp.floor(angle * (2.0 / math.pi) + 0.5)
    rest = ((angle - turns * 1.5703125) - turns * 4.837512969970703125e-4) - turns * 7.54978995489188e-8
    square = rest * rest
    sine = rest + rest * square * (
        -1.6666654611e-1 + square * (8.3321608736e-3 - square * 1.9515295891e-4)
    )
    cosine = 1.0 - 0.5 * square + square * square * (
        4.166664568298827e-2 + square * (-1.388731625493765e-3 + square * 2.443315711809948e-5)
    )
    quadrant = turns + jnp.where(low, 1.0, 0.0)
    half = jnp.floor(quadrant * 0.5)
    odd = quadrant - 2.0 * half > 0.5
    negative = half - 2.0 * jnp.floor(half * 0.5) > 0.5
    table = jnp.where(odd, cosine, sine)
    table = jnp.where(negative, -table, table)
    turned_table = pltpu.roll(table, HALF, 1)
    return jnp.where(low, table, turned_table), jnp.where(low, -turned_table, table)


def quarter(at, i):
    return (i + at.c) % 2 * 2 + i // 2


def mm(left, right, dims=((1,), (0,))):
    return lax.dot_general(left, right, (dims, ((), ())), preferred_element_type=WIDE)


TILE = 256

def softmax_tile(query, key, id_col, id_row):
    raw = mm(query, key, ((1,), (1,))) * SCALE
    raw = jnp.where(id_row <= id_col, raw, MASKED)
    top = jnp.max(raw, axis=-1, keepdims=True)
    exponent = jnp.exp(raw - top)
    return exponent * (1.0 / jnp.sum(exponent, axis=-1, keepdims=True))


def id_rows(at, marks, m, tiles):
    return jnp.concatenate([marks[quarter(at, i), m : m + 1, :] for i in range(tiles)], axis=1)


def attend_kernel(post, at, ins, outs, scratch):
    attn_in, qkv_all, inverse_in, marks_in, cot, *shards = ins[:8]
    levels = ins[8:]
    queries, keys, values, mixed, dy, cot_own, *more = outs
    climbed, dealt = more[: len(levels)], more[len(levels) :]
    rows, weight, inverse, marks, q_buf, k_buf, v_buf, mix_buf = scratch
    meet_swap(at)
    swap = Swap(post, at)
    cot_moved = [swap(cot.at[half], cot_own.at[half], cot_own.at[half]) for half in HALVES]
    local = [
        post.keep(inverse_in, inverse),
        post.keep(marks_in, marks),
        post.keep(qkv_all, weight),
        post.keep(attn_in.at[:, pl.ds(0, ROWS)], rows.at[0]),
        post.keep(attn_in.at[:, pl.ds(ROWS, ROWS)], rows.at[1]),
    ]
    spread = Spread(post, at, dy)
    deal = Deal(post, at, shards, 2, dealt)
    post.settle(local)
    width = rows.shape[-1]
    columns = weight.shape[-1]
    for m in range(2):
        for i in range(4):
            q = quarter(at, i)
            here = rows[m, pl.ds(2 * q, 2)].reshape(TILE, width)
            projected = mm(here, weight[...].reshape(width, columns))
            cos_full, sin_full = rope_full(marks[q], m, inverse[0:1])
            place = pl.ds(i * TILE, TILE)
            for g in range(2):
                lane = slice(g * HEAD_DIM, (g + 1) * HEAD_DIM)
                q_buf[m, place, lane] = rope(projected[:, lane], cos_full, sin_full).astype(NARROW)
            k_buf[m, place] = rope(projected[:, 256:384], cos_full, sin_full).astype(NARROW)
            v_buf[m, place] = projected[:, 384:512].astype(NARROW)
    for m in range(2):
        for i in range(4):
            n = min(i + 2, 4) * TILE
            q = quarter(at, i)
            id_col = marks[q].T[:, m : m + 1]
            id_row = id_rows(at, marks, m, n // TILE)
            for g in range(2):
                lane = slice(g * HEAD_DIM, (g + 1) * HEAD_DIM)
                prob = softmax_tile(
                    q_buf[m, i * TILE : (i + 1) * TILE, lane], k_buf[m, :n], id_col, id_row
                )
                value = mm(prob.astype(NARROW), v_buf[m, :n]).astype(NARROW)
                for h in range(2):
                    mix_buf[2 * q + h, m * ROWS : (m + 1) * ROWS, lane] = value[
                        h * ROWS : (h + 1) * ROWS
                    ]
        if m == 0:
            climbs = [Climb(post, at, level, out) for level, out in zip(levels, climbed)]
    for source, target in ((q_buf, queries), (k_buf, keys), (v_buf, values), (mix_buf, mixed)):
        post.keep(source, target)
    for half in range(2):
        cot_moved[half]()
        spread.own(half, cot_own.at[HALVES[half]])
    spread.relay(0)
    spread.relay(1)
    for climb in climbs:
        climb.forward()
    spread.corner()
    spread.finish()
    for climb in climbs:
        climb.finish()
    deal.finish()
    swap.finish()


def middle_kernel(post, at, ins, outs, scratch):
    mixed, out_all, x_own, gains_in, *shards = ins[:7]
    levels = ins[7:]
    mid_own, ffn_in, *more = outs
    climbed, dealt = more[: len(levels)], more[len(levels) :]
    mix_buf, weight, x_buf, gains, rows_out, *fold_scratch = scratch
    meet((at.side, at.core, at.row, at.cross, at.z1, at.z2))
    local = [
        post.keep(out_all.at[i // 4, i % 4], weight.at[:, pl.ds(i * LANES, LANES)])
        for i in range(16)
    ]
    local += [post.keep(mixed, mix_buf), post.keep(x_own, x_buf), post.keep(gains_in, gains)]
    post.settle(local)
    climbs = [Climb(post, at, level, out) for level, out in zip(levels, climbed)]

    def part(*blocks):
        return mm(jnp.concatenate([mix_buf[block] for block in blocks]), weight[...])

    fold = Fold(post, at, part, fold_scratch)
    fold.first()
    fold.second()
    deal = Deal(post, at, shards, 3, dealt)
    fold.third()
    gain = jnp.concatenate([gains[i // 4, i % 4, 1:2, :] for i in range(16)], axis=1)
    spread = Spread(post, at, ffn_in)
    for half in range(2):
        rows = pl.ds(half * ROWS, ROWS)
        value = fold.held[half] + x_buf[rows].astype(WIDE)
        fold.held[half] = value
        normed, _ = normed_rows(value)
        rows_out[half] = (normed * gain).astype(NARROW)
        spread.own(half, rows_out.at[half])
        post.keep(fold.held.at[half], mid_own.at[rows])
    spread.relay(0)
    for climb in climbs:
        climb.forward()
    spread.relay(1)
    spread.corner()
    spread.finish()
    for climb in climbs:
        climb.finish()
    deal.finish()


def small_arrays(block_ids, positions, attn_gain, ffn_gain):
    micro, _, span = positions.shape
    ids = lax.dynamic_slice_in_dim(block_ids[:, 0], lax.axis_index("ctx") * span, span, 1)
    rows = jnp.concatenate([ids, positions[:, 0]]).astype(WIDE)
    marks = jnp.pad(rows, ((0, 8 - 2 * micro), (0, 0)))
    gains = jnp.pad(jnp.stack([attn_gain, ffn_gain]).astype(WIDE), ((0, 6), (0, 0)))
    return marks, gains


def ffn_kernel(post, at, ins, outs, scratch):
    ffn_in, dy = ins[:2]
    ready = ins[2:10]
    levels = ins[10:]
    hidden, grads_pre, parts, ends_a, *climbed = outs
    x_buf, dy_buf, gate_buf, up_buf, down_buf, act, act_t, staged = scratch
    meet((at.z1, at.z3))
    climbs = [LineClimb(post, at, level, out) for level, out in zip(levels, climbed)]
    local = [post.keep(ffn_in, x_buf), post.keep(dy, dy_buf)]
    weights = list(ready) + list(climbed)

    def load(j):
        slot = j % 2
        gate, up, down = weights[3 * j : 3 * j + 3]
        copies = [post.keep(gate, gate_buf.at[slot]), post.keep(up, up_buf.at[slot])]
        for i in range(16):
            copies.append(
                post.keep(down.at[i // 4, i % 4], down_buf.at[slot, :, pl.ds(i * LANES, LANES)])
            )
        return copies

    loading = load(0)
    post.settle(local)
    width = x_buf.shape[-1]
    saved, sums_0 = [], []
    for j in range(4):
        slot = j % 2
        if loading is None:
            for climb in climbs[:1] if j == 2 else climbs[1:]:
                climb.finish()
            loading = load(j)
        post.settle(loading)
        loading = load(1) if j == 0 else None
        post.settle(saved)

        def rows(i, carry):
            blocks = pl.ds(i * 2, 2)
            x, grad = (buf[blocks].reshape(2 * TILE, width) for buf in (x_buf, dy_buf))
            gate = mm(x, gate_buf[slot].reshape(width, -1))
            up = mm(x, up_buf[slot].reshape(width, -1))
            grad_hidden = mm(grad, down_buf[slot], ((1,), (1,)))
            sig = jax.nn.sigmoid(gate)
            silu = gate * sig
            values = (
                grad_hidden * up * sig * (1.0 + gate * (1.0 - sig)),
                grad_hidden * silu,
                silu * up,
            )
            place = pl.ds(pl.multiple_of(i * 2 * TILE, 2 * TILE), 2 * TILE)
            for k in range(3):
                act[k, blocks] = values[k].astype(NARROW).reshape(2, TILE, -1)
                act_t[k, :, place] = values[k].T.astype(NARROW)
            return carry

        lax.fori_loop(0, 4, rows, 0)
        chunk = act.shape[-1]
        lane = pl.ds(j * chunk, chunk)
        saved = [
            post.keep(act.at[0], grads_pre.at[:, :, lane]),
            post.keep(act.at[1], grads_pre.at[:, :, pl.ds((4 + j) * chunk, chunk)]),
            post.keep(act.at[2], hidden.at[:, :, lane]),
        ]
        for climb in climbs[:1] if j == 1 else climbs[1:] if j == 2 else ():
            climb.last()
        for climb in climbs[:1] if j == 0 else climbs[1:] if j == 1 else ():
            climb.forward()

        def sums(n, carry):
            place = pl.ds(pl.multiple_of(n * TILE, TILE), TILE)
            x = x_buf[:, :, place].reshape(8 * TILE, TILE)
            grad = dy_buf[:, :, place].reshape(8 * TILE, TILE)
            both = mm(act_t[0:2].reshape(2 * chunk, -1), x).astype(NARROW)
            for k, value in enumerate((both[:chunk], both[chunk:], mm(act_t[2], grad).astype(NARROW))):
                staged[k, 2 * n] = value[:, :LANES]
                staged[k, 2 * n + 1] = value[:, LANES:]
            return carry

        lax.fori_loop(0, 8, sums, 0)
        stored = [
            post.keep(staged.at[k, pl.ds(4 * fl, 4)], parts.at[3 * j + k, fl])
            for k in range(3)
            for fl in range(4)
        ]
        if j < 2:
            post.settle(stored)
            sums_0.append(Ends(post, at, parts, 0, ends_a, 3 * j, (3, 1)[j]))
        else:
            saved += stored
    for step in sums_0:
        step.finish()


class Descend:
    def __init__(self, post, at, pieces, got):
        self.near = post.send(pieces.at[:, at.c1], got.at[0], at.z1, got.at[0])
        self.next = post.send(pieces.at[:, at.c3], got.at[1], at.z1, got.at[1])

    def finish(self):
        self.near.arrive()
        self.next.arrive()


def norm_back_rows(grad, values, gain):
    normed, factor = normed_rows(values)
    scaled = grad * gain
    inner_mean = jnp.mean(scaled * normed, axis=-1, keepdims=True)
    return factor * (scaled - normed * inner_mean), jnp.sum(grad * normed, axis=0, keepdims=True)


def back_kernel(post, at, ins, outs, scratch):
    grads_pre, mid_own, cot_own, gains_in, parts, ends_a, *weights = ins
    grad_mid_own, grad_mid, gain_part, ends_c, mates_b = outs
    pre_buf, weight, mid_buf, cot_buf, gains, rows_out, gain_out = scratch[:7]
    bufs_1, fold_scratch = scratch[7:9], scratch[9:]
    meet((at.side, at.core, at.row, at.z1, at.z3))
    downs = [
        Middle(post, at, 1, parts, 0, ends_a, mates_b, *bufs_1),
        Ends(post, at, parts, 4, ends_c),
    ]
    chunk = pre_buf.shape[-1] // 8
    local = [post.keep(grads_pre, pre_buf)]
    for a in range(2):
        for j in range(4):
            place = pl.ds((4 * a + j) * chunk, chunk)
            local.append(post.keep(weights[4 * a + j], weight.at[:, :, :, place]))
    local += [post.keep(mid_own, mid_buf), post.keep(cot_own, cot_buf), post.keep(gains_in, gains)]
    post.settle(local)
    width = mid_buf.shape[-1]

    def part(*blocks):
        rows = jnp.concatenate([pre_buf[block] for block in blocks])
        return mm(rows, weight[...].reshape(width, -1), ((1,), (1,)))

    downs[0].send()
    fold = Fold(post, at, part, fold_scratch)
    fold.first()
    fold.second()
    fold.third()
    gain = jnp.concatenate([gains[i // 4, i % 4, 1:2, :] for i in range(16)], axis=1)
    spread = Spread(post, at, grad_mid)
    total = jnp.zeros((1, width), WIDE)
    for half in range(2):
        rows = HALVES[half]
        back, piece = norm_back_rows(fold.held[half], mid_buf[rows], gain)
        total = total + piece
        value = cot_buf[rows].astype(WIDE) + back
        fold.held[half] = value
        rows_out[half] = value.astype(NARROW)
        spread.own(half, rows_out.at[half])
        post.keep(fold.held.at[half], grad_mid_own.at[rows])
    gain_out[...] = jnp.broadcast_to(total, gain_out.shape)
    post.keep(gain_out, gain_part)
    spread.relay(0)
    spread.relay(1)
    spread.corner()
    spread.finish()
    for down in downs:
        down.finish()


def attend_back_kernel(post, at, ins, outs, scratch):
    (
        grad_mid, queries, keys, values, marks_in, inverse_in, out_all, mixed, attn_in, hidden, mid_own, parts,
        ends_c, mates_b, *downs_in
    ) = ins
    grad_proj, parts_q, parts_o, got_o, out_home, ends_d, mates_c, outer_b = outs
    (
        gm_buf, q_buf, k_buf, v_buf, marks, inverse, weight, mix_buf, hid_buf, down_buf, gp_buf, gk_buf, gv_buf,
        staged, staged_o, mid_buf, out_buf
    ) = scratch[:17]
    bufs_1, bufs_2, fold_scratch = scratch[17:19], scratch[19:21], scratch[21:]
    meet_swap(at)
    swap = Swap(post, at, home=True)
    steps = [
        Middle(post, at, 1, parts, 4, ends_c, mates_c, *bufs_1),
        Middle(post, at, 2, parts, 0, mates_b, outer_b, *bufs_2),
        Ends(post, at, parts, 9, ends_d),
    ]

    chunk = hid_buf.shape[-1] // 4
    early = [post.keep(hidden, hid_buf)]
    for j in range(4):
        for i in range(16):
            target = down_buf.at[pl.ds(j * chunk, chunk), pl.ds(i * LANES, LANES)]
            early.append(post.keep(downs_in[j].at[i // 4, i % 4], target))
    late = [
        post.keep(source, target)
        for source, target in (
            (grad_mid, gm_buf), (queries, q_buf), (keys, k_buf), (values, v_buf), (marks_in, marks),
            (inverse_in, inverse), (mixed, mix_buf), (mid_own, mid_buf),
        )
    ]
    late += [
        post.keep(out_all.at[i // 4, i % 4], weight.at[:, pl.ds(i * LANES, LANES)])
        for i in range(16)
    ]
    post.settle(early)
    for step in steps[:2]:
        step.send()

    def part(*blocks):
        return mm(jnp.concatenate([hid_buf[block] for block in blocks]), down_buf[...])

    fold = Fold(post, at, part, fold_scratch)
    fold.first()
    post.settle(late)

    def fetch(n):
        place = pl.ds(n * TILE, TILE)
        return post.keep(attn_in.at[:, :, place], column(n))

    def column(n):
        return hid_buf.at[:, :, pl.ds(n % 2 * TILE, TILE)]

    mix_t, gp_t = down_buf.at[pl.ds(512, 256)], down_buf.at[pl.ds(0, 512)]
    fetched = fetch(0)
    width = gm_buf.shape[-1]
    for i in range(8):
        mix_t[:, i * TILE : (i + 1) * TILE] = mix_buf[i].astype(WIDE).T.astype(NARROW)
    for n in range(8):
        place = slice(n * TILE, (n + 1) * TILE)
        value = mm(mix_t[...], gm_buf[:, :, place].reshape(8 * TILE, TILE)).astype(NARROW)
        for h in range(2):
            block = 2 * n + h
            staged_o[block // 4, block % 4] = value[:, h * LANES : (h + 1) * LANES]
    post.settle([post.keep(staged_o, parts_o)])
    step_o = Descend(post, at, parts_o, got_o)
    for m in range(2):
        for i in range(4):
            q = quarter(at, i)
            n = min(i + 2, 4) * TILE
            place = slice(i * TILE, (i + 1) * TILE)
            id_col = marks[q].T[:, m : m + 1]
            id_row = id_rows(at, marks, m, n // TILE)
            cos_full, sin_full = rope_full(marks[q], m, inverse[0:1])
            rows = gm_buf[pl.ds(2 * q, 2), m * ROWS : (m + 1) * ROWS].reshape(TILE, width)
            grad_mixed = mm(rows, weight[...], ((1,), (1,))).astype(NARROW)
            for g in range(2):
                lane = slice(g * HEAD_DIM, (g + 1) * HEAD_DIM)
                query = q_buf[m, place, lane]
                prob = softmax_tile(query, k_buf[m, :n], id_col, id_row)
                grad = grad_mixed[:, lane]
                grad_prob = mm(grad, v_buf[m, :n], ((1,), (1,)))
                inner = jnp.sum(grad_prob * prob, axis=-1, keepdims=True)
                grad_scores = (SCALE * prob * (grad_prob - inner)).astype(NARROW)
                grad_query = mm(grad_scores, k_buf[m, :n])
                grad_key = mm(grad_scores, query, ((0,), (0,)))
                grad_value = mm(prob.astype(NARROW), grad, ((0,), (0,)))
                if i == 0 and g == 0:
                    gk_buf[:n], gv_buf[:n] = grad_key, grad_value
                    gk_buf[n:], gv_buf[n:] = (jnp.zeros_like(gk_buf[n:]),) * 2
                else:
                    gk_buf[:n] = gk_buf[:n] + grad_key
                    gv_buf[:n] = gv_buf[:n] + grad_value
                done = rope_back(grad_query, cos_full, sin_full).astype(NARROW)
                for h in range(2):
                    gp_buf[2 * q + h, m * ROWS : (m + 1) * ROWS, lane] = done[h * ROWS : (h + 1) * ROWS]
            if m == 1 and i == 1:
                fold.third()
                for half in HALVES:
                    k = half.start // ROWS
                    out_buf[half] = (fold.held[k] + mid_buf[half]).astype(NARROW)
                moved = [swap(out_buf.at[half], out_home.at[half], out_home.at[half]) for half in HALVES]
        for i in range(4):
            q = quarter(at, i)
            place = slice(i * TILE, (i + 1) * TILE)
            cos_full, sin_full = rope_full(marks[q], m, inverse[0:1])
            done = (
                rope_back(gk_buf[place], cos_full, sin_full).astype(NARROW),
                gv_buf[place].astype(NARROW),
            )
            for k in range(2):
                lane = slice((2 + k) * HEAD_DIM, (3 + k) * HEAD_DIM)
                for h in range(2):
                    gp_buf[2 * q + h, m * ROWS : (m + 1) * ROWS, lane] = done[k][h * ROWS : (h + 1) * ROWS]
        if m == 0:
            fold.second()
    post.keep(gp_buf, grad_proj)
    for i in range(8):
        place = slice(i * TILE, (i + 1) * TILE)
        gp_t[:, place] = gp_buf[i].astype(WIDE).T.astype(NARROW)
    for n in range(8):
        post.settle([fetched])
        if n < 7:
            fetched = fetch(n + 1)
        other = mm(gp_t[...], column(n)[...].reshape(8 * TILE, TILE)).astype(NARROW)
        for h in range(2):
            block = 2 * n + h
            staged[block // 4, block % 4] = other[:, h * LANES : (h + 1) * LANES]
    post.keep(staged, parts_q)
    step_o.finish()
    for arrive in moved:
        arrive()
    swap.finish()
    for step in steps:
        step.finish()


class Own:
    def __init__(self, post, at, parts, first, n, pieces, own, one, two):
        self.post, self.at, self.first, self.n = post, at, first, n
        self.own, self.one, self.two = own, one, two
        self.pieces = pieces
        count = 1 + max(len(pieces[0]) + len(pieces[1]), len(pieces[2]))
        self.sems = [post.local_sems.at[post.n_local + k] for k in range(count)]
        post.n_local += count
        self.parts = parts

        @pl.when(at.is_mid)
        def _():
            for copy in self.mid_copies():
                copy.start()

        @pl.when(at.is_end)
        def _():
            for copy in self.end_copies():
                copy.start()

    def laid(self, arrays, index, target):
        place, pairs = self.first, []
        for array in arrays:
            n = array.shape[0]
            source = array if index is None else array.at[:, :, index]
            pairs.append((source, target.at[pl.ds(place, n)]))
            place += n
        return pairs

    def copies(self, pairs):
        rows = pl.ds(self.first, self.n)
        pairs = [(self.parts.at[rows, :, self.at.c], self.own.at[rows])] + pairs
        return [pltpu.make_async_copy(*pair, sem) for pair, sem in zip(pairs, self.sems)]

    def mid_copies(self):
        c = self.at.c
        ends, mates, _ = self.pieces
        return self.copies(self.laid(ends, 2 * (c - 1), self.one) + self.laid(mates, 2 - c, self.two))

    def end_copies(self):
        return self.copies(self.laid(self.pieces[2], None, self.two))

    def add(self):
        def both(p, carry):
            value = self.own[p].astype(WIDE) + self.one[p].astype(WIDE) + self.two[p].astype(WIDE)
            self.own[p] = value.astype(NARROW)
            return carry

        def single(p, carry):
            self.own[p] = (self.own[p].astype(WIDE) + self.two[p].astype(WIDE)).astype(NARROW)
            return carry

        @pl.when(self.at.is_mid)
        def _():
            for copy in self.mid_copies():
                copy.wait()
            lax.fori_loop(self.first, self.first + self.n, both, 0)

        @pl.when(self.at.is_end)
        def _():
            for copy in self.end_copies():
                copy.wait()
            lax.fori_loop(self.first, self.first + self.n, single, 0)


def end_kernel(post, at, ins, outs, scratch):
    (
        grad_proj, qkv_all, x_own, gains_in, grad_mid_own, gain_ffn_part, parts, parts_q, parts_o, got_o,
        ends_a, ends_c, ends_d, mates_b, mates_c, outer_b
    ) = ins
    grad_home, gain_sums, mates_d, outer_c, outer_d, *home_sums = outs
    (
        gp_buf, weight, x_buf, gains, mid_buf, rows_out, gain_buf, gain_got, own_ffn, one_ffn, two_ffn,
        own_q, far_q, got_q, end_q, own_o, far_o, one_o, two_o, end_o
    ) = scratch[:20]
    bufs_1, bufs_2, bufs_3, fold_scratch = scratch[20:22], scratch[22:24], scratch[24:26], scratch[26:]
    f, c = at.f, at.c
    meet_swap(at)
    step_q = Descend(post, at, parts_q, got_q)
    steps = [
        Middle(post, at, 1, parts, 9, ends_d, mates_d, *bufs_1),
        Middle(post, at, 2, parts, 4, mates_c, outer_c, *bufs_2),
    ]
    swap = Swap(post, at, home=True)
    for_o = [post.keep(parts_o.at[:, at.c2], far_o), post.keep(got_o.at[1], two_o)]
    early = Own(
        post, at, parts, 0, 4, ((ends_a,), (mates_b,), (outer_b,)),
        own_ffn, one_ffn, two_ffn,
    )
    fold_in = [
        post.keep(grad_proj, gp_buf), post.keep(qkv_all, weight), post.keep(x_own, x_buf),
        post.keep(gains_in, gains), post.keep(grad_mid_own, mid_buf),
        post.keep(gain_ffn_part, gain_buf),
    ]
    later = [
        post.keep(parts_q.at[:, c], own_q), post.keep(parts_q.at[:, at.c2], far_q),
        post.keep(parts_o.at[:, c], own_o), post.keep(got_o.at[0], one_o),
    ]
    for step in steps:
        step.send()
    post.settle(for_o)

    def add_far(far, came):
        for k in range(4):
            far[k] = (far[k].astype(WIDE) + came[k].astype(WIDE)).astype(NARROW)

    def add_own(own, one, end):
        for k in range(4):
            own[k] = (own[k].astype(WIDE) + one[k].astype(WIDE) + end[k].astype(WIDE)).astype(NARROW)

    add_far(far_o, two_o)
    sent_o = post.send(far_o, end_o, at.z2, end_o)
    trades = []
    places = ((at.row, at.fy), (at.cross, at.fd), (at.core, at.fs))

    def trade(mine, out, *place):
        post.keep(mine(f), out.at[(f, *place)])
        for device, k in places:
            trades.append(
                post.send(mine(k), out.at[(f, *place)], device, out.at[(k, *place)])
            )

    def trade_ffn(p):
        trade(lambda k: own_ffn.at[p, k], home_sums[p % 3], p // 3)

    post.settle(fold_in)
    width = x_buf.shape[-1]

    def part(*blocks):
        rows = jnp.concatenate([gp_buf[block] for block in blocks])
        return mm(rows, weight[...].reshape(width, -1), ((1,), (1,)))

    fold = Fold(post, at, part, fold_scratch)
    fold.first()
    early.add()
    fold.second()
    fold.third()
    gain = jnp.concatenate([gains[i // 4, i % 4, 0:1, :] for i in range(16)], axis=1)
    total = jnp.zeros((1, width), WIDE)
    moved = []
    for half in range(2):
        rows = HALVES[half]
        back, piece = norm_back_rows(fold.held[half], x_buf[rows].astype(WIDE), gain)
        total = total + piece
        rows_out[rows] = (mid_buf[rows] + back).astype(NARROW)
        moved.append(swap(rows_out.at[rows], grad_home.at[rows], grad_home.at[rows]))
    gain_buf[0:1] = total
    gain_sent = [
        post.send(gain_buf, gain_got.at[k], device, gain_got.at[k])
        for k, device in enumerate(at.level)
    ]
    for p in range(4):
        trade_ffn(p)
    post.settle(later)
    step_q.finish()
    add_far(far_q, got_q.at[1])
    sent_q = post.send(far_q, end_q, at.z2, end_q)
    steps[0].finish()
    steps.append(Middle(post, at, 2, parts, 9, mates_d, outer_d, *bufs_3))
    steps[2].send()
    steps[1].finish()
    late = Own(
        post, at, parts, 4, 5, ((ends_c,), (mates_c,), (outer_c,)), own_ffn, one_ffn, two_ffn
    )
    sent_o.arrive()
    add_own(own_o, one_o, end_o)
    trade(lambda k: own_o.at[k], home_sums[3])
    late.add()
    for p in range(4, 9):
        trade_ffn(p)
    for sent in gain_sent:
        sent.arrive()
        sent.leave()
    post.out = [sent for sent in post.out if not any(sent is gone for gone in gain_sent)]
    gain_buf[...] = gain_buf[...] + sum(gain_got[k] for k in range(7))
    gain_sent = [
        post.send(gain_buf, gain_got.at[7 + k], device, gain_got.at[7 + k])
        for k, device in enumerate((at.z1, at.z2, at.z3))
    ]
    steps[2].finish()
    last = Own(
        post, at, parts, 9, 3, ((ends_d,), (mates_d,), (outer_d,)), own_ffn, one_ffn, two_ffn
    )
    last.add()
    for p in range(9, 12):
        trade_ffn(p)
    sent_q.arrive()
    add_own(own_q, got_q.at[0], end_q)
    trade(lambda k: own_q.at[k], home_sums[4])
    for sent in gain_sent:
        sent.arrive()
        sent.leave()
    post.out = [sent for sent in post.out if not any(sent is gone for gone in gain_sent)]
    gain_buf[...] = gain_buf[...] + sum(gain_got[7 + k] for k in range(3))
    place = pl.ds(pl.multiple_of((f * 4 + c) * LANES, LANES), LANES)
    post.keep(gain_buf.at[:, place], gain_sums)
    for sent in trades:
        sent.arrive()
    for arrive in moved:
        arrive()
    swap.finish()


def home_kernel(gate, up, down, qkv, out, gate_out, up_out, down_out, qkv_out, out_out):
    for source, target in ((gate, gate_out), (up, up_out), (qkv, qkv_out)):
        for n in range(source.shape[0] // 512):
            place = pl.ds(n * 512, 512)
            target[:, place] = source[place, :].astype(WIDE).T
    down_out[...] = down[...].astype(WIDE)
    out_out[...] = out[...].astype(WIDE)


def near_body(
    hidden_in, cotangent, block_ids, positions, attn_gain, wqkv, wo, ffn_gain, w_gate, w_up, w_down
):
    micro, _, rows, width = hidden_in.shape
    own = micro * rows
    ff = w_gate.shape[1]
    chunk = ff // 16
    shards = (w_gate, w_up, w_down)
    marks, gains = small_arrays(block_ids, positions, attn_gain, ffn_gain)
    inverse = THETA ** (-(jnp.arange(HALF, dtype=WIDE) * 2.0 / HEAD_DIM))
    inverse = jnp.broadcast_to(jnp.concatenate([inverse, inverse]), (8, HEAD_DIM))
    level_shapes = [shape(4, LANES, chunk), shape(4, LANES, chunk), shape(4, chunk, LANES)]
    whole_shapes = [shape(4, 4, LANES, chunk), shape(4, 4, LANES, chunk), shape(4, 4, chunk, LANES)]
    gains_shape = (4, 4, *gains.shape)
    x_own, attn_in, all_marks, all_gains, qkv_all, out_all, *level = call(
        start_kernel,
        "start",
        [
            shape(own, width), shape(8, own, width),
            shape(4, *marks.shape, dtype=WIDE), shape(*gains_shape, dtype=WIDE),
            shape(4, 4, LANES, wqkv.shape[1] // 4), shape(4, 4, wo.shape[0] // 4, LANES),
            *level_shapes, *level_shapes,
        ],
        (hidden_in.reshape(own, width), marks, gains, wqkv, wo, *shards),
        [pltpu.VMEM((own, width), NARROW), pltpu.VMEM((own, width), NARROW), pltpu.VMEM(gains_shape, WIDE)],
        72, 24, 1,
    )
    queries, keys, values, mixed, dy, cot_own, *more = call(
        attend_kernel,
        "attend",
        [
            shape(2, 1024, 256), shape(2, 1024, 128), shape(2, 1024, 128), shape(8, own, 256),
            shape(8, own, width), shape(own, width), *whole_shapes, *level_shapes,
        ],
        (attn_in, qkv_all, inverse, all_marks, cotangent.reshape(own, width), *shards, *level[:3]),
        [
            pltpu.VMEM((2, 8, ROWS, width), NARROW), pltpu.VMEM(qkv_all.shape, NARROW),
            pltpu.VMEM(inverse.shape, WIDE), pltpu.VMEM(all_marks.shape, WIDE),
            pltpu.VMEM((2, 1024, 256), NARROW), pltpu.VMEM((2, 1024, 128), NARROW),
            pltpu.VMEM((2, 1024, 128), NARROW), pltpu.VMEM((8, own, 256), NARROW),
        ],
        40, 24, 2,
    )
    whole, level = more[:3], level + more[3:]
    mid_own, ffn_in, *more = call(
        middle_kernel,
        "middle",
        [
            shape(own, width, dtype=WIDE), shape(8, own, width), *whole_shapes, *whole_shapes[:2],
            *level_shapes,
        ],
        (mixed, out_all, x_own, all_gains, *shards, *level[3:8]),
        [
            pltpu.VMEM((8, own, 256), NARROW), pltpu.VMEM((256, width), NARROW),
            pltpu.VMEM((own, width), NARROW), pltpu.VMEM(gains_shape, WIDE),
            pltpu.VMEM((2, ROWS, width), NARROW), *Fold.scratch(width),
        ],
        52, 32, 3,
    )
    whole, level = whole + more[:5], level + more[5:]
    hidden, grads_pre, parts, ends_a, *more = call(
        ffn_kernel,
        "ffn",
        [
            shape(8, own, ff // 4), shape(8, own, ff // 2), shape(12, 4, 4, chunk, LANES),
            shape(4, 4, 3, chunk, LANES),
            whole_shapes[2], *whole_shapes,
        ],
        (ffn_in, dy, *whole, *level[8:]),
        [
            pltpu.VMEM((8, own, width), NARROW), pltpu.VMEM((8, own, width), NARROW),
            pltpu.VMEM((2, 4, 4, LANES, chunk), NARROW), pltpu.VMEM((2, 4, 4, LANES, chunk), NARROW),
            pltpu.VMEM((2, chunk, width), NARROW), pltpu.VMEM((3, 8, own, chunk), NARROW),
            pltpu.VMEM((3, chunk, 8 * own), NARROW), pltpu.VMEM((3, 16, chunk, LANES), NARROW),
        ],
        48, 160, 4,
    )
    whole = whole + more
    fold_scratch = Fold.scratch(width)
    grad_mid_own, grad_mid, gain_ffn_part, ends_c, mates_b = call(
        back_kernel,
        "back",
        [
            shape(own, width, dtype=WIDE), shape(8, own, width), shape(8, width, dtype=WIDE),
            shape(5, 4, 3, chunk, LANES), shape(4, 4, 2, chunk, LANES),
        ],
        (grads_pre, mid_own, cot_own, all_gains, parts, ends_a, *whole[0::3], *whole[1::3]),
        [
            pltpu.VMEM((8, own, ff // 2), NARROW), pltpu.VMEM((4, 4, LANES, ff // 2), NARROW),
            pltpu.VMEM((own, width), WIDE), pltpu.VMEM((own, width), NARROW),
            pltpu.VMEM(gains_shape, WIDE), pltpu.VMEM((2, ROWS, width), NARROW),
            pltpu.VMEM((8, width), WIDE), *middle_scratch(1, 4), *fold_scratch,
        ],
        48, 32, 5,
    )
    grad_proj, parts_q, parts_o, got_o, out_home, ends_d, mates_c, outer_b = call(
        attend_back_kernel,
        "attend_back",
        [
            shape(8, own, 512), shape(4, 4, 512, LANES), shape(4, 4, 256, LANES), shape(2, 4, 256, LANES),
            shape(own, width),
            shape(3, 4, 3, chunk, LANES), shape(5, 4, 2, chunk, LANES), shape(4, 4, chunk, LANES),
        ],
        (
            grad_mid, queries, keys, values, all_marks, inverse, out_all, mixed, attn_in, hidden, mid_own, parts,
            ends_c, mates_b, *whole[2::3],
        ),
        [
            pltpu.VMEM((8, own, width), NARROW), pltpu.VMEM((2, 1024, 256), NARROW),
            pltpu.VMEM((2, 1024, 128), NARROW), pltpu.VMEM((2, 1024, 128), NARROW),
            pltpu.VMEM(all_marks.shape, WIDE), pltpu.VMEM(inverse.shape, WIDE),
            pltpu.VMEM((256, width), NARROW), pltpu.VMEM((8, own, 256), NARROW),
            pltpu.VMEM((8, own, ff // 4), NARROW), pltpu.VMEM((ff // 4, width), NARROW),
            pltpu.VMEM((8, own, 512), NARROW), pltpu.VMEM((1024, 128), WIDE),
            pltpu.VMEM((1024, 128), WIDE),
            pltpu.VMEM((4, 4, 512, LANES), NARROW), pltpu.VMEM((4, 4, 256, LANES), NARROW),
            pltpu.VMEM((own, width), WIDE), pltpu.VMEM((own, width), NARROW), *middle_scratch(1, 5), *middle_scratch(2, 4), *fold_scratch,
        ],
        32, 128, 6,
    )
    grad_home, gain_sums, _, _, _, *sums = call(
        end_kernel,
        "end",
        [
            shape(own, width), shape(8, LANES, dtype=WIDE), shape(3, 4, 2, chunk, LANES),
            shape(5, 4, chunk, LANES), shape(3, 4, chunk, LANES),
            *[shape(4, 4, chunk, LANES)] * 3, shape(4, 256, LANES), shape(4, 512, LANES),
        ],
        (
            grad_proj, qkv_all, x_own, all_gains, grad_mid_own, gain_ffn_part, parts, parts_q, parts_o, got_o,
            ends_a, ends_c, ends_d, mates_b, mates_c, outer_b,
        ),
        [
            pltpu.VMEM((8, own, 512), NARROW), pltpu.VMEM(qkv_all.shape, NARROW),
            pltpu.VMEM((own, width), NARROW), pltpu.VMEM(gains_shape, WIDE),
            pltpu.VMEM((own, width), WIDE), pltpu.VMEM((own, width), NARROW),
            pltpu.VMEM((8, width), WIDE), pltpu.VMEM((10, 8, width), WIDE),
            *[pltpu.VMEM((12, 4, chunk, LANES), NARROW)] * 3,
            *[pltpu.VMEM((4, 512, LANES), NARROW)] * 2, pltpu.VMEM((2, 4, 512, LANES), NARROW),
            pltpu.VMEM((4, 512, LANES), NARROW), *[pltpu.VMEM((4, 256, LANES), NARROW)] * 5,
            *middle_scratch(1, 3), *middle_scratch(2, 5), *middle_scratch(2, 3), *fold_scratch,
        ],
        88, 72, 7,
    )
    gate, up, down, out, qkv = (array.reshape(-1, LANES) for array in sums)
    grad_gate, grad_up, grad_down, grad_qkv, grad_out = pl.pallas_call(
        home_kernel,
        out_shape=[
            jax.ShapeDtypeStruct(array.shape, WIDE) for array in (w_gate, w_up, w_down, wqkv, wo)
        ],
        compiler_params=pltpu.CompilerParams(vmem_limit_bytes=48 << 20),
        name="home",
    )(gate, up, down, qkv, out)
    return (
        out_home.reshape(hidden_in.shape),
        grad_home.reshape(hidden_in.shape),
        gain_sums[0],
        grad_qkv,
        grad_out,
        gain_sums[1],
        grad_gate,
        grad_up,
        grad_down,
    )


def body(*shards):
    inner = KV_HEADS // lax.axis_size("tp")
    near = (lax.axis_size("fsdp"), lax.axis_size("ctx"), lax.axis_size("tp"), inner)
    return (near_body if near == (4, 4, 2, 4) else general_body)(*shards)


def solution(mesh):
    return jax.shard_map(
        body,
        mesh=mesh,
        in_specs=(
            P(None, "fsdp", ("ctx", "tp"), None),
            P(None, "fsdp", ("ctx", "tp"), None),
            P(None, "fsdp", None),
            P(None, "fsdp", "ctx"),
            P(("fsdp", "ctx")),
            P(("fsdp", "ctx"), "tp"),
            P("tp", ("fsdp", "ctx")),
            P(("fsdp", "ctx")),
            P(("fsdp", "ctx"), "tp"),
            P(("fsdp", "ctx"), "tp"),
            P("tp", ("fsdp", "ctx")),
        ),
        out_specs=(
            P(None, "fsdp", ("ctx", "tp"), None),
            P(None, "fsdp", ("ctx", "tp"), None),
            P(("fsdp", "ctx")),
            P(("fsdp", "ctx"), "tp"),
            P("tp", ("fsdp", "ctx")),
            P(("fsdp", "ctx")),
            P(("fsdp", "ctx"), "tp"),
            P(("fsdp", "ctx"), "tp"),
            P("tp", ("fsdp", "ctx")),
        ),
        check_vma=False,
    )
```

```python
import functools
import math

import jax
import jax.numpy as jnp
from jax import lax
from jax.sharding import PartitionSpec as P
from jax.experimental import pallas as pl
from jax.experimental.pallas import tpu as pltpu

HEADS = 16
KV_HEADS = 8
HEAD_DIM = 128


EPS = 1e-05
THETA = 1000000.0
MASKED = -1e30


def rope_tables(position_ids):
    half_dim = HEAD_DIM // 2
    inverse = THETA ** (-(jnp.arange(half_dim, dtype=jnp.float32) * 2.0 / HEAD_DIM))
    angles = position_ids.astype(jnp.float32)[..., None] * inverse
    angles = jnp.concatenate([angles, angles], axis=-1)
    return (jnp.cos(angles), jnp.sin(angles))


def turned(values):
    half_dim = values.shape[-1] // 2
    return jnp.concatenate([-values[..., half_dim:], values[..., :half_dim]], axis=-1)


def turned_back(values):
    half_dim = values.shape[-1] // 2
    return jnp.concatenate([values[..., half_dim:], -values[..., :half_dim]], axis=-1)


def norm_rows(stream, gain_row):
    factor = lax.rsqrt(jnp.mean(stream * stream, axis=-1, keepdims=True) + EPS)
    normed = stream * factor
    return (normed, factor, (normed * gain_row).astype(jnp.bfloat16))


def groups_of(fsdp, inner):
    near = [[high * inner + low for low in range(inner)] for high in range(fsdp // inner)]
    far = [[high * inner + low for high in range(fsdp // inner)] for low in range(inner)]
    return near, far


def general_body(
    hidden_in, cotangent, block_ids, positions, attn_gain, wqkv, wo, ffn_gain, w_gate, w_up, w_down
):
    fsdp, ctx, tp = lax.axis_size("fsdp"), lax.axis_size("ctx"), lax.axis_size("tp")
    inner = KV_HEADS // tp
    outer = fsdp // inner
    near, far = groups_of(fsdp, inner)
    micro, _, rows, width = hidden_in.shape
    score_scale = HEAD_DIM ** (-0.5)
    f_at, c_at = lax.axis_index("fsdp"), lax.axis_index("ctx")
    swap = [
        ((high * inner + low) * ctx + c, (high * inner + c) * ctx + low)
        for high in range(outer)
        for low in range(inner)
        for c in range(ctx)
    ]

    def rehome(array):
        return lax.ppermute(array, ("fsdp", "ctx"), swap)

    def trade(pieces):
        return lax.all_to_all(pieces, "fsdp", 0, 0, axis_index_groups=near)

    def spread(block):
        both = lax.all_gather(block, "tp")
        return lax.all_gather(both, "fsdp", axis_index_groups=near)

    def fold(parts):
        half = lax.psum_scatter(
            parts.astype(jnp.bfloat16), "fsdp", scatter_dimension=0, axis_index_groups=near
        )
        return lax.psum_scatter(half, "tp", scatter_dimension=0).astype(jnp.float32)

    def gather_levels(pieces):
        up = lax.all_gather(pieces, "ctx")
        if outer == 1:
            return up[None]
        return lax.all_gather(up, "fsdp", axis_index_groups=far)

    def scatter_levels(pieces):
        if outer == 1:
            pieces = pieces[0]
        else:
            pieces = lax.psum_scatter(pieces, "fsdp", scatter_dimension=0, axis_index_groups=far)
        return lax.psum_scatter(pieces, "ctx", scatter_dimension=0)

    def fetch_columns(shard):
        block, cols = shard.shape
        pieces = trade(shard.reshape(block, inner, cols // inner).transpose(1, 0, 2))
        whole = gather_levels(pieces).transpose(0, 2, 1, 3, 4)
        return whole.reshape(-1, cols // inner)

    def fetch_rows(shard):
        length, block = shard.shape
        pieces = trade(shard.reshape(inner, length // inner, block))
        whole = gather_levels(pieces).transpose(3, 0, 2, 1, 4)
        return whole.reshape(length // inner, -1)

    def return_columns(grad):
        total, cols = grad.shape
        grad = grad.astype(jnp.bfloat16).reshape(outer, inner, ctx, -1, cols)
        mine = trade(scatter_levels(grad.transpose(0, 2, 1, 3, 4)))
        return mine.transpose(1, 0, 2).reshape(mine.shape[1], -1).astype(jnp.float32)

    def return_rows(grad):
        length, total = grad.shape
        grad = grad.astype(jnp.bfloat16).reshape(length, outer, inner, ctx, -1)
        mine = trade(scatter_levels(grad.transpose(1, 3, 2, 0, 4)))
        return mine.reshape(inner * length, -1).astype(jnp.float32)

    def dot(left, right, dims):
        return lax.dot_general(left, right, (dims, ((), ())), preferred_element_type=jnp.float32)

    gains = lax.all_gather(jnp.stack([attn_gain, ffn_gain]), ("fsdp", "ctx"))
    gain_attn = gains[:, 0].reshape(-1).astype(jnp.float32)
    gain_ffn = gains[:, 1].reshape(-1).astype(jnp.float32)
    span = positions.shape[2]
    ids_here = lax.dynamic_slice_in_dim(block_ids[:, 0], c_at * span, span, 1)
    marks = lax.all_gather(jnp.stack([positions[:, 0], ids_here]), ("fsdp", "ctx"))
    my_seq = f_at // inner * inner + c_at
    marks = lax.dynamic_slice_in_dim(marks, my_seq * ctx, ctx, 0)
    marks = marks.transpose(1, 2, 0, 3).reshape(2, micro, ctx * span)
    pos, ids = marks[0], marks[1]

    weight_qkv = fetch_columns(wqkv)
    weight_out = fetch_rows(wo)
    weight_gate = fetch_columns(w_gate)
    weight_up = fetch_columns(w_up)
    weight_down = fetch_rows(w_down)

    stream = rehome(hidden_in).reshape(micro * rows, width).astype(jnp.float32)
    grad_out_low = rehome(cotangent).reshape(micro * rows, width)
    grad_out = grad_out_low.astype(jnp.float32)

    def to_heads(flat):
        split = flat.reshape(inner * tp, micro, rows, -1, HEAD_DIM).transpose(1, 0, 2, 3, 4)
        return split.reshape(micro, inner * tp * rows, -1, HEAD_DIM)

    def from_heads(heads):
        split = heads.reshape(micro, inner * tp, rows, -1).transpose(1, 0, 2, 3)
        return split.reshape(inner * tp * micro * rows, -1)

    normed_one, factor_one, attn_rows = norm_rows(stream, gain_attn)
    attn_in = spread(attn_rows).reshape(-1, width)
    projected = to_heads(dot(attn_in, weight_qkv, ((1,), (0,))))
    group = HEADS // KV_HEADS
    cos_table, sin_table = rope_tables(pos)
    cos_heads, sin_heads = cos_table[:, :, None], sin_table[:, :, None]
    turning = projected[:, :, : group + 1]
    turning = (turning * cos_heads + turned(turning) * sin_heads).astype(jnp.bfloat16)
    queries, keys = turning[:, :, :group], turning[:, :, group]
    values = projected[:, :, group + 1].astype(jnp.bfloat16)
    allowed = (ids[:, None, :] <= ids[:, :, None])[:, None]
    raw = jnp.einsum("blge,bme->bglm", queries, keys, preferred_element_type=jnp.float32)
    scores = jnp.where(allowed, raw * score_scale, MASKED)
    row_max = jnp.max(scores, axis=-1, keepdims=True)
    exponent = jnp.exp(scores - row_max)
    prob = exponent / jnp.sum(exponent, axis=-1, keepdims=True)
    prob_low = prob.astype(jnp.bfloat16)
    mixed = jnp.einsum("bglm,bme->blge", prob_low, values, preferred_element_type=jnp.float32)
    mixed = from_heads(mixed.astype(jnp.bfloat16))
    out_part = dot(mixed, weight_out, ((1,), (0,)))
    stream_mid = stream + fold(out_part.reshape(inner, tp, -1, width))
    normed_two, factor_two, ffn_rows = norm_rows(stream_mid, gain_ffn)
    ffn_in = spread(ffn_rows).reshape(-1, width)
    dy = spread(grad_out_low).reshape(-1, width)

    gate_pre = dot(ffn_in, weight_gate, ((1,), (0,)))
    up_pre = dot(ffn_in, weight_up, ((1,), (0,)))
    gate_sig = jax.nn.sigmoid(gate_pre)
    gate_act = gate_pre * gate_sig
    hidden = (gate_act * up_pre).astype(jnp.bfloat16)
    grad_hidden = dot(dy, weight_down, ((1,), (1,)))
    grad_gate_pre = (
        grad_hidden * up_pre * gate_sig * (1.0 + gate_pre * (1.0 - gate_sig))
    ).astype(jnp.bfloat16)
    grad_up_pre = (grad_hidden * gate_act).astype(jnp.bfloat16)
    grad_ffn_part = dot(grad_gate_pre, weight_gate, ((1,), (1,))) + dot(
        grad_up_pre, weight_up, ((1,), (1,))
    )
    grad_ffn_in = fold(grad_ffn_part.reshape(inner, tp, -1, width))
    down_part = dot(hidden, weight_down, ((1,), (0,)))
    stream_out = stream_mid + fold(down_part.reshape(inner, tp, -1, width))
    grad_down = return_rows(dot(hidden, dy, ((0,), (0,))))
    grad_gate = return_columns(dot(ffn_in, grad_gate_pre, ((0,), (0,))))
    grad_up = return_columns(dot(ffn_in, grad_up_pre, ((0,), (0,))))

    def back_rows(grad, normed, factor, gain_row):
        grad_normed = grad * gain_row
        inner_mean = jnp.mean(grad_normed * normed, axis=-1, keepdims=True)
        return factor * (grad_normed - normed * inner_mean), jnp.sum(grad * normed, axis=0)

    mid_norm, gain_ffn_part = back_rows(grad_ffn_in, normed_two, factor_two, gain_ffn)
    grad_mid = grad_out + mid_norm
    grad_mid_low = spread(grad_mid.astype(jnp.bfloat16)).reshape(-1, width)
    grad_mixed = to_heads(dot(grad_mid_low, weight_out, ((1,), (1,))).astype(jnp.bfloat16))
    grad_wo = return_rows(dot(mixed, grad_mid_low, ((0,), (0,))))
    grad_prob = jnp.einsum("blge,bme->bglm", grad_mixed, values, preferred_element_type=jnp.float32)
    inner_prob = jnp.sum(grad_prob * prob, axis=-1, keepdims=True)
    grad_scores = (score_scale * prob * (grad_prob - inner_prob)).astype(jnp.bfloat16)
    grad_queries = jnp.einsum(
        "bglm,bme->blge", grad_scores, keys, preferred_element_type=jnp.float32
    )
    grad_keys = jnp.einsum(
        "bglm,blge->bme", grad_scores, queries, preferred_element_type=jnp.float32
    )
    grad_values = jnp.einsum(
        "bglm,blge->bme", prob_low, grad_mixed, preferred_element_type=jnp.float32
    )
    grad_turning = jnp.concatenate([grad_queries, grad_keys[:, :, None]], axis=2)
    grad_turning = grad_turning * cos_heads + turned_back(grad_turning * sin_heads)
    grad_projected = jnp.concatenate([grad_turning, grad_values[:, :, None]], axis=2)
    grad_projected = from_heads(grad_projected.astype(jnp.bfloat16))
    grad_attn_in = fold(
        dot(grad_projected, weight_qkv, ((1,), (1,))).reshape(inner, tp, -1, width)
    )
    grad_wqkv = return_columns(dot(attn_in, grad_projected, ((0,), (0,))))
    in_norm, gain_attn_part = back_rows(grad_attn_in, normed_one, factor_one, gain_attn)
    grad_in = (grad_mid + in_norm).astype(jnp.bfloat16)

    gain_parts = jnp.stack([gain_attn_part, gain_ffn_part], axis=1).reshape(fsdp * ctx, -1, 2)
    gain_sums = lax.psum_scatter(gain_parts, ("fsdp", "ctx"), scatter_dimension=0)
    gain_sums = lax.psum(gain_sums, "tp")

    def home(array):
        return rehome(array.reshape(micro, 1, rows, width))

    return (
        home(stream_out.astype(jnp.bfloat16)),
        home(grad_in),
        gain_sums[:, 0],
        grad_wqkv,
        grad_wo,
        gain_sums[:, 1],
        grad_gate,
        grad_up,
        grad_down,
    )


MESH = pl.DeviceIdType.MESH
ROWS = 128
LANES = 128
NARROW = jnp.bfloat16
WIDE = jnp.float32
HALF = HEAD_DIM // 2
SCALE = HEAD_DIM ** (-0.5)
ANYWHERE = pl.BlockSpec(memory_space=pl.ANY)


class Place:
    def __init__(self):
        f, c, t = lax.axis_index("fsdp"), lax.axis_index("ctx"), lax.axis_index("tp")
        self.f, self.c, self.t = f, c, t
        fs, fy = f + 1 - 2 * (f % 2), (f + 2) % 4
        fd = (fs + 2) % 4
        self.fs, self.fy, self.fd = fs, fy, fd
        self.c1, self.c2 = c + 1 - 2 * (c % 2), (c + 2) % 4
        self.c3 = (self.c1 + 2) % 4
        self.side, self.core, self.row = (f, c, 1 - t), (fs, c, t), (fy, c, t)
        self.cross = (fd, c, t)
        self.z1, self.z2 = (f, self.c1, t), (f, self.c2, t)
        self.is_end, self.is_mid = c * (3 - c) == 0, c * (3 - c) != 0
        self.c_near, self.c_mate, self.c_outer = 1 + c // 3, 3 - c, 3 * c - 3
        self.z3 = (f, 3 - c, t)
        self.core_side, self.row_side = (fs, c, 1 - t), (fy, c, 1 - t)
        self.cross_side = (fd, c, 1 - t)
        self.level = (
            self.side, self.core, self.row, self.cross, self.core_side, self.row_side, self.cross_side
        )
        y, k, high, low = f // 2, f % 2, c // 2, c % 2
        self.to_f, self.to, self.whence, self.away = [], [], [], []
        for m in range(2):
            even = (y + m) % 2
            to_f, to_c = (low + even) % 2 * 2 + high, k * 2 + even
            self.to_f.append(to_f)
            self.to.append((to_f, to_c, t))
            self.whence.append(((low + m) % 2 * 2 + high, k * 2 + (y + low) % 2, t))
            self.away.append((to_f - f) * (to_f - f) + (to_c - c) * (to_c - c))
        self.b, self.b_side = f * 2 + t, f * 2 + 1 - t
        self.b_row, self.b_far = fy * 2 + t, fy * 2 + 1 - t
        self.b_core, self.b_core_side = fs * 2 + t, fs * 2 + 1 - t
        self.b_core_row, self.b_core_far = fd * 2 + t, fd * 2 + 1 - t


class Sent:
    def __init__(self, copy, landing):
        self.copy, self.landing = copy, landing

    def arrive(self):
        self.landing.wait_recv()

    def leave(self):
        self.copy.wait_send()


class Post:
    def __init__(self, send_sems, recv_sems, local_sems):
        self.sems = send_sems, recv_sems
        self.local_sems = local_sems
        self.n, self.n_local = 0, 0
        self.out, self.kept = [], []
        self.gates = []

    def make(self, source, target, device, lands):
        sems = dict(
            send_sem=self.sems[0].at[self.n],
            recv_sem=self.sems[1].at[self.n],
            device_id=device,
            device_id_type=MESH,
        )
        self.n += 1
        copy = pltpu.make_async_remote_copy(src_ref=source, dst_ref=target, **sems)
        landing = pltpu.make_async_remote_copy(src_ref=lands, dst_ref=lands, **sems)
        return Sent(copy, landing)

    def send(self, source, target, device, lands):
        sent = self.make(source, target, device, lands)
        sent.copy.start()
        self.out.append(sent)
        return sent

    def keep(self, source, target):
        copy = pltpu.make_async_copy(source, target, self.local_sems.at[self.n_local])
        self.n_local += 1
        copy.start()
        self.kept.append(copy)
        return copy

    def settle(self, copies):
        for copy in copies:
            copy.wait()
        self.kept = [kept for kept in self.kept if not any(kept is copy for copy in copies)]

    def close(self):
        for sent in self.out:
            sent.leave()
        for copy in self.kept:
            copy.wait()
        for gate in self.gates:
            gate.leave()
        self.out, self.kept, self.gates = [], [], []


class Gate:
    def __init__(self, post, sends, gets, what, lands):
        self.post, self.sends, self.gets, self.what, self.lands = post, sends, gets, what, lands
        self.n = post.n
        post.n += 1

    def copy(self, source, target, device):
        return pltpu.make_async_remote_copy(
            src_ref=source,
            dst_ref=target,
            send_sem=self.post.sems[0].at[self.n],
            recv_sem=self.post.sems[1].at[self.n],
            device_id=device,
            device_id_type=MESH,
        )

    def start(self):
        @pl.when(self.sends)
        def _():
            self.copy(*self.what()).start()

        self.post.gates.append(self)
        return self

    def arrive(self):
        @pl.when(self.gets)
        def _():
            there = self.lands()
            self.copy(there, there, self.post.anyone).wait_recv()

    def leave(self):
        @pl.when(self.sends)
        def _():
            self.copy(*self.what()).wait_send()


def meet(devices):
    bar = pltpu.get_barrier_semaphore()
    for device in devices:
        pl.semaphore_signal(bar, inc=1, device_id=device, device_id_type=MESH)
    pl.semaphore_wait(bar, len(devices))


class Spread:
    def __init__(self, post, at, out):
        self.post, self.at, self.out = post, at, out
        self.sent = {}

    def slot(self, block, half):
        return self.out.at[block, pl.ds(half * ROWS, ROWS)]

    def own(self, half, source):
        at, mine = self.at, self.slot(self.at.b, half)
        self.sent["side", half] = self.post.send(source, mine, at.side, self.slot(at.b_side, half))
        self.sent["row", half] = self.post.send(source, mine, at.row, self.slot(at.b_row, half))
        self.sent["core", half] = self.post.send(source, mine, at.core, self.slot(at.b_core, half))
        self.post.keep(source, mine)

    def pass_on(self, name, half, block, lands):
        here = self.slot(block, half)
        self.sent[name, half] = self.post.send(
            here, here, self.at.core, self.slot(lands, half)
        )

    def relay(self, half):
        at = self.at
        first = ("side", "row") if half == 0 else ("row", "side")
        for name in first:
            self.sent[name, half].arrive()
            block = at.b_side if name == "side" else at.b_row
            here = self.slot(block, half)
            if half == 0 and name == "side":
                self.sent["far", 0] = self.post.send(here, here, at.row, self.slot(at.b_far, 0))
            if half == 1 and name == "row":
                self.sent["far", 1] = self.post.send(here, here, at.side, self.slot(at.b_far, 1))
            lands = at.b_core_side if name == "side" else at.b_core_row
            self.pass_on("core_" + name, half, block, lands)

    def corner(self):
        for half in range(2):
            self.sent["far", half].arrive()
            self.pass_on("core_far", half, self.at.b_far, self.at.b_core_far)

    def finish(self):
        for name in ("core", "core_side", "core_row", "core_far"):
            for half in range(2):
                self.sent[name, half].arrive()


SPREAD_COPIES, SPREAD_KEPT = 14, 2


class Fold:
    copies = 10

    def __init__(self, post, at, part, scratch):
        self.post, self.at, self.part = post, at, part
        self.got, self.give, self.far, self.side, self.row, self.gx, self.gy, self.held = scratch

    @staticmethod
    def scratch(width):
        return [
            pltpu.VMEM((4, 2 * ROWS, width), NARROW),
            pltpu.VMEM((4, 2 * ROWS, width), NARROW),
            pltpu.VMEM((2, ROWS, width), NARROW),
            pltpu.VMEM((2, ROWS, width), NARROW),
            pltpu.VMEM((2, ROWS, width), NARROW),
            pltpu.VMEM((3, ROWS, width), NARROW),
            pltpu.VMEM((3, ROWS, width), NARROW),
            pltpu.VMEM((4, ROWS, width), WIDE),
        ]

    def pair(self, slot, for_core, for_own):
        both = self.part(for_core, for_own)
        self.give[slot] = both[: 2 * ROWS].astype(NARROW)
        sent = self.post.send(
            self.give.at[slot], self.got.at[slot], self.at.core, self.got.at[slot]
        )
        return sent, both[2 * ROWS :]

    def add_core(self, slot, pair):
        sent, value = pair
        sent.arrive()
        return value + self.got[slot].astype(WIDE)

    def first(self):
        at, post = self.at, self.post
        far = self.pair(3, at.b_core_far, at.b_far)
        side = self.pair(1, at.b_core_side, at.b_side)
        value = self.add_core(3, far).astype(NARROW)
        self.far[0] = value[:ROWS]
        self.far[1] = value[ROWS:]
        self.far_x = post.send(self.far.at[0], self.gx.at[0], at.side, self.gx.at[0])
        self.far_y = post.send(self.far.at[1], self.gy.at[0], at.row, self.gy.at[0])
        row = self.pair(2, at.b_core_row, at.b_row)
        value = self.add_core(1, side)
        self.side[0] = value[:ROWS].astype(NARROW)
        self.held[2] = value[ROWS:]
        self.side_x = post.send(self.side.at[0], self.gx.at[1], at.side, self.gx.at[1])
        own = self.pair(0, at.b_core, at.b)
        value = self.add_core(2, row)
        self.row[1] = value[ROWS:].astype(NARROW)
        self.held[3] = value[:ROWS]
        self.row_y = post.send(self.row.at[1], self.gy.at[1], at.row, self.gy.at[1])
        value = self.add_core(0, own)
        self.held[0] = value[:ROWS]
        self.held[1] = value[ROWS:]

    def second(self):
        at, post = self.at, self.post
        self.far_y.arrive()
        self.side[1] = (self.held[2] + self.gy[0].astype(WIDE)).astype(NARROW)
        self.side_b = post.send(self.side.at[1], self.gx.at[2], at.side, self.gx.at[2])
        self.far_x.arrive()
        self.row[0] = (self.held[3] + self.gx[0].astype(WIDE)).astype(NARROW)
        self.row_a = post.send(self.row.at[0], self.gy.at[2], at.row, self.gy.at[2])

    def third(self):
        self.side_x.arrive()
        self.row_y.arrive()
        self.held[0] = self.held[0] + self.gx[1].astype(WIDE)
        self.held[1] = self.held[1] + self.gy[1].astype(WIDE)
        self.row_a.arrive()
        self.held[0] = self.held[0] + self.gy[2].astype(WIDE)
        self.side_b.arrive()
        self.held[1] = self.held[1] + self.gx[2].astype(WIDE)


class Climb:
    copies, kept = 3, 1

    def __init__(self, post, at, level, out):
        self.post, self.at, self.out = post, at, out
        mine = out.at[:, at.c]
        self.far = post.send(level, mine, at.z2, out.at[:, at.c2])
        self.close = post.send(level, mine, at.z1, out.at[:, at.c1])
        self.own = post.keep(level, mine)

    def forward(self):
        at = self.at
        self.far.arrive()
        there = self.out.at[:, at.c2]
        self.last = self.post.send(there, there, at.z1, self.out.at[:, at.c3])

    def finish(self):
        self.close.arrive()
        self.last.arrive()
        self.post.settle([self.own])


class LineClimb:
    def __init__(self, post, at, level, out):
        self.post = post
        line = lambda c: (at.f, c, at.t)
        slot = lambda c: out.at[:, c]
        near, mate, outer = at.c_near, at.c_mate, at.c_outer
        end, mid = at.is_end, at.is_mid
        self.t0 = Gate(post, end, mid, lambda: (level, slot(at.c), line(near)), lambda: slot(outer))
        self.t1 = Gate(post, mid, end, lambda: (level, slot(at.c), line(outer)), lambda: slot(near))
        self.t2 = Gate(post, mid, mid, lambda: (level, slot(at.c), line(mate)), lambda: slot(mate))
        self.t3 = Gate(
            post, mid, mid, lambda: (slot(outer), slot(outer), line(mate)), lambda: slot(3 - outer)
        )
        self.t4 = Gate(
            post, mid, end, lambda: (slot(mate), slot(mate), line(outer)), lambda: slot(3 - near)
        )
        self.t5 = Gate(
            post, mid, end, lambda: (slot(3 - outer), slot(3 - outer), line(outer)), lambda: slot(3 - at.c)
        )
        for gate in (self.t0, self.t1, self.t2):
            gate.start()
        self.own = post.keep(level, slot(at.c))

    def forward(self):
        self.t2.arrive()
        self.t4.start()
        self.t0.arrive()
        self.t3.start()

    def last(self):
        self.t3.arrive()
        self.t5.start()

    def finish(self):
        for gate in (self.t1, self.t4, self.t5):
            gate.arrive()
        self.post.settle([self.own])


class Ends:
    def __init__(self, post, at, parts, first, got, start=0, count=None):
        count = got.shape[0] if count is None else count
        self.gates = [
            Gate(
                post, at.is_end, at.is_mid,
                lambda q=q: (
                    parts.at[first + q, :, pl.ds((3 - at.c) // 3, 3)], got.at[q], (at.f, at.c_near, at.t)
                ),
                lambda q=q: got.at[q],
            ).start()
            for q in range(start, start + count)
        ]

    def finish(self, count=None):
        count = len(self.gates) if count is None else count
        for gate in self.gates[:count]:
            gate.arrive()
        self.gates = self.gates[count:]


class Middle:
    def __init__(self, post, at, step, parts, first, came, out, own, more):
        self.post, self.at, self.out, self.own, self.more = post, at, out, own, more
        self.step, self.n = step, out.shape[0]
        self.sems = [post.local_sems.at[post.n_local + k] for k in range(2)]
        post.n_local += 2
        rows = pl.ds(first, self.n)

        def sources():
            if step == 1:
                return (
                    parts.at[rows, :, pl.ds(2 * (2 - at.c), 2)], came.at[:, :, pl.ds(2 - at.c, 2)]
                )
            return parts.at[rows, :, 3 * (at.c - 1)], came.at[:, :, at.c - 1]

        self.sources = sources

        @pl.when(at.is_mid)
        def _():
            for source, target, sem in zip(sources(), (own, more), self.sems):
                pltpu.make_async_copy(source, target, sem).start()

    def send(self):
        at, own, more = self.at, self.own, self.more

        @pl.when(at.is_mid)
        def _():
            for source, target, sem in zip(self.sources(), (own, more), self.sems):
                pltpu.make_async_copy(source, target, sem).wait()

            def add(q, carry):
                own[q] = (own[q].astype(WIDE) + more[q].astype(WIDE)).astype(NARROW)
                return carry

            lax.fori_loop(0, self.n, add, 0)

        c_to = at.c_mate if self.step == 1 else at.c_outer
        self.gate = Gate(
            self.post, at.is_mid, at.is_mid if self.step == 1 else at.is_end,
            lambda: (own, self.out, (at.f, c_to, at.t)), lambda: self.out,
        ).start()

    def finish(self):
        self.gate.arrive()


def middle_scratch(step, n):
    dims = (n, 4, 2, 256, LANES) if step == 1 else (n, 4, 256, LANES)
    return [pltpu.VMEM(dims, NARROW)] * 2


def call(kernel, name, outs, args, scratch, copies, kept, collective_id):
    sems = [
        pltpu.SemaphoreType.DMA((copies,)),
        pltpu.SemaphoreType.DMA((copies,)),
        pltpu.SemaphoreType.DMA((kept,)),
    ]
    n_in, n_out = len(args), len(outs)

    def inner(*refs):
        post, at = Post(*refs[len(refs) - 3 :]), Place()
        post.anyone = at.z1
        kernel(
            post, at, refs[:n_in], refs[n_in : n_in + n_out], refs[n_in + n_out : len(refs) - 3]
        )
        post.close()
        assert post.n <= copies and post.n_local <= kept, (post.n, post.n_local)

    return pl.pallas_call(
        inner,
        out_shape=outs,
        in_specs=[ANYWHERE] * n_in,
        out_specs=[ANYWHERE] * n_out,
        scratch_shapes=scratch + sems,
        compiler_params=pltpu.CompilerParams(
            collective_id=collective_id, has_side_effects=True, vmem_limit_bytes=62 << 20
        ),
        name=name,
    )(*args)


def shape(*dims, dtype=NARROW):
    return jax.ShapeDtypeStruct(dims, dtype)


def gain_row(gains_ref, which):
    return jnp.concatenate([gains_ref[i, which : which + 1, :] for i in range(16)], axis=1)


def normed_rows(values):
    factor = lax.rsqrt(jnp.mean(values * values, axis=-1, keepdims=True) + EPS)
    return values * factor, factor


class Swap:
    def __init__(self, post, at, home=False):
        self.post, self.at, self.moves = post, at, []
        self.devices = at.whence if home else at.to

    def __call__(self, m, source, target, lands):
        post, away = self.post, self.at.away[m]
        sent = post.make(source, target, self.devices[m], lands)
        local = pltpu.make_async_copy(source, target, post.local_sems.at[post.n_local])
        post.n_local += 1

        @pl.when(away != 0)
        def _():
            sent.copy.start()

        @pl.when(away == 0)
        def _():
            local.start()

        self.moves.append((away, sent))

        def arrive():
            @pl.when(away != 0)
            def _():
                sent.landing.wait_recv()

            @pl.when(away == 0)
            def _():
                local.wait()

        return arrive

    def finish(self):
        for away, sent in self.moves:
            @pl.when(away != 0)
            def _(sent=sent):
                sent.copy.wait_send()


def meet_swap(at):
    bar = pltpu.get_barrier_semaphore()
    partners = (*at.level, at.z1, at.z2, at.z3)
    for device in partners:
        pl.semaphore_signal(bar, inc=1, device_id=device, device_id_type=MESH)
    for m in range(2):
        @pl.when(at.away[m] != 0)
        def _(m=m):
            for device in (at.to[m], at.whence[m]):
                pl.semaphore_signal(bar, inc=1, device_id=device, device_id_type=MESH)

    pl.semaphore_wait(bar, len(partners) + sum(2 * ((away + 18) // 19) for away in at.away))


class Deal:
    def __init__(self, post, at, shards, j, outs):
        self.post, self.sent, self.kept = post, [], []
        gate, up, down = shards
        part = gate.shape[1] // 4
        chunk = part // 4
        for device, k in ((at.row, at.fy), (at.cross, at.fd), (at.core, at.fs), (None, at.f)):
            lane = pl.ds(pl.multiple_of(k * part + j * chunk, LANES), chunk)
            for source, out in zip((gate.at[:, lane], up.at[:, lane], down.at[lane]), outs):
                if device is None:
                    self.kept.append(post.keep(source, out.at[at.f]))
                else:
                    self.sent.append(post.send(source, out.at[at.f], device, out.at[k]))

    def finish(self):
        for sent in self.sent:
            sent.arrive()


HALVES = [pl.ds(half * ROWS, ROWS) for half in range(2)]


def start_kernel(post, at, ins, outs, scratch):
    hidden, marks, gains, wqkv, wo, *shards = ins
    x_own, attn_in, all_marks, all_gains, qkv_all, out_all, *levels_out = outs
    rows_in, rows_out, gain_buf = scratch
    f, c = at.f, at.c
    meet_swap(at)
    swap = Swap(post, at)
    x_moved = [
        swap(m, hidden.at[half], rows_in.at[half], rows_in.at[half]) for m, half in enumerate(HALVES)
    ]
    heads = wqkv.shape[1] // 4
    span = wo.shape[0] // 4
    first = []
    for device, k in ((at.row, at.fy), (at.cross, at.fd), (at.core, at.fs)):
        lane = pl.ds(pl.multiple_of(k * heads, LANES), heads)
        first.append(post.send(wqkv.at[:, lane], qkv_all.at[f, c], device, qkv_all.at[k, c]))
        row = pl.ds(pl.multiple_of(k * span, LANES), span)
        first.append(post.send(wo.at[row], out_all.at[f, c], device, out_all.at[k, c]))
    lane = pl.ds(pl.multiple_of(f * heads, LANES), heads)
    own = [post.keep(wqkv.at[:, lane], qkv_all.at[f, c])]
    row = pl.ds(pl.multiple_of(f * span, LANES), span)
    own.append(post.keep(wo.at[row], out_all.at[f, c]))
    marks_moved = [
        swap(m, marks, all_marks.at[m, at.to_f[m]], all_marks.at[m, f]) for m in range(2)
    ]

    mine = gain_buf.at[f, c]
    post.settle([post.keep(gains, mine)])
    step = post.send(mine, mine, at.core, gain_buf.at[at.fs, c])
    step.arrive()
    pair = gain_buf.at[pl.ds(f // 2 * 2, 2), c]
    step = post.send(pair, pair, at.row, gain_buf.at[pl.ds(at.fy // 2 * 2, 2), c])
    step.arrive()
    step = post.send(gain_buf.at[:, c], gain_buf.at[:, c], at.z1, gain_buf.at[:, at.c1])
    step.arrive()
    pair = gain_buf.at[:, pl.ds(c // 2 * 2, 2)]
    step = post.send(pair, pair, at.z2, gain_buf.at[:, pl.ds(at.c2 // 2 * 2, 2)])
    step.arrive()
    gain = jnp.concatenate([gain_buf[i // 4, i % 4, 0:1, :] for i in range(16)], axis=1)
    post.keep(gain_buf, all_gains)

    post.settle(own)
    for sent in first:
        sent.arrive()

    spread = Spread(post, at, attn_in)
    levels = []

    def climb():
        for out in (qkv_all, out_all):
            here, there = out.at[:, c], out.at[:, at.c2]
            far = post.send(here, here, at.z2, there)
            close = post.send(here, here, at.z1, out.at[:, at.c1])
            levels.append((far, close, there, out))

    for half in range(2):
        x_moved[half]()
        if half == 1:
            climb()
        normed, _ = normed_rows(rows_in[HALVES[half]].astype(WIDE))
        rows_out[HALVES[half]] = (normed * gain).astype(NARROW)
        spread.own(half, rows_out.at[HALVES[half]])
        post.keep(rows_in.at[HALVES[half]], x_own.at[HALVES[half]])

    for arrive in marks_moved:
        arrive()
    here = all_marks.at[:, f]
    small = post.send(here, here, at.core, all_marks.at[:, at.fs])
    spread.relay(0)
    small.arrive()
    pair = all_marks.at[:, pl.ds(f // 2 * 2, 2)]
    smaller = post.send(pair, pair, at.row, all_marks.at[:, pl.ds(at.fy // 2 * 2, 2)])
    spread.relay(1)
    forwards = []
    for far, close, there, out in levels:
        far.arrive()
        forwards.append((post.send(there, there, at.z1, out.at[:, at.c3]), close))
    deals = [Deal(post, at, shards, j, levels_out[3 * j : 3 * j + 3]) for j in range(2)]
    spread.corner()
    for last, close in forwards:
        last.arrive()
        close.arrive()
    spread.finish()
    smaller.arrive()
    for deal in deals:
        deal.finish()
    swap.finish()


def rope(values, cos_full, sin_full):
    return values * cos_full + pltpu.roll(values, HALF, 1) * sin_full


def rope_back(values, cos_full, sin_full):
    return values * cos_full - pltpu.roll(values, HALF, 1) * sin_full


def rope_full(marks, m, inverse):
    angle = marks.T[:, 2 + m : 3 + m] * inverse
    low = lax.broadcasted_iota(jnp.int32, angle.shape, 1) < HALF
    turns = jnp.floor(angle * (2.0 / math.pi) + 0.5)
    rest = ((angle - turns * 1.5703125) - turns * 4.837512969970703125e-4) - turns * 7.54978995489188e-8
    square = rest * rest
    sine = rest + rest * square * (
        -1.6666654611e-1 + square * (8.3321608736e-3 - square * 1.9515295891e-4)
    )
    cosine = 1.0 - 0.5 * square + square * square * (
        4.166664568298827e-2 + square * (-1.388731625493765e-3 + square * 2.443315711809948e-5)
    )
    quadrant = turns + jnp.where(low, 1.0, 0.0)
    half = jnp.floor(quadrant * 0.5)
    odd = quadrant - 2.0 * half > 0.5
    negative = half - 2.0 * jnp.floor(half * 0.5) > 0.5
    table = jnp.where(odd, cosine, sine)
    table = jnp.where(negative, -table, table)
    turned_table = pltpu.roll(table, HALF, 1)
    return jnp.where(low, table, turned_table), jnp.where(low, -turned_table, table)


def quarter(at, i):
    return (i + at.c) % 2 * 2 + i // 2


def mm(left, right, dims=((1,), (0,))):
    return lax.dot_general(left, right, (dims, ((), ())), preferred_element_type=WIDE)


TILE = 256

def softmax_tile(query, key, id_col, id_row):
    raw = mm(query, key, ((1,), (1,))) * SCALE
    raw = jnp.where(id_row <= id_col, raw, MASKED)
    top = jnp.max(raw, axis=-1, keepdims=True)
    exponent = jnp.exp(raw - top)
    return exponent * (1.0 / jnp.sum(exponent, axis=-1, keepdims=True))


def id_rows(at, marks, m, tiles):
    return jnp.concatenate([marks[m, quarter(at, i), m : m + 1, :] for i in range(tiles)], axis=1)


def attend_kernel(post, at, ins, outs, scratch):
    attn_in, qkv_all, inverse_in, marks_in, cot, *shards = ins[:8]
    levels = ins[8:]
    queries, keys, values, mixed, dy, cot_own, *more = outs
    climbed, dealt = more[: len(levels)], more[len(levels) :]
    rows, weight, inverse, marks, q_buf, k_buf, v_buf, mix_buf = scratch
    meet_swap(at)
    swap = Swap(post, at)
    cot_moved = [
        swap(m, cot.at[half], cot_own.at[half], cot_own.at[half]) for m, half in enumerate(HALVES)
    ]
    local = [
        post.keep(inverse_in, inverse),
        post.keep(marks_in, marks),
        post.keep(qkv_all, weight),
        post.keep(attn_in.at[:, pl.ds(0, ROWS)], rows.at[0]),
        post.keep(attn_in.at[:, pl.ds(ROWS, ROWS)], rows.at[1]),
    ]
    spread = Spread(post, at, dy)
    deal = Deal(post, at, shards, 2, dealt)
    post.settle(local)
    width = rows.shape[-1]
    columns = weight.shape[-1]
    for m in range(2):
        for i in range(4):
            q = quarter(at, i)
            here = rows[m, pl.ds(2 * q, 2)].reshape(TILE, width)
            projected = mm(here, weight[...].reshape(width, columns))
            cos_full, sin_full = rope_full(marks[m, q], m, inverse[0:1])
            place = pl.ds(i * TILE, TILE)
            for g in range(2):
                lane = slice(g * HEAD_DIM, (g + 1) * HEAD_DIM)
                q_buf[m, place, lane] = rope(projected[:, lane], cos_full, sin_full).astype(NARROW)
            k_buf[m, place] = rope(projected[:, 256:384], cos_full, sin_full).astype(NARROW)
            v_buf[m, place] = projected[:, 384:512].astype(NARROW)
    for m in range(2):
        for i in range(4):
            n = min(i + 2, 4) * TILE
            q = quarter(at, i)
            id_col = marks[m, q].T[:, m : m + 1]
            id_row = id_rows(at, marks, m, n // TILE)
            for g in range(2):
                lane = slice(g * HEAD_DIM, (g + 1) * HEAD_DIM)
                prob = softmax_tile(
                    q_buf[m, i * TILE : (i + 1) * TILE, lane], k_buf[m, :n], id_col, id_row
                )
                value = mm(prob.astype(NARROW), v_buf[m, :n]).astype(NARROW)
                for h in range(2):
                    mix_buf[2 * q + h, m * ROWS : (m + 1) * ROWS, lane] = value[
                        h * ROWS : (h + 1) * ROWS
                    ]
        if m == 0:
            climbs = [Climb(post, at, level, out) for level, out in zip(levels, climbed)]
    for source, target in ((q_buf, queries), (k_buf, keys), (v_buf, values), (mix_buf, mixed)):
        post.keep(source, target)
    for half in range(2):
        cot_moved[half]()
        spread.own(half, cot_own.at[HALVES[half]])
    spread.relay(0)
    spread.relay(1)
    for climb in climbs:
        climb.forward()
    spread.corner()
    spread.finish()
    for climb in climbs:
        climb.finish()
    deal.finish()
    swap.finish()


def middle_kernel(post, at, ins, outs, scratch):
    mixed, out_all, x_own, gains_in, *shards = ins[:7]
    levels = ins[7:]
    mid_own, ffn_in, *more = outs
    climbed, dealt = more[: len(levels)], more[len(levels) :]
    mix_buf, weight, x_buf, gains, rows_out, *fold_scratch = scratch
    meet((at.side, at.core, at.row, at.cross, at.z1, at.z2))
    local = [
        post.keep(out_all.at[i // 4, i % 4], weight.at[:, pl.ds(i * LANES, LANES)])
        for i in range(16)
    ]
    local += [post.keep(mixed, mix_buf), post.keep(x_own, x_buf), post.keep(gains_in, gains)]
    post.settle(local)
    climbs = [Climb(post, at, level, out) for level, out in zip(levels, climbed)]

    def part(*blocks):
        return mm(jnp.concatenate([mix_buf[block] for block in blocks]), weight[...])

    fold = Fold(post, at, part, fold_scratch)
    fold.first()
    fold.second()
    deal = Deal(post, at, shards, 3, dealt)
    fold.third()
    gain = jnp.concatenate([gains[i // 4, i % 4, 1:2, :] for i in range(16)], axis=1)
    spread = Spread(post, at, ffn_in)
    for half in range(2):
        rows = pl.ds(half * ROWS, ROWS)
        value = fold.held[half] + x_buf[rows].astype(WIDE)
        fold.held[half] = value
        normed, _ = normed_rows(value)
        rows_out[half] = (normed * gain).astype(NARROW)
        spread.own(half, rows_out.at[half])
        post.keep(fold.held.at[half], mid_own.at[rows])
    spread.relay(0)
    for climb in climbs:
        climb.forward()
    spread.relay(1)
    spread.corner()
    spread.finish()
    for climb in climbs:
        climb.finish()
    deal.finish()


def small_arrays(block_ids, positions, attn_gain, ffn_gain):
    micro, _, span = positions.shape
    ids = lax.dynamic_slice_in_dim(block_ids[:, 0], lax.axis_index("ctx") * span, span, 1)
    rows = jnp.concatenate([ids, positions[:, 0]]).astype(WIDE)
    marks = jnp.pad(rows, ((0, 8 - 2 * micro), (0, 0)))
    gains = jnp.pad(jnp.stack([attn_gain, ffn_gain]).astype(WIDE), ((0, 6), (0, 0)))
    return marks, gains


def ffn_kernel(post, at, ins, outs, scratch):
    ffn_in, dy = ins[:2]
    ready = ins[2:10]
    levels = ins[10:]
    hidden, grads_pre, parts, ends_a, *climbed = outs
    x_buf, dy_buf, gate_buf, up_buf, down_buf, act, act_t, staged = scratch
    meet((at.z1, at.z3))
    climbs = [LineClimb(post, at, level, out) for level, out in zip(levels, climbed)]
    local = [post.keep(ffn_in, x_buf), post.keep(dy, dy_buf)]
    weights = list(ready) + list(climbed)

    def load(j):
        slot = j % 2
        gate, up, down = weights[3 * j : 3 * j + 3]
        copies = [post.keep(gate, gate_buf.at[slot]), post.keep(up, up_buf.at[slot])]
        for i in range(16):
            copies.append(
                post.keep(down.at[i // 4, i % 4], down_buf.at[slot, :, pl.ds(i * LANES, LANES)])
            )
        return copies

    loading = load(0)
    post.settle(local)
    width = x_buf.shape[-1]
    saved, sums_0 = [], []
    for j in range(4):
        slot = j % 2
        if loading is None:
            for climb in climbs[:1] if j == 2 else climbs[1:]:
                climb.finish()
            loading = load(j)
        post.settle(loading)
        loading = load(1) if j == 0 else None
        post.settle(saved)

        def rows(i, carry):
            blocks = pl.ds(i * 2, 2)
            x, grad = (buf[blocks].reshape(2 * TILE, width) for buf in (x_buf, dy_buf))
            gate = mm(x, gate_buf[slot].reshape(width, -1))
            up = mm(x, up_buf[slot].reshape(width, -1))
            grad_hidden = mm(grad, down_buf[slot], ((1,), (1,)))
            sig = jax.nn.sigmoid(gate)
            silu = gate * sig
            values = (
                grad_hidden * up * sig * (1.0 + gate * (1.0 - sig)),
                grad_hidden * silu,
                silu * up,
            )
            place = pl.ds(pl.multiple_of(i * 2 * TILE, 2 * TILE), 2 * TILE)
            for k in range(3):
                act[k, blocks] = values[k].astype(NARROW).reshape(2, TILE, -1)
                act_t[k, :, place] = values[k].T.astype(NARROW)
            return carry

        lax.fori_loop(0, 4, rows, 0)
        chunk = act.shape[-1]
        lane = pl.ds(j * chunk, chunk)
        saved = [
            post.keep(act.at[0], grads_pre.at[:, :, lane]),
            post.keep(act.at[1], grads_pre.at[:, :, pl.ds((4 + j) * chunk, chunk)]),
            post.keep(act.at[2], hidden.at[:, :, lane]),
        ]
        for climb in climbs[:1] if j == 1 else climbs[1:] if j == 2 else ():
            climb.last()
        for climb in climbs[:1] if j == 0 else climbs[1:] if j == 1 else ():
            climb.forward()

        def sums(n, carry):
            place = pl.ds(pl.multiple_of(n * TILE, TILE), TILE)
            x = x_buf[:, :, place].reshape(8 * TILE, TILE)
            grad = dy_buf[:, :, place].reshape(8 * TILE, TILE)
            both = mm(act_t[0:2].reshape(2 * chunk, -1), x).astype(NARROW)
            for k, value in enumerate((both[:chunk], both[chunk:], mm(act_t[2], grad).astype(NARROW))):
                staged[k, 2 * n] = value[:, :LANES]
                staged[k, 2 * n + 1] = value[:, LANES:]
            return carry

        lax.fori_loop(0, 8, sums, 0)
        stored = [
            post.keep(staged.at[k, pl.ds(4 * fl, 4)], parts.at[3 * j + k, fl])
            for k in range(3)
            for fl in range(4)
        ]
        if j < 2:
            post.settle(stored)
            sums_0.append(Ends(post, at, parts, 0, ends_a, 3 * j, (3, 1)[j]))
        else:
            saved += stored
    for step in sums_0:
        step.finish()


class Descend:
    def __init__(self, post, at, pieces, got):
        self.near = post.send(pieces.at[:, at.c1], got.at[0], at.z1, got.at[0])
        self.next = post.send(pieces.at[:, at.c3], got.at[1], at.z1, got.at[1])

    def finish(self):
        self.near.arrive()
        self.next.arrive()


def norm_back_rows(grad, values, gain):
    normed, factor = normed_rows(values)
    scaled = grad * gain
    inner_mean = jnp.mean(scaled * normed, axis=-1, keepdims=True)
    return factor * (scaled - normed * inner_mean), jnp.sum(grad * normed, axis=0, keepdims=True)


def back_kernel(post, at, ins, outs, scratch):
    grads_pre, mid_own, cot_own, gains_in, parts, ends_a, *weights = ins
    grad_mid_own, grad_mid, gain_part, ends_c, mates_b, mates_e = outs
    pre_buf, weight, mid_buf, cot_buf, gains, rows_out, gain_out = scratch[:7]
    bufs_1, bufs_e, fold_scratch = scratch[7:9], scratch[9:11], scratch[11:]
    meet((at.side, at.core, at.row, at.z1, at.z3))
    downs = [
        Middle(post, at, 1, parts, 0, ends_a, mates_b, *bufs_1),
        Ends(post, at, parts, 4, ends_c),
    ]
    chunk = pre_buf.shape[-1] // 8
    local = [post.keep(grads_pre, pre_buf)]
    for a in range(2):
        for j in range(4):
            place = pl.ds((4 * a + j) * chunk, chunk)
            local.append(post.keep(weights[4 * a + j], weight.at[:, :, :, place]))
    local += [post.keep(mid_own, mid_buf), post.keep(cot_own, cot_buf), post.keep(gains_in, gains)]
    post.settle(local)
    width = mid_buf.shape[-1]

    def part(*blocks):
        rows = jnp.concatenate([pre_buf[block] for block in blocks])
        return mm(rows, weight[...].reshape(width, -1), ((1,), (1,)))

    downs[0].send()
    fold = Fold(post, at, part, fold_scratch)
    fold.first()
    fold.second()
    fold.third()
    gain = jnp.concatenate([gains[i // 4, i % 4, 1:2, :] for i in range(16)], axis=1)
    spread = Spread(post, at, grad_mid)
    total = jnp.zeros((1, width), WIDE)
    for half in range(2):
        rows = HALVES[half]
        back, piece = norm_back_rows(fold.held[half], mid_buf[rows], gain)
        total = total + piece
        value = cot_buf[rows].astype(WIDE) + back
        fold.held[half] = value
        rows_out[half] = value.astype(NARROW)
        spread.own(half, rows_out.at[half])
        post.keep(fold.held.at[half], grad_mid_own.at[rows])
    gain_out[...] = jnp.broadcast_to(total, gain_out.shape)
    post.keep(gain_out, gain_part)
    downs[1].finish(2)
    downs.append(Middle(post, at, 1, parts, 4, ends_c.at[pl.ds(0, 2)], mates_e, *bufs_e))
    spread.relay(0)
    downs[2].send()
    spread.relay(1)
    spread.corner()
    spread.finish()
    for down in downs:
        down.finish()


def attend_back_kernel(post, at, ins, outs, scratch):
    (
        grad_mid, queries, keys, values, marks_in, inverse_in, out_all, mixed, attn_in, hidden, mid_own, parts,
        ends_c, mates_b, mates_e, *downs_in
    ) = ins
    grad_proj, parts_q, sums_o, out_home, ends_d, mates_c, outer_b, outer_e = outs
    (
        gm_buf, q_buf, k_buf, v_buf, marks, inverse, weight, mix_buf, hid_buf, down_buf, gp_buf, gk_buf, gv_buf,
        staged, staged_o, got_o, far_o, end_o, mid_buf, out_buf
    ) = scratch[:20]
    bufs_1, bufs_2, bufs_e, fold_scratch = scratch[20:22], scratch[22:24], scratch[24:26], scratch[26:]
    meet_swap(at)
    swap = Swap(post, at, home=True)
    steps = [
        Middle(post, at, 1, parts, 6, ends_c.at[pl.ds(2, 3)], mates_c, *bufs_1),
        Middle(post, at, 2, parts, 0, mates_b, outer_b, *bufs_2),
        Middle(post, at, 2, parts, 4, mates_e, outer_e, *bufs_e),
        Ends(post, at, parts, 9, ends_d),
    ]

    chunk = hid_buf.shape[-1] // 4
    early = [post.keep(hidden, hid_buf)]
    for j in range(4):
        for i in range(16):
            target = down_buf.at[pl.ds(j * chunk, chunk), pl.ds(i * LANES, LANES)]
            early.append(post.keep(downs_in[j].at[i // 4, i % 4], target))
    late = [
        post.keep(source, target)
        for source, target in (
            (grad_mid, gm_buf), (queries, q_buf), (keys, k_buf), (values, v_buf), (marks_in, marks),
            (inverse_in, inverse), (mixed, mix_buf), (mid_own, mid_buf),
        )
    ]
    late += [
        post.keep(out_all.at[i // 4, i % 4], weight.at[:, pl.ds(i * LANES, LANES)])
        for i in range(16)
    ]
    post.settle(early)
    for step in steps[:3]:
        step.send()

    def part(*blocks):
        return mm(jnp.concatenate([hid_buf[block] for block in blocks]), down_buf[...])

    fold = Fold(post, at, part, fold_scratch)
    fold.first()
    post.settle(late)

    def fetch(n):
        place = pl.ds(n * TILE, TILE)
        return post.keep(attn_in.at[:, :, place], column(n))

    def column(n):
        return hid_buf.at[:, :, pl.ds(n % 2 * TILE, TILE)]

    mix_t, gp_t = down_buf.at[pl.ds(512, 256)], down_buf.at[pl.ds(0, 512)]
    fetched = fetch(0)
    width = gm_buf.shape[-1]
    for i in range(8):
        mix_t[:, i * TILE : (i + 1) * TILE] = mix_buf[i].astype(WIDE).T.astype(NARROW)
    for n in range(8):
        place = slice(n * TILE, (n + 1) * TILE)
        value = mm(mix_t[...], gm_buf[:, :, place].reshape(8 * TILE, TILE)).astype(NARROW)
        for h in range(2):
            block = 2 * n + h
            staged_o[block // 4, block % 4] = value[:, h * LANES : (h + 1) * LANES]
    step_o = Descend(post, at, staged_o, got_o)
    for m in range(2):
        for i in range(4):
            q = quarter(at, i)
            n = min(i + 2, 4) * TILE
            place = slice(i * TILE, (i + 1) * TILE)
            id_col = marks[m, q].T[:, m : m + 1]
            id_row = id_rows(at, marks, m, n // TILE)
            cos_full, sin_full = rope_full(marks[m, q], m, inverse[0:1])
            rows = gm_buf[pl.ds(2 * q, 2), m * ROWS : (m + 1) * ROWS].reshape(TILE, width)
            grad_mixed = mm(rows, weight[...], ((1,), (1,))).astype(NARROW)
            for g in range(2):
                lane = slice(g * HEAD_DIM, (g + 1) * HEAD_DIM)
                query = q_buf[m, place, lane]
                prob = softmax_tile(query, k_buf[m, :n], id_col, id_row)
                grad = grad_mixed[:, lane]
                grad_prob = mm(grad, v_buf[m, :n], ((1,), (1,)))
                inner = jnp.sum(grad_prob * prob, axis=-1, keepdims=True)
                grad_scores = (SCALE * prob * (grad_prob - inner)).astype(NARROW)
                grad_query = mm(grad_scores, k_buf[m, :n])
                grad_key = mm(grad_scores, query, ((0,), (0,)))
                grad_value = mm(prob.astype(NARROW), grad, ((0,), (0,)))
                if i == 0 and g == 0:
                    gk_buf[:n], gv_buf[:n] = grad_key, grad_value
                    gk_buf[n:], gv_buf[n:] = (jnp.zeros_like(gk_buf[n:]),) * 2
                else:
                    gk_buf[:n] = gk_buf[:n] + grad_key
                    gv_buf[:n] = gv_buf[:n] + grad_value
                done = rope_back(grad_query, cos_full, sin_full).astype(NARROW)
                for h in range(2):
                    gp_buf[2 * q + h, m * ROWS : (m + 1) * ROWS, lane] = done[h * ROWS : (h + 1) * ROWS]
            if m == 1 and i == 1:
                fold.third()
                for half in HALVES:
                    k = half.start // ROWS
                    out_buf[half] = (fold.held[k] + mid_buf[half]).astype(NARROW)
                moved = [
                    swap(k, out_buf.at[half], out_home.at[half], out_home.at[half])
                    for k, half in enumerate(HALVES)
                ]
        for i in range(4):
            q = quarter(at, i)
            place = slice(i * TILE, (i + 1) * TILE)
            cos_full, sin_full = rope_full(marks[m, q], m, inverse[0:1])
            done = (
                rope_back(gk_buf[place], cos_full, sin_full).astype(NARROW),
                gv_buf[place].astype(NARROW),
            )
            for k in range(2):
                lane = slice((2 + k) * HEAD_DIM, (3 + k) * HEAD_DIM)
                for h in range(2):
                    gp_buf[2 * q + h, m * ROWS : (m + 1) * ROWS, lane] = done[k][h * ROWS : (h + 1) * ROWS]
        if m == 0:
            fold.second()
    post.keep(gp_buf, grad_proj)
    for i in range(8):
        place = slice(i * TILE, (i + 1) * TILE)
        gp_t[:, place] = gp_buf[i].astype(WIDE).T.astype(NARROW)
    for n in range(8):
        post.settle([fetched])
        if n < 7:
            fetched = fetch(n + 1)
        other = mm(gp_t[...], column(n)[...].reshape(8 * TILE, TILE)).astype(NARROW)
        for h in range(2):
            block = 2 * n + h
            staged[block // 4, block % 4] = other[:, h * LANES : (h + 1) * LANES]
    post.keep(staged, parts_q)
    step_o.finish()
    for k in range(4):
        value = staged_o[k, at.c2].astype(WIDE) + got_o[1, k].astype(WIDE)
        far_o[k] = value.astype(NARROW)
    sent_o = post.send(far_o, end_o, at.z2, end_o)
    sent_o.arrive()
    for k in range(4):
        value = staged_o[k, at.c].astype(WIDE) + got_o[0, k].astype(WIDE) + end_o[k].astype(WIDE)
        got_o[1, k] = value.astype(NARROW)
    post.keep(got_o.at[1], sums_o)
    for arrive in moved:
        arrive()
    swap.finish()
    for step in steps:
        step.finish()


class Own:
    def __init__(self, post, at, parts, first, n, pieces, own, one, two):
        self.post, self.at, self.first, self.n = post, at, first, n
        self.own, self.one, self.two = own, one, two
        self.pieces = pieces
        count = 1 + max(len(pieces[0]) + len(pieces[1]), len(pieces[2]))
        self.sems = [post.local_sems.at[post.n_local + k] for k in range(count)]
        post.n_local += count
        self.parts = parts

        @pl.when(at.is_mid)
        def _():
            for copy in self.mid_copies():
                copy.start()

        @pl.when(at.is_end)
        def _():
            for copy in self.end_copies():
                copy.start()

    def laid(self, arrays, index, target):
        place, pairs = self.first, []
        for array in arrays:
            n = array.shape[0]
            source = array if index is None else array.at[:, :, index]
            pairs.append((source, target.at[pl.ds(place, n)]))
            place += n
        return pairs

    def copies(self, pairs):
        rows = pl.ds(self.first, self.n)
        pairs = [(self.parts.at[rows, :, self.at.c], self.own.at[rows])] + pairs
        return [pltpu.make_async_copy(*pair, sem) for pair, sem in zip(pairs, self.sems)]

    def mid_copies(self):
        c = self.at.c
        ends, mates, _ = self.pieces
        return self.copies(self.laid(ends, 2 * (c - 1), self.one) + self.laid(mates, 2 - c, self.two))

    def end_copies(self):
        return self.copies(self.laid(self.pieces[2], None, self.two))

    def add(self):
        def both(p, carry):
            value = self.own[p].astype(WIDE) + self.one[p].astype(WIDE) + self.two[p].astype(WIDE)
            self.own[p] = value.astype(NARROW)
            return carry

        def single(p, carry):
            self.own[p] = (self.own[p].astype(WIDE) + self.two[p].astype(WIDE)).astype(NARROW)
            return carry

        @pl.when(self.at.is_mid)
        def _():
            for copy in self.mid_copies():
                copy.wait()
            lax.fori_loop(self.first, self.first + self.n, both, 0)

        @pl.when(self.at.is_end)
        def _():
            for copy in self.end_copies():
                copy.wait()
            lax.fori_loop(self.first, self.first + self.n, single, 0)


def end_kernel(post, at, ins, outs, scratch):
    (
        grad_proj, qkv_all, x_own, gains_in, grad_mid_own, gain_ffn_part, parts, parts_q, sums_o,
        ends_a, ends_c, ends_d, mates_b, mates_c, mates_e, outer_b, outer_e
    ) = ins
    grad_home, gain_sums, mates_d, outer_c, outer_d, *home_sums = outs
    (
        gp_buf, weight, x_buf, gains, mid_buf, rows_out, gain_buf, gain_got, own_ffn, one_ffn, two_ffn,
        own_q, far_q, got_q, end_q
    ) = scratch[:15]
    bufs_1, bufs_2, bufs_3, fold_scratch = scratch[15:17], scratch[17:19], scratch[19:21], scratch[21:]
    f, c = at.f, at.c
    meet_swap(at)
    step_q = Descend(post, at, parts_q, got_q)
    steps = [
        Middle(post, at, 1, parts, 9, ends_d, mates_d, *bufs_1),
        Middle(post, at, 2, parts, 6, mates_c, outer_c, *bufs_2),
    ]
    swap = Swap(post, at, home=True)
    early = Own(
        post, at, parts, 0, 6,
        ((ends_a, ends_c.at[pl.ds(0, 2)]), (mates_b, mates_e), (outer_b, outer_e)),
        own_ffn, one_ffn, two_ffn,
    )
    fold_in = [
        post.keep(grad_proj, gp_buf), post.keep(qkv_all, weight), post.keep(x_own, x_buf),
        post.keep(gains_in, gains), post.keep(grad_mid_own, mid_buf),
        post.keep(gain_ffn_part, gain_buf),
    ]
    later = [
        post.keep(parts_q.at[:, c], own_q), post.keep(parts_q.at[:, at.c2], far_q),
    ]
    for step in steps:
        step.send()

    def add_far(far, came):
        for k in range(4):
            far[k] = (far[k].astype(WIDE) + came[k].astype(WIDE)).astype(NARROW)

    def add_own(own, one, end):
        for k in range(4):
            own[k] = (own[k].astype(WIDE) + one[k].astype(WIDE) + end[k].astype(WIDE)).astype(NARROW)

    trades = []
    places = ((at.row, at.fy), (at.cross, at.fd), (at.core, at.fs))

    def trade(mine, out, *place):
        post.keep(mine(f), out.at[(f, *place)])
        for device, k in places:
            trades.append(
                post.send(mine(k), out.at[(f, *place)], device, out.at[(k, *place)])
            )

    def trade_ffn(p):
        trade(lambda k: own_ffn.at[p, k], home_sums[p % 3], p // 3)

    post.settle(fold_in)
    width = x_buf.shape[-1]

    def part(*blocks):
        rows = jnp.concatenate([gp_buf[block] for block in blocks])
        return mm(rows, weight[...].reshape(width, -1), ((1,), (1,)))

    fold = Fold(post, at, part, fold_scratch)
    fold.first()
    early.add()
    fold.second()
    post.settle(later)
    step_q.finish()
    add_far(far_q, got_q.at[1])
    sent_q = post.send(far_q, end_q, at.z2, end_q)
    fold.third()
    gain = jnp.concatenate([gains[i // 4, i % 4, 0:1, :] for i in range(16)], axis=1)
    total = jnp.zeros((1, width), WIDE)
    moved = []
    for half in range(2):
        rows = HALVES[half]
        back, piece = norm_back_rows(fold.held[half], x_buf[rows].astype(WIDE), gain)
        total = total + piece
        rows_out[rows] = (mid_buf[rows] + back).astype(NARROW)
        moved.append(swap(half, rows_out.at[rows], grad_home.at[rows], grad_home.at[rows]))
    gain_buf[0:1] = total
    gain_sent = [
        post.send(gain_buf, gain_got.at[k], device, gain_got.at[k])
        for k, device in enumerate(at.level)
    ]
    steps[0].finish()
    steps.append(Middle(post, at, 2, parts, 9, mates_d, outer_d, *bufs_3))
    steps[2].send()
    for p in range(6):
        trade_ffn(p)
    trade(lambda k: sums_o.at[k], home_sums[3])
    sent_q.arrive()
    add_own(own_q, got_q.at[0], end_q)
    trade(lambda k: own_q.at[k], home_sums[4])
    steps[1].finish()
    late = Own(
        post, at, parts, 6, 3, ((ends_c.at[pl.ds(2, 3)],), (mates_c,), (outer_c,)), own_ffn, one_ffn, two_ffn
    )
    late.add()
    for p in range(6, 9):
        trade_ffn(p)
    for sent in gain_sent:
        sent.arrive()
        sent.leave()
    post.out = [sent for sent in post.out if not any(sent is gone for gone in gain_sent)]
    gain_buf[...] = gain_buf[...] + sum(gain_got[k] for k in range(7))
    gain_sent = [
        post.send(gain_buf, gain_got.at[7 + k], device, gain_got.at[7 + k])
        for k, device in enumerate((at.z1, at.z2, at.z3))
    ]
    steps[2].finish()
    last = Own(
        post, at, parts, 9, 3, ((ends_d,), (mates_d,), (outer_d,)), own_ffn, one_ffn, two_ffn
    )
    last.add()
    for p in range(9, 12):
        trade_ffn(p)
    for sent in gain_sent:
        sent.arrive()
        sent.leave()
    post.out = [sent for sent in post.out if not any(sent is gone for gone in gain_sent)]
    gain_buf[...] = gain_buf[...] + sum(gain_got[7 + k] for k in range(3))
    place = pl.ds(pl.multiple_of((f * 4 + c) * LANES, LANES), LANES)
    post.keep(gain_buf.at[:, place], gain_sums)
    for sent in trades:
        sent.arrive()
    for arrive in moved:
        arrive()
    swap.finish()


def home_kernel(gate, up, down, qkv, out, gate_out, up_out, down_out, qkv_out, out_out):
    for source, target in ((gate, gate_out), (up, up_out), (qkv, qkv_out)):
        for n in range(source.shape[0] // 512):
            place = pl.ds(n * 512, 512)
            target[:, place] = source[place, :].astype(WIDE).T
    down_out[...] = down[...].astype(WIDE)
    out_out[...] = out[...].astype(WIDE)


def near_body(
    hidden_in, cotangent, block_ids, positions, attn_gain, wqkv, wo, ffn_gain, w_gate, w_up, w_down
):
    micro, _, rows, width = hidden_in.shape
    own = micro * rows
    ff = w_gate.shape[1]
    chunk = ff // 16
    shards = (w_gate, w_up, w_down)
    marks, gains = small_arrays(block_ids, positions, attn_gain, ffn_gain)
    inverse = THETA ** (-(jnp.arange(HALF, dtype=WIDE) * 2.0 / HEAD_DIM))
    inverse = jnp.broadcast_to(jnp.concatenate([inverse, inverse]), (8, HEAD_DIM))
    level_shapes = [shape(4, LANES, chunk), shape(4, LANES, chunk), shape(4, chunk, LANES)]
    whole_shapes = [shape(4, 4, LANES, chunk), shape(4, 4, LANES, chunk), shape(4, 4, chunk, LANES)]
    gains_shape = (4, 4, *gains.shape)
    x_own, attn_in, all_marks, all_gains, qkv_all, out_all, *level = call(
        start_kernel,
        "start",
        [
            shape(own, width), shape(8, own, width),
            shape(2, 4, *marks.shape, dtype=WIDE), shape(*gains_shape, dtype=WIDE),
            shape(4, 4, LANES, wqkv.shape[1] // 4), shape(4, 4, wo.shape[0] // 4, LANES),
            *level_shapes, *level_shapes,
        ],
        (hidden_in.reshape(own, width), marks, gains, wqkv, wo, *shards),
        [pltpu.VMEM((own, width), NARROW), pltpu.VMEM((own, width), NARROW), pltpu.VMEM(gains_shape, WIDE)],
        72, 24, 1,
    )
    queries, keys, values, mixed, dy, cot_own, *more = call(
        attend_kernel,
        "attend",
        [
            shape(2, 1024, 256), shape(2, 1024, 128), shape(2, 1024, 128), shape(8, own, 256),
            shape(8, own, width), shape(own, width), *whole_shapes, *level_shapes,
        ],
        (attn_in, qkv_all, inverse, all_marks, cotangent.reshape(own, width), *shards, *level[:3]),
        [
            pltpu.VMEM((2, 8, ROWS, width), NARROW), pltpu.VMEM(qkv_all.shape, NARROW),
            pltpu.VMEM(inverse.shape, WIDE), pltpu.VMEM(all_marks.shape, WIDE),
            pltpu.VMEM((2, 1024, 256), NARROW), pltpu.VMEM((2, 1024, 128), NARROW),
            pltpu.VMEM((2, 1024, 128), NARROW), pltpu.VMEM((8, own, 256), NARROW),
        ],
        40, 24, 2,
    )
    whole, level = more[:3], level + more[3:]
    mid_own, ffn_in, *more = call(
        middle_kernel,
        "middle",
        [
            shape(own, width, dtype=WIDE), shape(8, own, width), *whole_shapes, *whole_shapes[:2],
            *level_shapes,
        ],
        (mixed, out_all, x_own, all_gains, *shards, *level[3:8]),
        [
            pltpu.VMEM((8, own, 256), NARROW), pltpu.VMEM((256, width), NARROW),
            pltpu.VMEM((own, width), NARROW), pltpu.VMEM(gains_shape, WIDE),
            pltpu.VMEM((2, ROWS, width), NARROW), *Fold.scratch(width),
        ],
        52, 32, 3,
    )
    whole, level = whole + more[:5], level + more[5:]
    hidden, grads_pre, parts, ends_a, *more = call(
        ffn_kernel,
        "ffn",
        [
            shape(8, own, ff // 4), shape(8, own, ff // 2), shape(12, 4, 4, chunk, LANES),
            shape(4, 4, 3, chunk, LANES),
            whole_shapes[2], *whole_shapes,
        ],
        (ffn_in, dy, *whole, *level[8:]),
        [
            pltpu.VMEM((8, own, width), NARROW), pltpu.VMEM((8, own, width), NARROW),
            pltpu.VMEM((2, 4, 4, LANES, chunk), NARROW), pltpu.VMEM((2, 4, 4, LANES, chunk), NARROW),
            pltpu.VMEM((2, chunk, width), NARROW), pltpu.VMEM((3, 8, own, chunk), NARROW),
            pltpu.VMEM((3, chunk, 8 * own), NARROW), pltpu.VMEM((3, 16, chunk, LANES), NARROW),
        ],
        48, 160, 4,
    )
    whole = whole + more
    fold_scratch = Fold.scratch(width)
    grad_mid_own, grad_mid, gain_ffn_part, ends_c, mates_b, mates_e = call(
        back_kernel,
        "back",
        [
            shape(own, width, dtype=WIDE), shape(8, own, width), shape(8, width, dtype=WIDE),
            shape(5, 4, 3, chunk, LANES), shape(4, 4, 2, chunk, LANES), shape(2, 4, 2, chunk, LANES),
        ],
        (grads_pre, mid_own, cot_own, all_gains, parts, ends_a, *whole[0::3], *whole[1::3]),
        [
            pltpu.VMEM((8, own, ff // 2), NARROW), pltpu.VMEM((4, 4, LANES, ff // 2), NARROW),
            pltpu.VMEM((own, width), WIDE), pltpu.VMEM((own, width), NARROW),
            pltpu.VMEM(gains_shape, WIDE), pltpu.VMEM((2, ROWS, width), NARROW),
            pltpu.VMEM((8, width), WIDE), *middle_scratch(1, 4), *middle_scratch(1, 2), *fold_scratch,
        ],
        48, 32, 5,
    )
    grad_proj, parts_q, sums_o, out_home, ends_d, mates_c, outer_b, outer_e = call(
        attend_back_kernel,
        "attend_back",
        [
            shape(8, own, 512), shape(4, 4, 512, LANES), shape(4, 256, LANES),
            shape(own, width),
            shape(3, 4, 3, chunk, LANES), shape(3, 4, 2, chunk, LANES), shape(4, 4, chunk, LANES),
            shape(2, 4, chunk, LANES),
        ],
        (
            grad_mid, queries, keys, values, all_marks, inverse, out_all, mixed, attn_in, hidden, mid_own, parts,
            ends_c, mates_b, mates_e, *whole[2::3],
        ),
        [
            pltpu.VMEM((8, own, width), NARROW), pltpu.VMEM((2, 1024, 256), NARROW),
            pltpu.VMEM((2, 1024, 128), NARROW), pltpu.VMEM((2, 1024, 128), NARROW),
            pltpu.VMEM(all_marks.shape, WIDE), pltpu.VMEM(inverse.shape, WIDE),
            pltpu.VMEM((256, width), NARROW), pltpu.VMEM((8, own, 256), NARROW),
            pltpu.VMEM((8, own, ff // 4), NARROW), pltpu.VMEM((ff // 4, width), NARROW),
            pltpu.VMEM((8, own, 512), NARROW), pltpu.VMEM((1024, 128), WIDE),
            pltpu.VMEM((1024, 128), WIDE),
            pltpu.VMEM((4, 4, 512, LANES), NARROW), pltpu.VMEM((4, 4, 256, LANES), NARROW),
            pltpu.VMEM((2, 4, 256, LANES), NARROW), *[pltpu.VMEM((4, 256, LANES), NARROW)] * 2,
            pltpu.VMEM((own, width), WIDE), pltpu.VMEM((own, width), NARROW), *middle_scratch(1, 3), *middle_scratch(2, 4),
            *middle_scratch(2, 2), *fold_scratch,
        ],
        32, 128, 6,
    )
    grad_home, gain_sums, _, _, _, *sums = call(
        end_kernel,
        "end",
        [
            shape(own, width), shape(8, LANES, dtype=WIDE), shape(3, 4, 2, chunk, LANES),
            shape(3, 4, chunk, LANES), shape(3, 4, chunk, LANES),
            *[shape(4, 4, chunk, LANES)] * 3, shape(4, 256, LANES), shape(4, 512, LANES),
        ],
        (
            grad_proj, qkv_all, x_own, all_gains, grad_mid_own, gain_ffn_part, parts, parts_q, sums_o,
            ends_a, ends_c, ends_d, mates_b, mates_c, mates_e, outer_b, outer_e,
        ),
        [
            pltpu.VMEM((8, own, 512), NARROW), pltpu.VMEM(qkv_all.shape, NARROW),
            pltpu.VMEM((own, width), NARROW), pltpu.VMEM(gains_shape, WIDE),
            pltpu.VMEM((own, width), WIDE), pltpu.VMEM((own, width), NARROW),
            pltpu.VMEM((8, width), WIDE), pltpu.VMEM((10, 8, width), WIDE),
            *[pltpu.VMEM((12, 4, chunk, LANES), NARROW)] * 3,
            *[pltpu.VMEM((4, 512, LANES), NARROW)] * 2, pltpu.VMEM((2, 4, 512, LANES), NARROW),
            pltpu.VMEM((4, 512, LANES), NARROW),
            *middle_scratch(1, 3), *middle_scratch(2, 3), *middle_scratch(2, 3), *fold_scratch,
        ],
        88, 72, 7,
    )
    gate, up, down, out, qkv = (array.reshape(-1, LANES) for array in sums)
    grad_gate, grad_up, grad_down, grad_qkv, grad_out = pl.pallas_call(
        home_kernel,
        out_shape=[
            jax.ShapeDtypeStruct(array.shape, WIDE) for array in (w_gate, w_up, w_down, wqkv, wo)
        ],
        compiler_params=pltpu.CompilerParams(vmem_limit_bytes=48 << 20),
        name="home",
    )(gate, up, down, qkv, out)
    return (
        out_home.reshape(hidden_in.shape),
        grad_home.reshape(hidden_in.shape),
        gain_sums[0],
        grad_qkv,
        grad_out,
        gain_sums[1],
        grad_gate,
        grad_up,
        grad_down,
    )


def body(*shards):
    inner = KV_HEADS // lax.axis_size("tp")
    near = (lax.axis_size("fsdp"), lax.axis_size("ctx"), lax.axis_size("tp"), inner)
    return (near_body if near == (4, 4, 2, 4) else general_body)(*shards)


def solution(mesh):
    return jax.shard_map(
        body,
        mesh=mesh,
        in_specs=(
            P(None, "fsdp", ("ctx", "tp"), None),
            P(None, "fsdp", ("ctx", "tp"), None),
            P(None, "fsdp", None),
            P(None, "fsdp", "ctx"),
            P(("fsdp", "ctx")),
            P(("fsdp", "ctx"), "tp"),
            P("tp", ("fsdp", "ctx")),
            P(("fsdp", "ctx")),
            P(("fsdp", "ctx"), "tp"),
            P(("fsdp", "ctx"), "tp"),
            P("tp", ("fsdp", "ctx")),
        ),
        out_specs=(
            P(None, "fsdp", ("ctx", "tp"), None),
            P(None, "fsdp", ("ctx", "tp"), None),
            P(("fsdp", "ctx")),
            P(("fsdp", "ctx"), "tp"),
            P("tp", ("fsdp", "ctx")),
            P(("fsdp", "ctx")),
            P(("fsdp", "ctx"), "tp"),
            P(("fsdp", "ctx"), "tp"),
            P("tp", ("fsdp", "ctx")),
        ),
        check_vma=False,
    )
```

```python
import functools
import math

import jax
import jax.numpy as jnp
from jax import lax
from jax.sharding import PartitionSpec as P
from jax.experimental import pallas as pl
from jax.experimental.pallas import tpu as pltpu

HEADS = 16
KV_HEADS = 8
HEAD_DIM = 128


EPS = 1e-05
THETA = 1000000.0
MASKED = -1e30


def rope_tables(position_ids):
    half_dim = HEAD_DIM // 2
    inverse = THETA ** (-(jnp.arange(half_dim, dtype=jnp.float32) * 2.0 / HEAD_DIM))
    angles = position_ids.astype(jnp.float32)[..., None] * inverse
    angles = jnp.concatenate([angles, angles], axis=-1)
    return (jnp.cos(angles), jnp.sin(angles))


def turned(values):
    half_dim = values.shape[-1] // 2
    return jnp.concatenate([-values[..., half_dim:], values[..., :half_dim]], axis=-1)


def turned_back(values):
    half_dim = values.shape[-1] // 2
    return jnp.concatenate([values[..., half_dim:], -values[..., :half_dim]], axis=-1)


def norm_rows(stream, gain_row):
    factor = lax.rsqrt(jnp.mean(stream * stream, axis=-1, keepdims=True) + EPS)
    normed = stream * factor
    return (normed, factor, (normed * gain_row).astype(jnp.bfloat16))


def groups_of(fsdp, inner):
    near = [[high * inner + low for low in range(inner)] for high in range(fsdp // inner)]
    far = [[high * inner + low for high in range(fsdp // inner)] for low in range(inner)]
    return near, far


def general_body(
    hidden_in, cotangent, block_ids, positions, attn_gain, wqkv, wo, ffn_gain, w_gate, w_up, w_down
):
    fsdp, ctx, tp = lax.axis_size("fsdp"), lax.axis_size("ctx"), lax.axis_size("tp")
    inner = KV_HEADS // tp
    outer = fsdp // inner
    near, far = groups_of(fsdp, inner)
    micro, _, rows, width = hidden_in.shape
    score_scale = HEAD_DIM ** (-0.5)
    f_at, c_at = lax.axis_index("fsdp"), lax.axis_index("ctx")
    swap = [
        ((high * inner + low) * ctx + c, (high * inner + c) * ctx + low)
        for high in range(outer)
        for low in range(inner)
        for c in range(ctx)
    ]

    def rehome(array):
        return lax.ppermute(array, ("fsdp", "ctx"), swap)

    def trade(pieces):
        return lax.all_to_all(pieces, "fsdp", 0, 0, axis_index_groups=near)

    def spread(block):
        both = lax.all_gather(block, "tp")
        return lax.all_gather(both, "fsdp", axis_index_groups=near)

    def fold(parts):
        half = lax.psum_scatter(
            parts.astype(jnp.bfloat16), "fsdp", scatter_dimension=0, axis_index_groups=near
        )
        return lax.psum_scatter(half, "tp", scatter_dimension=0).astype(jnp.float32)

    def gather_levels(pieces):
        up = lax.all_gather(pieces, "ctx")
        if outer == 1:
            return up[None]
        return lax.all_gather(up, "fsdp", axis_index_groups=far)

    def scatter_levels(pieces):
        if outer == 1:
            pieces = pieces[0]
        else:
            pieces = lax.psum_scatter(pieces, "fsdp", scatter_dimension=0, axis_index_groups=far)
        return lax.psum_scatter(pieces, "ctx", scatter_dimension=0)

    def fetch_columns(shard):
        block, cols = shard.shape
        pieces = trade(shard.reshape(block, inner, cols // inner).transpose(1, 0, 2))
        whole = gather_levels(pieces).transpose(0, 2, 1, 3, 4)
        return whole.reshape(-1, cols // inner)

    def fetch_rows(shard):
        length, block = shard.shape
        pieces = trade(shard.reshape(inner, length // inner, block))
        whole = gather_levels(pieces).transpose(3, 0, 2, 1, 4)
        return whole.reshape(length // inner, -1)

    def return_columns(grad):
        total, cols = grad.shape
        grad = grad.astype(jnp.bfloat16).reshape(outer, inner, ctx, -1, cols)
        mine = trade(scatter_levels(grad.transpose(0, 2, 1, 3, 4)))
        return mine.transpose(1, 0, 2).reshape(mine.shape[1], -1).astype(jnp.float32)

    def return_rows(grad):
        length, total = grad.shape
        grad = grad.astype(jnp.bfloat16).reshape(length, outer, inner, ctx, -1)
        mine = trade(scatter_levels(grad.transpose(1, 3, 2, 0, 4)))
        return mine.reshape(inner * length, -1).astype(jnp.float32)

    def dot(left, right, dims):
        return lax.dot_general(left, right, (dims, ((), ())), preferred_element_type=jnp.float32)

    gains = lax.all_gather(jnp.stack([attn_gain, ffn_gain]), ("fsdp", "ctx"))
    gain_attn = gains[:, 0].reshape(-1).astype(jnp.float32)
    gain_ffn = gains[:, 1].reshape(-1).astype(jnp.float32)
    span = positions.shape[2]
    ids_here = lax.dynamic_slice_in_dim(block_ids[:, 0], c_at * span, span, 1)
    marks = lax.all_gather(jnp.stack([positions[:, 0], ids_here]), ("fsdp", "ctx"))
    my_seq = f_at // inner * inner + c_at
    marks = lax.dynamic_slice_in_dim(marks, my_seq * ctx, ctx, 0)
    marks = marks.transpose(1, 2, 0, 3).reshape(2, micro, ctx * span)
    pos, ids = marks[0], marks[1]

    weight_qkv = fetch_columns(wqkv)
    weight_out = fetch_rows(wo)
    weight_gate = fetch_columns(w_gate)
    weight_up = fetch_columns(w_up)
    weight_down = fetch_rows(w_down)

    stream = rehome(hidden_in).reshape(micro * rows, width).astype(jnp.float32)
    grad_out_low = rehome(cotangent).reshape(micro * rows, width)
    grad_out = grad_out_low.astype(jnp.float32)

    def to_heads(flat):
        split = flat.reshape(inner * tp, micro, rows, -1, HEAD_DIM).transpose(1, 0, 2, 3, 4)
        return split.reshape(micro, inner * tp * rows, -1, HEAD_DIM)

    def from_heads(heads):
        split = heads.reshape(micro, inner * tp, rows, -1).transpose(1, 0, 2, 3)
        return split.reshape(inner * tp * micro * rows, -1)

    normed_one, factor_one, attn_rows = norm_rows(stream, gain_attn)
    attn_in = spread(attn_rows).reshape(-1, width)
    projected = to_heads(dot(attn_in, weight_qkv, ((1,), (0,))))
    group = HEADS // KV_HEADS
    cos_table, sin_table = rope_tables(pos)
    cos_heads, sin_heads = cos_table[:, :, None], sin_table[:, :, None]
    turning = projected[:, :, : group + 1]
    turning = (turning * cos_heads + turned(turning) * sin_heads).astype(jnp.bfloat16)
    queries, keys = turning[:, :, :group], turning[:, :, group]
    values = projected[:, :, group + 1].astype(jnp.bfloat16)
    allowed = (ids[:, None, :] <= ids[:, :, None])[:, None]
    raw = jnp.einsum("blge,bme->bglm", queries, keys, preferred_element_type=jnp.float32)
    scores = jnp.where(allowed, raw * score_scale, MASKED)
    row_max = jnp.max(scores, axis=-1, keepdims=True)
    exponent = jnp.exp(scores - row_max)
    prob = exponent / jnp.sum(exponent, axis=-1, keepdims=True)
    prob_low = prob.astype(jnp.bfloat16)
    mixed = jnp.einsum("bglm,bme->blge", prob_low, values, preferred_element_type=jnp.float32)
    mixed = from_heads(mixed.astype(jnp.bfloat16))
    out_part = dot(mixed, weight_out, ((1,), (0,)))
    stream_mid = stream + fold(out_part.reshape(inner, tp, -1, width))
    normed_two, factor_two, ffn_rows = norm_rows(stream_mid, gain_ffn)
    ffn_in = spread(ffn_rows).reshape(-1, width)
    dy = spread(grad_out_low).reshape(-1, width)

    gate_pre = dot(ffn_in, weight_gate, ((1,), (0,)))
    up_pre = dot(ffn_in, weight_up, ((1,), (0,)))
    gate_sig = jax.nn.sigmoid(gate_pre)
    gate_act = gate_pre * gate_sig
    hidden = (gate_act * up_pre).astype(jnp.bfloat16)
    grad_hidden = dot(dy, weight_down, ((1,), (1,)))
    grad_gate_pre = (
        grad_hidden * up_pre * gate_sig * (1.0 + gate_pre * (1.0 - gate_sig))
    ).astype(jnp.bfloat16)
    grad_up_pre = (grad_hidden * gate_act).astype(jnp.bfloat16)
    grad_ffn_part = dot(grad_gate_pre, weight_gate, ((1,), (1,))) + dot(
        grad_up_pre, weight_up, ((1,), (1,))
    )
    grad_ffn_in = fold(grad_ffn_part.reshape(inner, tp, -1, width))
    down_part = dot(hidden, weight_down, ((1,), (0,)))
    stream_out = stream_mid + fold(down_part.reshape(inner, tp, -1, width))
    grad_down = return_rows(dot(hidden, dy, ((0,), (0,))))
    grad_gate = return_columns(dot(ffn_in, grad_gate_pre, ((0,), (0,))))
    grad_up = return_columns(dot(ffn_in, grad_up_pre, ((0,), (0,))))

    def back_rows(grad, normed, factor, gain_row):
        grad_normed = grad * gain_row
        inner_mean = jnp.mean(grad_normed * normed, axis=-1, keepdims=True)
        return factor * (grad_normed - normed * inner_mean), jnp.sum(grad * normed, axis=0)

    mid_norm, gain_ffn_part = back_rows(grad_ffn_in, normed_two, factor_two, gain_ffn)
    grad_mid = grad_out + mid_norm
    grad_mid_low = spread(grad_mid.astype(jnp.bfloat16)).reshape(-1, width)
    grad_mixed = to_heads(dot(grad_mid_low, weight_out, ((1,), (1,))).astype(jnp.bfloat16))
    grad_wo = return_rows(dot(mixed, grad_mid_low, ((0,), (0,))))
    grad_prob = jnp.einsum("blge,bme->bglm", grad_mixed, values, preferred_element_type=jnp.float32)
    inner_prob = jnp.sum(grad_prob * prob, axis=-1, keepdims=True)
    grad_scores = (score_scale * prob * (grad_prob - inner_prob)).astype(jnp.bfloat16)
    grad_queries = jnp.einsum(
        "bglm,bme->blge", grad_scores, keys, preferred_element_type=jnp.float32
    )
    grad_keys = jnp.einsum(
        "bglm,blge->bme", grad_scores, queries, preferred_element_type=jnp.float32
    )
    grad_values = jnp.einsum(
        "bglm,blge->bme", prob_low, grad_mixed, preferred_element_type=jnp.float32
    )
    grad_turning = jnp.concatenate([grad_queries, grad_keys[:, :, None]], axis=2)
    grad_turning = grad_turning * cos_heads + turned_back(grad_turning * sin_heads)
    grad_projected = jnp.concatenate([grad_turning, grad_values[:, :, None]], axis=2)
    grad_projected = from_heads(grad_projected.astype(jnp.bfloat16))
    grad_attn_in = fold(
        dot(grad_projected, weight_qkv, ((1,), (1,))).reshape(inner, tp, -1, width)
    )
    grad_wqkv = return_columns(dot(attn_in, grad_projected, ((0,), (0,))))
    in_norm, gain_attn_part = back_rows(grad_attn_in, normed_one, factor_one, gain_attn)
    grad_in = (grad_mid + in_norm).astype(jnp.bfloat16)

    gain_parts = jnp.stack([gain_attn_part, gain_ffn_part], axis=1).reshape(fsdp * ctx, -1, 2)
    gain_sums = lax.psum_scatter(gain_parts, ("fsdp", "ctx"), scatter_dimension=0)
    gain_sums = lax.psum(gain_sums, "tp")

    def home(array):
        return rehome(array.reshape(micro, 1, rows, width))

    return (
        home(stream_out.astype(jnp.bfloat16)),
        home(grad_in),
        gain_sums[:, 0],
        grad_wqkv,
        grad_wo,
        gain_sums[:, 1],
        grad_gate,
        grad_up,
        grad_down,
    )


MESH = pl.DeviceIdType.MESH
ROWS = 128
LANES = 128
NARROW = jnp.bfloat16
WIDE = jnp.float32
HALF = HEAD_DIM // 2
SCALE = HEAD_DIM ** (-0.5)
ANYWHERE = pl.BlockSpec(memory_space=pl.ANY)


class Place:
    def __init__(self):
        f, c, t = lax.axis_index("fsdp"), lax.axis_index("ctx"), lax.axis_index("tp")
        self.f, self.c, self.t = f, c, t
        fs, fy = f + 1 - 2 * (f % 2), (f + 2) % 4
        fd = (fs + 2) % 4
        self.fs, self.fy, self.fd = fs, fy, fd
        self.c1, self.c2 = c + 1 - 2 * (c % 2), (c + 2) % 4
        self.c3 = (self.c1 + 2) % 4
        self.side, self.core, self.row = (f, c, 1 - t), (fs, c, t), (fy, c, t)
        self.cross = (fd, c, t)
        self.z1, self.z2 = (f, self.c1, t), (f, self.c2, t)
        self.is_end, self.is_mid = c * (3 - c) == 0, c * (3 - c) != 0
        self.c_near, self.c_mate, self.c_outer = 1 + c // 3, 3 - c, 3 * c - 3
        self.z3 = (f, 3 - c, t)
        self.core_side, self.row_side = (fs, c, 1 - t), (fy, c, 1 - t)
        self.cross_side = (fd, c, 1 - t)
        self.level = (
            self.side, self.core, self.row, self.cross, self.core_side, self.row_side, self.cross_side
        )
        y, k, high, low = f // 2, f % 2, c // 2, c % 2
        self.to_f, self.to, self.whence, self.away = [], [], [], []
        for m in range(2):
            even = (y + m) % 2
            to_f, to_c = (low + even) % 2 * 2 + high, k * 2 + even
            self.to_f.append(to_f)
            self.to.append((to_f, to_c, t))
            self.whence.append(((low + m) % 2 * 2 + high, k * 2 + (y + low) % 2, t))
            self.away.append((to_f - f) * (to_f - f) + (to_c - c) * (to_c - c))
        self.b, self.b_side = f * 2 + t, f * 2 + 1 - t
        self.b_row, self.b_far = fy * 2 + t, fy * 2 + 1 - t
        self.b_core, self.b_core_side = fs * 2 + t, fs * 2 + 1 - t
        self.b_core_row, self.b_core_far = fd * 2 + t, fd * 2 + 1 - t


class Sent:
    def __init__(self, copy, landing):
        self.copy, self.landing = copy, landing

    def arrive(self):
        self.landing.wait_recv()

    def leave(self):
        self.copy.wait_send()


class Post:
    def __init__(self, send_sems, recv_sems, local_sems):
        self.sems = send_sems, recv_sems
        self.local_sems = local_sems
        self.n, self.n_local = 0, 0
        self.out, self.kept = [], []
        self.gates = []

    def make(self, source, target, device, lands):
        sems = dict(
            send_sem=self.sems[0].at[self.n],
            recv_sem=self.sems[1].at[self.n],
            device_id=device,
            device_id_type=MESH,
        )
        self.n += 1
        copy = pltpu.make_async_remote_copy(src_ref=source, dst_ref=target, **sems)
        landing = pltpu.make_async_remote_copy(src_ref=lands, dst_ref=lands, **sems)
        return Sent(copy, landing)

    def send(self, source, target, device, lands):
        sent = self.make(source, target, device, lands)
        sent.copy.start()
        self.out.append(sent)
        return sent

    def keep(self, source, target):
        copy = pltpu.make_async_copy(source, target, self.local_sems.at[self.n_local])
        self.n_local += 1
        copy.start()
        self.kept.append(copy)
        return copy

    def settle(self, copies):
        for copy in copies:
            copy.wait()
        self.kept = [kept for kept in self.kept if not any(kept is copy for copy in copies)]

    def close(self):
        for sent in self.out:
            sent.leave()
        for copy in self.kept:
            copy.wait()
        for gate in self.gates:
            gate.leave()
        self.out, self.kept, self.gates = [], [], []


class Gate:
    def __init__(self, post, sends, gets, what, lands):
        self.post, self.sends, self.gets, self.what, self.lands = post, sends, gets, what, lands
        self.n = post.n
        post.n += 1

    def copy(self, source, target, device):
        return pltpu.make_async_remote_copy(
            src_ref=source,
            dst_ref=target,
            send_sem=self.post.sems[0].at[self.n],
            recv_sem=self.post.sems[1].at[self.n],
            device_id=device,
            device_id_type=MESH,
        )

    def start(self):
        @pl.when(self.sends)
        def _():
            self.copy(*self.what()).start()

        self.post.gates.append(self)
        return self

    def arrive(self):
        @pl.when(self.gets)
        def _():
            there = self.lands()
            self.copy(there, there, self.post.anyone).wait_recv()

    def leave(self):
        @pl.when(self.sends)
        def _():
            self.copy(*self.what()).wait_send()


def meet(devices):
    bar = pltpu.get_barrier_semaphore()
    for device in devices:
        pl.semaphore_signal(bar, inc=1, device_id=device, device_id_type=MESH)
    pl.semaphore_wait(bar, len(devices))


class Spread:
    def __init__(self, post, at, out):
        self.post, self.at, self.out = post, at, out
        self.sent = {}

    def slot(self, block, half):
        return self.out.at[block, pl.ds(half * ROWS, ROWS)]

    def own(self, half, source):
        at, mine = self.at, self.slot(self.at.b, half)
        self.sent["side", half] = self.post.send(source, mine, at.side, self.slot(at.b_side, half))
        self.sent["row", half] = self.post.send(source, mine, at.row, self.slot(at.b_row, half))
        self.sent["core", half] = self.post.send(source, mine, at.core, self.slot(at.b_core, half))
        self.post.keep(source, mine)

    def pass_on(self, name, half, block, lands):
        here = self.slot(block, half)
        self.sent[name, half] = self.post.send(
            here, here, self.at.core, self.slot(lands, half)
        )

    def relay(self, half):
        at = self.at
        first = ("side", "row") if half == 0 else ("row", "side")
        for name in first:
            self.sent[name, half].arrive()
            block = at.b_side if name == "side" else at.b_row
            here = self.slot(block, half)
            if half == 0 and name == "side":
                self.sent["far", 0] = self.post.send(here, here, at.row, self.slot(at.b_far, 0))
            if half == 1 and name == "row":
                self.sent["far", 1] = self.post.send(here, here, at.side, self.slot(at.b_far, 1))
            lands = at.b_core_side if name == "side" else at.b_core_row
            self.pass_on("core_" + name, half, block, lands)

    def corner(self):
        for half in range(2):
            self.sent["far", half].arrive()
            self.pass_on("core_far", half, self.at.b_far, self.at.b_core_far)

    def finish(self):
        for name in ("core", "core_side", "core_row", "core_far"):
            for half in range(2):
                self.sent[name, half].arrive()


SPREAD_COPIES, SPREAD_KEPT = 14, 2


class Fold:
    copies = 10

    def __init__(self, post, at, part, scratch):
        self.post, self.at, self.part = post, at, part
        self.got, self.give, self.far, self.side, self.row, self.gx, self.gy, self.held = scratch

    @staticmethod
    def scratch(width):
        return [
            pltpu.VMEM((4, 2 * ROWS, width), NARROW),
            pltpu.VMEM((4, 2 * ROWS, width), NARROW),
            pltpu.VMEM((2, ROWS, width), NARROW),
            pltpu.VMEM((2, ROWS, width), NARROW),
            pltpu.VMEM((2, ROWS, width), NARROW),
            pltpu.VMEM((3, ROWS, width), NARROW),
            pltpu.VMEM((3, ROWS, width), NARROW),
            pltpu.VMEM((4, ROWS, width), WIDE),
        ]

    def pair(self, slot, for_core, for_own):
        both = self.part(for_core, for_own)
        self.give[slot] = both[: 2 * ROWS].astype(NARROW)
        sent = self.post.send(
            self.give.at[slot], self.got.at[slot], self.at.core, self.got.at[slot]
        )
        return sent, both[2 * ROWS :]

    def add_core(self, slot, pair):
        sent, value = pair
        sent.arrive()
        return value + self.got[slot].astype(WIDE)

    def first(self):
        at, post = self.at, self.post
        far = self.pair(3, at.b_core_far, at.b_far)
        side = self.pair(1, at.b_core_side, at.b_side)
        value = self.add_core(3, far).astype(NARROW)
        self.far[0] = value[:ROWS]
        self.far[1] = value[ROWS:]
        self.far_x = post.send(self.far.at[0], self.gx.at[0], at.side, self.gx.at[0])
        self.far_y = post.send(self.far.at[1], self.gy.at[0], at.row, self.gy.at[0])
        row = self.pair(2, at.b_core_row, at.b_row)
        value = self.add_core(1, side)
        self.side[0] = value[:ROWS].astype(NARROW)
        self.held[2] = value[ROWS:]
        self.side_x = post.send(self.side.at[0], self.gx.at[1], at.side, self.gx.at[1])
        own = self.pair(0, at.b_core, at.b)
        value = self.add_core(2, row)
        self.row[1] = value[ROWS:].astype(NARROW)
        self.held[3] = value[:ROWS]
        self.row_y = post.send(self.row.at[1], self.gy.at[1], at.row, self.gy.at[1])
        value = self.add_core(0, own)
        self.held[0] = value[:ROWS]
        self.held[1] = value[ROWS:]

    def second(self):
        at, post = self.at, self.post
        self.far_y.arrive()
        self.side[1] = (self.held[2] + self.gy[0].astype(WIDE)).astype(NARROW)
        self.side_b = post.send(self.side.at[1], self.gx.at[2], at.side, self.gx.at[2])
        self.far_x.arrive()
        self.row[0] = (self.held[3] + self.gx[0].astype(WIDE)).astype(NARROW)
        self.row_a = post.send(self.row.at[0], self.gy.at[2], at.row, self.gy.at[2])

    def third(self):
        self.side_x.arrive()
        self.row_y.arrive()
        self.held[0] = self.held[0] + self.gx[1].astype(WIDE)
        self.held[1] = self.held[1] + self.gy[1].astype(WIDE)
        self.row_a.arrive()
        self.held[0] = self.held[0] + self.gy[2].astype(WIDE)
        self.side_b.arrive()
        self.held[1] = self.held[1] + self.gx[2].astype(WIDE)


class Climb:
    copies, kept = 3, 1

    def __init__(self, post, at, level, out):
        self.post, self.at, self.out = post, at, out
        mine = out.at[:, at.c]
        self.far = post.send(level, mine, at.z2, out.at[:, at.c2])
        self.close = post.send(level, mine, at.z1, out.at[:, at.c1])
        self.own = post.keep(level, mine)

    def forward(self):
        at = self.at
        self.far.arrive()
        there = self.out.at[:, at.c2]
        self.last = self.post.send(there, there, at.z1, self.out.at[:, at.c3])

    def finish(self):
        self.close.arrive()
        self.last.arrive()
        self.post.settle([self.own])


class LineClimb:
    def __init__(self, post, at, level, out):
        self.post = post
        line = lambda c: (at.f, c, at.t)
        slot = lambda c: out.at[:, c]
        near, mate, outer = at.c_near, at.c_mate, at.c_outer
        end, mid = at.is_end, at.is_mid
        self.t0 = Gate(post, end, mid, lambda: (level, slot(at.c), line(near)), lambda: slot(outer))
        self.t1 = Gate(post, mid, end, lambda: (level, slot(at.c), line(outer)), lambda: slot(near))
        self.t2 = Gate(post, mid, mid, lambda: (level, slot(at.c), line(mate)), lambda: slot(mate))
        self.t3 = Gate(
            post, mid, mid, lambda: (slot(outer), slot(outer), line(mate)), lambda: slot(3 - outer)
        )
        self.t4 = Gate(
            post, mid, end, lambda: (slot(mate), slot(mate), line(outer)), lambda: slot(3 - near)
        )
        self.t5 = Gate(
            post, mid, end, lambda: (slot(3 - outer), slot(3 - outer), line(outer)), lambda: slot(3 - at.c)
        )
        for gate in (self.t0, self.t1, self.t2):
            gate.start()
        self.own = post.keep(level, slot(at.c))

    def forward(self):
        self.t2.arrive()
        self.t4.start()
        self.t0.arrive()
        self.t3.start()

    def last(self):
        self.t3.arrive()
        self.t5.start()

    def finish(self):
        for gate in (self.t1, self.t4, self.t5):
            gate.arrive()
        self.post.settle([self.own])


class Ends:
    def __init__(self, post, at, parts, first, got, start=0, count=None):
        count = got.shape[0] if count is None else count
        self.gates = [
            Gate(
                post, at.is_end, at.is_mid,
                lambda q=q: (
                    parts.at[first + q, :, pl.ds((3 - at.c) // 3, 3)], got.at[q], (at.f, at.c_near, at.t)
                ),
                lambda q=q: got.at[q],
            ).start()
            for q in range(start, start + count)
        ]

    def finish(self, count=None):
        count = len(self.gates) if count is None else count
        for gate in self.gates[:count]:
            gate.arrive()
        self.gates = self.gates[count:]


class Middle:
    def __init__(self, post, at, step, parts, first, came, out, own, more):
        self.post, self.at, self.out, self.own, self.more = post, at, out, own, more
        self.step, self.n = step, out.shape[0]
        self.sems = [post.local_sems.at[post.n_local + k] for k in range(2)]
        post.n_local += 2
        rows = pl.ds(first, self.n)

        def sources():
            if step == 1:
                return (
                    parts.at[rows, :, pl.ds(2 * (2 - at.c), 2)], came.at[:, :, pl.ds(2 - at.c, 2)]
                )
            return parts.at[rows, :, 3 * (at.c - 1)], came.at[:, :, at.c - 1]

        self.sources = sources

        @pl.when(at.is_mid)
        def _():
            for source, target, sem in zip(sources(), (own, more), self.sems):
                pltpu.make_async_copy(source, target, sem).start()

    def send(self):
        at, own, more = self.at, self.own, self.more

        @pl.when(at.is_mid)
        def _():
            for source, target, sem in zip(self.sources(), (own, more), self.sems):
                pltpu.make_async_copy(source, target, sem).wait()

            def add(q, carry):
                own[q] = (own[q].astype(WIDE) + more[q].astype(WIDE)).astype(NARROW)
                return carry

            lax.fori_loop(0, self.n, add, 0)

        c_to = at.c_mate if self.step == 1 else at.c_outer
        self.gate = Gate(
            self.post, at.is_mid, at.is_mid if self.step == 1 else at.is_end,
            lambda: (own, self.out, (at.f, c_to, at.t)), lambda: self.out,
        ).start()

    def finish(self):
        self.gate.arrive()


def middle_scratch(step, n):
    dims = (n, 4, 2, 256, LANES) if step == 1 else (n, 4, 256, LANES)
    return [pltpu.VMEM(dims, NARROW)] * 2


def call(kernel, name, outs, args, scratch, copies, kept, collective_id):
    sems = [
        pltpu.SemaphoreType.DMA((copies,)),
        pltpu.SemaphoreType.DMA((copies,)),
        pltpu.SemaphoreType.DMA((kept,)),
    ]
    n_in, n_out = len(args), len(outs)

    def inner(*refs):
        post, at = Post(*refs[len(refs) - 3 :]), Place()
        post.anyone = at.z1
        kernel(
            post, at, refs[:n_in], refs[n_in : n_in + n_out], refs[n_in + n_out : len(refs) - 3]
        )
        post.close()
        assert post.n <= copies and post.n_local <= kept, (post.n, post.n_local)

    return pl.pallas_call(
        inner,
        out_shape=outs,
        in_specs=[ANYWHERE] * n_in,
        out_specs=[ANYWHERE] * n_out,
        scratch_shapes=scratch + sems,
        compiler_params=pltpu.CompilerParams(
            collective_id=collective_id, has_side_effects=True, vmem_limit_bytes=62 << 20
        ),
        name=name,
    )(*args)


def shape(*dims, dtype=NARROW):
    return jax.ShapeDtypeStruct(dims, dtype)


def gain_row(gains_ref, which):
    return jnp.concatenate([gains_ref[i, which : which + 1, :] for i in range(16)], axis=1)


def normed_rows(values):
    factor = lax.rsqrt(jnp.mean(values * values, axis=-1, keepdims=True) + EPS)
    return values * factor, factor


class Swap:
    def __init__(self, post, at, home=False):
        self.post, self.at, self.moves = post, at, []
        self.devices = at.whence if home else at.to

    def __call__(self, m, source, target, lands):
        post, away = self.post, self.at.away[m]
        sent = post.make(source, target, self.devices[m], lands)
        local = pltpu.make_async_copy(source, target, post.local_sems.at[post.n_local])
        post.n_local += 1

        @pl.when(away != 0)
        def _():
            sent.copy.start()

        @pl.when(away == 0)
        def _():
            local.start()

        self.moves.append((away, sent))

        def arrive():
            @pl.when(away != 0)
            def _():
                sent.landing.wait_recv()

            @pl.when(away == 0)
            def _():
                local.wait()

        return arrive

    def finish(self):
        for away, sent in self.moves:
            @pl.when(away != 0)
            def _(sent=sent):
                sent.copy.wait_send()


def meet_swap(at):
    bar = pltpu.get_barrier_semaphore()
    partners = (*at.level, at.z1, at.z2, at.z3)
    for device in partners:
        pl.semaphore_signal(bar, inc=1, device_id=device, device_id_type=MESH)
    for m in range(2):
        @pl.when(at.away[m] != 0)
        def _(m=m):
            for device in (at.to[m], at.whence[m]):
                pl.semaphore_signal(bar, inc=1, device_id=device, device_id_type=MESH)

    pl.semaphore_wait(bar, len(partners) + sum(2 * ((away + 18) // 19) for away in at.away))


class Deal:
    def __init__(self, post, at, shards, j, outs):
        self.post, self.sent, self.kept = post, [], []
        gate, up, down = shards
        part = gate.shape[1] // 4
        chunk = part // 4
        for device, k in ((at.row, at.fy), (at.cross, at.fd), (at.core, at.fs), (None, at.f)):
            lane = pl.ds(pl.multiple_of(k * part + j * chunk, LANES), chunk)
            for source, out in zip((gate.at[:, lane], up.at[:, lane], down.at[lane]), outs):
                if device is None:
                    self.kept.append(post.keep(source, out.at[at.f]))
                else:
                    self.sent.append(post.send(source, out.at[at.f], device, out.at[k]))

    def finish(self):
        for sent in self.sent:
            sent.arrive()


HALVES = [pl.ds(half * ROWS, ROWS) for half in range(2)]


def start_kernel(post, at, ins, outs, scratch):
    hidden, marks, gains, wqkv, wo, *shards = ins
    x_own, attn_in, all_marks, all_gains, qkv_all, out_all, *levels_out = outs
    rows_in, rows_out, gain_buf = scratch
    f, c = at.f, at.c
    meet_swap(at)
    swap = Swap(post, at)
    x_moved = [
        swap(m, hidden.at[half], rows_in.at[half], rows_in.at[half]) for m, half in enumerate(HALVES)
    ]
    heads = wqkv.shape[1] // 4
    span = wo.shape[0] // 4
    first = []
    for device, k in ((at.row, at.fy), (at.cross, at.fd), (at.core, at.fs)):
        lane = pl.ds(pl.multiple_of(k * heads, LANES), heads)
        first.append(post.send(wqkv.at[:, lane], qkv_all.at[f, c], device, qkv_all.at[k, c]))
        row = pl.ds(pl.multiple_of(k * span, LANES), span)
        first.append(post.send(wo.at[row], out_all.at[f, c], device, out_all.at[k, c]))
    lane = pl.ds(pl.multiple_of(f * heads, LANES), heads)
    own = [post.keep(wqkv.at[:, lane], qkv_all.at[f, c])]
    row = pl.ds(pl.multiple_of(f * span, LANES), span)
    own.append(post.keep(wo.at[row], out_all.at[f, c]))
    marks_moved = [
        swap(m, marks, all_marks.at[m, at.to_f[m]], all_marks.at[m, f]) for m in range(2)
    ]

    mine = gain_buf.at[f, c]
    post.settle([post.keep(gains, mine)])
    step = post.send(mine, mine, at.core, gain_buf.at[at.fs, c])
    step.arrive()
    pair = gain_buf.at[pl.ds(f // 2 * 2, 2), c]
    step = post.send(pair, pair, at.row, gain_buf.at[pl.ds(at.fy // 2 * 2, 2), c])
    step.arrive()
    step = post.send(gain_buf.at[:, c], gain_buf.at[:, c], at.z1, gain_buf.at[:, at.c1])
    step.arrive()
    pair = gain_buf.at[:, pl.ds(c // 2 * 2, 2)]
    step = post.send(pair, pair, at.z2, gain_buf.at[:, pl.ds(at.c2 // 2 * 2, 2)])
    step.arrive()
    gain = jnp.concatenate([gain_buf[i // 4, i % 4, 0:1, :] for i in range(16)], axis=1)
    post.keep(gain_buf, all_gains)

    post.settle(own)
    for sent in first:
        sent.arrive()

    spread = Spread(post, at, attn_in)
    levels = []

    def climb():
        for out in (qkv_all, out_all):
            here, there = out.at[:, c], out.at[:, at.c2]
            far = post.send(here, here, at.z2, there)
            close = post.send(here, here, at.z1, out.at[:, at.c1])
            levels.append((far, close, there, out))

    for half in range(2):
        x_moved[half]()
        if half == 1:
            climb()
        normed, _ = normed_rows(rows_in[HALVES[half]].astype(WIDE))
        rows_out[HALVES[half]] = (normed * gain).astype(NARROW)
        spread.own(half, rows_out.at[HALVES[half]])
        post.keep(rows_in.at[HALVES[half]], x_own.at[HALVES[half]])

    for arrive in marks_moved:
        arrive()
    here = all_marks.at[:, f]
    small = post.send(here, here, at.core, all_marks.at[:, at.fs])
    spread.relay(0)
    small.arrive()
    pair = all_marks.at[:, pl.ds(f // 2 * 2, 2)]
    smaller = post.send(pair, pair, at.row, all_marks.at[:, pl.ds(at.fy // 2 * 2, 2)])
    spread.relay(1)
    forwards = []
    for far, close, there, out in levels:
        far.arrive()
        forwards.append((post.send(there, there, at.z1, out.at[:, at.c3]), close))
    deals = [Deal(post, at, shards, j, levels_out[3 * j : 3 * j + 3]) for j in range(2)]
    spread.corner()
    for last, close in forwards:
        last.arrive()
        close.arrive()
    spread.finish()
    smaller.arrive()
    for deal in deals:
        deal.finish()
    swap.finish()


def rope(values, cos_full, sin_full):
    return values * cos_full + pltpu.roll(values, HALF, 1) * sin_full


def rope_back(values, cos_full, sin_full):
    return values * cos_full - pltpu.roll(values, HALF, 1) * sin_full


def rope_full(marks, m, inverse):
    angle = marks.T[:, 2 + m : 3 + m] * inverse
    low = lax.broadcasted_iota(jnp.int32, angle.shape, 1) < HALF
    turns = jnp.floor(angle * (2.0 / math.pi) + 0.5)
    rest = ((angle - turns * 1.5703125) - turns * 4.837512969970703125e-4) - turns * 7.54978995489188e-8
    square = rest * rest
    sine = rest + rest * square * (
        -1.6666654611e-1 + square * (8.3321608736e-3 - square * 1.9515295891e-4)
    )
    cosine = 1.0 - 0.5 * square + square * square * (
        4.166664568298827e-2 + square * (-1.388731625493765e-3 + square * 2.443315711809948e-5)
    )
    quadrant = turns + jnp.where(low, 1.0, 0.0)
    half = jnp.floor(quadrant * 0.5)
    odd = quadrant - 2.0 * half > 0.5
    negative = half - 2.0 * jnp.floor(half * 0.5) > 0.5
    table = jnp.where(odd, cosine, sine)
    table = jnp.where(negative, -table, table)
    turned_table = pltpu.roll(table, HALF, 1)
    return jnp.where(low, table, turned_table), jnp.where(low, -turned_table, table)


def quarter(at, i):
    return (i + at.c) % 2 * 2 + i // 2


def mm(left, right, dims=((1,), (0,))):
    return lax.dot_general(left, right, (dims, ((), ())), preferred_element_type=WIDE)


TILE = 256

def softmax_tile(query, key, id_col, id_row):
    raw = mm(query, key, ((1,), (1,))) * SCALE
    raw = jnp.where(id_row <= id_col, raw, MASKED)
    top = jnp.max(raw, axis=-1, keepdims=True)
    exponent = jnp.exp(raw - top)
    return exponent * (1.0 / jnp.sum(exponent, axis=-1, keepdims=True))


def id_rows(at, marks, m, tiles):
    return jnp.concatenate([marks[m, quarter(at, i), m : m + 1, :] for i in range(tiles)], axis=1)


def attend_kernel(post, at, ins, outs, scratch):
    attn_in, qkv_all, inverse_in, marks_in, cot, *shards = ins[:8]
    levels = ins[8:]
    queries, keys, values, mixed, dy, cot_own, *more = outs
    climbed, dealt = more[: len(levels)], more[len(levels) :]
    rows, weight, inverse, marks, q_buf, k_buf, v_buf, mix_buf = scratch
    meet_swap(at)
    swap = Swap(post, at)
    cot_moved = [
        swap(m, cot.at[half], cot_own.at[half], cot_own.at[half]) for m, half in enumerate(HALVES)
    ]
    local = [
        post.keep(inverse_in, inverse),
        post.keep(marks_in, marks),
        post.keep(qkv_all, weight),
        post.keep(attn_in.at[:, pl.ds(0, ROWS)], rows.at[0]),
        post.keep(attn_in.at[:, pl.ds(ROWS, ROWS)], rows.at[1]),
    ]
    spread = Spread(post, at, dy)
    deal = Deal(post, at, shards, 2, dealt)
    post.settle(local)
    width = rows.shape[-1]
    columns = weight.shape[-1]
    for m in range(2):
        for i in range(4):
            q = quarter(at, i)
            here = rows[m, pl.ds(2 * q, 2)].reshape(TILE, width)
            projected = mm(here, weight[...].reshape(width, columns))
            cos_full, sin_full = rope_full(marks[m, q], m, inverse[0:1])
            place = pl.ds(i * TILE, TILE)
            for g in range(2):
                lane = slice(g * HEAD_DIM, (g + 1) * HEAD_DIM)
                q_buf[m, place, lane] = rope(projected[:, lane], cos_full, sin_full).astype(NARROW)
            k_buf[m, place] = rope(projected[:, 256:384], cos_full, sin_full).astype(NARROW)
            v_buf[m, place] = projected[:, 384:512].astype(NARROW)
    for m in range(2):
        for i in range(4):
            n = min(i + 2, 4) * TILE
            q = quarter(at, i)
            id_col = marks[m, q].T[:, m : m + 1]
            id_row = id_rows(at, marks, m, n // TILE)
            for g in range(2):
                lane = slice(g * HEAD_DIM, (g + 1) * HEAD_DIM)
                prob = softmax_tile(
                    q_buf[m, i * TILE : (i + 1) * TILE, lane], k_buf[m, :n], id_col, id_row
                )
                value = mm(prob.astype(NARROW), v_buf[m, :n]).astype(NARROW)
                for h in range(2):
                    mix_buf[2 * q + h, m * ROWS : (m + 1) * ROWS, lane] = value[
                        h * ROWS : (h + 1) * ROWS
                    ]
        if m == 0:
            climbs = [Climb(post, at, level, out) for level, out in zip(levels, climbed)]
    for source, target in ((q_buf, queries), (k_buf, keys), (v_buf, values), (mix_buf, mixed)):
        post.keep(source, target)
    for half in range(2):
        cot_moved[half]()
        spread.own(half, cot_own.at[HALVES[half]])
    spread.relay(0)
    spread.relay(1)
    for climb in climbs:
        climb.forward()
    spread.corner()
    spread.finish()
    for climb in climbs:
        climb.finish()
    deal.finish()
    swap.finish()


def middle_kernel(post, at, ins, outs, scratch):
    mixed, out_all, x_own, gains_in, *shards = ins[:7]
    levels = ins[7:]
    mid_own, ffn_in, *more = outs
    climbed, dealt = more[: len(levels)], more[len(levels) :]
    mix_buf, weight, x_buf, gains, rows_out, *fold_scratch = scratch
    meet((at.side, at.core, at.row, at.cross, at.z1, at.z2))
    local = [
        post.keep(out_all.at[i // 4, i % 4], weight.at[:, pl.ds(i * LANES, LANES)])
        for i in range(16)
    ]
    local += [post.keep(mixed, mix_buf), post.keep(x_own, x_buf), post.keep(gains_in, gains)]
    post.settle(local)
    climbs = [Climb(post, at, level, out) for level, out in zip(levels, climbed)]

    def part(*blocks):
        return mm(jnp.concatenate([mix_buf[block] for block in blocks]), weight[...])

    fold = Fold(post, at, part, fold_scratch)
    fold.first()
    fold.second()
    deal = Deal(post, at, shards, 3, dealt)
    fold.third()
    gain = jnp.concatenate([gains[i // 4, i % 4, 1:2, :] for i in range(16)], axis=1)
    spread = Spread(post, at, ffn_in)
    for half in range(2):
        rows = pl.ds(half * ROWS, ROWS)
        value = fold.held[half] + x_buf[rows].astype(WIDE)
        fold.held[half] = value
        normed, _ = normed_rows(value)
        rows_out[half] = (normed * gain).astype(NARROW)
        spread.own(half, rows_out.at[half])
        post.keep(fold.held.at[half], mid_own.at[rows])
    spread.relay(0)
    for climb in climbs:
        climb.forward()
    spread.relay(1)
    spread.corner()
    spread.finish()
    for climb in climbs:
        climb.finish()
    deal.finish()


def small_arrays(block_ids, positions, attn_gain, ffn_gain):
    micro, _, span = positions.shape
    ids = lax.dynamic_slice_in_dim(block_ids[:, 0], lax.axis_index("ctx") * span, span, 1)
    rows = jnp.concatenate([ids, positions[:, 0]]).astype(WIDE)
    marks = jnp.pad(rows, ((0, 8 - 2 * micro), (0, 0)))
    gains = jnp.pad(jnp.stack([attn_gain, ffn_gain]).astype(WIDE), ((0, 6), (0, 0)))
    return marks, gains


def ffn_kernel(post, at, ins, outs, scratch):
    ffn_in, dy = ins[:2]
    ready = ins[2:10]
    levels = ins[10:]
    hidden, grads_pre, parts, ends_a, *climbed = outs
    x_buf, dy_buf, gate_buf, up_buf, down_buf, act, act_t, staged = scratch
    meet((at.z1, at.z3))
    climbs = [LineClimb(post, at, level, out) for level, out in zip(levels, climbed)]
    local = [post.keep(ffn_in, x_buf), post.keep(dy, dy_buf)]
    weights = list(ready) + list(climbed)

    def load(j):
        slot = j % 2
        gate, up, down = weights[3 * j : 3 * j + 3]
        copies = [post.keep(gate, gate_buf.at[slot]), post.keep(up, up_buf.at[slot])]
        for i in range(16):
            copies.append(
                post.keep(down.at[i // 4, i % 4], down_buf.at[slot, :, pl.ds(i * LANES, LANES)])
            )
        return copies

    loading = load(0)
    post.settle(local)
    width = x_buf.shape[-1]
    saved, sums_0 = [], []
    for j in range(4):
        slot = j % 2
        if loading is None:
            for climb in climbs[:1] if j == 2 else climbs[1:]:
                climb.finish()
            loading = load(j)
        post.settle(loading)
        loading = load(1) if j == 0 else None
        post.settle(saved)

        def rows(i, carry):
            blocks = pl.ds(i * 2, 2)
            x, grad = (buf[blocks].reshape(2 * TILE, width) for buf in (x_buf, dy_buf))
            gate = mm(x, gate_buf[slot].reshape(width, -1))
            up = mm(x, up_buf[slot].reshape(width, -1))
            grad_hidden = mm(grad, down_buf[slot], ((1,), (1,)))
            sig = jax.nn.sigmoid(gate)
            silu = gate * sig
            values = (
                grad_hidden * up * sig * (1.0 + gate * (1.0 - sig)),
                grad_hidden * silu,
                silu * up,
            )
            place = pl.ds(pl.multiple_of(i * 2 * TILE, 2 * TILE), 2 * TILE)
            for k in range(3):
                act[k, blocks] = values[k].astype(NARROW).reshape(2, TILE, -1)
                act_t[k, :, place] = values[k].T.astype(NARROW)
            return carry

        lax.fori_loop(0, 4, rows, 0)
        chunk = act.shape[-1]
        lane = pl.ds(j * chunk, chunk)
        saved = [
            post.keep(act.at[0], grads_pre.at[:, :, lane]),
            post.keep(act.at[1], grads_pre.at[:, :, pl.ds((4 + j) * chunk, chunk)]),
            post.keep(act.at[2], hidden.at[:, :, lane]),
        ]
        for climb in climbs[:1] if j == 1 else climbs[1:] if j == 2 else ():
            climb.last()
        for climb in climbs[:1] if j == 0 else climbs[1:] if j == 1 else ():
            climb.forward()

        def sums(n, carry):
            place = pl.ds(pl.multiple_of(n * TILE, TILE), TILE)
            x = x_buf[:, :, place].reshape(8 * TILE, TILE)
            grad = dy_buf[:, :, place].reshape(8 * TILE, TILE)
            both = mm(act_t[0:2].reshape(2 * chunk, -1), x).astype(NARROW)
            for k, value in enumerate((both[:chunk], both[chunk:], mm(act_t[2], grad).astype(NARROW))):
                staged[k, 2 * n] = value[:, :LANES]
                staged[k, 2 * n + 1] = value[:, LANES:]
            return carry

        lax.fori_loop(0, 8, sums, 0)
        stored = [
            post.keep(staged.at[k, pl.ds(4 * fl, 4)], parts.at[3 * j + k, fl])
            for k in range(3)
            for fl in range(4)
        ]
        if j < 2:
            post.settle(stored)
            sums_0.append(Ends(post, at, parts, 0, ends_a, 3 * j, (3, 1)[j]))
        else:
            saved += stored
    for step in sums_0:
        step.finish()


class Descend:
    def __init__(self, post, at, pieces, got):
        self.near = post.send(pieces.at[:, at.c1], got.at[0], at.z1, got.at[0])
        self.next = post.send(pieces.at[:, at.c3], got.at[1], at.z1, got.at[1])

    def finish(self):
        self.near.arrive()
        self.next.arrive()


def norm_back_rows(grad, values, gain):
    normed, factor = normed_rows(values)
    scaled = grad * gain
    inner_mean = jnp.mean(scaled * normed, axis=-1, keepdims=True)
    return factor * (scaled - normed * inner_mean), jnp.sum(grad * normed, axis=0, keepdims=True)


def back_kernel(post, at, ins, outs, scratch):
    grads_pre, mid_own, cot_own, gains_in, parts, ends_a, *weights = ins
    grad_mid_own, grad_mid, gain_part, ends_c, mates_b, mates_e = outs
    pre_buf, weight, mid_buf, cot_buf, gains, rows_out, gain_out = scratch[:7]
    bufs_1, bufs_e, fold_scratch = scratch[7:9], scratch[9:11], scratch[11:]
    meet((at.side, at.core, at.row, at.z1, at.z3))
    downs = [
        Middle(post, at, 1, parts, 0, ends_a, mates_b, *bufs_1),
        Ends(post, at, parts, 4, ends_c),
    ]
    chunk = pre_buf.shape[-1] // 8
    local = [post.keep(grads_pre, pre_buf)]
    for a in range(2):
        for j in range(4):
            place = pl.ds((4 * a + j) * chunk, chunk)
            local.append(post.keep(weights[4 * a + j], weight.at[:, :, :, place]))
    local += [post.keep(mid_own, mid_buf), post.keep(cot_own, cot_buf), post.keep(gains_in, gains)]
    post.settle(local)
    width = mid_buf.shape[-1]

    def part(*blocks):
        rows = jnp.concatenate([pre_buf[block] for block in blocks])
        return mm(rows, weight[...].reshape(width, -1), ((1,), (1,)))

    downs[0].send()
    fold = Fold(post, at, part, fold_scratch)
    fold.first()
    fold.second()
    fold.third()
    gain = jnp.concatenate([gains[i // 4, i % 4, 1:2, :] for i in range(16)], axis=1)
    spread = Spread(post, at, grad_mid)
    total = jnp.zeros((1, width), WIDE)
    for half in range(2):
        rows = HALVES[half]
        back, piece = norm_back_rows(fold.held[half], mid_buf[rows], gain)
        total = total + piece
        value = cot_buf[rows].astype(WIDE) + back
        fold.held[half] = value
        rows_out[half] = value.astype(NARROW)
        spread.own(half, rows_out.at[half])
        post.keep(fold.held.at[half], grad_mid_own.at[rows])
    gain_out[...] = jnp.broadcast_to(total, gain_out.shape)
    post.keep(gain_out, gain_part)
    downs[1].finish(2)
    downs.append(Middle(post, at, 1, parts, 4, ends_c.at[pl.ds(0, 2)], mates_e, *bufs_e))
    spread.relay(0)
    downs[2].send()
    spread.relay(1)
    spread.corner()
    spread.finish()
    for down in downs:
        down.finish()


def attend_back_kernel(post, at, ins, outs, scratch):
    (
        grad_mid, queries, keys, values, marks_in, inverse_in, out_all, mixed, attn_in, hidden, mid_own, parts,
        ends_a, ends_c, mates_b, mates_e, *downs_in
    ) = ins
    grad_proj, parts_q, sums_o, out_home, ends_d, mates_c, outer_b, outer_e, first_sums = outs
    (
        gm_buf, q_buf, k_buf, v_buf, marks, inverse, weight, mix_buf, hid_buf, down_buf, gp_buf, gk_buf, gv_buf,
        staged, staged_o, got_o, far_o, end_o, mid_buf, out_buf
    ) = scratch[:20]
    bufs_1, bufs_2, bufs_e, bufs_own = scratch[20:22], scratch[22:24], scratch[24:26], scratch[26:29]
    fold_scratch = scratch[29:]
    meet_swap(at)
    swap = Swap(post, at, home=True)
    steps = [
        Middle(post, at, 1, parts, 6, ends_c.at[pl.ds(2, 3)], mates_c, *bufs_1),
        Middle(post, at, 2, parts, 0, mates_b, outer_b, *bufs_2),
        Middle(post, at, 2, parts, 4, mates_e, outer_e, *bufs_e),
        Ends(post, at, parts, 9, ends_d),
    ]

    chunk = hid_buf.shape[-1] // 4
    early = [post.keep(hidden, hid_buf)]
    for j in range(4):
        for i in range(16):
            target = down_buf.at[pl.ds(j * chunk, chunk), pl.ds(i * LANES, LANES)]
            early.append(post.keep(downs_in[j].at[i // 4, i % 4], target))
    late = [
        post.keep(source, target)
        for source, target in (
            (grad_mid, gm_buf), (queries, q_buf), (keys, k_buf), (values, v_buf), (marks_in, marks),
            (inverse_in, inverse), (mixed, mix_buf), (mid_own, mid_buf),
        )
    ]
    late += [
        post.keep(out_all.at[i // 4, i % 4], weight.at[:, pl.ds(i * LANES, LANES)])
        for i in range(16)
    ]
    post.settle(early)
    for step in steps[:3]:
        step.send()

    def part(*blocks):
        return mm(jnp.concatenate([hid_buf[block] for block in blocks]), down_buf[...])

    fold = Fold(post, at, part, fold_scratch)
    fold.first()
    post.settle(late)

    def fetch(n):
        place = pl.ds(n * TILE, TILE)
        return post.keep(attn_in.at[:, :, place], column(n))

    def column(n):
        return hid_buf.at[:, :, pl.ds(n % 2 * TILE, TILE)]

    mix_t, gp_t = down_buf.at[pl.ds(512, 256)], down_buf.at[pl.ds(0, 512)]
    fetched = fetch(0)
    width = gm_buf.shape[-1]
    for i in range(8):
        mix_t[:, i * TILE : (i + 1) * TILE] = mix_buf[i].astype(WIDE).T.astype(NARROW)
    for n in range(8):
        place = slice(n * TILE, (n + 1) * TILE)
        value = mm(mix_t[...], gm_buf[:, :, place].reshape(8 * TILE, TILE)).astype(NARROW)
        for h in range(2):
            block = 2 * n + h
            staged_o[block // 4, block % 4] = value[:, h * LANES : (h + 1) * LANES]
    step_o = Descend(post, at, staged_o, got_o)
    for m in range(2):
        for i in range(4):
            q = quarter(at, i)
            n = min(i + 2, 4) * TILE
            place = slice(i * TILE, (i + 1) * TILE)
            id_col = marks[m, q].T[:, m : m + 1]
            id_row = id_rows(at, marks, m, n // TILE)
            cos_full, sin_full = rope_full(marks[m, q], m, inverse[0:1])
            rows = gm_buf[pl.ds(2 * q, 2), m * ROWS : (m + 1) * ROWS].reshape(TILE, width)
            grad_mixed = mm(rows, weight[...], ((1,), (1,))).astype(NARROW)
            for g in range(2):
                lane = slice(g * HEAD_DIM, (g + 1) * HEAD_DIM)
                query = q_buf[m, place, lane]
                prob = softmax_tile(query, k_buf[m, :n], id_col, id_row)
                grad = grad_mixed[:, lane]
                grad_prob = mm(grad, v_buf[m, :n], ((1,), (1,)))
                inner = jnp.sum(grad_prob * prob, axis=-1, keepdims=True)
                grad_scores = (SCALE * prob * (grad_prob - inner)).astype(NARROW)
                grad_query = mm(grad_scores, k_buf[m, :n])
                grad_key = mm(grad_scores, query, ((0,), (0,)))
                grad_value = mm(prob.astype(NARROW), grad, ((0,), (0,)))
                if i == 0 and g == 0:
                    gk_buf[:n], gv_buf[:n] = grad_key, grad_value
                    gk_buf[n:], gv_buf[n:] = (jnp.zeros_like(gk_buf[n:]),) * 2
                else:
                    gk_buf[:n] = gk_buf[:n] + grad_key
                    gv_buf[:n] = gv_buf[:n] + grad_value
                done = rope_back(grad_query, cos_full, sin_full).astype(NARROW)
                for h in range(2):
                    gp_buf[2 * q + h, m * ROWS : (m + 1) * ROWS, lane] = done[h * ROWS : (h + 1) * ROWS]
            if m == 1 and i == 1:
                fold.third()
                for half in HALVES:
                    k = half.start // ROWS
                    out_buf[half] = (fold.held[k] + mid_buf[half]).astype(NARROW)
                moved = [
                    swap(k, out_buf.at[half], out_home.at[half], out_home.at[half])
                    for k, half in enumerate(HALVES)
                ]
        for i in range(4):
            q = quarter(at, i)
            place = slice(i * TILE, (i + 1) * TILE)
            cos_full, sin_full = rope_full(marks[m, q], m, inverse[0:1])
            done = (
                rope_back(gk_buf[place], cos_full, sin_full).astype(NARROW),
                gv_buf[place].astype(NARROW),
            )
            for k in range(2):
                lane = slice((2 + k) * HEAD_DIM, (3 + k) * HEAD_DIM)
                for h in range(2):
                    gp_buf[2 * q + h, m * ROWS : (m + 1) * ROWS, lane] = done[k][h * ROWS : (h + 1) * ROWS]
        if m == 0:
            fold.second()
    post.keep(gp_buf, grad_proj)
    for i in range(8):
        place = slice(i * TILE, (i + 1) * TILE)
        gp_t[:, place] = gp_buf[i].astype(WIDE).T.astype(NARROW)
    steps[1].finish()
    early = Own(
        post, at, parts, 0, 3,
        ((ends_a.at[pl.ds(0, 3)],), (mates_b.at[pl.ds(0, 3)],), (outer_b.at[pl.ds(0, 3)],)), *bufs_own,
    )
    for n in range(8):
        post.settle([fetched])
        if n < 7:
            fetched = fetch(n + 1)
        other = mm(gp_t[...], column(n)[...].reshape(8 * TILE, TILE)).astype(NARROW)
        for h in range(2):
            block = 2 * n + h
            staged[block // 4, block % 4] = other[:, h * LANES : (h + 1) * LANES]
    post.keep(staged, parts_q)
    early.add()
    trades = []
    for p in range(3):
        post.keep(bufs_own[0].at[p, at.f], first_sums.at[at.f, p])
        for device, k in ((at.row, at.fy), (at.cross, at.fd), (at.core, at.fs)):
            trades.append(
                post.send(bufs_own[0].at[p, k], first_sums.at[at.f, p], device, first_sums.at[k, p])
            )
    step_o.finish()
    for k in range(4):
        value = staged_o[k, at.c2].astype(WIDE) + got_o[1, k].astype(WIDE)
        far_o[k] = value.astype(NARROW)
    sent_o = post.send(far_o, end_o, at.z2, end_o)
    sent_o.arrive()
    for k in range(4):
        value = staged_o[k, at.c].astype(WIDE) + got_o[0, k].astype(WIDE) + end_o[k].astype(WIDE)
        got_o[1, k] = value.astype(NARROW)
    post.keep(got_o.at[1], sums_o)
    for arrive in moved:
        arrive()
    swap.finish()
    for sent in trades:
        sent.arrive()
    steps.pop(1)
    for step in steps:
        step.finish()


class Own:
    def __init__(self, post, at, parts, first, n, pieces, own, one, two):
        self.post, self.at, self.first, self.n = post, at, first, n
        self.own, self.one, self.two = own, one, two
        self.pieces = pieces
        count = 1 + max(len(pieces[0]) + len(pieces[1]), len(pieces[2]))
        self.sems = [post.local_sems.at[post.n_local + k] for k in range(count)]
        post.n_local += count
        self.parts = parts

        @pl.when(at.is_mid)
        def _():
            for copy in self.mid_copies():
                copy.start()

        @pl.when(at.is_end)
        def _():
            for copy in self.end_copies():
                copy.start()

    def laid(self, arrays, index, target):
        place, pairs = self.first, []
        for array in arrays:
            n = array.shape[0]
            source = array if index is None else array.at[:, :, index]
            pairs.append((source, target.at[pl.ds(place, n)]))
            place += n
        return pairs

    def copies(self, pairs):
        rows = pl.ds(self.first, self.n)
        pairs = [(self.parts.at[rows, :, self.at.c], self.own.at[rows])] + pairs
        return [pltpu.make_async_copy(*pair, sem) for pair, sem in zip(pairs, self.sems)]

    def mid_copies(self):
        c = self.at.c
        ends, mates, _ = self.pieces
        return self.copies(self.laid(ends, 2 * (c - 1), self.one) + self.laid(mates, 2 - c, self.two))

    def end_copies(self):
        return self.copies(self.laid(self.pieces[2], None, self.two))

    def add(self):
        def both(p, carry):
            value = self.own[p].astype(WIDE) + self.one[p].astype(WIDE) + self.two[p].astype(WIDE)
            self.own[p] = value.astype(NARROW)
            return carry

        def single(p, carry):
            self.own[p] = (self.own[p].astype(WIDE) + self.two[p].astype(WIDE)).astype(NARROW)
            return carry

        @pl.when(self.at.is_mid)
        def _():
            for copy in self.mid_copies():
                copy.wait()
            lax.fori_loop(self.first, self.first + self.n, both, 0)

        @pl.when(self.at.is_end)
        def _():
            for copy in self.end_copies():
                copy.wait()
            lax.fori_loop(self.first, self.first + self.n, single, 0)


def end_kernel(post, at, ins, outs, scratch):
    (
        grad_proj, qkv_all, x_own, gains_in, grad_mid_own, gain_ffn_part, parts, parts_q, sums_o,
        ends_a, ends_c, ends_d, mates_b, mates_c, mates_e, outer_b, outer_e
    ) = ins
    grad_home, gain_sums, mates_d, outer_c, outer_d, *home_sums = outs
    (
        gp_buf, weight, x_buf, gains, mid_buf, rows_out, gain_buf, gain_got, own_ffn, one_ffn, two_ffn,
        own_q, far_q, got_q, end_q
    ) = scratch[:15]
    bufs_1, bufs_2, bufs_3, fold_scratch = scratch[15:17], scratch[17:19], scratch[19:21], scratch[21:]
    f, c = at.f, at.c
    meet_swap(at)
    step_q = Descend(post, at, parts_q, got_q)
    steps = [
        Middle(post, at, 1, parts, 9, ends_d, mates_d, *bufs_1),
        Middle(post, at, 2, parts, 6, mates_c, outer_c, *bufs_2),
    ]
    swap = Swap(post, at, home=True)
    early = Own(
        post, at, parts, 3, 3,
        (
            (ends_a.at[pl.ds(3, 1)], ends_c.at[pl.ds(0, 2)]),
            (mates_b.at[pl.ds(3, 1)], mates_e),
            (outer_b.at[pl.ds(3, 1)], outer_e),
        ),
        own_ffn, one_ffn, two_ffn,
    )
    fold_in = [
        post.keep(grad_proj, gp_buf), post.keep(qkv_all, weight), post.keep(x_own, x_buf),
        post.keep(gains_in, gains), post.keep(grad_mid_own, mid_buf),
        post.keep(gain_ffn_part, gain_buf),
    ]
    later = [
        post.keep(parts_q.at[:, c], own_q), post.keep(parts_q.at[:, at.c2], far_q),
    ]
    for step in steps:
        step.send()

    def add_far(far, came):
        for k in range(4):
            far[k] = (far[k].astype(WIDE) + came[k].astype(WIDE)).astype(NARROW)

    def add_own(own, one, end):
        for k in range(4):
            own[k] = (own[k].astype(WIDE) + one[k].astype(WIDE) + end[k].astype(WIDE)).astype(NARROW)

    trades = []
    places = ((at.row, at.fy), (at.cross, at.fd), (at.core, at.fs))

    def trade(mine, out, *place):
        post.keep(mine(f), out.at[(f, *place)])
        for device, k in places:
            trades.append(
                post.send(mine(k), out.at[(f, *place)], device, out.at[(k, *place)])
            )

    def trade_ffn(p):
        trade(lambda k: own_ffn.at[p, k], home_sums[p % 3], p // 3 - 1)

    post.settle(fold_in)
    width = x_buf.shape[-1]

    def part(*blocks):
        rows = jnp.concatenate([gp_buf[block] for block in blocks])
        return mm(rows, weight[...].reshape(width, -1), ((1,), (1,)))

    fold = Fold(post, at, part, fold_scratch)
    fold.first()
    early.add()
    fold.second()
    post.settle(later)
    step_q.finish()
    add_far(far_q, got_q.at[1])
    sent_q = post.send(far_q, end_q, at.z2, end_q)
    fold.third()
    gain = jnp.concatenate([gains[i // 4, i % 4, 0:1, :] for i in range(16)], axis=1)
    total = jnp.zeros((1, width), WIDE)
    moved = []
    for half in range(2):
        rows = HALVES[half]
        back, piece = norm_back_rows(fold.held[half], x_buf[rows].astype(WIDE), gain)
        total = total + piece
        rows_out[rows] = (mid_buf[rows] + back).astype(NARROW)
        moved.append(swap(half, rows_out.at[rows], grad_home.at[rows], grad_home.at[rows]))
    gain_buf[0:1] = total
    gain_sent = [
        post.send(gain_buf, gain_got.at[k], device, gain_got.at[k])
        for k, device in enumerate(at.level)
    ]
    steps[0].finish()
    steps.append(Middle(post, at, 2, parts, 9, mates_d, outer_d, *bufs_3))
    steps[2].send()
    for p in range(3, 6):
        trade_ffn(p)
    trade(lambda k: sums_o.at[k], home_sums[3])
    sent_q.arrive()
    add_own(own_q, got_q.at[0], end_q)
    trade(lambda k: own_q.at[k], home_sums[4])
    steps[1].finish()
    late = Own(
        post, at, parts, 6, 3, ((ends_c.at[pl.ds(2, 3)],), (mates_c,), (outer_c,)), own_ffn, one_ffn, two_ffn
    )
    late.add()
    for p in range(6, 9):
        trade_ffn(p)
    for sent in gain_sent:
        sent.arrive()
        sent.leave()
    post.out = [sent for sent in post.out if not any(sent is gone for gone in gain_sent)]
    gain_buf[...] = gain_buf[...] + sum(gain_got[k] for k in range(7))
    gain_sent = [
        post.send(gain_buf, gain_got.at[7 + k], device, gain_got.at[7 + k])
        for k, device in enumerate((at.z1, at.z2, at.z3))
    ]
    steps[2].finish()
    last = Own(
        post, at, parts, 9, 3, ((ends_d,), (mates_d,), (outer_d,)), own_ffn, one_ffn, two_ffn
    )
    last.add()
    for p in range(9, 12):
        trade_ffn(p)
    for sent in gain_sent:
        sent.arrive()
        sent.leave()
    post.out = [sent for sent in post.out if not any(sent is gone for gone in gain_sent)]
    gain_buf[...] = gain_buf[...] + sum(gain_got[7 + k] for k in range(3))
    place = pl.ds(pl.multiple_of((f * 4 + c) * LANES, LANES), LANES)
    post.keep(gain_buf.at[:, place], gain_sums)
    for sent in trades:
        sent.arrive()
    for arrive in moved:
        arrive()
    swap.finish()


def home_kernel(*refs):
    first, gate, up, down, out, qkv, gate_out, up_out, down_out, qkv_out, out_out = refs[:11]
    gate_buf, up_buf, down_buf, out_buf, qkv_buf, sems = refs[11:]
    pairs = []
    for a, (array, buf) in enumerate(((gate, gate_buf), (up, up_buf), (down, down_buf))):
        pairs.append((first.at[:, a], buf.at[:, 0]))
        pairs.append((array, buf.at[:, pl.ds(1, 3)]))
    pairs += [(out, out_buf), (qkv, qkv_buf)]
    copies = [pltpu.make_async_copy(*pair, sems.at[n]) for n, pair in enumerate(pairs)]
    for copy in copies:
        copy.start()
    for a, (buf, target) in enumerate(((gate_buf, gate_out), (up_buf, up_out))):
        for copy in copies[2 * a : 2 * a + 2]:
            copy.wait()
        for n in range(8):
            value = buf[n // 2, pl.ds(n % 2 * 2, 2)].reshape(512, LANES)
            target[:, pl.ds(n * 512, 512)] = value.astype(WIDE).T
    for copy in copies[4:]:
        copy.wait()
    for n in range(4):
        rows = pl.ds(n * 1024, 1024)
        down_out[rows] = down_buf[n].reshape(1024, LANES).astype(WIDE)
        out_out[pl.ds(n * 256, 256)] = out_buf[n].astype(WIDE)
        qkv_out[:, pl.ds(n * 512, 512)] = qkv_buf[n].astype(WIDE).T


def near_body(
    hidden_in, cotangent, block_ids, positions, attn_gain, wqkv, wo, ffn_gain, w_gate, w_up, w_down
):
    micro, _, rows, width = hidden_in.shape
    own = micro * rows
    ff = w_gate.shape[1]
    chunk = ff // 16
    shards = (w_gate, w_up, w_down)
    marks, gains = small_arrays(block_ids, positions, attn_gain, ffn_gain)
    inverse = THETA ** (-(jnp.arange(HALF, dtype=WIDE) * 2.0 / HEAD_DIM))
    inverse = jnp.broadcast_to(jnp.concatenate([inverse, inverse]), (8, HEAD_DIM))
    level_shapes = [shape(4, LANES, chunk), shape(4, LANES, chunk), shape(4, chunk, LANES)]
    whole_shapes = [shape(4, 4, LANES, chunk), shape(4, 4, LANES, chunk), shape(4, 4, chunk, LANES)]
    gains_shape = (4, 4, *gains.shape)
    x_own, attn_in, all_marks, all_gains, qkv_all, out_all, *level = call(
        start_kernel,
        "start",
        [
            shape(own, width), shape(8, own, width),
            shape(2, 4, *marks.shape, dtype=WIDE), shape(*gains_shape, dtype=WIDE),
            shape(4, 4, LANES, wqkv.shape[1] // 4), shape(4, 4, wo.shape[0] // 4, LANES),
            *level_shapes, *level_shapes,
        ],
        (hidden_in.reshape(own, width), marks, gains, wqkv, wo, *shards),
        [pltpu.VMEM((own, width), NARROW), pltpu.VMEM((own, width), NARROW), pltpu.VMEM(gains_shape, WIDE)],
        72, 24, 1,
    )
    queries, keys, values, mixed, dy, cot_own, *more = call(
        attend_kernel,
        "attend",
        [
            shape(2, 1024, 256), shape(2, 1024, 128), shape(2, 1024, 128), shape(8, own, 256),
            shape(8, own, width), shape(own, width), *whole_shapes, *level_shapes,
        ],
        (attn_in, qkv_all, inverse, all_marks, cotangent.reshape(own, width), *shards, *level[:3]),
        [
            pltpu.VMEM((2, 8, ROWS, width), NARROW), pltpu.VMEM(qkv_all.shape, NARROW),
            pltpu.VMEM(inverse.shape, WIDE), pltpu.VMEM(all_marks.shape, WIDE),
            pltpu.VMEM((2, 1024, 256), NARROW), pltpu.VMEM((2, 1024, 128), NARROW),
            pltpu.VMEM((2, 1024, 128), NARROW), pltpu.VMEM((8, own, 256), NARROW),
        ],
        40, 24, 2,
    )
    whole, level = more[:3], level + more[3:]
    mid_own, ffn_in, *more = call(
        middle_kernel,
        "middle",
        [
            shape(own, width, dtype=WIDE), shape(8, own, width), *whole_shapes, *whole_shapes[:2],
            *level_shapes,
        ],
        (mixed, out_all, x_own, all_gains, *shards, *level[3:8]),
        [
            pltpu.VMEM((8, own, 256), NARROW), pltpu.VMEM((256, width), NARROW),
            pltpu.VMEM((own, width), NARROW), pltpu.VMEM(gains_shape, WIDE),
            pltpu.VMEM((2, ROWS, width), NARROW), *Fold.scratch(width),
        ],
        52, 32, 3,
    )
    whole, level = whole + more[:5], level + more[5:]
    hidden, grads_pre, parts, ends_a, *more = call(
        ffn_kernel,
        "ffn",
        [
            shape(8, own, ff // 4), shape(8, own, ff // 2), shape(12, 4, 4, chunk, LANES),
            shape(4, 4, 3, chunk, LANES),
            whole_shapes[2], *whole_shapes,
        ],
        (ffn_in, dy, *whole, *level[8:]),
        [
            pltpu.VMEM((8, own, width), NARROW), pltpu.VMEM((8, own, width), NARROW),
            pltpu.VMEM((2, 4, 4, LANES, chunk), NARROW), pltpu.VMEM((2, 4, 4, LANES, chunk), NARROW),
            pltpu.VMEM((2, chunk, width), NARROW), pltpu.VMEM((3, 8, own, chunk), NARROW),
            pltpu.VMEM((3, chunk, 8 * own), NARROW), pltpu.VMEM((3, 16, chunk, LANES), NARROW),
        ],
        48, 160, 4,
    )
    whole = whole + more
    fold_scratch = Fold.scratch(width)
    grad_mid_own, grad_mid, gain_ffn_part, ends_c, mates_b, mates_e = call(
        back_kernel,
        "back",
        [
            shape(own, width, dtype=WIDE), shape(8, own, width), shape(8, width, dtype=WIDE),
            shape(5, 4, 3, chunk, LANES), shape(4, 4, 2, chunk, LANES), shape(2, 4, 2, chunk, LANES),
        ],
        (grads_pre, mid_own, cot_own, all_gains, parts, ends_a, *whole[0::3], *whole[1::3]),
        [
            pltpu.VMEM((8, own, ff // 2), NARROW), pltpu.VMEM((4, 4, LANES, ff // 2), NARROW),
            pltpu.VMEM((own, width), WIDE), pltpu.VMEM((own, width), NARROW),
            pltpu.VMEM(gains_shape, WIDE), pltpu.VMEM((2, ROWS, width), NARROW),
            pltpu.VMEM((8, width), WIDE), *middle_scratch(1, 4), *middle_scratch(1, 2), *fold_scratch,
        ],
        48, 32, 5,
    )
    grad_proj, parts_q, sums_o, out_home, ends_d, mates_c, outer_b, outer_e, first_sums = call(
        attend_back_kernel,
        "attend_back",
        [
            shape(8, own, 512), shape(4, 4, 512, LANES), shape(4, 256, LANES),
            shape(own, width),
            shape(3, 4, 3, chunk, LANES), shape(3, 4, 2, chunk, LANES), shape(4, 4, chunk, LANES),
            shape(2, 4, chunk, LANES), shape(4, 3, chunk, LANES),
        ],
        (
            grad_mid, queries, keys, values, all_marks, inverse, out_all, mixed, attn_in, hidden, mid_own, parts,
            ends_a, ends_c, mates_b, mates_e, *whole[2::3],
        ),
        [
            pltpu.VMEM((8, own, width), NARROW), pltpu.VMEM((2, 1024, 256), NARROW),
            pltpu.VMEM((2, 1024, 128), NARROW), pltpu.VMEM((2, 1024, 128), NARROW),
            pltpu.VMEM(all_marks.shape, WIDE), pltpu.VMEM(inverse.shape, WIDE),
            pltpu.VMEM((256, width), NARROW), pltpu.VMEM((8, own, 256), NARROW),
            pltpu.VMEM((8, own, ff // 4), NARROW), pltpu.VMEM((ff // 4, width), NARROW),
            pltpu.VMEM((8, own, 512), NARROW), pltpu.VMEM((1024, 128), WIDE),
            pltpu.VMEM((1024, 128), WIDE),
            pltpu.VMEM((4, 4, 512, LANES), NARROW), pltpu.VMEM((4, 4, 256, LANES), NARROW),
            pltpu.VMEM((2, 4, 256, LANES), NARROW), *[pltpu.VMEM((4, 256, LANES), NARROW)] * 2,
            pltpu.VMEM((own, width), WIDE), pltpu.VMEM((own, width), NARROW), *middle_scratch(1, 3), *middle_scratch(2, 4),
            *middle_scratch(2, 2), *[pltpu.VMEM((3, 4, chunk, LANES), NARROW)] * 3, *fold_scratch,
        ],
        48, 128, 6,
    )
    grad_home, gain_sums, _, _, _, *sums = call(
        end_kernel,
        "end",
        [
            shape(own, width), shape(8, LANES, dtype=WIDE), shape(3, 4, 2, chunk, LANES),
            shape(3, 4, chunk, LANES), shape(3, 4, chunk, LANES),
            *[shape(4, 3, chunk, LANES)] * 3, shape(4, 256, LANES), shape(4, 512, LANES),
        ],
        (
            grad_proj, qkv_all, x_own, all_gains, grad_mid_own, gain_ffn_part, parts, parts_q, sums_o,
            ends_a, ends_c, ends_d, mates_b, mates_c, mates_e, outer_b, outer_e,
        ),
        [
            pltpu.VMEM((8, own, 512), NARROW), pltpu.VMEM(qkv_all.shape, NARROW),
            pltpu.VMEM((own, width), NARROW), pltpu.VMEM(gains_shape, WIDE),
            pltpu.VMEM((own, width), WIDE), pltpu.VMEM((own, width), NARROW),
            pltpu.VMEM((8, width), WIDE), pltpu.VMEM((10, 8, width), WIDE),
            *[pltpu.VMEM((12, 4, chunk, LANES), NARROW)] * 3,
            *[pltpu.VMEM((4, 512, LANES), NARROW)] * 2, pltpu.VMEM((2, 4, 512, LANES), NARROW),
            pltpu.VMEM((4, 512, LANES), NARROW),
            *middle_scratch(1, 3), *middle_scratch(2, 3), *middle_scratch(2, 3), *fold_scratch,
        ],
        88, 72, 7,
    )
    grad_gate, grad_up, grad_down, grad_qkv, grad_out = pl.pallas_call(
        home_kernel,
        out_shape=[
            jax.ShapeDtypeStruct(array.shape, WIDE) for array in (w_gate, w_up, w_down, wqkv, wo)
        ],
        in_specs=[ANYWHERE] * 6,
        scratch_shapes=[
            *[pltpu.VMEM((4, 4, chunk, LANES), NARROW)] * 3, pltpu.VMEM((4, 256, LANES), NARROW),
            pltpu.VMEM((4, 512, LANES), NARROW), pltpu.SemaphoreType.DMA((8,)),
        ],
        compiler_params=pltpu.CompilerParams(vmem_limit_bytes=48 << 20),
        name="home",
    )(first_sums, *sums)
    return (
        out_home.reshape(hidden_in.shape),
        grad_home.reshape(hidden_in.shape),
        gain_sums[0],
        grad_qkv,
        grad_out,
        gain_sums[1],
        grad_gate,
        grad_up,
        grad_down,
    )


def body(*shards):
    inner = KV_HEADS // lax.axis_size("tp")
    near = (lax.axis_size("fsdp"), lax.axis_size("ctx"), lax.axis_size("tp"), inner)
    return (near_body if near == (4, 4, 2, 4) else general_body)(*shards)


def solution(mesh):
    return jax.shard_map(
        body,
        mesh=mesh,
        in_specs=(
            P(None, "fsdp", ("ctx", "tp"), None),
            P(None, "fsdp", ("ctx", "tp"), None),
            P(None, "fsdp", None),
            P(None, "fsdp", "ctx"),
            P(("fsdp", "ctx")),
            P(("fsdp", "ctx"), "tp"),
            P("tp", ("fsdp", "ctx")),
            P(("fsdp", "ctx")),
            P(("fsdp", "ctx"), "tp"),
            P(("fsdp", "ctx"), "tp"),
            P("tp", ("fsdp", "ctx")),
        ),
        out_specs=(
            P(None, "fsdp", ("ctx", "tp"), None),
            P(None, "fsdp", ("ctx", "tp"), None),
            P(("fsdp", "ctx")),
            P(("fsdp", "ctx"), "tp"),
            P("tp", ("fsdp", "ctx")),
            P(("fsdp", "ctx")),
            P(("fsdp", "ctx"), "tp"),
            P(("fsdp", "ctx"), "tp"),
            P("tp", ("fsdp", "ctx")),
        ),
        check_vma=False,
    )
```

```python
import functools
import math

import jax
import jax.numpy as jnp
from jax import lax
from jax.sharding import PartitionSpec as P
from jax.experimental import pallas as pl
from jax.experimental.pallas import tpu as pltpu

HEADS = 16
KV_HEADS = 8
HEAD_DIM = 128


EPS = 1e-05
THETA = 1000000.0
MASKED = -1e30


def rope_tables(position_ids):
    half_dim = HEAD_DIM // 2
    inverse = THETA ** (-(jnp.arange(half_dim, dtype=jnp.float32) * 2.0 / HEAD_DIM))
    angles = position_ids.astype(jnp.float32)[..., None] * inverse
    angles = jnp.concatenate([angles, angles], axis=-1)
    return (jnp.cos(angles), jnp.sin(angles))


def turned(values):
    half_dim = values.shape[-1] // 2
    return jnp.concatenate([-values[..., half_dim:], values[..., :half_dim]], axis=-1)


def turned_back(values):
    half_dim = values.shape[-1] // 2
    return jnp.concatenate([values[..., half_dim:], -values[..., :half_dim]], axis=-1)


def norm_rows(stream, gain_row):
    factor = lax.rsqrt(jnp.mean(stream * stream, axis=-1, keepdims=True) + EPS)
    normed = stream * factor
    return (normed, factor, (normed * gain_row).astype(jnp.bfloat16))


def groups_of(fsdp, inner):
    near = [[high * inner + low for low in range(inner)] for high in range(fsdp // inner)]
    far = [[high * inner + low for high in range(fsdp // inner)] for low in range(inner)]
    return near, far


def general_body(
    hidden_in, cotangent, block_ids, positions, attn_gain, wqkv, wo, ffn_gain, w_gate, w_up, w_down
):
    fsdp, ctx, tp = lax.axis_size("fsdp"), lax.axis_size("ctx"), lax.axis_size("tp")
    inner = KV_HEADS // tp
    outer = fsdp // inner
    near, far = groups_of(fsdp, inner)
    micro, _, rows, width = hidden_in.shape
    score_scale = HEAD_DIM ** (-0.5)
    f_at, c_at = lax.axis_index("fsdp"), lax.axis_index("ctx")
    swap = [
        ((high * inner + low) * ctx + c, (high * inner + c) * ctx + low)
        for high in range(outer)
        for low in range(inner)
        for c in range(ctx)
    ]

    def rehome(array):
        return lax.ppermute(array, ("fsdp", "ctx"), swap)

    def trade(pieces):
        return lax.all_to_all(pieces, "fsdp", 0, 0, axis_index_groups=near)

    def spread(block):
        both = lax.all_gather(block, "tp")
        return lax.all_gather(both, "fsdp", axis_index_groups=near)

    def fold(parts):
        half = lax.psum_scatter(
            parts.astype(jnp.bfloat16), "fsdp", scatter_dimension=0, axis_index_groups=near
        )
        return lax.psum_scatter(half, "tp", scatter_dimension=0).astype(jnp.float32)

    def gather_levels(pieces):
        up = lax.all_gather(pieces, "ctx")
        if outer == 1:
            return up[None]
        return lax.all_gather(up, "fsdp", axis_index_groups=far)

    def scatter_levels(pieces):
        if outer == 1:
            pieces = pieces[0]
        else:
            pieces = lax.psum_scatter(pieces, "fsdp", scatter_dimension=0, axis_index_groups=far)
        return lax.psum_scatter(pieces, "ctx", scatter_dimension=0)

    def fetch_columns(shard):
        block, cols = shard.shape
        pieces = trade(shard.reshape(block, inner, cols // inner).transpose(1, 0, 2))
        whole = gather_levels(pieces).transpose(0, 2, 1, 3, 4)
        return whole.reshape(-1, cols // inner)

    def fetch_rows(shard):
        length, block = shard.shape
        pieces = trade(shard.reshape(inner, length // inner, block))
        whole = gather_levels(pieces).transpose(3, 0, 2, 1, 4)
        return whole.reshape(length // inner, -1)

    def return_columns(grad):
        total, cols = grad.shape
        grad = grad.astype(jnp.bfloat16).reshape(outer, inner, ctx, -1, cols)
        mine = trade(scatter_levels(grad.transpose(0, 2, 1, 3, 4)))
        return mine.transpose(1, 0, 2).reshape(mine.shape[1], -1).astype(jnp.float32)

    def return_rows(grad):
        length, total = grad.shape
        grad = grad.astype(jnp.bfloat16).reshape(length, outer, inner, ctx, -1)
        mine = trade(scatter_levels(grad.transpose(1, 3, 2, 0, 4)))
        return mine.reshape(inner * length, -1).astype(jnp.float32)

    def dot(left, right, dims):
        return lax.dot_general(left, right, (dims, ((), ())), preferred_element_type=jnp.float32)

    gains = lax.all_gather(jnp.stack([attn_gain, ffn_gain]), ("fsdp", "ctx"))
    gain_attn = gains[:, 0].reshape(-1).astype(jnp.float32)
    gain_ffn = gains[:, 1].reshape(-1).astype(jnp.float32)
    span = positions.shape[2]
    ids_here = lax.dynamic_slice_in_dim(block_ids[:, 0], c_at * span, span, 1)
    marks = lax.all_gather(jnp.stack([positions[:, 0], ids_here]), ("fsdp", "ctx"))
    my_seq = f_at // inner * inner + c_at
    marks = lax.dynamic_slice_in_dim(marks, my_seq * ctx, ctx, 0)
    marks = marks.transpose(1, 2, 0, 3).reshape(2, micro, ctx * span)
    pos, ids = marks[0], marks[1]

    weight_qkv = fetch_columns(wqkv)
    weight_out = fetch_rows(wo)
    weight_gate = fetch_columns(w_gate)
    weight_up = fetch_columns(w_up)
    weight_down = fetch_rows(w_down)

    stream = rehome(hidden_in).reshape(micro * rows, width).astype(jnp.float32)
    grad_out_low = rehome(cotangent).reshape(micro * rows, width)
    grad_out = grad_out_low.astype(jnp.float32)

    def to_heads(flat):
        split = flat.reshape(inner * tp, micro, rows, -1, HEAD_DIM).transpose(1, 0, 2, 3, 4)
        return split.reshape(micro, inner * tp * rows, -1, HEAD_DIM)

    def from_heads(heads):
        split = heads.reshape(micro, inner * tp, rows, -1).transpose(1, 0, 2, 3)
        return split.reshape(inner * tp * micro * rows, -1)

    normed_one, factor_one, attn_rows = norm_rows(stream, gain_attn)
    attn_in = spread(attn_rows).reshape(-1, width)
    projected = to_heads(dot(attn_in, weight_qkv, ((1,), (0,))))
    group = HEADS // KV_HEADS
    cos_table, sin_table = rope_tables(pos)
    cos_heads, sin_heads = cos_table[:, :, None], sin_table[:, :, None]
    turning = projected[:, :, : group + 1]
    turning = (turning * cos_heads + turned(turning) * sin_heads).astype(jnp.bfloat16)
    queries, keys = turning[:, :, :group], turning[:, :, group]
    values = projected[:, :, group + 1].astype(jnp.bfloat16)
    allowed = (ids[:, None, :] <= ids[:, :, None])[:, None]
    raw = jnp.einsum("blge,bme->bglm", queries, keys, preferred_element_type=jnp.float32)
    scores = jnp.where(allowed, raw * score_scale, MASKED)
    row_max = jnp.max(scores, axis=-1, keepdims=True)
    exponent = jnp.exp(scores - row_max)
    prob = exponent / jnp.sum(exponent, axis=-1, keepdims=True)
    prob_low = prob.astype(jnp.bfloat16)
    mixed = jnp.einsum("bglm,bme->blge", prob_low, values, preferred_element_type=jnp.float32)
    mixed = from_heads(mixed.astype(jnp.bfloat16))
    out_part = dot(mixed, weight_out, ((1,), (0,)))
    stream_mid = stream + fold(out_part.reshape(inner, tp, -1, width))
    normed_two, factor_two, ffn_rows = norm_rows(stream_mid, gain_ffn)
    ffn_in = spread(ffn_rows).reshape(-1, width)
    dy = spread(grad_out_low).reshape(-1, width)

    gate_pre = dot(ffn_in, weight_gate, ((1,), (0,)))
    up_pre = dot(ffn_in, weight_up, ((1,), (0,)))
    gate_sig = jax.nn.sigmoid(gate_pre)
    gate_act = gate_pre * gate_sig
    hidden = (gate_act * up_pre).astype(jnp.bfloat16)
    grad_hidden = dot(dy, weight_down, ((1,), (1,)))
    grad_gate_pre = (
        grad_hidden * up_pre * gate_sig * (1.0 + gate_pre * (1.0 - gate_sig))
    ).astype(jnp.bfloat16)
    grad_up_pre = (grad_hidden * gate_act).astype(jnp.bfloat16)
    grad_ffn_part = dot(grad_gate_pre, weight_gate, ((1,), (1,))) + dot(
        grad_up_pre, weight_up, ((1,), (1,))
    )
    grad_ffn_in = fold(grad_ffn_part.reshape(inner, tp, -1, width))
    down_part = dot(hidden, weight_down, ((1,), (0,)))
    stream_out = stream_mid + fold(down_part.reshape(inner, tp, -1, width))
    grad_down = return_rows(dot(hidden, dy, ((0,), (0,))))
    grad_gate = return_columns(dot(ffn_in, grad_gate_pre, ((0,), (0,))))
    grad_up = return_columns(dot(ffn_in, grad_up_pre, ((0,), (0,))))

    def back_rows(grad, normed, factor, gain_row):
        grad_normed = grad * gain_row
        inner_mean = jnp.mean(grad_normed * normed, axis=-1, keepdims=True)
        return factor * (grad_normed - normed * inner_mean), jnp.sum(grad * normed, axis=0)

    mid_norm, gain_ffn_part = back_rows(grad_ffn_in, normed_two, factor_two, gain_ffn)
    grad_mid = grad_out + mid_norm
    grad_mid_low = spread(grad_mid.astype(jnp.bfloat16)).reshape(-1, width)
    grad_mixed = to_heads(dot(grad_mid_low, weight_out, ((1,), (1,))).astype(jnp.bfloat16))
    grad_wo = return_rows(dot(mixed, grad_mid_low, ((0,), (0,))))
    grad_prob = jnp.einsum("blge,bme->bglm", grad_mixed, values, preferred_element_type=jnp.float32)
    inner_prob = jnp.sum(grad_prob * prob, axis=-1, keepdims=True)
    grad_scores = (score_scale * prob * (grad_prob - inner_prob)).astype(jnp.bfloat16)
    grad_queries = jnp.einsum(
        "bglm,bme->blge", grad_scores, keys, preferred_element_type=jnp.float32
    )
    grad_keys = jnp.einsum(
        "bglm,blge->bme", grad_scores, queries, preferred_element_type=jnp.float32
    )
    grad_values = jnp.einsum(
        "bglm,blge->bme", prob_low, grad_mixed, preferred_element_type=jnp.float32
    )
    grad_turning = jnp.concatenate([grad_queries, grad_keys[:, :, None]], axis=2)
    grad_turning = grad_turning * cos_heads + turned_back(grad_turning * sin_heads)
    grad_projected = jnp.concatenate([grad_turning, grad_values[:, :, None]], axis=2)
    grad_projected = from_heads(grad_projected.astype(jnp.bfloat16))
    grad_attn_in = fold(
        dot(grad_projected, weight_qkv, ((1,), (1,))).reshape(inner, tp, -1, width)
    )
    grad_wqkv = return_columns(dot(attn_in, grad_projected, ((0,), (0,))))
    in_norm, gain_attn_part = back_rows(grad_attn_in, normed_one, factor_one, gain_attn)
    grad_in = (grad_mid + in_norm).astype(jnp.bfloat16)

    gain_parts = jnp.stack([gain_attn_part, gain_ffn_part], axis=1).reshape(fsdp * ctx, -1, 2)
    gain_sums = lax.psum_scatter(gain_parts, ("fsdp", "ctx"), scatter_dimension=0)
    gain_sums = lax.psum(gain_sums, "tp")

    def home(array):
        return rehome(array.reshape(micro, 1, rows, width))

    return (
        home(stream_out.astype(jnp.bfloat16)),
        home(grad_in),
        gain_sums[:, 0],
        grad_wqkv,
        grad_wo,
        gain_sums[:, 1],
        grad_gate,
        grad_up,
        grad_down,
    )


MESH = pl.DeviceIdType.MESH
ROWS = 128
LANES = 128
NARROW = jnp.bfloat16
WIDE = jnp.float32
HALF = HEAD_DIM // 2
SCALE = HEAD_DIM ** (-0.5)
ANYWHERE = pl.BlockSpec(memory_space=pl.ANY)


class Place:
    def __init__(self):
        f, c, t = lax.axis_index("fsdp"), lax.axis_index("ctx"), lax.axis_index("tp")
        self.f, self.c, self.t = f, c, t
        fs, fy = f + 1 - 2 * (f % 2), (f + 2) % 4
        fd = (fs + 2) % 4
        self.fs, self.fy, self.fd = fs, fy, fd
        self.c1, self.c2 = c + 1 - 2 * (c % 2), (c + 2) % 4
        self.c3 = (self.c1 + 2) % 4
        self.side, self.core, self.row = (f, c, 1 - t), (fs, c, t), (fy, c, t)
        self.cross = (fd, c, t)
        self.z1, self.z2 = (f, self.c1, t), (f, self.c2, t)
        self.is_end, self.is_mid = c * (3 - c) == 0, c * (3 - c) != 0
        self.c_near, self.c_mate, self.c_outer = 1 + c // 3, 3 - c, 3 * c - 3
        self.z3 = (f, 3 - c, t)
        self.core_side, self.row_side = (fs, c, 1 - t), (fy, c, 1 - t)
        self.cross_side = (fd, c, 1 - t)
        self.level = (
            self.side, self.core, self.row, self.cross, self.core_side, self.row_side, self.cross_side
        )
        y, k, high, low = f // 2, f % 2, c // 2, c % 2
        self.to_f, self.to, self.whence, self.away = [], [], [], []
        for m in range(2):
            even = (y + m) % 2
            to_f, to_c = (low + even) % 2 * 2 + high, k * 2 + even
            self.to_f.append(to_f)
            self.to.append((to_f, to_c, t))
            self.whence.append(((low + m) % 2 * 2 + high, k * 2 + (y + low) % 2, t))
            self.away.append((to_f - f) * (to_f - f) + (to_c - c) * (to_c - c))
        self.b, self.b_side = f * 2 + t, f * 2 + 1 - t
        self.b_row, self.b_far = fy * 2 + t, fy * 2 + 1 - t
        self.b_core, self.b_core_side = fs * 2 + t, fs * 2 + 1 - t
        self.b_core_row, self.b_core_far = fd * 2 + t, fd * 2 + 1 - t


class Sent:
    def __init__(self, copy, landing):
        self.copy, self.landing = copy, landing

    def arrive(self):
        self.landing.wait_recv()

    def leave(self):
        self.copy.wait_send()


class Post:
    def __init__(self, send_sems, recv_sems, local_sems):
        self.sems = send_sems, recv_sems
        self.local_sems = local_sems
        self.n, self.n_local = 0, 0
        self.out, self.kept = [], []
        self.gates = []

    def make(self, source, target, device, lands):
        sems = dict(
            send_sem=self.sems[0].at[self.n],
            recv_sem=self.sems[1].at[self.n],
            device_id=device,
            device_id_type=MESH,
        )
        self.n += 1
        copy = pltpu.make_async_remote_copy(src_ref=source, dst_ref=target, **sems)
        landing = pltpu.make_async_remote_copy(src_ref=lands, dst_ref=lands, **sems)
        return Sent(copy, landing)

    def send(self, source, target, device, lands):
        sent = self.make(source, target, device, lands)
        sent.copy.start()
        self.out.append(sent)
        return sent

    def keep(self, source, target):
        copy = pltpu.make_async_copy(source, target, self.local_sems.at[self.n_local])
        self.n_local += 1
        copy.start()
        self.kept.append(copy)
        return copy

    def settle(self, copies):
        for copy in copies:
            copy.wait()
        self.kept = [kept for kept in self.kept if not any(kept is copy for copy in copies)]

    def close(self):
        for sent in self.out:
            sent.leave()
        for copy in self.kept:
            copy.wait()
        for gate in self.gates:
            gate.leave()
        self.out, self.kept, self.gates = [], [], []


class Gate:
    def __init__(self, post, sends, gets, what, lands):
        self.post, self.sends, self.gets, self.what, self.lands = post, sends, gets, what, lands
        self.n = post.n
        post.n += 1

    def copy(self, source, target, device):
        return pltpu.make_async_remote_copy(
            src_ref=source,
            dst_ref=target,
            send_sem=self.post.sems[0].at[self.n],
            recv_sem=self.post.sems[1].at[self.n],
            device_id=device,
            device_id_type=MESH,
        )

    def start(self):
        @pl.when(self.sends)
        def _():
            self.copy(*self.what()).start()

        self.post.gates.append(self)
        return self

    def arrive(self):
        @pl.when(self.gets)
        def _():
            there = self.lands()
            self.copy(there, there, self.post.anyone).wait_recv()

    def leave(self):
        @pl.when(self.sends)
        def _():
            self.copy(*self.what()).wait_send()


def meet(devices):
    bar = pltpu.get_barrier_semaphore()
    for device in devices:
        pl.semaphore_signal(bar, inc=1, device_id=device, device_id_type=MESH)
    pl.semaphore_wait(bar, len(devices))


class Spread:
    def __init__(self, post, at, out):
        self.post, self.at, self.out = post, at, out
        self.sent = {}

    def slot(self, block, half):
        return self.out.at[block, pl.ds(half * ROWS, ROWS)]

    def own(self, half, source):
        at, mine = self.at, self.slot(self.at.b, half)
        self.sent["side", half] = self.post.send(source, mine, at.side, self.slot(at.b_side, half))
        self.sent["row", half] = self.post.send(source, mine, at.row, self.slot(at.b_row, half))
        self.sent["core", half] = self.post.send(source, mine, at.core, self.slot(at.b_core, half))
        self.post.keep(source, mine)

    def pass_on(self, name, half, block, lands):
        here = self.slot(block, half)
        self.sent[name, half] = self.post.send(
            here, here, self.at.core, self.slot(lands, half)
        )

    def relay(self, half):
        at = self.at
        first = ("side", "row") if half == 0 else ("row", "side")
        for name in first:
            self.sent[name, half].arrive()
            block = at.b_side if name == "side" else at.b_row
            here = self.slot(block, half)
            if half == 0 and name == "side":
                self.sent["far", 0] = self.post.send(here, here, at.row, self.slot(at.b_far, 0))
            if half == 1 and name == "row":
                self.sent["far", 1] = self.post.send(here, here, at.side, self.slot(at.b_far, 1))
            lands = at.b_core_side if name == "side" else at.b_core_row
            self.pass_on("core_" + name, half, block, lands)

    def corner(self):
        for half in range(2):
            self.sent["far", half].arrive()
            self.pass_on("core_far", half, self.at.b_far, self.at.b_core_far)

    def finish(self):
        for name in ("core", "core_side", "core_row", "core_far"):
            for half in range(2):
                self.sent[name, half].arrive()


SPREAD_COPIES, SPREAD_KEPT = 14, 2


class Fold:
    copies = 10

    def __init__(self, post, at, part, scratch):
        self.post, self.at, self.part = post, at, part
        self.got, self.give, self.far, self.side, self.row, self.gx, self.gy, self.held = scratch

    @staticmethod
    def scratch(width):
        return [
            pltpu.VMEM((4, 2 * ROWS, width), NARROW),
            pltpu.VMEM((4, 2 * ROWS, width), NARROW),
            pltpu.VMEM((2, ROWS, width), NARROW),
            pltpu.VMEM((2, ROWS, width), NARROW),
            pltpu.VMEM((2, ROWS, width), NARROW),
            pltpu.VMEM((3, ROWS, width), NARROW),
            pltpu.VMEM((3, ROWS, width), NARROW),
            pltpu.VMEM((4, ROWS, width), WIDE),
        ]

    def pair(self, slot, for_core, for_own):
        both = self.part(for_core, for_own)
        self.give[slot] = both[: 2 * ROWS].astype(NARROW)
        sent = self.post.send(
            self.give.at[slot], self.got.at[slot], self.at.core, self.got.at[slot]
        )
        return sent, both[2 * ROWS :]

    def add_core(self, slot, pair):
        sent, value = pair
        sent.arrive()
        return value + self.got[slot].astype(WIDE)

    def first(self):
        at, post = self.at, self.post
        far = self.pair(3, at.b_core_far, at.b_far)
        side = self.pair(1, at.b_core_side, at.b_side)
        value = self.add_core(3, far).astype(NARROW)
        self.far[0] = value[:ROWS]
        self.far[1] = value[ROWS:]
        self.far_x = post.send(self.far.at[0], self.gx.at[0], at.side, self.gx.at[0])
        self.far_y = post.send(self.far.at[1], self.gy.at[0], at.row, self.gy.at[0])
        row = self.pair(2, at.b_core_row, at.b_row)
        value = self.add_core(1, side)
        self.side[0] = value[:ROWS].astype(NARROW)
        self.held[2] = value[ROWS:]
        self.side_x = post.send(self.side.at[0], self.gx.at[1], at.side, self.gx.at[1])
        own = self.pair(0, at.b_core, at.b)
        value = self.add_core(2, row)
        self.row[1] = value[ROWS:].astype(NARROW)
        self.held[3] = value[:ROWS]
        self.row_y = post.send(self.row.at[1], self.gy.at[1], at.row, self.gy.at[1])
        value = self.add_core(0, own)
        self.held[0] = value[:ROWS]
        self.held[1] = value[ROWS:]

    def second(self):
        at, post = self.at, self.post
        self.far_y.arrive()
        self.side[1] = (self.held[2] + self.gy[0].astype(WIDE)).astype(NARROW)
        self.side_b = post.send(self.side.at[1], self.gx.at[2], at.side, self.gx.at[2])
        self.far_x.arrive()
        self.row[0] = (self.held[3] + self.gx[0].astype(WIDE)).astype(NARROW)
        self.row_a = post.send(self.row.at[0], self.gy.at[2], at.row, self.gy.at[2])

    def third(self):
        self.side_x.arrive()
        self.row_y.arrive()
        self.held[0] = self.held[0] + self.gx[1].astype(WIDE)
        self.held[1] = self.held[1] + self.gy[1].astype(WIDE)
        self.row_a.arrive()
        self.held[0] = self.held[0] + self.gy[2].astype(WIDE)
        self.side_b.arrive()
        self.held[1] = self.held[1] + self.gx[2].astype(WIDE)


class Climb:
    copies, kept = 3, 1

    def __init__(self, post, at, level, out):
        self.post, self.at, self.out = post, at, out
        mine = out.at[:, at.c]
        self.far = post.send(level, mine, at.z2, out.at[:, at.c2])
        self.close = post.send(level, mine, at.z1, out.at[:, at.c1])
        self.own = post.keep(level, mine)

    def forward(self):
        at = self.at
        self.far.arrive()
        there = self.out.at[:, at.c2]
        self.last = self.post.send(there, there, at.z1, self.out.at[:, at.c3])

    def finish(self):
        self.close.arrive()
        self.last.arrive()
        self.post.settle([self.own])


class LineClimb:
    def __init__(self, post, at, level, out):
        self.post = post
        line = lambda c: (at.f, c, at.t)
        slot = lambda c: out.at[:, c]
        near, mate, outer = at.c_near, at.c_mate, at.c_outer
        end, mid = at.is_end, at.is_mid
        self.t0 = Gate(post, end, mid, lambda: (level, slot(at.c), line(near)), lambda: slot(outer))
        self.t1 = Gate(post, mid, end, lambda: (level, slot(at.c), line(outer)), lambda: slot(near))
        self.t2 = Gate(post, mid, mid, lambda: (level, slot(at.c), line(mate)), lambda: slot(mate))
        self.t3 = Gate(
            post, mid, mid, lambda: (slot(outer), slot(outer), line(mate)), lambda: slot(3 - outer)
        )
        self.t4 = Gate(
            post, mid, end, lambda: (slot(mate), slot(mate), line(outer)), lambda: slot(3 - near)
        )
        self.t5 = Gate(
            post, mid, end, lambda: (slot(3 - outer), slot(3 - outer), line(outer)), lambda: slot(3 - at.c)
        )
        for gate in (self.t0, self.t1, self.t2):
            gate.start()
        self.own = post.keep(level, slot(at.c))

    def forward(self):
        self.t2.arrive()
        self.t4.start()
        self.t0.arrive()
        self.t3.start()

    def last(self):
        self.t3.arrive()
        self.t5.start()

    def finish(self):
        for gate in (self.t1, self.t4, self.t5):
            gate.arrive()
        self.post.settle([self.own])


class Ends:
    def __init__(self, post, at, parts, first, got, start=0, count=None):
        count = got.shape[0] if count is None else count
        self.gates = [
            Gate(
                post, at.is_end, at.is_mid,
                lambda q=q: (
                    parts.at[first + q, :, pl.ds((3 - at.c) // 3, 3)], got.at[q], (at.f, at.c_near, at.t)
                ),
                lambda q=q: got.at[q],
            ).start()
            for q in range(start, start + count)
        ]

    def finish(self, count=None):
        count = len(self.gates) if count is None else count
        for gate in self.gates[:count]:
            gate.arrive()
        self.gates = self.gates[count:]


class Middle:
    def __init__(self, post, at, step, parts, first, came, out, own, more):
        self.post, self.at, self.out, self.own, self.more = post, at, out, own, more
        self.step, self.n = step, out.shape[0]
        self.sems = [post.local_sems.at[post.n_local + k] for k in range(2)]
        post.n_local += 2
        rows = pl.ds(first, self.n)

        def sources():
            if step == 1:
                return (
                    parts.at[rows, :, pl.ds(2 * (2 - at.c), 2)], came.at[:, :, pl.ds(2 - at.c, 2)]
                )
            return parts.at[rows, :, 3 * (at.c - 1)], came.at[:, :, at.c - 1]

        self.sources = sources

        @pl.when(at.is_mid)
        def _():
            for source, target, sem in zip(sources(), (own, more), self.sems):
                pltpu.make_async_copy(source, target, sem).start()

    def send(self):
        at, own, more = self.at, self.own, self.more

        @pl.when(at.is_mid)
        def _():
            for source, target, sem in zip(self.sources(), (own, more), self.sems):
                pltpu.make_async_copy(source, target, sem).wait()

            def add(q, carry):
                own[q] = (own[q].astype(WIDE) + more[q].astype(WIDE)).astype(NARROW)
                return carry

            lax.fori_loop(0, self.n, add, 0)

        c_to = at.c_mate if self.step == 1 else at.c_outer
        self.gate = Gate(
            self.post, at.is_mid, at.is_mid if self.step == 1 else at.is_end,
            lambda: (own, self.out, (at.f, c_to, at.t)), lambda: self.out,
        ).start()

    def finish(self):
        self.gate.arrive()


def middle_scratch(step, n):
    dims = (n, 4, 2, 256, LANES) if step == 1 else (n, 4, 256, LANES)
    return [pltpu.VMEM(dims, NARROW)] * 2


def call(kernel, name, outs, args, scratch, copies, kept, collective_id):
    sems = [
        pltpu.SemaphoreType.DMA((copies,)),
        pltpu.SemaphoreType.DMA((copies,)),
        pltpu.SemaphoreType.DMA((kept,)),
    ]
    n_in, n_out = len(args), len(outs)

    def inner(*refs):
        post, at = Post(*refs[len(refs) - 3 :]), Place()
        post.anyone = at.z1
        kernel(
            post, at, refs[:n_in], refs[n_in : n_in + n_out], refs[n_in + n_out : len(refs) - 3]
        )
        post.close()
        assert post.n <= copies and post.n_local <= kept, (post.n, post.n_local)

    return pl.pallas_call(
        inner,
        out_shape=outs,
        in_specs=[ANYWHERE] * n_in,
        out_specs=[ANYWHERE] * n_out,
        scratch_shapes=scratch + sems,
        compiler_params=pltpu.CompilerParams(
            collective_id=collective_id, has_side_effects=True, vmem_limit_bytes=62 << 20
        ),
        name=name,
    )(*args)


def shape(*dims, dtype=NARROW):
    return jax.ShapeDtypeStruct(dims, dtype)


def gain_row(gains_ref, which):
    return jnp.concatenate([gains_ref[i, which : which + 1, :] for i in range(16)], axis=1)


def normed_rows(values):
    factor = lax.rsqrt(jnp.mean(values * values, axis=-1, keepdims=True) + EPS)
    return values * factor, factor


class Swap:
    def __init__(self, post, at, home=False):
        self.post, self.at, self.moves = post, at, []
        self.devices = at.whence if home else at.to

    def __call__(self, m, source, target, lands):
        post, away = self.post, self.at.away[m]
        sent = post.make(source, target, self.devices[m], lands)
        local = pltpu.make_async_copy(source, target, post.local_sems.at[post.n_local])
        post.n_local += 1

        @pl.when(away != 0)
        def _():
            sent.copy.start()

        @pl.when(away == 0)
        def _():
            local.start()

        self.moves.append((away, sent))

        def arrive():
            @pl.when(away != 0)
            def _():
                sent.landing.wait_recv()

            @pl.when(away == 0)
            def _():
                local.wait()

        return arrive

    def finish(self):
        for away, sent in self.moves:
            @pl.when(away != 0)
            def _(sent=sent):
                sent.copy.wait_send()


def meet_swap(at):
    bar = pltpu.get_barrier_semaphore()
    partners = (*at.level, at.z1, at.z2, at.z3)
    for device in partners:
        pl.semaphore_signal(bar, inc=1, device_id=device, device_id_type=MESH)
    for m in range(2):
        @pl.when(at.away[m] != 0)
        def _(m=m):
            for device in (at.to[m], at.whence[m]):
                pl.semaphore_signal(bar, inc=1, device_id=device, device_id_type=MESH)

    pl.semaphore_wait(bar, len(partners) + sum(2 * ((away + 18) // 19) for away in at.away))


class Deal:
    def __init__(self, post, at, shards, j, outs):
        self.post, self.sent, self.kept = post, [], []
        gate, up, down = shards
        part = gate.shape[1] // 4
        chunk = part // 4
        for device, k in ((at.row, at.fy), (at.cross, at.fd), (at.core, at.fs), (None, at.f)):
            lane = pl.ds(pl.multiple_of(k * part + j * chunk, LANES), chunk)
            for source, out in zip((gate.at[:, lane], up.at[:, lane], down.at[lane]), outs):
                if device is None:
                    self.kept.append(post.keep(source, out.at[at.f]))
                else:
                    self.sent.append(post.send(source, out.at[at.f], device, out.at[k]))

    def finish(self):
        for sent in self.sent:
            sent.arrive()


HALVES = [pl.ds(half * ROWS, ROWS) for half in range(2)]


def start_kernel(post, at, ins, outs, scratch):
    hidden, marks, gains, wqkv, wo, *shards = ins
    x_own, attn_in, all_marks, all_gains, qkv_all, out_all, *levels_out = outs
    rows_in, rows_out, gain_buf = scratch
    f, c = at.f, at.c
    meet_swap(at)
    swap = Swap(post, at)
    x_moved = [
        swap(m, hidden.at[half], rows_in.at[half], rows_in.at[half]) for m, half in enumerate(HALVES)
    ]
    heads = wqkv.shape[1] // 4
    span = wo.shape[0] // 4
    first = []
    for device, k in ((at.row, at.fy), (at.cross, at.fd), (at.core, at.fs)):
        lane = pl.ds(pl.multiple_of(k * heads, LANES), heads)
        first.append(post.send(wqkv.at[:, lane], qkv_all.at[f, c], device, qkv_all.at[k, c]))
        row = pl.ds(pl.multiple_of(k * span, LANES), span)
        first.append(post.send(wo.at[row], out_all.at[f, c], device, out_all.at[k, c]))
    lane = pl.ds(pl.multiple_of(f * heads, LANES), heads)
    own = [post.keep(wqkv.at[:, lane], qkv_all.at[f, c])]
    row = pl.ds(pl.multiple_of(f * span, LANES), span)
    own.append(post.keep(wo.at[row], out_all.at[f, c]))
    marks_moved = [
        swap(m, marks, all_marks.at[m, at.to_f[m]], all_marks.at[m, f]) for m in range(2)
    ]

    mine = gain_buf.at[f, c]
    post.settle([post.keep(gains, mine)])
    step = post.send(mine, mine, at.core, gain_buf.at[at.fs, c])
    step.arrive()
    pair = gain_buf.at[pl.ds(f // 2 * 2, 2), c]
    step = post.send(pair, pair, at.row, gain_buf.at[pl.ds(at.fy // 2 * 2, 2), c])
    step.arrive()
    step = post.send(gain_buf.at[:, c], gain_buf.at[:, c], at.z1, gain_buf.at[:, at.c1])
    step.arrive()
    pair = gain_buf.at[:, pl.ds(c // 2 * 2, 2)]
    step = post.send(pair, pair, at.z2, gain_buf.at[:, pl.ds(at.c2 // 2 * 2, 2)])
    step.arrive()
    gain = jnp.concatenate([gain_buf[i // 4, i % 4, 0:1, :] for i in range(16)], axis=1)
    post.keep(gain_buf, all_gains)

    post.settle(own)
    for sent in first:
        sent.arrive()

    spread = Spread(post, at, attn_in)
    levels = []

    def climb():
        for out in (qkv_all, out_all):
            here, there = out.at[:, c], out.at[:, at.c2]
            far = post.send(here, here, at.z2, there)
            close = post.send(here, here, at.z1, out.at[:, at.c1])
            levels.append((far, close, there, out))

    for half in range(2):
        x_moved[half]()
        if half == 1:
            climb()
        normed, _ = normed_rows(rows_in[HALVES[half]].astype(WIDE))
        rows_out[HALVES[half]] = (normed * gain).astype(NARROW)
        spread.own(half, rows_out.at[HALVES[half]])
        post.keep(rows_in.at[HALVES[half]], x_own.at[HALVES[half]])

    for arrive in marks_moved:
        arrive()
    here = all_marks.at[:, f]
    small = post.send(here, here, at.core, all_marks.at[:, at.fs])
    spread.relay(0)
    small.arrive()
    pair = all_marks.at[:, pl.ds(f // 2 * 2, 2)]
    smaller = post.send(pair, pair, at.row, all_marks.at[:, pl.ds(at.fy // 2 * 2, 2)])
    spread.relay(1)
    forwards = []
    for far, close, there, out in levels:
        far.arrive()
        forwards.append((post.send(there, there, at.z1, out.at[:, at.c3]), close))
    deals = [Deal(post, at, shards, j, levels_out[3 * j : 3 * j + 3]) for j in range(2)]
    spread.corner()
    for last, close in forwards:
        last.arrive()
        close.arrive()
    spread.finish()
    smaller.arrive()
    for deal in deals:
        deal.finish()
    swap.finish()


def rope(values, cos_full, sin_full):
    return values * cos_full + pltpu.roll(values, HALF, 1) * sin_full


def rope_back(values, cos_full, sin_full):
    return values * cos_full - pltpu.roll(values, HALF, 1) * sin_full


def rope_full(marks, m, inverse):
    angle = marks.T[:, 2 + m : 3 + m] * inverse
    low = lax.broadcasted_iota(jnp.int32, angle.shape, 1) < HALF
    turns = jnp.floor(angle * (2.0 / math.pi) + 0.5)
    rest = ((angle - turns * 1.5703125) - turns * 4.837512969970703125e-4) - turns * 7.54978995489188e-8
    square = rest * rest
    sine = rest + rest * square * (
        -1.6666654611e-1 + square * (8.3321608736e-3 - square * 1.9515295891e-4)
    )
    cosine = 1.0 - 0.5 * square + square * square * (
        4.166664568298827e-2 + square * (-1.388731625493765e-3 + square * 2.443315711809948e-5)
    )
    quadrant = turns + jnp.where(low, 1.0, 0.0)
    half = jnp.floor(quadrant * 0.5)
    odd = quadrant - 2.0 * half > 0.5
    negative = half - 2.0 * jnp.floor(half * 0.5) > 0.5
    table = jnp.where(odd, cosine, sine)
    table = jnp.where(negative, -table, table)
    turned_table = pltpu.roll(table, HALF, 1)
    return jnp.where(low, table, turned_table), jnp.where(low, -turned_table, table)


def quarter(at, i):
    return (i + at.c) % 2 * 2 + i // 2


def mm(left, right, dims=((1,), (0,))):
    return lax.dot_general(left, right, (dims, ((), ())), preferred_element_type=WIDE)


TILE = 256

def softmax_tile(query, key, id_col, id_row):
    raw = mm(query, key, ((1,), (1,))) * SCALE
    raw = jnp.where(id_row <= id_col, raw, MASKED)
    top = jnp.max(raw, axis=-1, keepdims=True)
    exponent = jnp.exp(raw - top)
    return exponent * (1.0 / jnp.sum(exponent, axis=-1, keepdims=True))


def id_rows(at, marks, m, tiles):
    return jnp.concatenate([marks[m, quarter(at, i), m : m + 1, :] for i in range(tiles)], axis=1)


def attend_kernel(post, at, ins, outs, scratch):
    attn_in, qkv_all, inverse_in, marks_in, cot, *shards = ins[:8]
    levels = ins[8:]
    queries, keys, values, mixed, dy, cot_own, *more = outs
    climbed, dealt = more[: len(levels)], more[len(levels) :]
    rows, weight, inverse, marks, q_buf, k_buf, v_buf, mix_buf = scratch
    meet_swap(at)
    swap = Swap(post, at)
    cot_moved = [
        swap(m, cot.at[half], cot_own.at[half], cot_own.at[half]) for m, half in enumerate(HALVES)
    ]
    local = [
        post.keep(inverse_in, inverse),
        post.keep(marks_in, marks),
        post.keep(qkv_all, weight),
        post.keep(attn_in.at[:, pl.ds(0, ROWS)], rows.at[0]),
        post.keep(attn_in.at[:, pl.ds(ROWS, ROWS)], rows.at[1]),
    ]
    spread = Spread(post, at, dy)
    deal = Deal(post, at, shards, 2, dealt)
    post.settle(local)
    width = rows.shape[-1]
    columns = weight.shape[-1]
    for m in range(2):
        for i in range(4):
            q = quarter(at, i)
            here = rows[m, pl.ds(2 * q, 2)].reshape(TILE, width)
            projected = mm(here, weight[...].reshape(width, columns))
            cos_full, sin_full = rope_full(marks[m, q], m, inverse[0:1])
            place = pl.ds(i * TILE, TILE)
            for g in range(2):
                lane = slice(g * HEAD_DIM, (g + 1) * HEAD_DIM)
                q_buf[m, place, lane] = rope(projected[:, lane], cos_full, sin_full).astype(NARROW)
            k_buf[m, place] = rope(projected[:, 256:384], cos_full, sin_full).astype(NARROW)
            v_buf[m, place] = projected[:, 384:512].astype(NARROW)
    for m in range(2):
        for i in range(4):
            n = min(i + 2, 4) * TILE
            q = quarter(at, i)
            id_col = marks[m, q].T[:, m : m + 1]
            id_row = id_rows(at, marks, m, n // TILE)
            for g in range(2):
                lane = slice(g * HEAD_DIM, (g + 1) * HEAD_DIM)
                prob = softmax_tile(
                    q_buf[m, i * TILE : (i + 1) * TILE, lane], k_buf[m, :n], id_col, id_row
                )
                value = mm(prob.astype(NARROW), v_buf[m, :n]).astype(NARROW)
                for h in range(2):
                    mix_buf[2 * q + h, m * ROWS : (m + 1) * ROWS, lane] = value[
                        h * ROWS : (h + 1) * ROWS
                    ]
        if m == 0:
            climbs = [Climb(post, at, level, out) for level, out in zip(levels, climbed)]
    for source, target in ((q_buf, queries), (k_buf, keys), (v_buf, values), (mix_buf, mixed)):
        post.keep(source, target)
    for half in range(2):
        cot_moved[half]()
        spread.own(half, cot_own.at[HALVES[half]])
    spread.relay(0)
    spread.relay(1)
    for climb in climbs:
        climb.forward()
    spread.corner()
    spread.finish()
    for climb in climbs:
        climb.finish()
    deal.finish()
    swap.finish()


def middle_kernel(post, at, ins, outs, scratch):
    mixed, out_all, x_own, gains_in, *shards = ins[:7]
    levels = ins[7:]
    mid_own, ffn_in, *more = outs
    climbed, dealt = more[: len(levels)], more[len(levels) :]
    mix_buf, weight, x_buf, gains, rows_out, *fold_scratch = scratch
    meet((at.side, at.core, at.row, at.cross, at.z1, at.z2))
    local = [
        post.keep(out_all.at[i // 4, i % 4], weight.at[:, pl.ds(i * LANES, LANES)])
        for i in range(16)
    ]
    local += [post.keep(mixed, mix_buf), post.keep(x_own, x_buf), post.keep(gains_in, gains)]
    post.settle(local)
    climbs = [Climb(post, at, level, out) for level, out in zip(levels, climbed)]

    def part(*blocks):
        return mm(jnp.concatenate([mix_buf[block] for block in blocks]), weight[...])

    fold = Fold(post, at, part, fold_scratch)
    fold.first()
    fold.second()
    deal = Deal(post, at, shards, 3, dealt)
    fold.third()
    gain = jnp.concatenate([gains[i // 4, i % 4, 1:2, :] for i in range(16)], axis=1)
    spread = Spread(post, at, ffn_in)
    for half in range(2):
        rows = pl.ds(half * ROWS, ROWS)
        value = fold.held[half] + x_buf[rows].astype(WIDE)
        fold.held[half] = value
        normed, _ = normed_rows(value)
        rows_out[half] = (normed * gain).astype(NARROW)
        spread.own(half, rows_out.at[half])
        post.keep(fold.held.at[half], mid_own.at[rows])
    spread.relay(0)
    for climb in climbs:
        climb.forward()
    spread.relay(1)
    spread.corner()
    spread.finish()
    for climb in climbs:
        climb.finish()
    deal.finish()


def small_arrays(block_ids, positions, attn_gain, ffn_gain):
    micro, _, span = positions.shape
    ids = lax.dynamic_slice_in_dim(block_ids[:, 0], lax.axis_index("ctx") * span, span, 1)
    rows = jnp.concatenate([ids, positions[:, 0]]).astype(WIDE)
    marks = jnp.pad(rows, ((0, 8 - 2 * micro), (0, 0)))
    gains = jnp.pad(jnp.stack([attn_gain, ffn_gain]).astype(WIDE), ((0, 6), (0, 0)))
    return marks, gains


def ffn_kernel(post, at, ins, outs, scratch):
    ffn_in, dy = ins[:2]
    ready = ins[2:10]
    levels = ins[10:]
    hidden, grads_pre, parts, ends_a, *climbed = outs
    x_buf, dy_buf, gate_buf, up_buf, down_buf, act, act_t, staged = scratch
    meet((at.z1, at.z3))
    climbs = [LineClimb(post, at, level, out) for level, out in zip(levels, climbed)]
    local = [post.keep(ffn_in, x_buf), post.keep(dy, dy_buf)]
    weights = list(ready) + list(climbed)

    def load(j):
        slot = j % 2
        gate, up, down = weights[3 * j : 3 * j + 3]
        copies = [post.keep(gate, gate_buf.at[slot]), post.keep(up, up_buf.at[slot])]
        for i in range(16):
            copies.append(
                post.keep(down.at[i // 4, i % 4], down_buf.at[slot, :, pl.ds(i * LANES, LANES)])
            )
        return copies

    loading = load(0)
    post.settle(local)
    width = x_buf.shape[-1]
    saved, sums_0 = [], []
    for j in range(4):
        slot = j % 2
        if loading is None:
            for climb in climbs[:1] if j == 2 else climbs[1:]:
                climb.finish()
            loading = load(j)
        post.settle(loading)
        loading = load(1) if j == 0 else None
        post.settle(saved)

        def rows(i, carry):
            blocks = pl.ds(i * 2, 2)
            x, grad = (buf[blocks].reshape(2 * TILE, width) for buf in (x_buf, dy_buf))
            gate = mm(x, gate_buf[slot].reshape(width, -1))
            up = mm(x, up_buf[slot].reshape(width, -1))
            grad_hidden = mm(grad, down_buf[slot], ((1,), (1,)))
            sig = jax.nn.sigmoid(gate)
            silu = gate * sig
            values = (
                grad_hidden * up * sig * (1.0 + gate * (1.0 - sig)),
                grad_hidden * silu,
                silu * up,
            )
            place = pl.ds(pl.multiple_of(i * 2 * TILE, 2 * TILE), 2 * TILE)
            for k in range(3):
                act[k, blocks] = values[k].astype(NARROW).reshape(2, TILE, -1)
                act_t[k, :, place] = values[k].T.astype(NARROW)
            return carry

        lax.fori_loop(0, 4, rows, 0)
        chunk = act.shape[-1]
        lane = pl.ds(j * chunk, chunk)
        saved = [
            post.keep(act.at[0], grads_pre.at[:, :, lane]),
            post.keep(act.at[1], grads_pre.at[:, :, pl.ds((4 + j) * chunk, chunk)]),
            post.keep(act.at[2], hidden.at[:, :, lane]),
        ]
        for climb in climbs[:1] if j == 1 else climbs[1:] if j == 2 else ():
            climb.last()
        for climb in climbs[:1] if j == 0 else climbs[1:] if j == 1 else ():
            climb.forward()

        def sums(n, carry):
            place = pl.ds(pl.multiple_of(n * TILE, TILE), TILE)
            x = x_buf[:, :, place].reshape(8 * TILE, TILE)
            grad = dy_buf[:, :, place].reshape(8 * TILE, TILE)
            both = mm(act_t[0:2].reshape(2 * chunk, -1), x).astype(NARROW)
            for k, value in enumerate((both[:chunk], both[chunk:], mm(act_t[2], grad).astype(NARROW))):
                staged[k, 2 * n] = value[:, :LANES]
                staged[k, 2 * n + 1] = value[:, LANES:]
            return carry

        lax.fori_loop(0, 8, sums, 0)
        stored = [
            post.keep(staged.at[k, pl.ds(4 * fl, 4)], parts.at[3 * j + k, fl])
            for k in range(3)
            for fl in range(4)
        ]
        if j < 2:
            post.settle(stored)
            sums_0.append(Ends(post, at, parts, 0, ends_a, 3 * j, (3, 1)[j]))
        else:
            saved += stored
    for step in sums_0:
        step.finish()


class Descend:
    def __init__(self, post, at, pieces, got):
        self.near = post.send(pieces.at[:, at.c1], got.at[0], at.z1, got.at[0])
        self.next = post.send(pieces.at[:, at.c3], got.at[1], at.z1, got.at[1])

    def finish(self):
        self.near.arrive()
        self.next.arrive()


def norm_back_rows(grad, values, gain):
    normed, factor = normed_rows(values)
    scaled = grad * gain
    inner_mean = jnp.mean(scaled * normed, axis=-1, keepdims=True)
    return factor * (scaled - normed * inner_mean), jnp.sum(grad * normed, axis=0, keepdims=True)


def back_kernel(post, at, ins, outs, scratch):
    grads_pre, mid_own, cot_own, gains_in, parts, ends_a, *weights = ins
    grad_mid_own, grad_mid, gain_part, ends_c, mates_b, mates_e = outs
    pre_buf, weight, mid_buf, cot_buf, gains, rows_out, gain_out = scratch[:7]
    bufs_1, bufs_e, fold_scratch = scratch[7:9], scratch[9:11], scratch[11:]
    meet((at.side, at.core, at.row, at.z1, at.z3))
    downs = [
        Middle(post, at, 1, parts, 0, ends_a, mates_b, *bufs_1),
        Ends(post, at, parts, 4, ends_c),
    ]
    chunk = pre_buf.shape[-1] // 8
    local = [post.keep(grads_pre, pre_buf)]
    for a in range(2):
        for j in range(4):
            place = pl.ds((4 * a + j) * chunk, chunk)
            local.append(post.keep(weights[4 * a + j], weight.at[:, :, :, place]))
    local += [post.keep(mid_own, mid_buf), post.keep(cot_own, cot_buf), post.keep(gains_in, gains)]
    post.settle(local)
    width = mid_buf.shape[-1]

    def part(*blocks):
        rows = jnp.concatenate([pre_buf[block] for block in blocks])
        return mm(rows, weight[...].reshape(width, -1), ((1,), (1,)))

    downs[0].send()
    fold = Fold(post, at, part, fold_scratch)
    fold.first()
    fold.second()
    fold.third()
    gain = jnp.concatenate([gains[i // 4, i % 4, 1:2, :] for i in range(16)], axis=1)
    spread = Spread(post, at, grad_mid)
    total = jnp.zeros((1, width), WIDE)
    for half in range(2):
        rows = HALVES[half]
        back, piece = norm_back_rows(fold.held[half], mid_buf[rows], gain)
        total = total + piece
        value = cot_buf[rows].astype(WIDE) + back
        fold.held[half] = value
        rows_out[half] = value.astype(NARROW)
        spread.own(half, rows_out.at[half])
        post.keep(fold.held.at[half], grad_mid_own.at[rows])
    gain_out[...] = jnp.broadcast_to(total, gain_out.shape)
    post.keep(gain_out, gain_part)
    downs[1].finish(2)
    downs.append(Middle(post, at, 1, parts, 4, ends_c.at[pl.ds(0, 2)], mates_e, *bufs_e))
    spread.relay(0)
    downs[2].send()
    spread.relay(1)
    spread.corner()
    spread.finish()
    for down in downs:
        down.finish()


def attend_back_kernel(post, at, ins, outs, scratch):
    (
        grad_mid, queries, keys, values, marks_in, inverse_in, out_all, mixed, attn_in, hidden, mid_own, parts,
        ends_a, ends_c, mates_b, mates_e, *downs_in
    ) = ins
    grad_proj, parts_q, sums_o, out_home, ends_d, mates_c, outer_b, outer_e, first_sums = outs
    (
        gm_buf, q_buf, k_buf, v_buf, marks, inverse, weight, mix_buf, hid_buf, down_buf, gp_buf, gk_buf, gv_buf,
        staged, staged_o, got_o, far_o, end_o, mid_buf, out_buf
    ) = scratch[:20]
    bufs_1, bufs_2, bufs_e, bufs_own = scratch[20:22], scratch[22:24], scratch[24:26], scratch[26:29]
    fold_scratch = scratch[29:]
    meet_swap(at)
    swap = Swap(post, at, home=True)
    steps = [
        Middle(post, at, 1, parts, 6, ends_c.at[pl.ds(2, 3)], mates_c, *bufs_1),
        Middle(post, at, 2, parts, 0, mates_b, outer_b, *bufs_2),
        Middle(post, at, 2, parts, 4, mates_e, outer_e, *bufs_e),
        Ends(post, at, parts, 9, ends_d),
    ]

    chunk = hid_buf.shape[-1] // 4
    early = [post.keep(hidden, hid_buf)]
    for j in range(4):
        for i in range(16):
            target = down_buf.at[pl.ds(j * chunk, chunk), pl.ds(i * LANES, LANES)]
            early.append(post.keep(downs_in[j].at[i // 4, i % 4], target))
    late = [
        post.keep(source, target)
        for source, target in (
            (grad_mid, gm_buf), (queries, q_buf), (keys, k_buf), (values, v_buf), (marks_in, marks),
            (inverse_in, inverse), (mixed, mix_buf), (mid_own, mid_buf),
        )
    ]
    late += [
        post.keep(out_all.at[i // 4, i % 4], weight.at[:, pl.ds(i * LANES, LANES)])
        for i in range(16)
    ]
    post.settle(early)
    for step in steps[:3]:
        step.send()

    def part(*blocks):
        return mm(jnp.concatenate([hid_buf[block] for block in blocks]), down_buf[...])

    fold = Fold(post, at, part, fold_scratch)
    fold.first()
    post.settle(late)

    def fetch(n):
        place = pl.ds(n * TILE, TILE)
        return post.keep(attn_in.at[:, :, place], column(n))

    def column(n):
        return hid_buf.at[:, :, pl.ds(n % 2 * TILE, TILE)]

    mix_t, gp_t = down_buf.at[pl.ds(512, 256)], down_buf.at[pl.ds(0, 512)]
    fetched = fetch(0)
    width = gm_buf.shape[-1]
    for i in range(8):
        mix_t[:, i * TILE : (i + 1) * TILE] = mix_buf[i].astype(WIDE).T.astype(NARROW)
    for n in range(8):
        place = slice(n * TILE, (n + 1) * TILE)
        value = mm(mix_t[...], gm_buf[:, :, place].reshape(8 * TILE, TILE)).astype(NARROW)
        for h in range(2):
            block = 2 * n + h
            staged_o[block // 4, block % 4] = value[:, h * LANES : (h + 1) * LANES]
    step_o = Descend(post, at, staged_o, got_o)
    for m in range(2):
        for i in range(4):
            q = quarter(at, i)
            n = min(i + 2, 4) * TILE
            place = slice(i * TILE, (i + 1) * TILE)
            id_col = marks[m, q].T[:, m : m + 1]
            id_row = id_rows(at, marks, m, n // TILE)
            cos_full, sin_full = rope_full(marks[m, q], m, inverse[0:1])
            rows = gm_buf[pl.ds(2 * q, 2), m * ROWS : (m + 1) * ROWS].reshape(TILE, width)
            grad_mixed = mm(rows, weight[...], ((1,), (1,))).astype(NARROW)
            for g in range(2):
                lane = slice(g * HEAD_DIM, (g + 1) * HEAD_DIM)
                query = q_buf[m, place, lane]
                prob = softmax_tile(query, k_buf[m, :n], id_col, id_row)
                grad = grad_mixed[:, lane]
                grad_prob = mm(grad, v_buf[m, :n], ((1,), (1,)))
                inner = jnp.sum(grad_prob * prob, axis=-1, keepdims=True)
                grad_scores = (SCALE * prob * (grad_prob - inner)).astype(NARROW)
                grad_query = mm(grad_scores, k_buf[m, :n])
                grad_key = mm(grad_scores, query, ((0,), (0,)))
                grad_value = mm(prob.astype(NARROW), grad, ((0,), (0,)))
                if i == 0 and g == 0:
                    gk_buf[:n], gv_buf[:n] = grad_key, grad_value
                    gk_buf[n:], gv_buf[n:] = (jnp.zeros_like(gk_buf[n:]),) * 2
                else:
                    gk_buf[:n] = gk_buf[:n] + grad_key
                    gv_buf[:n] = gv_buf[:n] + grad_value
                done = rope_back(grad_query, cos_full, sin_full).astype(NARROW)
                for h in range(2):
                    gp_buf[2 * q + h, m * ROWS : (m + 1) * ROWS, lane] = done[h * ROWS : (h + 1) * ROWS]
            if m == 1 and i == 1:
                fold.third()
                for half in HALVES:
                    k = half.start // ROWS
                    out_buf[half] = (fold.held[k] + mid_buf[half]).astype(NARROW)
                moved = [
                    swap(k, out_buf.at[half], out_home.at[half], out_home.at[half])
                    for k, half in enumerate(HALVES)
                ]
        for i in range(4):
            q = quarter(at, i)
            place = slice(i * TILE, (i + 1) * TILE)
            cos_full, sin_full = rope_full(marks[m, q], m, inverse[0:1])
            done = (
                rope_back(gk_buf[place], cos_full, sin_full).astype(NARROW),
                gv_buf[place].astype(NARROW),
            )
            for k in range(2):
                lane = slice((2 + k) * HEAD_DIM, (3 + k) * HEAD_DIM)
                for h in range(2):
                    gp_buf[2 * q + h, m * ROWS : (m + 1) * ROWS, lane] = done[k][h * ROWS : (h + 1) * ROWS]
        if m == 0:
            fold.second()
    post.keep(gp_buf, grad_proj)
    for i in range(8):
        place = slice(i * TILE, (i + 1) * TILE)
        gp_t[:, place] = gp_buf[i].astype(WIDE).T.astype(NARROW)
    steps[1].finish()
    early = Own(
        post, at, parts, 0, 3,
        ((ends_a.at[pl.ds(0, 3)],), (mates_b.at[pl.ds(0, 3)],), (outer_b.at[pl.ds(0, 3)],)), *bufs_own,
    )
    for n in range(8):
        post.settle([fetched])
        if n < 7:
            fetched = fetch(n + 1)
        other = mm(gp_t[...], column(n)[...].reshape(8 * TILE, TILE)).astype(NARROW)
        for h in range(2):
            block = 2 * n + h
            staged[block // 4, block % 4] = other[:, h * LANES : (h + 1) * LANES]
    post.keep(staged, parts_q)
    early.add()
    trades = []
    for p in range(3):
        post.keep(bufs_own[0].at[p, at.f], first_sums.at[at.f, p])
        for device, k in ((at.row, at.fy), (at.cross, at.fd), (at.core, at.fs)):
            trades.append(
                post.send(bufs_own[0].at[p, k], first_sums.at[at.f, p], device, first_sums.at[k, p])
            )
    step_o.finish()
    for k in range(4):
        value = staged_o[k, at.c2].astype(WIDE) + got_o[1, k].astype(WIDE)
        far_o[k] = value.astype(NARROW)
    sent_o = post.send(far_o, end_o, at.z2, end_o)
    sent_o.arrive()
    for k in range(4):
        value = staged_o[k, at.c].astype(WIDE) + got_o[0, k].astype(WIDE) + end_o[k].astype(WIDE)
        got_o[1, k] = value.astype(NARROW)
    post.keep(got_o.at[1], sums_o)
    for arrive in moved:
        arrive()
    swap.finish()
    for sent in trades:
        sent.arrive()
    steps.pop(1)
    for step in steps:
        step.finish()


class Own:
    def __init__(self, post, at, parts, first, n, pieces, own, one, two):
        self.post, self.at, self.first, self.n = post, at, first, n
        self.own, self.one, self.two = own, one, two
        self.pieces = pieces
        count = 1 + max(len(pieces[0]) + len(pieces[1]), len(pieces[2]))
        self.sems = [post.local_sems.at[post.n_local + k] for k in range(count)]
        post.n_local += count
        self.parts = parts

        @pl.when(at.is_mid)
        def _():
            for copy in self.mid_copies():
                copy.start()

        @pl.when(at.is_end)
        def _():
            for copy in self.end_copies():
                copy.start()

    def laid(self, arrays, index, target):
        place, pairs = self.first, []
        for array in arrays:
            n = array.shape[0]
            source = array if index is None else array.at[:, :, index]
            pairs.append((source, target.at[pl.ds(place, n)]))
            place += n
        return pairs

    def copies(self, pairs):
        rows = pl.ds(self.first, self.n)
        pairs = [(self.parts.at[rows, :, self.at.c], self.own.at[rows])] + pairs
        return [pltpu.make_async_copy(*pair, sem) for pair, sem in zip(pairs, self.sems)]

    def mid_copies(self):
        c = self.at.c
        ends, mates, _ = self.pieces
        return self.copies(self.laid(ends, 2 * (c - 1), self.one) + self.laid(mates, 2 - c, self.two))

    def end_copies(self):
        return self.copies(self.laid(self.pieces[2], None, self.two))

    def add(self):
        def both(p, carry):
            value = self.own[p].astype(WIDE) + self.one[p].astype(WIDE) + self.two[p].astype(WIDE)
            self.own[p] = value.astype(NARROW)
            return carry

        def single(p, carry):
            self.own[p] = (self.own[p].astype(WIDE) + self.two[p].astype(WIDE)).astype(NARROW)
            return carry

        @pl.when(self.at.is_mid)
        def _():
            for copy in self.mid_copies():
                copy.wait()
            lax.fori_loop(self.first, self.first + self.n, both, 0)

        @pl.when(self.at.is_end)
        def _():
            for copy in self.end_copies():
                copy.wait()
            lax.fori_loop(self.first, self.first + self.n, single, 0)


def end_kernel(post, at, ins, outs, scratch):
    (
        grad_proj, qkv_all, x_own, gains_in, grad_mid_own, gain_ffn_part, parts, parts_q, sums_o,
        ends_a, ends_c, ends_d, mates_b, mates_c, mates_e, outer_b, outer_e
    ) = ins
    grad_home, gain_sums, mates_d, outer_c, outer_d, *home_sums = outs
    (
        gp_buf, weight, x_buf, gains, mid_buf, rows_out, gain_buf, gain_got, own_ffn, one_ffn, two_ffn,
        own_q, far_q, got_q, end_q
    ) = scratch[:15]
    bufs_1, bufs_2, bufs_3, fold_scratch = scratch[15:17], scratch[17:19], scratch[19:21], scratch[21:]
    f, c = at.f, at.c
    meet_swap(at)
    step_q = Descend(post, at, parts_q, got_q)
    steps = [
        Middle(post, at, 1, parts, 9, ends_d, mates_d, *bufs_1),
        Middle(post, at, 2, parts, 6, mates_c, outer_c, *bufs_2),
    ]
    swap = Swap(post, at, home=True)
    early = Own(
        post, at, parts, 3, 3,
        (
            (ends_a.at[pl.ds(3, 1)], ends_c.at[pl.ds(0, 2)]),
            (mates_b.at[pl.ds(3, 1)], mates_e),
            (outer_b.at[pl.ds(3, 1)], outer_e),
        ),
        own_ffn, one_ffn, two_ffn,
    )
    fold_in = [
        post.keep(grad_proj, gp_buf), post.keep(qkv_all, weight), post.keep(x_own, x_buf),
        post.keep(gains_in, gains), post.keep(grad_mid_own, mid_buf),
        post.keep(gain_ffn_part, gain_buf),
    ]
    later = [
        post.keep(parts_q.at[:, c], own_q), post.keep(parts_q.at[:, at.c2], far_q),
    ]
    for step in steps:
        step.send()

    def add_far(far, came):
        for k in range(4):
            far[k] = (far[k].astype(WIDE) + came[k].astype(WIDE)).astype(NARROW)

    def add_own(own, one, end):
        for k in range(4):
            own[k] = (own[k].astype(WIDE) + one[k].astype(WIDE) + end[k].astype(WIDE)).astype(NARROW)

    trades = []
    places = ((at.row, at.fy), (at.cross, at.fd), (at.core, at.fs))

    def trade(mine, out, *place):
        post.keep(mine(f), out.at[(f, *place)])
        for device, k in places:
            trades.append(
                post.send(mine(k), out.at[(f, *place)], device, out.at[(k, *place)])
            )

    def trade_ffn(p):
        trade(lambda k: own_ffn.at[p, k], home_sums[p % 3], p // 3 - 1)

    post.settle(fold_in)
    width = x_buf.shape[-1]

    def part(*blocks):
        rows = jnp.concatenate([gp_buf[block] for block in blocks])
        return mm(rows, weight[...].reshape(width, -1), ((1,), (1,)))

    fold = Fold(post, at, part, fold_scratch)
    fold.first()
    early.add()
    fold.second()
    post.settle(later)
    step_q.finish()
    add_far(far_q, got_q.at[1])
    sent_q = post.send(far_q, end_q, at.z2, end_q)
    fold.third()
    gain = jnp.concatenate([gains[i // 4, i % 4, 0:1, :] for i in range(16)], axis=1)
    total = jnp.zeros((1, width), WIDE)
    moved = []
    for half in range(2):
        rows = HALVES[half]
        back, piece = norm_back_rows(fold.held[half], x_buf[rows].astype(WIDE), gain)
        total = total + piece
        rows_out[rows] = (mid_buf[rows] + back).astype(NARROW)
        moved.append(swap(half, rows_out.at[rows], grad_home.at[rows], grad_home.at[rows]))
    gain_buf[0:1] = total
    gain_sent = [
        post.send(gain_buf, gain_got.at[k], device, gain_got.at[k])
        for k, device in enumerate(at.level)
    ]
    steps[0].finish()
    steps.append(Middle(post, at, 2, parts, 9, mates_d, outer_d, *bufs_3))
    steps[2].send()
    for p in range(3, 6):
        trade_ffn(p)
    trade(lambda k: sums_o.at[k], home_sums[3])
    sent_q.arrive()
    add_own(own_q, got_q.at[0], end_q)
    trade(lambda k: own_q.at[k], home_sums[4])
    steps[1].finish()
    late = Own(
        post, at, parts, 6, 3, ((ends_c.at[pl.ds(2, 3)],), (mates_c,), (outer_c,)), own_ffn, one_ffn, two_ffn
    )
    late.add()
    for p in range(6, 9):
        trade_ffn(p)
    for sent in gain_sent:
        sent.arrive()
        sent.leave()
    post.out = [sent for sent in post.out if not any(sent is gone for gone in gain_sent)]
    gain_buf[...] = gain_buf[...] + sum(gain_got[k] for k in range(7))
    gain_sent = [
        post.send(gain_buf, gain_got.at[7 + k], device, gain_got.at[7 + k])
        for k, device in enumerate((at.z1, at.z2, at.z3))
    ]
    steps[2].finish()
    last = Own(
        post, at, parts, 9, 3, ((ends_d,), (mates_d,), (outer_d,)), own_ffn, one_ffn, two_ffn
    )
    last.add()
    for p in range(9, 12):
        trade_ffn(p)
    for sent in gain_sent:
        sent.arrive()
        sent.leave()
    post.out = [sent for sent in post.out if not any(sent is gone for gone in gain_sent)]
    gain_buf[...] = gain_buf[...] + sum(gain_got[7 + k] for k in range(3))
    place = pl.ds(pl.multiple_of((f * 4 + c) * LANES, LANES), LANES)
    post.keep(gain_buf.at[:, place], gain_sums)
    for sent in trades:
        sent.arrive()
    for arrive in moved:
        arrive()
    swap.finish()


def home_kernel(*refs):
    first, gate, up, down, out, qkv, gate_out, up_out, down_out, qkv_out, out_out = refs[:11]
    gate_buf, up_buf, down_buf, out_buf, qkv_buf, sems = refs[11:]
    pairs = []
    for a, (array, buf) in enumerate(((gate, gate_buf), (up, up_buf), (down, down_buf))):
        pairs.append((first.at[:, a], buf.at[:, 0]))
        pairs.append((array, buf.at[:, pl.ds(1, 3)]))
    pairs += [(out, out_buf), (qkv, qkv_buf)]
    copies = [pltpu.make_async_copy(*pair, sems.at[n]) for n, pair in enumerate(pairs)]
    for copy in copies:
        copy.start()
    for a, (buf, target) in enumerate(((gate_buf, gate_out), (up_buf, up_out))):
        for copy in copies[2 * a : 2 * a + 2]:
            copy.wait()
        for n in range(8):
            value = buf[n // 2, pl.ds(n % 2 * 2, 2)].reshape(512, LANES)
            target[:, pl.ds(n * 512, 512)] = value.astype(WIDE).T
    for copy in copies[4:]:
        copy.wait()
    for n in range(4):
        rows = pl.ds(n * 1024, 1024)
        down_out[rows] = down_buf[n].reshape(1024, LANES).astype(WIDE)
        out_out[pl.ds(n * 256, 256)] = out_buf[n].astype(WIDE)
        qkv_out[:, pl.ds(n * 512, 512)] = qkv_buf[n].astype(WIDE).T


def near_body(
    hidden_in, cotangent, block_ids, positions, attn_gain, wqkv, wo, ffn_gain, w_gate, w_up, w_down
):
    micro, _, rows, width = hidden_in.shape
    own = micro * rows
    ff = w_gate.shape[1]
    chunk = ff // 16
    shards = (w_gate, w_up, w_down)
    marks, gains = small_arrays(block_ids, positions, attn_gain, ffn_gain)
    inverse = THETA ** (-(jnp.arange(HALF, dtype=WIDE) * 2.0 / HEAD_DIM))
    inverse = jnp.broadcast_to(jnp.concatenate([inverse, inverse]), (8, HEAD_DIM))
    level_shapes = [shape(4, LANES, chunk), shape(4, LANES, chunk), shape(4, chunk, LANES)]
    whole_shapes = [shape(4, 4, LANES, chunk), shape(4, 4, LANES, chunk), shape(4, 4, chunk, LANES)]
    gains_shape = (4, 4, *gains.shape)
    x_own, attn_in, all_marks, all_gains, qkv_all, out_all, *level = call(
        start_kernel,
        "start",
        [
            shape(own, width), shape(8, own, width),
            shape(2, 4, *marks.shape, dtype=WIDE), shape(*gains_shape, dtype=WIDE),
            shape(4, 4, LANES, wqkv.shape[1] // 4), shape(4, 4, wo.shape[0] // 4, LANES),
            *level_shapes, *level_shapes,
        ],
        (hidden_in.reshape(own, width), marks, gains, wqkv, wo, *shards),
        [pltpu.VMEM((own, width), NARROW), pltpu.VMEM((own, width), NARROW), pltpu.VMEM(gains_shape, WIDE)],
        72, 24, 1,
    )
    queries, keys, values, mixed, dy, cot_own, *more = call(
        attend_kernel,
        "attend",
        [
            shape(2, 1024, 256), shape(2, 1024, 128), shape(2, 1024, 128), shape(8, own, 256),
            shape(8, own, width), shape(own, width), *whole_shapes, *level_shapes,
        ],
        (attn_in, qkv_all, inverse, all_marks, cotangent.reshape(own, width), *shards, *level[:3]),
        [
            pltpu.VMEM((2, 8, ROWS, width), NARROW), pltpu.VMEM(qkv_all.shape, NARROW),
            pltpu.VMEM(inverse.shape, WIDE), pltpu.VMEM(all_marks.shape, WIDE),
            pltpu.VMEM((2, 1024, 256), NARROW), pltpu.VMEM((2, 1024, 128), NARROW),
            pltpu.VMEM((2, 1024, 128), NARROW), pltpu.VMEM((8, own, 256), NARROW),
        ],
        40, 24, 2,
    )
    whole, level = more[:3], level + more[3:]
    mid_own, ffn_in, *more = call(
        middle_kernel,
        "middle",
        [
            shape(own, width, dtype=WIDE), shape(8, own, width), *whole_shapes, *whole_shapes[:2],
            *level_shapes,
        ],
        (mixed, out_all, x_own, all_gains, *shards, *level[3:8]),
        [
            pltpu.VMEM((8, own, 256), NARROW), pltpu.VMEM((256, width), NARROW),
            pltpu.VMEM((own, width), NARROW), pltpu.VMEM(gains_shape, WIDE),
            pltpu.VMEM((2, ROWS, width), NARROW), *Fold.scratch(width),
        ],
        52, 32, 3,
    )
    whole, level = whole + more[:5], level + more[5:]
    hidden, grads_pre, parts, ends_a, *more = call(
        ffn_kernel,
        "ffn",
        [
            shape(8, own, ff // 4), shape(8, own, ff // 2), shape(12, 4, 4, chunk, LANES),
            shape(4, 4, 3, chunk, LANES),
            whole_shapes[2], *whole_shapes,
        ],
        (ffn_in, dy, *whole, *level[8:]),
        [
            pltpu.VMEM((8, own, width), NARROW), pltpu.VMEM((8, own, width), NARROW),
            pltpu.VMEM((2, 4, 4, LANES, chunk), NARROW), pltpu.VMEM((2, 4, 4, LANES, chunk), NARROW),
            pltpu.VMEM((2, chunk, width), NARROW), pltpu.VMEM((3, 8, own, chunk), NARROW),
            pltpu.VMEM((3, chunk, 8 * own), NARROW), pltpu.VMEM((3, 16, chunk, LANES), NARROW),
        ],
        48, 160, 4,
    )
    whole = whole + more
    fold_scratch = Fold.scratch(width)
    grad_mid_own, grad_mid, gain_ffn_part, ends_c, mates_b, mates_e = call(
        back_kernel,
        "back",
        [
            shape(own, width, dtype=WIDE), shape(8, own, width), shape(8, width, dtype=WIDE),
            shape(5, 4, 3, chunk, LANES), shape(4, 4, 2, chunk, LANES), shape(2, 4, 2, chunk, LANES),
        ],
        (grads_pre, mid_own, cot_own, all_gains, parts, ends_a, *whole[0::3], *whole[1::3]),
        [
            pltpu.VMEM((8, own, ff // 2), NARROW), pltpu.VMEM((4, 4, LANES, ff // 2), NARROW),
            pltpu.VMEM((own, width), WIDE), pltpu.VMEM((own, width), NARROW),
            pltpu.VMEM(gains_shape, WIDE), pltpu.VMEM((2, ROWS, width), NARROW),
            pltpu.VMEM((8, width), WIDE), *middle_scratch(1, 4), *middle_scratch(1, 2), *fold_scratch,
        ],
        48, 32, 5,
    )
    grad_proj, parts_q, sums_o, out_home, ends_d, mates_c, outer_b, outer_e, first_sums = call(
        attend_back_kernel,
        "attend_back",
        [
            shape(8, own, 512), shape(4, 4, 512, LANES), shape(4, 256, LANES),
            shape(own, width),
            shape(3, 4, 3, chunk, LANES), shape(3, 4, 2, chunk, LANES), shape(4, 4, chunk, LANES),
            shape(2, 4, chunk, LANES), shape(4, 3, chunk, LANES),
        ],
        (
            grad_mid, queries, keys, values, all_marks, inverse, out_all, mixed, attn_in, hidden, mid_own, parts,
            ends_a, ends_c, mates_b, mates_e, *whole[2::3],
        ),
        [
            pltpu.VMEM((8, own, width), NARROW), pltpu.VMEM((2, 1024, 256), NARROW),
            pltpu.VMEM((2, 1024, 128), NARROW), pltpu.VMEM((2, 1024, 128), NARROW),
            pltpu.VMEM(all_marks.shape, WIDE), pltpu.VMEM(inverse.shape, WIDE),
            pltpu.VMEM((256, width), NARROW), pltpu.VMEM((8, own, 256), NARROW),
            pltpu.VMEM((8, own, ff // 4), NARROW), pltpu.VMEM((ff // 4, width), NARROW),
            pltpu.VMEM((8, own, 512), NARROW), pltpu.VMEM((1024, 128), WIDE),
            pltpu.VMEM((1024, 128), WIDE),
            pltpu.VMEM((4, 4, 512, LANES), NARROW), pltpu.VMEM((4, 4, 256, LANES), NARROW),
            pltpu.VMEM((2, 4, 256, LANES), NARROW), *[pltpu.VMEM((4, 256, LANES), NARROW)] * 2,
            pltpu.VMEM((own, width), WIDE), pltpu.VMEM((own, width), NARROW), *middle_scratch(1, 3), *middle_scratch(2, 4),
            *middle_scratch(2, 2), *[pltpu.VMEM((3, 4, chunk, LANES), NARROW)] * 3, *fold_scratch,
        ],
        48, 128, 6,
    )
    grad_home, gain_sums, _, _, _, *sums = call(
        end_kernel,
        "end",
        [
            shape(own, width), shape(8, LANES, dtype=WIDE), shape(3, 4, 2, chunk, LANES),
            shape(3, 4, chunk, LANES), shape(3, 4, chunk, LANES),
            *[shape(4, 3, chunk, LANES)] * 3, shape(4, 256, LANES), shape(4, 512, LANES),
        ],
        (
            grad_proj, qkv_all, x_own, all_gains, grad_mid_own, gain_ffn_part, parts, parts_q, sums_o,
            ends_a, ends_c, ends_d, mates_b, mates_c, mates_e, outer_b, outer_e,
        ),
        [
            pltpu.VMEM((8, own, 512), NARROW), pltpu.VMEM(qkv_all.shape, NARROW),
            pltpu.VMEM((own, width), NARROW), pltpu.VMEM(gains_shape, WIDE),
            pltpu.VMEM((own, width), WIDE), pltpu.VMEM((own, width), NARROW),
            pltpu.VMEM((8, width), WIDE), pltpu.VMEM((10, 8, width), WIDE),
            *[pltpu.VMEM((12, 4, chunk, LANES), NARROW)] * 3,
            *[pltpu.VMEM((4, 512, LANES), NARROW)] * 2, pltpu.VMEM((2, 4, 512, LANES), NARROW),
            pltpu.VMEM((4, 512, LANES), NARROW),
            *middle_scratch(1, 3), *middle_scratch(2, 3), *middle_scratch(2, 3), *fold_scratch,
        ],
        88, 72, 7,
    )
    grad_gate, grad_up, grad_down, grad_qkv, grad_out = pl.pallas_call(
        home_kernel,
        out_shape=[
            jax.ShapeDtypeStruct(array.shape, WIDE) for array in (w_gate, w_up, w_down, wqkv, wo)
        ],
        in_specs=[ANYWHERE] * 6,
        scratch_shapes=[
            *[pltpu.VMEM((4, 4, chunk, LANES), NARROW)] * 3, pltpu.VMEM((4, 256, LANES), NARROW),
            pltpu.VMEM((4, 512, LANES), NARROW), pltpu.SemaphoreType.DMA((8,)),
        ],
        compiler_params=pltpu.CompilerParams(vmem_limit_bytes=62 << 20),
        name="home",
    )(first_sums, *sums)
    return (
        out_home.reshape(hidden_in.shape),
        grad_home.reshape(hidden_in.shape),
        gain_sums[0],
        grad_qkv,
        grad_out,
        gain_sums[1],
        grad_gate,
        grad_up,
        grad_down,
    )


def body(*shards):
    inner = KV_HEADS // lax.axis_size("tp")
    near = (lax.axis_size("fsdp"), lax.axis_size("ctx"), lax.axis_size("tp"), inner)
    return (near_body if near == (4, 4, 2, 4) else general_body)(*shards)


def solution(mesh):
    return jax.shard_map(
        body,
        mesh=mesh,
        in_specs=(
            P(None, "fsdp", ("ctx", "tp"), None),
            P(None, "fsdp", ("ctx", "tp"), None),
            P(None, "fsdp", None),
            P(None, "fsdp", "ctx"),
            P(("fsdp", "ctx")),
            P(("fsdp", "ctx"), "tp"),
            P("tp", ("fsdp", "ctx")),
            P(("fsdp", "ctx")),
            P(("fsdp", "ctx"), "tp"),
            P(("fsdp", "ctx"), "tp"),
            P("tp", ("fsdp", "ctx")),
        ),
        out_specs=(
            P(None, "fsdp", ("ctx", "tp"), None),
            P(None, "fsdp", ("ctx", "tp"), None),
            P(("fsdp", "ctx")),
            P(("fsdp", "ctx"), "tp"),
            P("tp", ("fsdp", "ctx")),
            P(("fsdp", "ctx")),
            P(("fsdp", "ctx"), "tp"),
            P(("fsdp", "ctx"), "tp"),
            P("tp", ("fsdp", "ctx")),
        ),
        check_vma=False,
    )
```
